32 devices in a mesh: dp: 8 (over z, x), tensor: 4 (over y, core).
Axes of the slice: x: 2, y: 2, z: 4, core: 2. Of those that a mesh axis runs over, the one named last changes fastest.
Arguments:
- tokens: bfloat16 [37824, 768], P(('dp', 'tensor')), may hold values from -6 to 6
- qkv_weight: bfloat16 [3, 768, 768], P(None, 'dp', 'tensor'), may hold values from -0.21875 to 0.21875
- out_weight: bfloat16 [768, 768], P('tensor', 'dp'), may hold values from -1.75 to 1.75
- router: bfloat16 [768, 8], P('tensor', 'dp'), may hold values from -0.109375 to 0.109375
- norm_params: bfloat16 [4, 768], P('tensor', 'dp'), may hold values from -1 to 1.5, as said below
- expert_in: bfloat16 [8, 768, 3072], P('dp', None, 'tensor'), may hold values from -2 to 2
- expert_out: bfloat16 [8, 3072, 768], P('dp', 'tensor'), may hold values from -1.75 to 1.75
- cotangent: bfloat16 [37824, 768], P(('dp', 'tensor')), may hold values from -6 to 6
Outputs:
- output: bfloat16 [37824, 768], P(('dp', 'tensor'))
- input_grad: float32 [37824, 768], P(('dp', 'tensor'))
- qkv_grad: float32 [3, 768, 768], P(None, 'dp', 'tensor')
- out_grad: float32 [768, 768], P('tensor', 'dp')
- router_grad: float32 [768, 8], P('tensor', 'dp')
- norm_grad: float32 [4, 768], P('tensor', 'dp')
- expert_in_grad: float32 [8, 768, 3072], P('dp', None, 'tensor')
- expert_out_grad: float32 [8, 3072, 768], P('dp', 'tensor')
The draws below stay inside these ranges and needn't reach their ends.
Inputs may be any that keep to these rules, and one draw needn't show every extreme that they name: `norm_params`: rows 0 and 2 are gains, rows 1 and 3 biases.
All inputs are finite; a program needn't handle non-finite values.
Results may differ from the reference program's by a relative error of at most 0.025.
Values may be sent and summed in bfloat16 or wider, within the bound.
No kernel may reach another device: no remote copies, remote signals or barrier semaphores. Data moves between devices by JAX's collectives and lax.ppermute only.
A program may use at most 128 MiB of HBM per device.

```python
import jax
import jax.numpy as jnp
from jax import lax

D = 768
HEADS = 12
HEAD_DIM = 64
FF = 3072
SEQ = 197
IMG_DP = 24
EXPERTS = 8
IMAGES = 192
TOKENS = 37824
N_TENSOR = 4


def draw_norm_params(key, part):
    key = jax.random.fold_in(key, 11)
    gain_key, shift_key = jax.random.split(key)
    gains = jax.random.uniform(gain_key, (2, D), jnp.float32, 0.5, 1.5)
    shifts = 0.1 * jax.random.normal(shift_key, (2, D), jnp.float32)
    return jnp.stack([gains[0], shifts[0], gains[1], shifts[1]]).astype(jnp.bfloat16)


def block_scale(rng, extent, cuts, smallest, high):
    def one(dim, shards_of):
        steps = jax.random.uniform(jax.random.fold_in(jax.random.fold_in(rng, 6), dim), (shards_of,), jnp.float32, smallest / len(cuts), high / len(cuts))
        return jnp.repeat(jnp.exp(steps), extent[dim] // shards_of).reshape((-1,) + (1,) * (len(extent) - dim - 1))

    loudness = one(*cuts[0])
    for cut in cuts[1:]:
        loudness = loudness * one(*cut)
    return loudness


def scatter_about(key, dims, width, limit, pieces=(), dtype=jnp.bfloat16):
    gain = block_scale(key, dims, pieces, -0.22, 0.18) if pieces else 1.0
    drawn = jax.random.normal(key, dims, jnp.float32) * width * gain
    return jnp.minimum(jnp.maximum(drawn, -limit), limit).astype(dtype)


def setup_inputs(seed: int = 0) -> dict:
    key_of = jax.random.split(jax.random.key(seed), 9)
    return {
        "tokens": scatter_about(key_of[0], (TOKENS, D), 1.0, 6.0, ((0, 32),)),
        "qkv_weight": scatter_about(key_of[1], (3, D, D), D ** -0.5, 0.21875, ((1, 8), (2, 4))),
        "out_weight": scatter_about(key_of[2], (D, D), (max(D // 64, 1)) ** -0.5, 1.75, ((0, 4), (1, 8))),
        "router": scatter_about(key_of[3], (D, EXPERTS), (4 * D) ** -0.5, 0.109375, ((0, 4), (1, 8))),
        "norm_params": draw_norm_params(jax.random.fold_in(key_of[8], 71), 0),
        "expert_in": scatter_about(key_of[5], (EXPERTS, D, FF), (max(D // 96, 1)) ** -0.5, 2.0, ((0, 8), (2, 4))),
        "expert_out": scatter_about(key_of[6], (EXPERTS, FF, D), (max(FF // 256, 1)) ** -0.5, 1.75, ((0, 8), (1, 4))),
        "cotangent": scatter_about(key_of[7], (TOKENS, D), 1.0, 6.0, ((0, 32),)),
    }


@jax.custom_vjp
def low(v):
    return lax.optimization_barrier(v.astype(jnp.bfloat16)).astype(jnp.float32)

@jax.custom_vjp
def low_back(v):
    return v

def low_keep(v):
    return (low(v), None)

def low_pass(kept, grad):
    return (grad,)

def back_keep(v):
    return (v, None)

def back_low(kept, grad):
    return (low(grad),)
low.defvjp(low_keep, low_pass)
low_back.defvjp(back_keep, back_low)

def product(formula, left_side, right_side):
    return jnp.einsum(formula, left_side, right_side, precision=lax.Precision.HIGHEST)

def layer_norm(values, gain_row, shift_row):
    centre = lax.optimization_barrier(jnp.mean(values, axis=-1, keepdims=True))
    centred = values - centre
    spread = lax.optimization_barrier(jnp.mean(centred * centred, axis=-1, keepdims=True))
    return centred * lax.rsqrt(spread + 1e-06) * gain_row + shift_row

def softmax_over(values, axis_index):
    highest = lax.optimization_barrier(jnp.max(values, axis=axis_index, keepdims=True))
    scaled = jnp.exp(values - highest)
    return scaled / lax.optimization_barrier(jnp.sum(scaled, axis=axis_index, keepdims=True))

def block_forward(params, image_block):
    qkv_w, out_w, router_w, norm_w, first_w, second_w = params
    images = image_block.shape[0]
    normed_one = low(layer_norm(image_block, norm_w[0], norm_w[1]))
    projected = low(low_back(product('isd,kdc->kisc', normed_one, qkv_w)))
    shaped = projected.reshape(3, images, SEQ, HEADS, HEAD_DIM)
    scores = low_back(product('iqhc,ikhc->ihqk', shaped[0], shaped[1]) * HEAD_DIM ** (-0.5))
    weights = low(softmax_over(scores, -1))
    mixed_heads = product('ihqk,ikhc->iqhc', weights, shaped[2]).reshape(images, SEQ, HEADS * HEAD_DIM)
    mixed_heads = low(low_back(mixed_heads))
    residual = image_block + low_back(product('isc,cd->isd', mixed_heads, out_w))
    normed_two = low(layer_norm(residual, norm_w[2], norm_w[3]))
    logits = low_back(product('isd,de->ise', normed_two, router_w))
    dispatch = low(softmax_over(logits, 1))
    combine = low(softmax_over(logits, 2))
    slot_inputs = low(low_back(product('ise,isd->ied', dispatch, normed_two)))
    pre_act = low_back(product('ied,edf->ief', slot_inputs, first_w))
    hidden = low(jax.nn.gelu(pre_act, approximate=False))
    returned = low(low_back(product('ief,efd->ied', hidden, second_w)))
    mixture = low_back(product('ise,ied->isd', combine, returned))
    return residual + mixture

def reference(tokens, qkv_weight, out_weight, router, norm_params, expert_in, expert_out, cotangent):
    per_block = max(IMG_DP // N_TENSOR, 1)
    inputs = tokens.astype(jnp.float32).reshape(IMAGES // per_block, per_block, SEQ, D)
    params = (qkv_weight.astype(jnp.float32), out_weight.astype(jnp.float32), router.astype(jnp.float32), norm_params.astype(jnp.float32), expert_in.astype(jnp.float32), expert_out.astype(jnp.float32))

    def forward(image_blocks, weights_all):
        one_block = jax.checkpoint(lambda image_block: block_forward(weights_all, image_block))
        return lax.map(one_block, image_blocks)
    outputs, pullback = jax.vjp(forward, inputs, params)
    grad_blocks, grad_params = pullback(cotangent.astype(jnp.float32).reshape(inputs.shape))
    return (outputs.reshape(TOKENS, D).astype(jnp.bfloat16), grad_blocks.reshape(TOKENS, D), grad_params[0], grad_params[1], grad_params[2], grad_params[3], grad_params[4], grad_params[5])
```

```python
import functools

import jax
import jax.numpy as jnp
from jax import lax
from jax.experimental import pallas as pl
from jax.experimental.pallas import tpu as pltpu
from jax.sharding import PartitionSpec as P

HEAD_DIM = 64
SEQ = 197
PAD = 208
SLOT_ROWS = 16
AXES = ("dp", "tensor")
BF = jnp.bfloat16
F32 = jnp.float32
LAST = (((1,), (1,)), ((), ()))
FIRST = (((0,), (0,)), ((), ()))
MIDDLE = (((1,), (0,)), ((), ()))
VMEM_LIMIT = 56 * 1024 * 1024


def dot(a, b, dims=MIDDLE):
    return lax.dot_general(a, b, dims, preferred_element_type=F32)


def params():
    return pltpu.CompilerParams(vmem_limit_bytes=VMEM_LIMIT)


def whole(shape):
    return pl.BlockSpec(shape, lambda i: (0,) * len(shape))


def per_image(shape, column=0):
    return pl.BlockSpec((1,) + shape, lambda i: (i, 0, column))


def layer_stats(values):
    centre = jnp.mean(values, axis=-1, keepdims=True)
    centred = values - centre
    spread = jnp.mean(centred * centred, axis=-1, keepdims=True)
    inv_std = lax.rsqrt(spread + 1e-06)
    return centred * inv_std, inv_std


def lane_ids(shape):
    return lax.broadcasted_iota(jnp.int32, shape, len(shape) - 1)


def row_ids(shape):
    return lax.broadcasted_iota(jnp.int32, shape, len(shape) - 2)


def norm_kernel(x_ref, norms_ref, out_ref):
    unit, _ = layer_stats(x_ref[0].astype(F32))
    out_ref[0] = (unit * norms_ref[0:1, :] + norms_ref[1:2, :]).astype(BF)


def first_norm(x_img, norms):
    images, rows, width = x_img.shape
    return pl.pallas_call(
        norm_kernel,
        grid=(images,),
        in_specs=[per_image((rows, width)), whole(norms.shape)],
        out_specs=per_image((rows, width)),
        out_shape=jax.ShapeDtypeStruct((images, rows, width), BF),
        compiler_params=params(),
        name="first_norm",
    )(x_img, norms)


def attend_kernel(pairs, n_ref, w_ref, qkv_ref, mixed_ref, probs_ref):
    span = pairs * 128
    rows = n_ref.shape[1]
    proj = dot(n_ref[0], w_ref[...])
    low = lane_ids((rows, 128)) < HEAD_DIM
    key_ok = row_ids((rows, rows)) < SEQ
    zero = jnp.zeros((rows, 128), BF)
    for p in range(pairs):
        at = slice(p * 128, (p + 1) * 128)
        q = (proj[:, p * 128 : (p + 1) * 128] * HEAD_DIM ** (-0.5)).astype(BF)
        k = proj[:, span + p * 128 : span + (p + 1) * 128].astype(BF)
        v = proj[:, 2 * span + p * 128 : 2 * span + (p + 1) * 128].astype(BF)
        qkv_ref[0, :, at] = q
        qkv_ref[0, :, span + p * 128 : span + (p + 1) * 128] = k
        qkv_ref[0, :, 2 * span + p * 128 : 2 * span + (p + 1) * 128] = v
        v_t = v.T
        mixed_t = []
        for h in range(2):
            q_one = jnp.where(low, q, zero) if h == 0 else jnp.where(low, zero, q)
            scores = jnp.where(key_ok, dot(k, q_one, LAST), -1e30)
            highest = jnp.max(scores, axis=0, keepdims=True)
            scaled = jnp.exp(scores - highest)
            inv = 1.0 / jnp.sum(scaled, axis=0, keepdims=True)
            weights = (scaled * inv).astype(BF)
            probs_ref[0, 2 * p + h] = weights
            mixed_t.append(dot(v_t[h * HEAD_DIM : (h + 1) * HEAD_DIM, :], weights))
        mixed_ref[0, :, at] = jnp.concatenate(mixed_t, axis=0).T.astype(BF)


def attend(normed, weights):
    images, rows, width = normed.shape
    span = weights.shape[1] // 3
    heads = span // HEAD_DIM
    return pl.pallas_call(
        functools.partial(attend_kernel, span // 128),
        grid=(images,),
        in_specs=[per_image((rows, width)), whole(weights.shape)],
        out_specs=[
            per_image((rows, 3 * span)),
            per_image((rows, span)),
            pl.BlockSpec((1, heads, rows, rows), lambda i: (i, 0, 0, 0)),
        ],
        out_shape=[
            jax.ShapeDtypeStruct((images, rows, 3 * span), BF),
            jax.ShapeDtypeStruct((images, rows, span), BF),
            jax.ShapeDtypeStruct((images, heads, rows, rows), BF),
        ],
        compiler_params=params(),
        name="attend",
    )(normed, weights)


def softmaxes(logits):
    ok = lane_ids(logits.shape) < SEQ
    masked = jnp.where(ok, logits, -1e30)
    up = jnp.exp(masked - jnp.max(masked, axis=1, keepdims=True))
    dispatch = up / jnp.sum(up, axis=1, keepdims=True)
    up = jnp.exp(logits - jnp.max(logits, axis=0, keepdims=True))
    combine = up / jnp.sum(up, axis=0, keepdims=True)
    return dispatch, combine


def place_rows(experts, image, offset):
    shape = (experts * SLOT_ROWS, experts)
    return (row_ids(shape) == lane_ids(shape) * SLOT_ROWS + offset + image).astype(BF)


def pick_rows(experts, image, offset):
    shape = (experts, experts * SLOT_ROWS)
    return (lane_ids(shape) == row_ids(shape) * SLOT_ROWS + offset + image).astype(BF)


def route_kernel(
    half, x_ref, m1_ref, m2_ref, out_w_ref, norms_ref, router_ref, g_ref, y_ref, logits_ref, send_ref, acc
):
    image = pl.program_id(0)
    experts = router_ref.shape[0]
    out_w = out_w_ref[...]
    attn = dot(m1_ref[0], out_w[:, :half], LAST) + dot(m2_ref[0], out_w[:, half:], LAST)
    y = x_ref[0].astype(F32) + attn
    y_ref[0] = y
    unit, _ = layer_stats(y)
    normed = (unit * norms_ref[2:3, :] + norms_ref[3:4, :]).astype(BF)
    logits = dot(router_ref[...], normed, LAST)
    logits_ref[0] = logits
    dispatch, combine = softmaxes(logits)
    slots = dot(dispatch.astype(BF), normed).astype(BF)
    grad_returned = dot(combine.astype(BF), g_ref[0]).astype(BF)
    placed = dot(place_rows(experts, image, 0), slots) + dot(
        place_rows(experts, image, SLOT_ROWS // 2), grad_returned
    )

    @pl.when(image == 0)
    def _():
        acc[...] = placed

    @pl.when(image > 0)
    def _():
        acc[...] += placed

    @pl.when(image == pl.num_programs(0) - 1)
    def _():
        send_ref[...] = acc[...].astype(BF)


def route(x_img, mixed_one, mixed_two, out_w, norms, router, g_img):
    images, rows, width = x_img.shape
    experts = router.shape[0]
    half = mixed_one.shape[2]
    return pl.pallas_call(
        functools.partial(route_kernel, half),
        grid=(images,),
        in_specs=[
            per_image((rows, width)),
            per_image((rows, half)),
            per_image((rows, width - half)),
            whole(out_w.shape),
            whole(norms.shape),
            whole(router.shape),
            per_image((rows, width)),
        ],
        out_specs=[
            per_image((rows, width)),
            per_image((experts, rows)),
            whole((experts * SLOT_ROWS, width)),
        ],
        out_shape=[
            jax.ShapeDtypeStruct((images, rows, width), F32),
            jax.ShapeDtypeStruct((images, experts, rows), F32),
            jax.ShapeDtypeStruct((experts * SLOT_ROWS, width), BF),
        ],
        scratch_shapes=[pltpu.VMEM((experts * SLOT_ROWS, width), F32)],
        compiler_params=params(),
        name="route",
    )(x_img, mixed_one, mixed_two, out_w, norms, router, g_img)


def split_rows(blocks):
    wide = blocks.astype(F32)
    half = SLOT_ROWS // 2
    flat = (blocks.shape[0] * half, blocks.shape[2])
    return wide[:, :half].reshape(flat).astype(BF), wide[:, half:].reshape(flat).astype(BF)


def join_rows(ones, twos):
    half = SLOT_ROWS // 2
    shape = (ones.shape[0] // half, half, ones.shape[1])
    return jnp.concatenate([ones.reshape(shape), twos.reshape(shape)], axis=1).astype(BF)


def gelu_parts(pre):
    cdf = 0.5 * (1.0 + lax.erf(pre * (0.5**0.5)))
    density = jnp.exp(-0.5 * pre * pre) * 0.3989422804014327
    return pre * cdf, cdf + pre * density


def expert_kernel(own_ref, near_ref, w1_ref, w2_ref, keep_ref, send_ref, d1_ref, d2_ref):
    count = own_ref.shape[0]
    blocks = jnp.concatenate([own_ref[...], near_ref[...]], axis=0)
    slots, grads = split_rows(blocks)
    pre = dot(slots, w1_ref[...])
    hidden, slope = gelu_parts(pre)
    hidden = hidden.astype(BF)
    returned = dot(hidden, w2_ref[...])
    grad_pre = (dot(grads, w2_ref[...], LAST) * slope).astype(BF)
    grad_slots = dot(grad_pre, w1_ref[...], LAST)
    joined = join_rows(returned, grad_slots)
    keep_ref[...] = joined[:count]
    send_ref[...] = joined[count:]
    d1_ref[...] = dot(slots, grad_pre, FIRST)
    d2_ref[...] = dot(hidden, grads, FIRST)


def run_expert(own, near, first_weight, second_weight):
    width, units = first_weight.shape
    return pl.pallas_call(
        expert_kernel,
        out_shape=[
            jax.ShapeDtypeStruct(own.shape, BF),
            jax.ShapeDtypeStruct(near.shape, BF),
            jax.ShapeDtypeStruct((width, units), F32),
            jax.ShapeDtypeStruct((units, width), F32),
        ],
        compiler_params=params(),
        name="expert",
    )(own, near, first_weight, second_weight)


def moe_back_kernel(
    half,
    y_ref,
    g_ref,
    logits_ref,
    back_ref,
    norms_ref,
    router_ref,
    out_w_ref,
    m1_ref,
    m2_ref,
    out_ref,
    grad_y_ref,
    grad_mixed_ref,
    out_grad_ref,
    small_ref,
):
    image = pl.program_id(0)
    experts = router_ref.shape[0]
    y = y_ref[0]
    g_low = g_ref[0]
    back = back_ref[...]
    returned = dot(pick_rows(experts, image, 0), back).astype(BF)
    grad_slots = dot(pick_rows(experts, image, SLOT_ROWS // 2), back).astype(BF)
    dispatch, combine = softmaxes(logits_ref[0])
    unit, inv_std = layer_stats(y)
    gain = norms_ref[2:3, :]
    normed = (unit * gain + norms_ref[3:4, :]).astype(BF)
    out_ref[0] = (y + dot(combine.astype(BF), returned, FIRST)).astype(BF)
    grad_combine = dot(returned, g_low, LAST)
    grad_dispatch = dot(grad_slots, normed, LAST)
    grad_logits = dispatch * (
        grad_dispatch - jnp.sum(grad_dispatch * dispatch, axis=1, keepdims=True)
    ) + combine * (grad_combine - jnp.sum(grad_combine * combine, axis=0, keepdims=True))
    grad_logits = grad_logits.astype(BF)
    router_grad = dot(grad_logits, normed)
    grad_two = dot(dispatch.astype(BF), grad_slots, FIRST) + dot(grad_logits, router_ref[...], FIRST)
    gain_grad = jnp.sum(grad_two * unit, axis=0, keepdims=True)
    shift_grad = jnp.sum(grad_two, axis=0, keepdims=True)
    scaled = grad_two * gain
    mean_one = jnp.mean(scaled, axis=-1, keepdims=True)
    mean_two = jnp.mean(scaled * unit, axis=-1, keepdims=True)
    grad_y = g_low.astype(F32) + inv_std * (scaled - mean_one - unit * mean_two)
    grad_y_ref[0] = grad_y
    grad_attn = grad_y.astype(BF)
    grad_mixed_ref[0] = dot(grad_attn, out_w_ref[...]).astype(BF)

    @pl.when(image == 0)
    def _():
        out_grad_ref[...] = jnp.zeros_like(out_grad_ref)
        small_ref[...] = jnp.zeros_like(small_ref)

    out_grad_ref[:, :half] += dot(grad_attn, m1_ref[0], FIRST)
    out_grad_ref[:, half:] += dot(grad_attn, m2_ref[0], FIRST)
    small_ref[0:1, :] += gain_grad
    small_ref[1:2, :] += shift_grad
    small_ref[8 : 8 + experts, :] += router_grad


def moe_back(y, g_img, logits, back, norms, router, out_w, mixed_one, mixed_two):
    images, rows, width = y.shape
    experts = router.shape[0]
    half = mixed_one.shape[2]
    return pl.pallas_call(
        functools.partial(moe_back_kernel, half),
        grid=(images,),
        in_specs=[
            per_image((rows, width)),
            per_image((rows, width)),
            per_image((experts, rows)),
            whole(back.shape),
            whole(norms.shape),
            whole(router.shape),
            whole(out_w.shape),
            per_image((rows, half)),
            per_image((rows, width - half)),
        ],
        out_specs=[
            per_image((rows, width)),
            per_image((rows, width)),
            per_image((rows, width)),
            whole((width, width)),
            whole((8 + experts, width)),
        ],
        out_shape=[
            jax.ShapeDtypeStruct((images, rows, width), BF),
            jax.ShapeDtypeStruct((images, rows, width), F32),
            jax.ShapeDtypeStruct((images, rows, width), BF),
            jax.ShapeDtypeStruct((width, width), F32),
            jax.ShapeDtypeStruct((8 + experts, width), F32),
        ],
        compiler_params=params(),
        name="moe_back",
    )(y, g_img, logits, back, norms, router, out_w, mixed_one, mixed_two)


def attend_back_kernel(pairs, n_ref, qkv_ref, probs_ref, mixed_ref, gm_ref, grads_ref, dw_ref):
    image = pl.program_id(0)
    span = pairs * 128
    rows = n_ref.shape[1]
    low = lane_ids((rows, 128)) < HEAD_DIM
    zero = jnp.zeros((rows, 128), BF)
    minus = jnp.full((rows, 128), -1.0, BF)
    for p in range(pairs):
        at = slice(p * 128, (p + 1) * 128)
        q = qkv_ref[0, :, at]
        k = qkv_ref[0, :, span + p * 128 : span + (p + 1) * 128]
        v = qkv_ref[0, :, 2 * span + p * 128 : 2 * span + (p + 1) * 128]
        gm = gm_ref[0, :, at]
        inner = pltpu.roll(gm.astype(F32) * mixed_ref[0, :, at].astype(F32), HEAD_DIM, 1).astype(BF)
        k_t = k.T
        grad_q_t, grad_k, grad_v = [], 0.0, 0.0
        for h in range(2):
            mine = low if h == 0 else jnp.logical_not(low)
            weights = probs_ref[0, 2 * p + h]
            centred = dot(jnp.where(mine, v, minus), jnp.where(mine, gm, inner), LAST)
            grad_scores = (weights.astype(F32) * centred).astype(BF)
            grad_v = grad_v + dot(weights, jnp.where(mine, gm, zero))
            grad_k = grad_k + dot(grad_scores, jnp.where(mine, q, zero))
            grad_q_t.append(dot(k_t[h * HEAD_DIM : (h + 1) * HEAD_DIM, :], grad_scores))
        grad_q = jnp.concatenate(grad_q_t, axis=0).T * HEAD_DIM ** (-0.5)
        grads_ref[0, :, at] = grad_q.astype(BF)
        grads_ref[0, :, span + p * 128 : span + (p + 1) * 128] = grad_k.astype(BF)
        grads_ref[0, :, 2 * span + p * 128 : 2 * span + (p + 1) * 128] = grad_v.astype(BF)

    @pl.when(image == 0)
    def _():
        dw_ref[...] = jnp.zeros_like(dw_ref)

    dw_ref[...] += dot(n_ref[0], grads_ref[0], FIRST)


def attend_back(normed, qkv, probs, mixed, grad_mixed, piece):
    images, rows, width = normed.shape
    span = mixed.shape[2]
    heads = span // HEAD_DIM
    return pl.pallas_call(
        functools.partial(attend_back_kernel, span // 128),
        grid=(images,),
        in_specs=[
            per_image((rows, width)),
            per_image((rows, 3 * span)),
            pl.BlockSpec((1, heads, rows, rows), lambda i: (i, 0, 0, 0)),
            per_image((rows, span)),
            per_image((rows, span), piece),
        ],
        out_specs=[per_image((rows, 3 * span)), whole((width, 3 * span))],
        out_shape=[
            jax.ShapeDtypeStruct((images, rows, 3 * span), BF),
            jax.ShapeDtypeStruct((width, 3 * span), F32),
        ],
        compiler_params=params(),
        name="attend_back",
    )(normed, qkv, probs, mixed, grad_mixed)


def input_back_kernel(x_ref, gy_ref, p1_ref, p2_ref, w1_ref, w2_ref, norms_ref, out_ref, small_ref):
    image = pl.program_id(0)
    unit, inv_std = layer_stats(x_ref[0].astype(F32))
    grad_one = dot(p1_ref[0], w1_ref[...], LAST) + dot(p2_ref[0], w2_ref[...], LAST)
    scaled = grad_one * norms_ref[0:1, :]
    mean_one = jnp.mean(scaled, axis=-1, keepdims=True)
    mean_two = jnp.mean(scaled * unit, axis=-1, keepdims=True)
    out_ref[0] = gy_ref[0] + inv_std * (scaled - mean_one - unit * mean_two)

    @pl.when(image == 0)
    def _():
        small_ref[...] = jnp.zeros_like(small_ref)

    small_ref[0:1, :] += jnp.sum(grad_one * unit, axis=0, keepdims=True)
    small_ref[1:2, :] += jnp.sum(grad_one, axis=0, keepdims=True)


def input_back(x_img, grad_y, grads_one, grads_two, weight_one, weight_two, norms):
    images, rows, width = x_img.shape
    return pl.pallas_call(
        input_back_kernel,
        grid=(images,),
        in_specs=[
            per_image((rows, width)),
            per_image((rows, width)),
            per_image(grads_one.shape[1:]),
            per_image(grads_two.shape[1:]),
            whole(weight_one.shape),
            whole(weight_two.shape),
            whole(norms.shape),
        ],
        out_specs=[per_image((rows, width)), whole((8, width))],
        out_shape=[
            jax.ShapeDtypeStruct((images, rows, width), F32),
            jax.ShapeDtypeStruct((8, width), F32),
        ],
        compiler_params=params(),
        name="input_back",
    )(x_img, grad_y, grads_one, grads_two, weight_one, weight_two, norms)


def swap(value, dp_size, tensor_size, dp_mask, tensor_mask):
    pairs = [
        (d * tensor_size + t, (d ^ dp_mask) * tensor_size + (t ^ tensor_mask))
        for d in range(dp_size)
        for t in range(tensor_size)
    ]
    return lax.ppermute(value, AXES, pairs)


def steps_of(dp_size):
    bits = dp_size.bit_length() - 1
    down = list(range(bits))[::-1]
    return [down, down[-1:] + down[:-1]]


def step_pairs(dp_size, tensor_size, step):
    orders = steps_of(dp_size)
    return [
        (d * tensor_size + t, (d ^ (1 << orders[t % 2][step])) * tensor_size + t)
        for d in range(dp_size)
        for t in range(tensor_size)
    ]


def places(dp_size, dp_index, core):
    away = dp_index ^ jnp.arange(dp_size, dtype=jnp.int32)
    both = []
    for order in steps_of(dp_size):
        at = jnp.zeros_like(away)
        for step, bit in enumerate(order):
            at = at | (((away >> bit) & 1) << step)
        both.append(at)
    return jnp.where(core == 0, both[0], both[1]), jnp.where(core == 0, both[1], both[0])


def gather_steps(block, dp_size, tensor_size):
    held = block[None]
    for step in range(dp_size.bit_length() - 1):
        got = lax.ppermute(held, AXES, step_pairs(dp_size, tensor_size, step))
        held = jnp.concatenate([held, got], axis=0)
    return held


def scatter_steps(blocks, dp_size, tensor_size):
    held = blocks
    for step in range(dp_size.bit_length() - 1)[::-1]:
        half = 1 << step
        got = lax.ppermute(held[half:], AXES, step_pairs(dp_size, tensor_size, step))
        held = (held[:half].astype(F32) + got.astype(F32)).astype(BF)
    return held[0]


def assemble_kernel(part, core_ref, own_place, sib_place, own_ref, sib_ref, out_ref):
    core = core_ref[0]
    for k in range(own_ref.shape[0]):
        for place, ref, which in ((own_place, own_ref, core), (sib_place, sib_ref, 1 - core)):
            row = pl.multiple_of(2 * part * k + part * which, 16)
            out_ref[pl.ds(row, part), :] = ref[place[k], 0:part, :]


def assemble(own, sib, part, core, own_place, sib_place):
    return pl.pallas_call(
        functools.partial(assemble_kernel, part),
        in_specs=[pl.BlockSpec(memory_space=pltpu.SMEM)] * 3 + [pl.BlockSpec(memory_space=pltpu.VMEM)] * 2,
        out_shape=jax.ShapeDtypeStruct((own.shape[0] * 2 * part, own.shape[2]), BF),
        compiler_params=params(),
        name="assemble",
    )(core, own_place, sib_place, own, sib)


def deal_kernel(part, core_ref, own_place, sib_place, full_ref, own_ref, sib_ref):
    core = core_ref[0]
    for k in range(own_ref.shape[0]):
        for place, ref, which in ((own_place, own_ref, core), (sib_place, sib_ref, 1 - core)):
            row = pl.multiple_of(2 * part * k + part * which, 16)
            ref[place[k]] = full_ref[pl.ds(row, part), :].astype(BF)


def deal(full, part, dp_size, core, own_place, sib_place):
    shape = jax.ShapeDtypeStruct((dp_size, part, full.shape[1]), BF)
    return pl.pallas_call(
        functools.partial(deal_kernel, part),
        in_specs=[pl.BlockSpec(memory_space=pltpu.SMEM)] * 3 + [pl.BlockSpec(memory_space=pltpu.VMEM)],
        out_shape=[shape, shape],
        compiler_params=params(),
        name="deal",
    )(core, own_place, sib_place, full)


def gather_weights(qkv_weight, out_weight, router, norm_params, sizes, ids, tables):
    dp_size, tensor_size = sizes
    dp_index, _, core = ids
    rows = qkv_weight.shape[1]
    columns = qkv_weight.shape[2]
    width = rows * dp_size
    half = width // 2
    part = rows // 2
    turned = jnp.concatenate([qkv_weight, out_weight.T[None]], axis=0)
    turned = turned.transpose(1, 0, 2).reshape(rows, 4 * columns)
    small = jnp.concatenate(
        [jnp.pad(norm_params, ((0, 0), (0, 4 * columns - rows))), jnp.pad(router.T, ((0, 0), (0, 3 * columns)))],
        axis=0,
    )
    packed = jnp.concatenate([turned, jnp.pad(small, ((0, 14), (0, 0)))], axis=0)
    spread = lax.all_gather(packed, "tensor", axis=0)
    norm_cols = spread[:, rows, :rows]
    router_row = spread[:, rows + 1, :columns].reshape(1, width)
    by_kind = spread[:, :rows].reshape(tensor_size, rows, 4, columns)
    by_kind = lax.dynamic_slice_in_dim(by_kind, core * part, part, axis=1)
    by_kind = by_kind.transpose(1, 2, 0, 3).reshape(part, 4, width)
    one = by_kind[:, :3, :half].reshape(part, 3 * half)
    two = by_kind[:, :3, half:].reshape(part, 3 * half)
    out_rows = by_kind[:, 3]
    experts = dp_size * router.shape[1]
    extra_rows = -(-(4 + experts) // 16) * 16
    extra = jnp.zeros((extra_rows, 3 * half), BF)
    extra = lax.dynamic_update_slice(extra, norm_cols, (0, dp_index * rows))
    extra = lax.dynamic_update_slice(extra, router_row, (4 + dp_index, 0))
    got_one = gather_steps(jnp.concatenate([one, extra], axis=0), dp_size, tensor_size)
    sib_one = swap(got_one, dp_size, tensor_size, 0, 1)
    smalls = jnp.sum(got_one[:, part:, :width].astype(F32), axis=0)
    got_two = gather_steps(two, dp_size, tensor_size)
    sib_two = swap(got_two, dp_size, tensor_size, 0, 1)
    got_out = gather_steps(out_rows, dp_size, tensor_size)
    sib_out = swap(got_out, dp_size, tensor_size, 0, 1)
    weight_one = assemble(got_one, sib_one, part, *tables)
    weight_two = assemble(got_two, sib_two, part, *tables)
    out_w = assemble(got_out, sib_out, part, *tables)
    return weight_one, weight_two, out_w, smalls[:4], smalls[4 : 4 + experts].astype(BF)


def gather_weights_plain(qkv_weight, out_weight, router, norm_params):
    qkv = lax.all_gather(qkv_weight, "dp", axis=1, tiled=True)
    qkv = lax.all_gather(qkv, "tensor", axis=2, tiled=True)
    out_w, router, norms = (
        lax.all_gather(lax.all_gather(w, "dp", axis=1, tiled=True), "tensor", axis=0, tiled=True)
        for w in (out_weight, router, norm_params)
    )
    width = qkv.shape[1]
    half = width // 2
    one = qkv[:, :, :half].transpose(1, 0, 2).reshape(width, 3 * half)
    two = qkv[:, :, half:].transpose(1, 0, 2).reshape(width, 3 * half)
    return one, two, out_w.T, norms.astype(F32), router.T


def scatter_weight(full, part, sizes, tables):
    dp_size, tensor_size = sizes
    own, sib = deal(full, part, dp_size, *tables)
    got = swap(sib, dp_size, tensor_size, 0, 1)
    return scatter_steps((own.astype(F32) + got.astype(F32)).astype(BF), dp_size, tensor_size)


def sum_small(values, sizes):
    dp_size, tensor_size = sizes
    mask = 1
    while mask < tensor_size:
        values = values + swap(values, dp_size, tensor_size, 0, mask)
        mask *= 2
    mask = 1
    while mask < dp_size:
        values = values + swap(values, dp_size, tensor_size, mask, 0)
        mask *= 2
    return values


def pad_images(rows):
    images = rows.shape[0] // SEQ
    return jnp.pad(rows.reshape(images, SEQ, -1), ((0, 0), (0, PAD - SEQ), (0, 0)))


def trim_images(padded):
    return padded[:, :SEQ].reshape(-1, padded.shape[2])


def on_device(
    sizes, tokens, qkv_weight, out_weight, router, norm_params, expert_in, expert_out, cotangent
):
    dp_size, tensor_size = sizes
    dp_index = lax.axis_index("dp")
    tensor_index = lax.axis_index("tensor")
    core = tensor_index % 2
    high = tensor_index // 2
    width = tokens.shape[1]
    half = width // 2
    rows = qkv_weight.shape[1]
    columns = qkv_weight.shape[2]
    part = rows // 2
    stepwise = rows % 32 == 0
    x_img = pad_images(tokens)
    g_img = pad_images(cotangent)
    if stepwise:
        tables = (core.reshape(1).astype(jnp.int32),) + places(dp_size, dp_index, core)
        weight_one, weight_two, out_w, norms, router_t = gather_weights(
            qkv_weight, out_weight, router, norm_params, sizes, (dp_index, tensor_index, core), tables
        )
    else:
        weight_one, weight_two, out_w, norms, router_t = gather_weights_plain(
            qkv_weight, out_weight, router, norm_params
        )
    experts = router_t.shape[0]
    normed = first_norm(x_img, norms)
    qkv_one, mixed_one, probs_one = attend(normed, weight_one)
    qkv_two, mixed_two, probs_two = attend(normed, weight_two)
    y, logits, outgoing = route(x_img, mixed_one, mixed_two, out_w, norms, router_t, g_img)

    outgoing = outgoing.reshape(experts, SLOT_ROWS, width)
    arrived = lax.all_to_all(outgoing, "dp", split_axis=0, concat_axis=0, tiled=True)
    across = swap(arrived, dp_size, tensor_size, 0, 2)
    pair = jnp.concatenate([arrived, across], axis=0)
    near = swap(pair, dp_size, tensor_size, 0, 1)
    keep, away, first_grad, second_grad = run_expert(pair, near, expert_in[0], expert_out[0])
    got = swap(away, dp_size, tensor_size, 0, 1)
    summed = (keep.astype(F32) + got.astype(F32)).astype(BF)
    got = swap(summed[dp_size:], dp_size, tensor_size, 0, 2)
    summed = (summed[:dp_size].astype(F32) + got.astype(F32)).astype(BF)
    back = lax.all_to_all(summed, "dp", split_axis=0, concat_axis=0, tiled=True)
    back = back.reshape(experts * SLOT_ROWS, width)

    out_img, grad_y, grad_mixed, out_grad_t, small_two = moe_back(
        y, g_img, logits, back, norms, router_t, out_w, mixed_one, mixed_two
    )
    grads_one, dw_one = attend_back(normed, qkv_one, probs_one, mixed_one, grad_mixed, 0)
    grads_two, dw_two = attend_back(normed, qkv_two, probs_two, mixed_two, grad_mixed, 1)
    in_img, small_one = input_back(
        x_img, grad_y, grads_one, grads_two, weight_one, weight_two, norms
    )
    small = sum_small(
        jnp.concatenate([small_one[0:2], small_two[0:2], small_two[8:]], axis=0), sizes
    )
    norm_grad = lax.dynamic_slice(small, (tensor_index, dp_index * rows), (1, rows))
    router_grad = lax.dynamic_slice(
        small, (4 + dp_index, tensor_index * columns), (1, columns)
    ).reshape(columns, 1)

    if stepwise:
        one = scatter_weight(dw_one, part, sizes, tables).reshape(part, 3, half)
        two = scatter_weight(dw_two, part, sizes, tables).reshape(part, 3, half)
        out_t = scatter_weight(out_grad_t, part, sizes, tables).reshape(part, 2, half)
        stacked = jnp.stack(
            [jnp.concatenate([one, out_t[:, :1]], axis=1), jnp.concatenate([two, out_t[:, 1:]], axis=1)]
        )
        mine = jnp.where(high == 0, stacked[0], stacked[1])
        other = jnp.where(high == 0, stacked[1], stacked[0])
        got = swap(other, dp_size, tensor_size, 0, 2)
        total = (mine.astype(F32) + got.astype(F32)).reshape(part, 4, 2, columns)
        keep = jnp.where(core == 0, total[:, :, 0], total[:, :, 1])
        give = jnp.where(core == 0, total[:, :, 1], total[:, :, 0])
        got = swap(give, dp_size, tensor_size, 0, 1)
        top = jnp.where(core == 0, keep, got)
        bottom = jnp.where(core == 0, got, keep)
        both = jnp.concatenate([top, bottom], axis=0).transpose(1, 0, 2)
        qkv_grad = both[:3]
        out_grad = both[3].T
    else:
        full = jnp.concatenate(
            [dw_one.reshape(width, 3, half), dw_two.reshape(width, 3, half)], axis=2
        ).transpose(1, 0, 2)
        qkv_grad = lax.psum_scatter(full, "dp", scatter_dimension=1, tiled=True)
        qkv_grad = lax.psum_scatter(qkv_grad, "tensor", scatter_dimension=2, tiled=True)
        out_grad = lax.psum_scatter(out_grad_t.T, "dp", scatter_dimension=1, tiled=True)
        out_grad = lax.psum_scatter(out_grad, "tensor", scatter_dimension=0, tiled=True)
    return (
        trim_images(out_img),
        trim_images(in_img),
        qkv_grad,
        out_grad,
        router_grad,
        norm_grad,
        first_grad[None],
        second_grad[None],
    )


def solution(mesh):
    sizes = (mesh.shape["dp"], mesh.shape["tensor"])
    return jax.shard_map(
        functools.partial(on_device, sizes),
        mesh=mesh,
        in_specs=(
            P(("dp", "tensor"), None),
            P(None, "dp", "tensor"),
            P("tensor", "dp"),
            P("tensor", "dp"),
            P("tensor", "dp"),
            P("dp", None, "tensor"),
            P("dp", "tensor", None),
            P(("dp", "tensor"), None),
        ),
        out_specs=(
            P(("dp", "tensor"), None),
            P(("dp", "tensor"), None),
            P(None, "dp", "tensor"),
            P("tensor", "dp"),
            P("tensor", "dp"),
            P("tensor", "dp"),
            P("dp", None, "tensor"),
            P("dp", "tensor", None),
        ),
        check_vma=False,
    )
```

```python
import functools

import jax
import jax.numpy as jnp
from jax import lax
from jax.experimental import pallas as pl
from jax.experimental.pallas import tpu as pltpu
from jax.sharding import PartitionSpec as P

HEAD_DIM = 64
SEQ = 197
PAD = 208
SLOT_ROWS = 16
AXES = ("dp", "tensor")
BF = jnp.bfloat16
F32 = jnp.float32
LAST = (((1,), (1,)), ((), ()))
FIRST = (((0,), (0,)), ((), ()))
MIDDLE = (((1,), (0,)), ((), ()))
VMEM_LIMIT = 56 * 1024 * 1024


def dot(a, b, dims=MIDDLE):
    return lax.dot_general(a, b, dims, preferred_element_type=F32)


def params():
    return pltpu.CompilerParams(vmem_limit_bytes=VMEM_LIMIT)


def cost(flops, moved):
    return pl.CostEstimate(flops=int(flops), bytes_accessed=int(moved), transcendentals=0)


def whole(shape, column=0):
    return pl.BlockSpec(shape, lambda *_: (0,) * (len(shape) - 1) + (column,))


def per_image(shape, column=0):
    return pl.BlockSpec((1,) + shape, lambda i, *_: (i, 0, column))


def layer_stats(values):
    centre = jnp.mean(values, axis=-1, keepdims=True)
    centred = values - centre
    spread = jnp.mean(centred * centred, axis=-1, keepdims=True)
    inv_std = lax.rsqrt(spread + 1e-06)
    return centred * inv_std, inv_std


def lane_ids(shape):
    return lax.broadcasted_iota(jnp.int32, shape, len(shape) - 1)


def row_ids(shape):
    return lax.broadcasted_iota(jnp.int32, shape, len(shape) - 2)


def shift_ids(rows):
    first = pl.program_id(0) * SEQ
    start = pl.multiple_of((first // 8) * 8, 8)
    return start, first - start


def pad_kernel(x_ref, g_ref, x_out, g_out, x_wide, g_wide):
    count = x_ref.shape[0]
    for ref, out, wide in ((x_ref, x_out, x_wide), (g_ref, g_out, g_wide)):

        @pl.when(pl.program_id(0) == 0)
        def _():
            wide[0:count, :] = ref[...].astype(F32)
            wide[count:, :] = jnp.zeros((wide.shape[0] - count, wide.shape[1]), F32)

        start, offset = shift_ids(count)
        window = wide[pl.ds(start, PAD), :].astype(BF)
        shape = (PAD, PAD)
        pick = jnp.logical_and(lane_ids(shape) == row_ids(shape) + offset, row_ids(shape) < SEQ)
        out[0] = dot(pick.astype(BF), window).astype(BF)


def window_rows(count):
    images = count // SEQ
    return max(((images - 1) * SEQ // 8) * 8 + PAD, -(-count // 8) * 8)


def pad_images(tokens, cotangent):
    count, width = tokens.shape
    images = count // SEQ
    shape = jax.ShapeDtypeStruct((images, PAD, width), BF)
    return pl.pallas_call(
        pad_kernel,
        grid=(images,),
        in_specs=[whole(tokens.shape), whole(cotangent.shape)],
        out_specs=[per_image((PAD, width))] * 2,
        out_shape=[shape, shape],
        scratch_shapes=[pltpu.VMEM((window_rows(count), width), F32)] * 2,
        compiler_params=params(),
        cost_estimate=cost(4 * images * PAD * PAD * width, 16 * count * width),
        name="pad_images",
    )(tokens, cotangent)


def attend_image(normed, w_ref, qkv_ref, mixed_ref, probs_ref):
    span = mixed_ref.shape[2]
    rows = normed.shape[0]
    proj = dot(normed, w_ref[...])
    low = lane_ids((rows, 128)) < HEAD_DIM
    key_ok = row_ids((rows, rows)) < SEQ
    zero = jnp.zeros((rows, 128), BF)
    for p in range(span // 128):
        at = slice(p * 128, (p + 1) * 128)
        q = (proj[:, p * 128 : (p + 1) * 128] * HEAD_DIM ** (-0.5)).astype(BF)
        k = proj[:, span + p * 128 : span + (p + 1) * 128].astype(BF)
        v = proj[:, 2 * span + p * 128 : 2 * span + (p + 1) * 128].astype(BF)
        qkv_ref[0, :, at] = q
        qkv_ref[0, :, span + p * 128 : span + (p + 1) * 128] = k
        qkv_ref[0, :, 2 * span + p * 128 : 2 * span + (p + 1) * 128] = v
        v_t = v.T
        mixed_t = []
        for h in range(2):
            q_one = jnp.where(low, q, zero) if h == 0 else jnp.where(low, zero, q)
            scores = jnp.where(key_ok, dot(k, q_one, LAST), -1e30)
            highest = jnp.max(scores, axis=0, keepdims=True)
            scaled = jnp.exp(scores - highest)
            inv = 1.0 / jnp.sum(scaled, axis=0, keepdims=True)
            weights = (scaled * inv).astype(BF)
            probs_ref[0, 2 * p + h] = weights
            mixed_t.append(dot(v_t[h * HEAD_DIM : (h + 1) * HEAD_DIM, :], weights))
        mixed_ref[0, :, at] = jnp.concatenate(mixed_t, axis=0).T.astype(BF)


def assemble_rows(tables, own_ref, sib_ref, pieces):
    core_ref, own_place, sib_place = tables
    core = core_ref[0]
    part = own_ref.shape[1]
    for k in range(own_ref.shape[0]):
        for place, ref, which in ((own_place, own_ref, core), (sib_place, sib_ref, 1 - core)):
            row = pl.multiple_of(2 * part * k + part * which, 16)
            for lane, out_ref, at in pieces:
                out_ref[pl.ds(row, part), at] = ref[place[k], :, lane : lane + at.stop - at.start]


def assemble_smalls(place, ref, lane, norms_ref, router_ref):
    count = ref.shape[0]
    tile = jnp.concatenate([ref[place[k], 0:16, lane : lane + 128] for k in range(count)], axis=0)
    width = norms_ref.shape[1]
    columns = width // count
    norms = 0.0
    for k in range(count):
        shape = (128, width)
        spot = jnp.logical_and(lane_ids(shape) == row_ids(shape) + columns * k, row_ids(shape) < columns)
        norms = norms + dot(tile[16 * k : 16 * k + 16], spot.astype(BF))
    norms_ref[...] = norms[0:8]
    shape = (count, 16 * count)
    for j in range(width // 128):
        spot = lane_ids(shape) == row_ids(shape) * 16 + 4 + j
        router_ref[:, j * 128 : (j + 1) * 128] = dot(spot.astype(BF), tile).astype(BF)


def attend_first_kernel(stepwise, *refs):
    if stepwise:
        tables, refs = refs[:3], refs[3:]
        x_ref, own_ref, sib_ref, n_ref, qkv_ref, mixed_ref, probs_ref, w_ref, norms_ref, router_ref = refs

        @pl.when(pl.program_id(0) == 0)
        def _():
            assemble_rows(tables, own_ref, sib_ref, [(0, w_ref, slice(0, w_ref.shape[1]))])
            assemble_smalls(tables[1], own_ref, w_ref.shape[1], norms_ref, router_ref)
    else:
        x_ref, w_ref, norms_ref, n_ref, qkv_ref, mixed_ref, probs_ref = refs
    unit, _ = layer_stats(x_ref[0].astype(F32))
    normed = (unit * norms_ref[0:1, :] + norms_ref[1:2, :]).astype(BF)
    n_ref[0] = normed
    attend_image(normed, w_ref, qkv_ref, mixed_ref, probs_ref)


def attend_second_kernel(stepwise, *refs):
    if stepwise:
        tables, refs = refs[:3], refs[3:]
        n_ref, own_ref, sib_ref, qkv_ref, mixed_ref, probs_ref, w_ref, out_w_ref = refs
        span = mixed_ref.shape[2]

        @pl.when(pl.program_id(0) == 0)
        def _():
            assemble_rows(
                tables,
                own_ref,
                sib_ref,
                [
                    (0, w_ref, slice(0, 3 * span)),
                    (3 * span, out_w_ref, slice(span, 2 * span)),
                    (4 * span, out_w_ref, slice(0, span)),
                ],
            )
    else:
        n_ref, w_ref, qkv_ref, mixed_ref, probs_ref = refs
    attend_image(n_ref[0], w_ref, qkv_ref, mixed_ref, probs_ref)


def attend_specs(images, rows, span):
    heads = span // HEAD_DIM
    return (
        [
            per_image((rows, 3 * span)),
            per_image((rows, span)),
            pl.BlockSpec((1, heads, rows, rows), lambda i, *_: (i, 0, 0, 0)),
        ],
        [
            jax.ShapeDtypeStruct((images, rows, 3 * span), BF),
            jax.ShapeDtypeStruct((images, rows, span), BF),
            jax.ShapeDtypeStruct((images, heads, rows, rows), BF),
        ],
    )


def call_kernel(kernel, name, images, tables, operands, in_specs, out_specs, out_shape, flops, scratch=()):
    moved = sum(o.size * o.dtype.itemsize for o in operands) + sum(
        o.size * o.dtype.itemsize for o in out_shape
    )
    return pl.pallas_call(
        kernel,
        grid_spec=pltpu.PrefetchScalarGridSpec(
            num_scalar_prefetch=len(tables),
            grid=(images,),
            in_specs=in_specs,
            out_specs=out_specs,
            scratch_shapes=list(scratch),
        ),
        out_shape=out_shape,
        compiler_params=params(),
        cost_estimate=cost(flops, moved),
        name=name,
    )(*tables, *operands)


def attend_flops(images, rows, width, span):
    return 2 * images * rows * (3 * width * span + 2 * rows * span)


def attend_first(x_img, tables, operands, span, experts):
    images, rows, width = x_img.shape
    specs, shapes = attend_specs(images, rows, span)
    specs = [per_image((rows, width))] + specs
    shapes = [jax.ShapeDtypeStruct((images, rows, width), BF)] + shapes
    if tables:
        extra = [((width, 3 * span), BF), ((8, width), F32), ((experts, width), BF)]
        specs += [whole(shape) for shape, _ in extra]
        shapes += [jax.ShapeDtypeStruct(*e) for e in extra]
    return call_kernel(
        functools.partial(attend_first_kernel, bool(tables)),
        "attend_first",
        images,
        tables,
        (x_img,) + operands,
        [per_image((rows, width))] + [whole(o.shape) for o in operands],
        specs,
        shapes,
        attend_flops(images, rows, width, span),
    )


def attend_second(normed, tables, operands, span):
    images, rows, width = normed.shape
    specs, shapes = attend_specs(images, rows, span)
    if tables:
        extra = [((width, 3 * span), BF), ((width, 2 * span), BF)]
        specs += [whole(shape) for shape, _ in extra]
        shapes += [jax.ShapeDtypeStruct(*e) for e in extra]
    return call_kernel(
        functools.partial(attend_second_kernel, bool(tables)),
        "attend_second",
        images,
        tables,
        (normed,) + operands,
        [per_image((rows, width))] + [whole(o.shape) for o in operands],
        specs,
        shapes,
        attend_flops(images, rows, width, span),
    )


def softmaxes(logits):
    ok = lane_ids(logits.shape) < SEQ
    masked = jnp.where(ok, logits, -1e30)
    up = jnp.exp(masked - jnp.max(masked, axis=1, keepdims=True))
    dispatch = up / jnp.sum(up, axis=1, keepdims=True)
    up = jnp.exp(logits - jnp.max(logits, axis=0, keepdims=True))
    combine = up / jnp.sum(up, axis=0, keepdims=True)
    return dispatch, combine


def place_rows(experts, image, offset):
    shape = (experts * SLOT_ROWS, experts)
    return (row_ids(shape) == lane_ids(shape) * SLOT_ROWS + offset + image).astype(BF)


def pick_rows(experts, image, offset):
    shape = (experts, experts * SLOT_ROWS)
    return (lane_ids(shape) == row_ids(shape) * SLOT_ROWS + offset + image).astype(BF)


def route_kernel(
    half, x_ref, m1_ref, m2_ref, out_w_ref, norms_ref, router_ref, g_ref, y_ref, logits_ref, send_ref, acc
):
    image = pl.program_id(0)
    experts = router_ref.shape[0]
    out_w = out_w_ref[...]
    attn = dot(m1_ref[0], out_w[:, :half], LAST) + dot(m2_ref[0], out_w[:, half:], LAST)
    y = x_ref[0].astype(F32) + attn
    y_ref[0] = y
    unit, _ = layer_stats(y)
    normed = (unit * norms_ref[2:3, :] + norms_ref[3:4, :]).astype(BF)
    logits = dot(router_ref[...], normed, LAST)
    logits_ref[0] = logits
    dispatch, combine = softmaxes(logits)
    slots = dot(dispatch.astype(BF), normed).astype(BF)
    grad_returned = dot(combine.astype(BF), g_ref[0]).astype(BF)
    placed = dot(place_rows(experts, image, 0), slots) + dot(
        place_rows(experts, image, SLOT_ROWS // 2), grad_returned
    )

    @pl.when(image == 0)
    def _():
        acc[...] = placed

    @pl.when(image > 0)
    def _():
        acc[...] += placed

    @pl.when(image == pl.num_programs(0) - 1)
    def _():
        send_ref[...] = acc[...].astype(BF)


def route(x_img, mixed_one, mixed_two, out_w, norms, router, g_img):
    images, rows, width = x_img.shape
    experts = router.shape[0]
    half = mixed_one.shape[2]
    return pl.pallas_call(
        functools.partial(route_kernel, half),
        grid=(images,),
        in_specs=[
            per_image((rows, width)),
            per_image((rows, half)),
            per_image((rows, width - half)),
            whole(out_w.shape),
            whole(norms.shape),
            whole(router.shape),
            per_image((rows, width)),
        ],
        out_specs=[
            per_image((rows, width)),
            per_image((experts, rows)),
            whole((experts * SLOT_ROWS, width)),
        ],
        out_shape=[
            jax.ShapeDtypeStruct((images, rows, width), F32),
            jax.ShapeDtypeStruct((images, experts, rows), F32),
            jax.ShapeDtypeStruct((experts * SLOT_ROWS, width), BF),
        ],
        scratch_shapes=[pltpu.VMEM((experts * SLOT_ROWS, width), F32)],
        compiler_params=params(),
        name="route",
    )(x_img, mixed_one, mixed_two, out_w, norms, router, g_img)


def split_rows(blocks):
    wide = blocks.astype(F32)
    half = SLOT_ROWS // 2
    flat = (blocks.shape[0] * half, blocks.shape[2])
    return wide[:, :half].reshape(flat).astype(BF), wide[:, half:].reshape(flat).astype(BF)


def join_rows(ones, twos):
    half = SLOT_ROWS // 2
    shape = (ones.shape[0] // half, half, ones.shape[1])
    return jnp.concatenate([ones.reshape(shape), twos.reshape(shape)], axis=1).astype(BF)


def gelu_parts(pre):
    cdf = 0.5 * (1.0 + lax.erf(pre * (0.5**0.5)))
    density = jnp.exp(-0.5 * pre * pre) * 0.3989422804014327
    return pre * cdf, cdf + pre * density


def expert_kernel(
    own_ref, near_ref, w1_ref, w2_ref, keep_ref, send_ref, slots_ref, grads_ref, hidden_ref, pre_ref
):
    count = own_ref.shape[0]
    blocks = jnp.concatenate([own_ref[...], near_ref[...]], axis=0)
    slots, grads = split_rows(blocks)
    pre = dot(slots, w1_ref[...])
    hidden, slope = gelu_parts(pre)
    hidden = hidden.astype(BF)
    returned = dot(hidden, w2_ref[...])
    grad_pre = (dot(grads, w2_ref[...], LAST) * slope).astype(BF)
    grad_slots = dot(grad_pre, w1_ref[...], LAST)
    joined = join_rows(returned, grad_slots)
    keep_ref[...] = joined[:count]
    send_ref[...] = joined[count:]
    slots_ref[...] = slots
    grads_ref[...] = grads
    hidden_ref[...] = hidden
    pre_ref[...] = grad_pre


def run_expert(own, near, first_weight, second_weight):
    width, units = first_weight.shape
    rows = (own.shape[0] + near.shape[0]) * SLOT_ROWS // 2
    return pl.pallas_call(
        expert_kernel,
        out_shape=[
            jax.ShapeDtypeStruct(own.shape, BF),
            jax.ShapeDtypeStruct(near.shape, BF),
            jax.ShapeDtypeStruct((rows, width), BF),
            jax.ShapeDtypeStruct((rows, width), BF),
            jax.ShapeDtypeStruct((rows, units), BF),
            jax.ShapeDtypeStruct((rows, units), BF),
        ],
        compiler_params=params(),
        cost_estimate=cost(8 * rows * width * units, 4 * width * units + 16 * rows * width),
        name="expert",
    )(own, near, first_weight, second_weight)


def expert_grad_kernel(slots_ref, grads_ref, hidden_ref, pre_ref, d1_ref, d2_ref):
    d1_ref[...] = dot(slots_ref[...], pre_ref[...], FIRST)
    d2_ref[...] = dot(hidden_ref[...], grads_ref[...], FIRST)


def expert_grads(slots, grads, hidden, grad_pre):
    rows, width = slots.shape
    units = hidden.shape[1]
    return pl.pallas_call(
        expert_grad_kernel,
        out_shape=[
            jax.ShapeDtypeStruct((width, units), F32),
            jax.ShapeDtypeStruct((units, width), F32),
        ],
        compiler_params=params(),
        cost_estimate=cost(4 * rows * width * units, 8 * width * units + 8 * rows * width),
        name="expert_grads",
    )(slots, grads, hidden, grad_pre)


def moe_back_kernel(
    half,
    y_ref,
    g_ref,
    logits_ref,
    back_ref,
    norms_ref,
    router_ref,
    out_w_ref,
    m1_ref,
    m2_ref,
    grad_y_ref,
    grad_mixed_ref,
    out_grad_ref,
    small_ref,
):
    image = pl.program_id(0)
    experts = router_ref.shape[0]
    y = y_ref[0]
    g_low = g_ref[0]
    back = back_ref[...]
    returned = dot(pick_rows(experts, image, 0), back).astype(BF)
    grad_slots = dot(pick_rows(experts, image, SLOT_ROWS // 2), back).astype(BF)
    dispatch, combine = softmaxes(logits_ref[0])
    unit, inv_std = layer_stats(y)
    gain = norms_ref[2:3, :]
    normed = (unit * gain + norms_ref[3:4, :]).astype(BF)
    grad_combine = dot(returned, g_low, LAST)
    grad_dispatch = dot(grad_slots, normed, LAST)
    grad_logits = dispatch * (
        grad_dispatch - jnp.sum(grad_dispatch * dispatch, axis=1, keepdims=True)
    ) + combine * (grad_combine - jnp.sum(grad_combine * combine, axis=0, keepdims=True))
    grad_logits = grad_logits.astype(BF)
    router_grad = dot(grad_logits, normed)
    grad_two = dot(dispatch.astype(BF), grad_slots, FIRST) + dot(grad_logits, router_ref[...], FIRST)
    gain_grad = jnp.sum(grad_two * unit, axis=0, keepdims=True)
    shift_grad = jnp.sum(grad_two, axis=0, keepdims=True)
    scaled = grad_two * gain
    mean_one = jnp.mean(scaled, axis=-1, keepdims=True)
    mean_two = jnp.mean(scaled * unit, axis=-1, keepdims=True)
    grad_y = g_low.astype(F32) + inv_std * (scaled - mean_one - unit * mean_two)
    grad_y_ref[0] = grad_y
    grad_attn = grad_y.astype(BF)
    grad_mixed_ref[0] = dot(grad_attn, out_w_ref[...]).astype(BF)

    @pl.when(image == 0)
    def _():
        out_grad_ref[...] = jnp.zeros_like(out_grad_ref)
        small_ref[...] = jnp.zeros_like(small_ref)

    out_grad_ref[:, :half] += dot(grad_attn, m1_ref[0], FIRST)
    out_grad_ref[:, half:] += dot(grad_attn, m2_ref[0], FIRST)
    small_ref[0:1, :] += gain_grad
    small_ref[1:2, :] += shift_grad
    small_ref[8 : 8 + experts, :] += router_grad


def moe_back(y, g_img, logits, back, norms, router, out_w, mixed_one, mixed_two):
    images, rows, width = y.shape
    experts = router.shape[0]
    half = mixed_one.shape[2]
    return pl.pallas_call(
        functools.partial(moe_back_kernel, half),
        grid=(images,),
        in_specs=[
            per_image((rows, width)),
            per_image((rows, width)),
            per_image((experts, rows)),
            whole(back.shape),
            whole(norms.shape),
            whole(router.shape),
            whole(out_w.shape),
            per_image((rows, half)),
            per_image((rows, width - half)),
        ],
        out_specs=[
            per_image((rows, width)),
            per_image((rows, width)),
            whole((width, width)),
            whole((8 + experts, width)),
        ],
        out_shape=[
            jax.ShapeDtypeStruct((images, rows, width), F32),
            jax.ShapeDtypeStruct((images, rows, width), BF),
            jax.ShapeDtypeStruct((width, width), F32),
            jax.ShapeDtypeStruct((8 + experts, width), F32),
        ],
        compiler_params=params(),
        cost_estimate=cost(4 * images * rows * width * width, 14 * images * rows * width),
        name="moe_back",
    )(y, g_img, logits, back, norms, router, out_w, mixed_one, mixed_two)


def join_images(wide, padded, exact):
    start, offset = shift_ids(wide.shape[0])
    shape = (PAD, PAD)
    pick = jnp.logical_and(row_ids(shape) == lane_ids(shape) + offset, lane_ids(shape) < SEQ).astype(BF)
    high = padded.astype(BF)
    moved = dot(pick, high)
    if exact:
        rest = padded - high.astype(F32)
        middle = rest.astype(BF)
        moved = moved + dot(pick, middle) + dot(pick, (rest - middle.astype(F32)).astype(BF))

    @pl.when(pl.program_id(0) == 0)
    def _():
        wide[...] = jnp.zeros_like(wide)

    wide[pl.ds(start, PAD), :] += moved


def output_kernel(y_ref, logits_ref, back_ref, out_ref, wide):
    image = pl.program_id(0)
    experts = logits_ref.shape[1]
    returned = dot(pick_rows(experts, image, 0), back_ref[...]).astype(BF)
    _, combine = softmaxes(logits_ref[0])
    join_images(wide, y_ref[0] + dot(combine.astype(BF), returned, FIRST), False)

    @pl.when(image == pl.num_programs(0) - 1)
    def _():
        out_ref[...] = wide[0 : out_ref.shape[0], :].astype(BF)


def block_output(y, logits, back):
    images, rows, width = y.shape
    count = images * SEQ
    return pl.pallas_call(
        output_kernel,
        grid=(images,),
        in_specs=[per_image((rows, width)), per_image(logits.shape[1:]), whole(back.shape)],
        out_specs=whole((count, width)),
        out_shape=jax.ShapeDtypeStruct((count, width), BF),
        scratch_shapes=[pltpu.VMEM((window_rows(count), width), F32)],
        compiler_params=params(),
        cost_estimate=cost(2 * images * rows * rows * width, 6 * images * rows * width),
        name="block_output",
    )(y, logits, back)


def deal_rows(tables, full_ref, own_ref, sib_ref, lane):
    core_ref, own_place, sib_place = tables
    core = core_ref[0]
    count, part, _ = own_ref.shape
    span = full_ref.shape[1]
    for k in range(count):
        for place, ref, which in ((own_place, own_ref, core), (sib_place, sib_ref, 1 - core)):
            row = pl.multiple_of(2 * part * k + part * which, 16)
            ref[place[k], :, lane : lane + span] = full_ref[pl.ds(row, part), :].astype(BF)


def attend_back_kernel(stepwise, *refs):
    if stepwise:
        tables, refs = refs[:3], refs[3:]
        n_ref, qkv_ref, probs_ref, mixed_ref, gm_ref, og_ref, grads_ref, own_ref, sib_ref, dw_ref = refs
    else:
        n_ref, qkv_ref, probs_ref, mixed_ref, gm_ref, grads_ref, dw_ref = refs
    image = pl.program_id(0)
    span = mixed_ref.shape[2]
    rows = n_ref.shape[1]
    low = lane_ids((rows, 128)) < HEAD_DIM
    zero = jnp.zeros((rows, 128), BF)
    minus = jnp.full((rows, 128), -1.0, BF)
    for p in range(span // 128):
        at = slice(p * 128, (p + 1) * 128)
        q = qkv_ref[0, :, at]
        k = qkv_ref[0, :, span + p * 128 : span + (p + 1) * 128]
        v = qkv_ref[0, :, 2 * span + p * 128 : 2 * span + (p + 1) * 128]
        gm = gm_ref[0, :, at]
        inner = pltpu.roll(gm.astype(F32) * mixed_ref[0, :, at].astype(F32), HEAD_DIM, 1).astype(BF)
        k_t = k.T
        grad_q_t, grad_k, grad_v = [], 0.0, 0.0
        for h in range(2):
            mine = low if h == 0 else jnp.logical_not(low)
            weights = probs_ref[0, 2 * p + h]
            centred = dot(jnp.where(mine, v, minus), jnp.where(mine, gm, inner), LAST)
            grad_scores = (weights.astype(F32) * centred).astype(BF)
            grad_v = grad_v + dot(weights, jnp.where(mine, gm, zero))
            grad_k = grad_k + dot(grad_scores, jnp.where(mine, q, zero))
            grad_q_t.append(dot(k_t[h * HEAD_DIM : (h + 1) * HEAD_DIM, :], grad_scores))
        grad_q = jnp.concatenate(grad_q_t, axis=0).T * HEAD_DIM ** (-0.5)
        grads_ref[0, :, at] = grad_q.astype(BF)
        grads_ref[0, :, span + p * 128 : span + (p + 1) * 128] = grad_k.astype(BF)
        grads_ref[0, :, 2 * span + p * 128 : 2 * span + (p + 1) * 128] = grad_v.astype(BF)

    @pl.when(image == 0)
    def _():
        dw_ref[...] = jnp.zeros_like(dw_ref)

    dw_ref[...] += dot(n_ref[0], grads_ref[0], FIRST)

    if stepwise:

        @pl.when(image == pl.num_programs(0) - 1)
        def _():
            deal_rows(tables, dw_ref, own_ref, sib_ref, 0)
            deal_rows(tables, og_ref, own_ref, sib_ref, 3 * span)


def attend_back(normed, qkv, probs, mixed, grad_mixed, out_grad_t, piece, tables, sizes):
    images, rows, width = normed.shape
    span = mixed.shape[2]
    heads = span // HEAD_DIM
    operands = (normed, qkv, probs, mixed, grad_mixed)
    in_specs = [
        per_image((rows, width)),
        per_image((rows, 3 * span)),
        pl.BlockSpec((1, heads, rows, rows), lambda i, *_: (i, 0, 0, 0)),
        per_image((rows, span)),
        per_image((rows, span), piece),
    ]
    out_specs = [per_image((rows, 3 * span))]
    out_shape = [jax.ShapeDtypeStruct((images, rows, 3 * span), BF)]
    scratch = ()
    if tables:
        operands += (out_grad_t,)
        in_specs.append(whole((width, span), piece))
        block = (sizes[0], width // sizes[0] // 2, 4 * span)
        out_specs += [whole(block)] * 2
        out_shape += [jax.ShapeDtypeStruct(block, BF)] * 2
        scratch = (pltpu.VMEM((width, 3 * span), F32),)
    else:
        out_specs.append(whole((width, 3 * span)))
        out_shape.append(jax.ShapeDtypeStruct((width, 3 * span), F32))
    return call_kernel(
        functools.partial(attend_back_kernel, bool(tables)),
        "attend_back",
        images,
        tables,
        operands,
        in_specs,
        out_specs,
        out_shape,
        2 * images * rows * (3 * width * span + 4 * rows * span),
        scratch,
    )


def input_back_kernel(x_ref, gy_ref, p1_ref, p2_ref, w1_ref, w2_ref, norms_ref, out_ref, small_ref, wide):
    image = pl.program_id(0)
    unit, inv_std = layer_stats(x_ref[0].astype(F32))
    grad_one = dot(p1_ref[0], w1_ref[...], LAST) + dot(p2_ref[0], w2_ref[...], LAST)
    scaled = grad_one * norms_ref[0:1, :]
    mean_one = jnp.mean(scaled, axis=-1, keepdims=True)
    mean_two = jnp.mean(scaled * unit, axis=-1, keepdims=True)
    join_images(wide, gy_ref[0] + inv_std * (scaled - mean_one - unit * mean_two), True)

    @pl.when(image == 0)
    def _():
        small_ref[...] = jnp.zeros_like(small_ref)

    small_ref[0:1, :] += jnp.sum(grad_one * unit, axis=0, keepdims=True)
    small_ref[1:2, :] += jnp.sum(grad_one, axis=0, keepdims=True)

    @pl.when(image == pl.num_programs(0) - 1)
    def _():
        out_ref[...] = wide[0 : out_ref.shape[0], :]


def input_back(x_img, grad_y, grads_one, grads_two, weight_one, weight_two, norms):
    images, rows, width = x_img.shape
    count = images * SEQ
    return pl.pallas_call(
        input_back_kernel,
        grid=(images,),
        in_specs=[
            per_image((rows, width)),
            per_image((rows, width)),
            per_image(grads_one.shape[1:]),
            per_image(grads_two.shape[1:]),
            whole(weight_one.shape),
            whole(weight_two.shape),
            whole(norms.shape),
        ],
        out_specs=[whole((count, width)), whole((8, width))],
        out_shape=[
            jax.ShapeDtypeStruct((count, width), F32),
            jax.ShapeDtypeStruct((8, width), F32),
        ],
        scratch_shapes=[pltpu.VMEM((window_rows(count), width), F32)],
        compiler_params=params(),
        cost_estimate=cost(6 * images * rows * width * width, 18 * images * rows * width),
        name="input_back",
    )(x_img, grad_y, grads_one, grads_two, weight_one, weight_two, norms)


def merge_kernel(place, own_ref, core_ref, high_ref, small_ref, out_ref):
    count, part, span = own_ref.shape
    width = small_ref.shape[1]
    columns = width // count
    for k in range(count):
        total = own_ref[k].astype(F32) + core_ref[k].astype(F32) + high_ref[k].astype(F32)
        out_ref[k, :, 0:span] = total.astype(BF)
    norms = small_ref[0:16, :].astype(BF)
    routers = small_ref[16 : 16 + count, :].astype(BF)
    for k in range(count):
        shape = (width, 128)
        spot = jnp.logical_and(row_ids(shape) == lane_ids(shape) + columns * k, lane_ids(shape) < columns)
        rows = dot(norms, spot.astype(BF))
        shape = (16, count)
        for j in range(width // 128):
            spot = jnp.logical_and(row_ids(shape) == 4 + j, lane_ids(shape) == k)
            rows = rows + dot(spot.astype(BF), routers[:, j * 128 : (j + 1) * 128])
        out_ref[place[k], 0:16, span:] = rows.astype(BF)
        out_ref[place[k], 16:, span:] = jnp.zeros((part - 16, 128), BF)


def merge(place, own, from_core, from_high, small):
    count, part, span = own.shape
    return pl.pallas_call(
        merge_kernel,
        in_specs=[pl.BlockSpec(memory_space=pltpu.SMEM)] + [pl.BlockSpec(memory_space=pltpu.VMEM)] * 4,
        out_shape=jax.ShapeDtypeStruct((count, part, span + 128), BF),
        compiler_params=params(),
        cost_estimate=cost(own.size, 8 * own.size),
        name="merge",
    )(place, own, from_core, from_high, small)


def swap(value, dp_size, tensor_size, dp_mask, tensor_mask):
    pairs = [
        (d * tensor_size + t, (d ^ dp_mask) * tensor_size + (t ^ tensor_mask))
        for d in range(dp_size)
        for t in range(tensor_size)
    ]
    return lax.ppermute(value, AXES, pairs)


def steps_of(dp_size):
    bits = dp_size.bit_length() - 1
    down = list(range(bits))[::-1]
    return [down, down[-1:] + down[:-1]]


def step_pairs(dp_size, tensor_size, step):
    orders = steps_of(dp_size)
    return [
        (d * tensor_size + t, (d ^ (1 << orders[t % 2][step])) * tensor_size + t)
        for d in range(dp_size)
        for t in range(tensor_size)
    ]


def places(dp_size, dp_index, core):
    away = dp_index ^ jnp.arange(dp_size, dtype=jnp.int32)
    both = []
    for order in steps_of(dp_size):
        at = jnp.zeros_like(away)
        for step, bit in enumerate(order):
            at = at | (((away >> bit) & 1) << step)
        both.append(at)
    return jnp.where(core == 0, both[0], both[1]), jnp.where(core == 0, both[1], both[0])


def scatter_steps(blocks, dp_size, tensor_size):
    held = blocks
    for step in range(dp_size.bit_length() - 1)[::-1]:
        half = 1 << step
        got = lax.ppermute(held[half:], AXES, step_pairs(dp_size, tensor_size, step))
        held = (held[:half].astype(F32) + got.astype(F32)).astype(BF)
    return held[0]


def pick(core, zero, one):
    return jnp.where(core == 0, zero, one), jnp.where(core == 0, one, zero)


def gather_weights(qkv_weight, out_weight, router, norm_params, sizes, ids, along):
    core, high = ids
    rows, columns = qkv_weight.shape[1:]
    part = rows // 2
    small = jnp.concatenate([jnp.pad(norm_params, ((0, 0), (0, columns - rows))), router.T], axis=0)
    small_high = swap(small, *sizes, 0, 2)
    turned = jnp.concatenate([qkv_weight, out_weight.T[None]], axis=0)
    keep = lax.dynamic_slice_in_dim(turned, core * part, part, axis=1)
    give = lax.dynamic_slice_in_dim(turned, (1 - core) * part, part, axis=1)
    got = swap(give, *sizes, 0, 1)
    first, second = pick(core, keep, got)
    mine = jnp.concatenate([first, second], axis=2)
    mine = mine.transpose(1, 0, 2).reshape(part, 8 * columns)
    other = swap(mine, *sizes, 0, 2)
    small_pair = jnp.stack([small, small_high])
    small_near = swap(small_pair, *sizes, 0, 1)
    first, second = pick(core, small_pair, small_near)
    by_core = jnp.stack([first, second], axis=1)
    first, second = pick(high, by_core[0], by_core[1])
    smalls = jnp.stack([first, second]).reshape(4, 2, columns)
    norm_rows = jnp.pad(smalls[:, 0, :rows], ((0, 0), (0, 128 - rows)))
    tile = jnp.concatenate([norm_rows, smalls[:, 1].reshape(-1, 128)], axis=0)
    tile = jnp.pad(tile, ((0, part - tile.shape[0]), (0, 0)))
    block_one = jnp.concatenate([mine[:, : 6 * columns], tile], axis=1)
    block_two = jnp.concatenate([other, mine[:, 6 * columns :]], axis=1)
    held_one, held_two = block_one[None], block_two[None]
    steps = sizes[0].bit_length() - 1
    for step in range(steps):
        got = lax.ppermute(held_one, AXES, step_pairs(*sizes, step))
        if step == 0:
            got, along = lax.optimization_barrier((got, pad_images(*along)))
        held_one = jnp.concatenate([held_one, got], axis=0)
    sib_one = swap(held_one, *sizes, 0, 1)
    held_one, held_two = lax.optimization_barrier((held_one, held_two))
    for step in range(steps):
        got = lax.ppermute(held_two, AXES, step_pairs(*sizes, step))
        held_two = jnp.concatenate([held_two, got], axis=0)
    sib_two = swap(held_two, *sizes, 0, 1)
    return (held_one, sib_one), (held_two, sib_two), along


def gather_weights_plain(qkv_weight, out_weight, router, norm_params):
    qkv = lax.all_gather(qkv_weight, "dp", axis=1, tiled=True)
    qkv = lax.all_gather(qkv, "tensor", axis=2, tiled=True)
    out_w, router, norms = (
        lax.all_gather(lax.all_gather(w, "dp", axis=1, tiled=True), "tensor", axis=0, tiled=True)
        for w in (out_weight, router, norm_params)
    )
    width = qkv.shape[1]
    half = width // 2
    one = qkv[:, :, :half].transpose(1, 0, 2).reshape(width, 3 * half)
    two = qkv[:, :, half:].transpose(1, 0, 2).reshape(width, 3 * half)
    return one, two, out_w.T, norms.astype(F32), router.T


def sum_small(values, sizes):
    dp_size, tensor_size = sizes
    mask = 1
    while mask < tensor_size:
        values = values + swap(values, dp_size, tensor_size, 0, mask)
        mask *= 2
    mask = 1
    while mask < dp_size:
        values = values + swap(values, dp_size, tensor_size, mask, 0)
        mask *= 2
    return values


def scatter_weights(own_one, got_core, got_high, small, sizes, ids, place, rows, columns):
    core, tensor_index = ids
    part = rows // 2
    blocks = merge(place, own_one, got_core, got_high, small)
    mine = scatter_steps(blocks, *sizes)
    span = mine.shape[1] - 128
    tile = mine[:, span:]
    norm_grad = lax.dynamic_slice(tile, (tensor_index, 0), (1, rows)).astype(F32)
    router_grad = lax.dynamic_slice(
        tile[4 : 4 + tensor_count(span, columns) * columns // 128].reshape(-1), (tensor_index * columns,), (columns,)
    )
    by_core = mine[:, :span].reshape(part, 4, 2, columns)
    keep, give = pick(core, by_core[:, :, 0], by_core[:, :, 1])
    got = swap(give, *sizes, 0, 1)
    top, bottom = pick(core, keep, got)
    both = jnp.concatenate([top, bottom], axis=0).astype(F32).transpose(1, 0, 2)
    return both[:3], both[3].T, router_grad.astype(F32).reshape(columns, 1), norm_grad


def tensor_count(span, columns):
    return span // (2 * columns)


def on_device(
    sizes, tokens, qkv_weight, out_weight, router, norm_params, expert_in, expert_out, cotangent
):
    dp_size, tensor_size = sizes
    dp_index = lax.axis_index("dp")
    tensor_index = lax.axis_index("tensor")
    core = tensor_index % 2
    high = tensor_index // 2
    width = tokens.shape[1]
    half = width // 2
    rows = qkv_weight.shape[1]
    columns = qkv_weight.shape[2]
    experts = dp_size * router.shape[1]
    stepwise = rows % 32 == 0 and tensor_size == 4
    tables = ()
    if stepwise:
        tables = (core.reshape(1).astype(jnp.int32),) + places(dp_size, dp_index, core)
        pair_one, pair_two, (x_img, g_img) = gather_weights(
            qkv_weight, out_weight, router, norm_params, sizes, (core, high), (tokens, cotangent)
        )
        normed, qkv_one, mixed_one, probs_one, weight_one, norms, router_t = attend_first(
            x_img, tables, pair_one, half, experts
        )
        qkv_two, mixed_two, probs_two, weight_two, out_w = attend_second(normed, tables, pair_two, half)
    else:
        x_img, g_img = pad_images(tokens, cotangent)
        weight_one, weight_two, out_w, norms, router_t = gather_weights_plain(
            qkv_weight, out_weight, router, norm_params
        )
        normed, qkv_one, mixed_one, probs_one = attend_first(x_img, (), (weight_one, norms), half, experts)
        qkv_two, mixed_two, probs_two = attend_second(normed, (), (weight_two,), half)
    y, logits, outgoing = route(x_img, mixed_one, mixed_two, out_w, norms, router_t, g_img)

    outgoing = outgoing.reshape(experts, SLOT_ROWS, width)
    arrived = lax.all_to_all(outgoing, "dp", split_axis=0, concat_axis=0, tiled=True)
    across = swap(arrived, *sizes, 0, 2)
    pair = jnp.concatenate([arrived, across], axis=0)
    near = swap(pair, *sizes, 0, 1)
    keep, away, *kept = run_expert(pair, near, expert_in[0], expert_out[0])
    first_grad, second_grad = expert_grads(*kept)
    got = swap(away, *sizes, 0, 1)
    summed = (keep.astype(F32) + got.astype(F32)).astype(BF)
    got = swap(summed[dp_size:], *sizes, 0, 2)
    summed = (summed[:dp_size].astype(F32) + got.astype(F32)).astype(BF)
    back = lax.all_to_all(summed, "dp", split_axis=0, concat_axis=0, tiled=True)
    back = back.reshape(experts * SLOT_ROWS, width)

    grad_y, grad_mixed, out_grad_t, small_two = moe_back(
        y, g_img, logits, back, norms, router_t, out_w, mixed_one, mixed_two
    )
    output = block_output(y, logits, back)
    grads_two, *dealt = attend_back(
        normed, qkv_two, probs_two, mixed_two, grad_mixed, out_grad_t, 1, tables, sizes
    )
    if stepwise:
        own, sib = dealt
        got = swap(sib, *sizes, 0, 1)
        paired = (own.astype(F32) + got.astype(F32)).astype(BF)
        paired, grad_mixed = lax.optimization_barrier((paired, grad_mixed))
        got_high = swap(paired, *sizes, 0, 2)
    grads_one, *dealt_one = attend_back(
        normed, qkv_one, probs_one, mixed_one, grad_mixed, out_grad_t, 0, tables, sizes
    )
    if stepwise:
        own, sib = dealt_one
        got_core = swap(sib, *sizes, 0, 1)
    input_grad, small_one = input_back(
        x_img, grad_y, grads_one, grads_two, weight_one, weight_two, norms
    )
    small = jnp.concatenate([small_one[0:2], small_two[0:2], small_two[8:]], axis=0)
    if stepwise:
        small = small + swap(small, *sizes, 0, 1)
        small = small + swap(small, *sizes, 0, 2)
        small = jnp.concatenate(
            [small[:4], jnp.zeros((12, width), F32), small[4:], jnp.zeros((-experts % 16, width), F32)], axis=0
        )
        qkv_grad, out_grad, router_grad, norm_grad = scatter_weights(
            own, got_core, got_high, small, sizes, (core, tensor_index), tables[1], rows, columns
        )
    else:
        small = sum_small(small, sizes)
        norm_grad = lax.dynamic_slice(small, (tensor_index, dp_index * rows), (1, rows))
        router_grad = lax.dynamic_slice(
            small, (4 + dp_index, tensor_index * columns), (1, columns)
        ).reshape(columns, 1)
        full = jnp.concatenate(
            [dealt_one[0].reshape(width, 3, half), dealt[0].reshape(width, 3, half)], axis=2
        ).transpose(1, 0, 2)
        qkv_grad = lax.psum_scatter(full, "dp", scatter_dimension=1, tiled=True)
        qkv_grad = lax.psum_scatter(qkv_grad, "tensor", scatter_dimension=2, tiled=True)
        out_grad = lax.psum_scatter(out_grad_t.T, "dp", scatter_dimension=1, tiled=True)
        out_grad = lax.psum_scatter(out_grad, "tensor", scatter_dimension=0, tiled=True)
    return (
        output,
        input_grad,
        qkv_grad,
        out_grad,
        router_grad,
        norm_grad,
        first_grad[None],
        second_grad[None],
    )


def solution(mesh):
    sizes = (mesh.shape["dp"], mesh.shape["tensor"])
    return jax.shard_map(
        functools.partial(on_device, sizes),
        mesh=mesh,
        in_specs=(
            P(("dp", "tensor"), None),
            P(None, "dp", "tensor"),
            P("tensor", "dp"),
            P("tensor", "dp"),
            P("tensor", "dp"),
            P("dp", None, "tensor"),
            P("dp", "tensor", None),
            P(("dp", "tensor"), None),
        ),
        out_specs=(
            P(("dp", "tensor"), None),
            P(("dp", "tensor"), None),
            P(None, "dp", "tensor"),
            P("tensor", "dp"),
            P("tensor", "dp"),
            P("tensor", "dp"),
            P("dp", None, "tensor"),
            P("dp", "tensor", None),
        ),
        check_vma=False,
    )
```

```python
import functools

import jax
import jax.numpy as jnp
from jax import lax
from jax.experimental import pallas as pl
from jax.experimental.pallas import tpu as pltpu
from jax.sharding import PartitionSpec as P

HEAD_DIM = 64
SEQ = 197
PAD = 208
SLOT_ROWS = 16
AXES = ("dp", "tensor")
BF = jnp.bfloat16
F32 = jnp.float32
LAST = (((1,), (1,)), ((), ()))
FIRST = (((0,), (0,)), ((), ()))
MIDDLE = (((1,), (0,)), ((), ()))
MIB = 1024 * 1024


def dot(a, b, dims=MIDDLE):
    return lax.dot_general(a, b, dims, preferred_element_type=F32)


def shape_of(shape, dtype):
    return jax.ShapeDtypeStruct(shape, dtype)


def size_of(array):
    return array.size * array.dtype.itemsize


def run(kernel, name, operands, results, limit, flops=0, scratch=(), scalars=0):
    memory = [pltpu.SMEM] * scalars + [pltpu.VMEM] * (len(operands) - scalars)
    moved = sum(map(size_of, operands)) + sum(map(size_of, results))
    return pl.pallas_call(
        kernel,
        in_specs=[pl.BlockSpec(memory_space=m) for m in memory],
        out_specs=[pl.BlockSpec(memory_space=pltpu.VMEM) for _ in results],
        out_shape=list(results),
        scratch_shapes=list(scratch),
        compiler_params=pltpu.CompilerParams(vmem_limit_bytes=limit * MIB),
        cost_estimate=pl.CostEstimate(flops=int(flops), bytes_accessed=int(moved), transcendentals=0),
        name=name,
    )(*operands)


def layer_stats(values):
    centre = jnp.mean(values, axis=-1, keepdims=True)
    centred = values - centre
    spread = jnp.mean(centred * centred, axis=-1, keepdims=True)
    inv_std = lax.rsqrt(spread + 1e-06)
    return centred * inv_std, inv_std


def lane_ids(shape):
    return lax.broadcasted_iota(jnp.int32, shape, len(shape) - 1)


def row_ids(shape):
    return lax.broadcasted_iota(jnp.int32, shape, len(shape) - 2)


def flat(ref):
    images, rows, columns = ref.shape
    return ref[...].reshape(images * rows, columns)


def prepare_kernel(x_ref, g_ref, x_out, g_out, unit_out, inv_out, wide):
    count, width = x_ref.shape
    real = row_ids((PAD, width)) < SEQ
    wide[count:, :] = jnp.zeros((wide.shape[0] - count, width), F32)
    for ref, out in ((x_ref, x_out), (g_ref, g_out)):
        wide[0:count, :] = ref[...].astype(F32)
        for i in range(out.shape[0]):
            rows = jnp.where(real, wide[SEQ * i : SEQ * i + PAD, :], 0.0)
            out[i] = rows.astype(BF)
            if ref is x_ref:
                unit, inv_std = layer_stats(rows)
                unit_out[i] = unit
                inv_out[i] = inv_std


def prepare(tokens, cotangent):
    count, width = tokens.shape
    images = count // SEQ
    rows = shape_of((images, PAD, width), BF)
    return run(
        prepare_kernel,
        "prepare",
        (tokens, cotangent),
        (rows, rows, shape_of((images, PAD, width), F32), shape_of((images, PAD, 1), F32)),
        14,
        scratch=[pltpu.VMEM((-(-count // 8) * 8 + 16, width), F32)],
    )


def attend_rows(normed, w_ref, qkv_ref, mixed_ref, probs_ref):
    images, rows, span = mixed_ref.shape
    low = lane_ids((rows, 128)) < HEAD_DIM
    key_ok = row_ids((rows, rows)) < SEQ
    zero = jnp.zeros((rows, 128), BF)
    proj = dot(normed, w_ref[...])
    qkv_ref[:, :, 0:span] = (proj[:, 0:span] * HEAD_DIM ** (-0.5)).astype(BF).reshape(images, rows, span)
    qkv_ref[:, :, span:] = proj[:, span:].astype(BF).reshape(images, rows, 2 * span)

    def image(i, carry):
        for p in range(span // 128):
            at = slice(p * 128, (p + 1) * 128)
            q = qkv_ref[i, :, at]
            k = qkv_ref[i, :, span + p * 128 : span + (p + 1) * 128]
            v = qkv_ref[i, :, 2 * span + p * 128 : 2 * span + (p + 1) * 128]
            mixed = []
            for h in range(2):
                q_one = jnp.where(low, q, zero) if h == 0 else jnp.where(low, zero, q)
                scores = jnp.where(key_ok, dot(k, q_one, LAST), -1e30)
                scaled = jnp.exp(scores - jnp.max(scores, axis=0, keepdims=True))
                weights = (scaled * (1.0 / jnp.sum(scaled, axis=0, keepdims=True))).astype(BF)
                probs_ref[i, 2 * p + h] = weights
                mixed.append(dot(weights, v, FIRST))
            mixed_ref[i, :, at] = jnp.where(low, mixed[0], mixed[1]).astype(BF)
        return carry

    lax.fori_loop(0, images, image, 0, unroll=3 if images % 3 == 0 else 1)


def assemble_rows(tables, own_ref, sib_ref, pieces):
    core_ref, own_place, sib_place = tables
    core = core_ref[0]
    part = own_ref.shape[1]
    for k in range(own_ref.shape[0]):
        for place, ref, which in ((own_place, own_ref, core), (sib_place, sib_ref, 1 - core)):
            row = pl.multiple_of(2 * part * k + part * which, 16)
            for lane, out_ref, at in pieces:
                out_ref[pl.ds(row, part), at] = ref[place[k], :, lane : lane + at.stop - at.start]


def assemble_smalls(place, ref, lane, norms_ref, router_ref):
    count = ref.shape[0]
    tile = jnp.concatenate([ref[place[k], 0:16, lane : lane + 128] for k in range(count)], axis=0)
    width = norms_ref.shape[1]
    columns = width // count
    norms = 0.0
    for k in range(count):
        shape = (128, width)
        spot = jnp.logical_and(lane_ids(shape) == row_ids(shape) + columns * k, row_ids(shape) < columns)
        norms = norms + dot(tile[16 * k : 16 * k + 16], spot.astype(BF))
    norms_ref[...] = norms[0:8]
    shape = (count, 16 * count)
    for j in range(width // 128):
        spot = lane_ids(shape) == row_ids(shape) * 16 + 4 + j
        router_ref[:, j * 128 : (j + 1) * 128] = dot(spot.astype(BF), tile).astype(BF)


def attend_first_kernel(stepwise, *refs):
    if stepwise:
        tables, refs = refs[:3], refs[3:]
        unit_ref, own_ref, sib_ref, n_ref, qkv_ref, mixed_ref, probs_ref, w_ref, norms_ref, router_ref = refs
        assemble_rows(tables, own_ref, sib_ref, [(0, w_ref, slice(0, w_ref.shape[1]))])
        assemble_smalls(tables[1], own_ref, w_ref.shape[1], norms_ref, router_ref)
    else:
        unit_ref, w_ref, norms_ref, n_ref, qkv_ref, mixed_ref, probs_ref = refs
    normed = (flat(unit_ref) * norms_ref[0:1, :] + norms_ref[1:2, :]).astype(BF)
    n_ref[...] = normed.reshape(n_ref.shape)
    attend_rows(normed, w_ref, qkv_ref, mixed_ref, probs_ref)


def attend_second_kernel(stepwise, *refs):
    if stepwise:
        tables, refs = refs[:3], refs[3:]
        n_ref, own_ref, sib_ref, own_out, sib_out, qkv_ref, mixed_ref, probs_ref, w_ref, out_w_ref = refs
        assemble_rows(tables, own_ref, sib_ref, [(0, w_ref, slice(0, w_ref.shape[1]))])
        assemble_rows(tables, own_out, sib_out, [(0, out_w_ref, slice(0, out_w_ref.shape[1]))])
    else:
        n_ref, w_ref, qkv_ref, mixed_ref, probs_ref = refs
    attend_rows(flat(n_ref), w_ref, qkv_ref, mixed_ref, probs_ref)


def attend_results(images, rows, span):
    return (
        shape_of((images, rows, 3 * span), BF),
        shape_of((images, rows, span), BF),
        shape_of((images, span // HEAD_DIM, rows, rows), BF),
    )


def attend_flops(images, rows, width, span):
    return 2 * images * rows * (3 * width * span + 2 * rows * span)


def attend_first(unit, tables, operands, span, experts):
    images, rows, width = unit.shape
    results = (shape_of((images, rows, width), BF),) + attend_results(images, rows, span)
    if tables:
        results += (
            shape_of((width, 3 * span), BF),
            shape_of((8, width), F32),
            shape_of((experts, width), BF),
        )
    return run(
        functools.partial(attend_first_kernel, bool(tables)),
        "attend_first",
        tables + (unit,) + operands,
        results,
        16,
        attend_flops(images, rows, width, span),
        scalars=len(tables),
    )


def attend_second(normed, tables, operands, span):
    images, rows, width = normed.shape
    results = attend_results(images, rows, span)
    if tables:
        results += (shape_of((width, 3 * span), BF), shape_of((width, 2 * span), BF))
    return run(
        functools.partial(attend_second_kernel, bool(tables)),
        "attend_second",
        tables + (normed,) + operands,
        results,
        16,
        attend_flops(images, rows, width, span),
        scalars=len(tables),
    )


def softmaxes(logits):
    ok = lane_ids(logits.shape) < SEQ
    masked = jnp.where(ok, logits, -1e30)
    up = jnp.exp(masked - jnp.max(masked, axis=1, keepdims=True))
    dispatch = up / jnp.sum(up, axis=1, keepdims=True)
    up = jnp.exp(logits - jnp.max(logits, axis=0, keepdims=True))
    combine = up / jnp.sum(up, axis=0, keepdims=True)
    return dispatch, combine


def place_rows(experts, image, offset):
    shape = (experts * SLOT_ROWS, experts)
    return (row_ids(shape) == lane_ids(shape) * SLOT_ROWS + offset + image).astype(BF)


def pick_rows(experts, image, offset):
    shape = (experts, experts * SLOT_ROWS)
    return (lane_ids(shape) == row_ids(shape) * SLOT_ROWS + offset + image).astype(BF)


def route_kernel(
    x_ref, m1_ref, m2_ref, out_w_ref, norms_ref, router_ref, g_ref, y_ref, n_ref, logits_ref, send_ref
):
    images, rows, width = x_ref.shape
    experts = router_ref.shape[0]
    half = m1_ref.shape[2]
    attn = dot(flat(m1_ref), out_w_ref[:, :half], LAST) + dot(flat(m2_ref), out_w_ref[:, half:], LAST)
    y = flat(x_ref).astype(F32) + attn
    y_ref[...] = y.reshape(y_ref.shape)
    unit, _ = layer_stats(y)
    normed = (unit * norms_ref[2:3, :] + norms_ref[3:4, :]).astype(BF)
    n_ref[...] = normed.reshape(n_ref.shape)
    placed = 0.0
    for i in range(images):
        logits = dot(router_ref[...], n_ref[i], LAST)
        logits_ref[i] = logits
        dispatch, combine = softmaxes(logits)
        slots = dot(dispatch.astype(BF), n_ref[i]).astype(BF)
        grad_returned = dot(combine.astype(BF), g_ref[i]).astype(BF)
        placed = placed + dot(place_rows(experts, i, 0), slots)
        placed = placed + dot(place_rows(experts, i, SLOT_ROWS // 2), grad_returned)
    send_ref[...] = placed.astype(BF)


def route(x_img, mixed_one, mixed_two, out_w, norms, router, g_img):
    images, rows, width = x_img.shape
    experts = router.shape[0]
    return run(
        route_kernel,
        "route",
        (x_img, mixed_one, mixed_two, out_w, norms, router, g_img),
        (
            shape_of((images, rows, width), F32),
            shape_of((images, rows, width), BF),
            shape_of((images, experts, rows), F32),
            shape_of((experts * SLOT_ROWS, width), BF),
        ),
        16,
        2 * images * rows * width * width,
    )


def split_rows(blocks):
    wide = blocks.astype(F32)
    half = SLOT_ROWS // 2
    shape = (blocks.shape[0] * half, blocks.shape[2])
    return wide[:, :half].reshape(shape).astype(BF), wide[:, half:].reshape(shape).astype(BF)


def join_rows(ones, twos):
    half = SLOT_ROWS // 2
    shape = (ones.shape[0] // half, half, ones.shape[1])
    return jnp.concatenate([ones.reshape(shape), twos.reshape(shape)], axis=1).astype(BF)


def gelu_parts(pre):
    cdf = 0.5 * (1.0 + lax.erf(pre * (0.5**0.5)))
    density = jnp.exp(-0.5 * pre * pre) * 0.3989422804014327
    return pre * cdf, cdf + pre * density


def expert_kernel(
    own_ref, near_ref, w1_ref, w2_ref, keep_ref, send_ref, slots_ref, grads_ref, hidden_ref, pre_ref
):
    count = own_ref.shape[0]
    blocks = jnp.concatenate([own_ref[...], near_ref[...]], axis=0)
    slots, grads = split_rows(blocks)
    pre = dot(slots, w1_ref[...])
    hidden, slope = gelu_parts(pre)
    hidden = hidden.astype(BF)
    returned = dot(hidden, w2_ref[...])
    grad_pre = (dot(grads, w2_ref[...], LAST) * slope).astype(BF)
    grad_slots = dot(grad_pre, w1_ref[...], LAST)
    joined = join_rows(returned, grad_slots)
    keep_ref[...] = joined[:count]
    send_ref[...] = joined[count:]
    slots_ref[...] = slots
    grads_ref[...] = grads
    hidden_ref[...] = hidden
    pre_ref[...] = grad_pre


def run_expert(own, near, first_weight, second_weight):
    width, units = first_weight.shape
    rows = (own.shape[0] + near.shape[0]) * SLOT_ROWS // 2
    return run(
        expert_kernel,
        "expert",
        (own, near, first_weight, second_weight),
        (
            shape_of(own.shape, BF),
            shape_of(near.shape, BF),
            shape_of((rows, width), BF),
            shape_of((rows, width), BF),
            shape_of((rows, units), BF),
            shape_of((rows, units), BF),
        ),
        16 if rows <= 512 else 48,
        8 * rows * width * units,
    )


def expert_grad_kernel(slots_ref, grads_ref, hidden_ref, pre_ref, d1_ref, d2_ref):
    d1_ref[...] = dot(slots_ref[...], pre_ref[...], FIRST)
    d2_ref[...] = dot(hidden_ref[...], grads_ref[...], FIRST)


def expert_grads(slots, grads, hidden, grad_pre):
    rows, width = slots.shape
    units = hidden.shape[1]
    return run(
        expert_grad_kernel,
        "expert_grads",
        (slots, grads, hidden, grad_pre),
        (shape_of((width, units), F32), shape_of((units, width), F32)),
        16 if rows <= 512 else 32,
        4 * rows * width * units,
    )


def moe_back_kernel(
    y_ref,
    n_ref,
    g_ref,
    logits_ref,
    back_ref,
    norms_ref,
    router_ref,
    out_w_ref,
    m1_ref,
    m2_ref,
    grad_y_ref,
    grad_mixed_ref,
    out_grad_ref,
    small_ref,
    attn_ref,
):
    images, rows, width = y_ref.shape
    experts = router_ref.shape[0]
    half = m1_ref.shape[2]
    gain = norms_ref[2:3, :]
    router_grad, gain_grad, shift_grad = 0.0, 0.0, 0.0
    for i in range(images):
        returned = dot(pick_rows(experts, i, 0), back_ref[...]).astype(BF)
        grad_slots = dot(pick_rows(experts, i, SLOT_ROWS // 2), back_ref[...]).astype(BF)
        dispatch, combine = softmaxes(logits_ref[i])
        grad_combine = dot(returned, g_ref[i], LAST)
        grad_dispatch = dot(grad_slots, n_ref[i], LAST)
        grad_logits = dispatch * (
            grad_dispatch - jnp.sum(grad_dispatch * dispatch, axis=1, keepdims=True)
        ) + combine * (grad_combine - jnp.sum(grad_combine * combine, axis=0, keepdims=True))
        grad_logits = grad_logits.astype(BF)
        router_grad = router_grad + dot(grad_logits, n_ref[i])
        grad_two = dot(dispatch.astype(BF), grad_slots, FIRST) + dot(grad_logits, router_ref[...], FIRST)
        unit, inv_std = layer_stats(y_ref[i])
        gain_grad = gain_grad + jnp.sum(grad_two * unit, axis=0, keepdims=True)
        shift_grad = shift_grad + jnp.sum(grad_two, axis=0, keepdims=True)
        scaled = grad_two * gain
        mean_one = jnp.mean(scaled, axis=-1, keepdims=True)
        mean_two = jnp.mean(scaled * unit, axis=-1, keepdims=True)
        grad_y = g_ref[i].astype(F32) + inv_std * (scaled - mean_one - unit * mean_two)
        grad_y_ref[i] = grad_y
        attn_ref[i] = grad_y.astype(BF)
    small_ref[...] = jnp.zeros_like(small_ref)
    small_ref[0:1, :] = gain_grad
    small_ref[1:2, :] = shift_grad
    small_ref[8 : 8 + experts, :] = router_grad
    grad_attn = flat(attn_ref)
    grad_mixed_ref[...] = dot(grad_attn, out_w_ref[...]).astype(BF).reshape(grad_mixed_ref.shape)
    out_grad_ref[:, :half] = dot(grad_attn, flat(m1_ref), FIRST)
    out_grad_ref[:, half:] = dot(grad_attn, flat(m2_ref), FIRST)


def moe_back(y, normed, g_img, logits, back, norms, router, out_w, mixed_one, mixed_two):
    images, rows, width = y.shape
    experts = router.shape[0]
    return run(
        moe_back_kernel,
        "moe_back",
        (y, normed, g_img, logits, back, norms, router, out_w, mixed_one, mixed_two),
        (
            shape_of((images, rows, width), F32),
            shape_of((images, rows, width), BF),
            shape_of((width, width), F32),
            shape_of((8 + experts, width), F32),
        ),
        16,
        4 * images * rows * width * width,
        scratch=[pltpu.VMEM((images, rows, width), BF)],
    )


def output_kernel(y_ref, logits_ref, back_ref, out_ref, wide):
    images, experts, _ = logits_ref.shape
    for i in range(images):
        returned = dot(pick_rows(experts, i, 0), back_ref[...]).astype(BF)
        _, combine = softmaxes(logits_ref[i])
        total = y_ref[i] + dot(combine.astype(BF), returned, FIRST)
        wide[SEQ * i : SEQ * (i + 1), :] = total[0:SEQ]
    out_ref[...] = wide[...].astype(BF)


def block_output(y, logits, back):
    images, rows, width = y.shape
    count = images * SEQ
    return run(
        output_kernel,
        "block_output",
        (y, logits, back),
        (shape_of((count, width), BF),),
        12,
        images * rows * width,
        scratch=[pltpu.VMEM((count, width), F32)],
    )[0]


def deal_rows(tables, full_ref, lanes, own_ref, sib_ref, lane):
    core_ref, own_place, sib_place = tables
    core = core_ref[0]
    count, part, _ = own_ref.shape
    span = lanes.stop - lanes.start
    for k in range(count):
        for place, ref, which in ((own_place, own_ref, core), (sib_place, sib_ref, 1 - core)):
            row = pl.multiple_of(2 * part * k + part * which, 16)
            ref[place[k], :, lane : lane + span] = full_ref[pl.ds(row, part), lanes].astype(BF)


def attend_back_kernel(stepwise, piece, *refs):
    if stepwise:
        tables, refs = refs[:3], refs[3:]
        n_ref, qkv_ref, probs_ref, mixed_ref, gm_ref, og_ref, grads_ref, own_ref, sib_ref, dw_ref = refs
    else:
        n_ref, qkv_ref, probs_ref, mixed_ref, gm_ref, grads_ref, dw_ref = refs
    images, rows, span = mixed_ref.shape
    low = lane_ids((rows, 128)) < HEAD_DIM
    zero = jnp.zeros((rows, 128), BF)
    minus = jnp.full((rows, 128), -1.0, BF)

    def image(i, carry):
        for p in range(span // 128):
            at = slice(p * 128, (p + 1) * 128)
            at_k = slice(span + p * 128, span + (p + 1) * 128)
            at_v = slice(2 * span + p * 128, 2 * span + (p + 1) * 128)
            q, k, v = qkv_ref[i, :, at], qkv_ref[i, :, at_k], qkv_ref[i, :, at_v]
            gm = gm_ref[i, :, piece * span + p * 128 : piece * span + (p + 1) * 128]
            inner = pltpu.roll(gm.astype(F32) * mixed_ref[i, :, at].astype(F32), HEAD_DIM, 1).astype(BF)
            grad_q, grad_k, grad_v = 0.0, 0.0, 0.0
            for h in range(2):
                mine = low if h == 0 else jnp.logical_not(low)
                weights = probs_ref[i, 2 * p + h]
                centred = dot(jnp.where(mine, v, minus), jnp.where(mine, gm, inner), LAST)
                grad_scores = (weights.astype(F32) * centred).astype(BF)
                grad_v = grad_v + dot(weights, jnp.where(mine, gm, zero))
                grad_k = grad_k + dot(grad_scores, jnp.where(mine, q, zero))
                grad_q = grad_q + dot(grad_scores, jnp.where(mine, k, zero), FIRST)
            grads_ref[i, :, at] = (grad_q * HEAD_DIM ** (-0.5)).astype(BF)
            grads_ref[i, :, at_k] = grad_k.astype(BF)
            grads_ref[i, :, at_v] = grad_v.astype(BF)
        return carry

    lax.fori_loop(0, images, image, 0, unroll=3 if images % 3 == 0 else 1)
    dw_ref[...] = dot(flat(n_ref), flat(grads_ref), FIRST)
    if stepwise:
        deal_rows(tables, dw_ref, slice(0, 3 * span), own_ref, sib_ref, 0)
        deal_rows(tables, og_ref, slice(piece * span, (piece + 1) * span), own_ref, sib_ref, 3 * span)


def attend_back(normed, qkv, probs, mixed, grad_mixed, out_grad_t, piece, tables, sizes):
    images, rows, width = normed.shape
    span = mixed.shape[2]
    operands = (normed, qkv, probs, mixed, grad_mixed)
    results = (shape_of((images, rows, 3 * span), BF),)
    scratch = ()
    if tables:
        operands += (out_grad_t,)
        results += (shape_of((sizes[0], width // sizes[0] // 2, 4 * span), BF),) * 2
        scratch = (pltpu.VMEM((width, 3 * span), F32),)
    else:
        results += (shape_of((width, 3 * span), F32),)
    return run(
        functools.partial(attend_back_kernel, bool(tables), piece),
        "attend_back",
        tables + operands,
        results,
        16,
        2 * images * rows * (3 * width * span + 4 * rows * span),
        scratch,
        scalars=len(tables),
    )


def input_back_kernel(unit_ref, inv_ref, gy_ref, p1_ref, p2_ref, w1_ref, w2_ref, norms_ref, out_ref, small_ref):
    images, rows, width = unit_ref.shape
    gain = norms_ref[0:1, :]
    grad_all = dot(flat(p1_ref), w1_ref[...], LAST) + dot(flat(p2_ref), w2_ref[...], LAST)
    gain_grad, shift_grad = 0.0, 0.0
    for i in range(images):
        grad_one = grad_all[i * rows : (i + 1) * rows]
        unit = unit_ref[i]
        gain_grad = gain_grad + jnp.sum(grad_one * unit, axis=0, keepdims=True)
        shift_grad = shift_grad + jnp.sum(grad_one, axis=0, keepdims=True)
        scaled = grad_one * gain
        mean_one = jnp.mean(scaled, axis=-1, keepdims=True)
        mean_two = jnp.mean(scaled * unit, axis=-1, keepdims=True)
        total = gy_ref[i] + inv_ref[i] * (scaled - mean_one - unit * mean_two)
        out_ref[SEQ * i : SEQ * (i + 1), :] = total[0:SEQ]
    small_ref[...] = jnp.zeros_like(small_ref)
    small_ref[0:1, :] = gain_grad
    small_ref[1:2, :] = shift_grad


def input_back(unit, inv_std, grad_y, grads_one, grads_two, weight_one, weight_two, norms):
    images, rows, width = unit.shape
    return run(
        input_back_kernel,
        "input_back",
        (unit, inv_std, grad_y, grads_one, grads_two, weight_one, weight_two, norms),
        (shape_of((images * SEQ, width), F32), shape_of((8, width), F32)),
        16,
        6 * images * rows * width * width,
    )


def merge_kernel(place, own_ref, core_ref, high_ref, small_ref, out_ref):
    count, part, span = own_ref.shape
    width = small_ref.shape[1]
    columns = width // count
    for k in range(count):
        total = own_ref[k].astype(F32) + core_ref[k].astype(F32) + high_ref[k].astype(F32)
        out_ref[k, :, 0:span] = total.astype(BF)
    norms = small_ref[0:16, :].astype(BF)
    routers = small_ref[16 : 16 + count, :].astype(BF)
    for k in range(count):
        shape = (width, 128)
        spot = jnp.logical_and(row_ids(shape) == lane_ids(shape) + columns * k, lane_ids(shape) < columns)
        rows = dot(norms, spot.astype(BF))
        shape = (16, count)
        for j in range(width // 128):
            spot = jnp.logical_and(row_ids(shape) == 4 + j, lane_ids(shape) == k)
            rows = rows + dot(spot.astype(BF), routers[:, j * 128 : (j + 1) * 128])
        out_ref[place[k], 0:16, span:] = rows.astype(BF)
        out_ref[place[k], 16:, span:] = jnp.zeros((part - 16, 128), BF)


def merge(place, own, from_core, from_high, small):
    count, part, span = own.shape
    return run(
        merge_kernel,
        "merge",
        (place, own, from_core, from_high, small),
        (shape_of((count, part, span + 128), BF),),
        12,
        scalars=1,
    )[0]


def swap(value, dp_size, tensor_size, dp_mask, tensor_mask):
    pairs = [
        (d * tensor_size + t, (d ^ dp_mask) * tensor_size + (t ^ tensor_mask))
        for d in range(dp_size)
        for t in range(tensor_size)
    ]
    return lax.ppermute(value, AXES, pairs)


def steps_of(dp_size):
    bits = dp_size.bit_length() - 1
    down = list(range(bits))[::-1]
    return [down, down[-1:] + down[:-1]]


def step_pairs(dp_size, tensor_size, step):
    orders = steps_of(dp_size)
    return [
        (d * tensor_size + t, (d ^ (1 << orders[t % 2][step])) * tensor_size + t)
        for d in range(dp_size)
        for t in range(tensor_size)
    ]


def places(dp_size, dp_index, core):
    away = dp_index ^ jnp.arange(dp_size, dtype=jnp.int32)
    both = []
    for order in steps_of(dp_size):
        at = jnp.zeros_like(away)
        for step, bit in enumerate(order):
            at = at | (((away >> bit) & 1) << step)
        both.append(at)
    return jnp.where(core == 0, both[0], both[1]), jnp.where(core == 0, both[1], both[0])


def pick(core, zero, one):
    return jnp.where(core == 0, zero, one), jnp.where(core == 0, one, zero)


def gather_first(qkv_weight, out_weight, router, norm_params, sizes, ids, along):
    core, high = ids
    rows, columns = qkv_weight.shape[1:]
    part = rows // 2
    small = jnp.concatenate([jnp.pad(norm_params, ((0, 0), (0, columns - rows))), router.T], axis=0)
    small_high = swap(small, *sizes, 0, 2)
    turned = jnp.concatenate([qkv_weight, out_weight.T[None]], axis=0)
    keep = lax.dynamic_slice_in_dim(turned, core * part, part, axis=1)
    give = lax.dynamic_slice_in_dim(turned, (1 - core) * part, part, axis=1)
    got = swap(give, *sizes, 0, 1)
    first, second = pick(core, keep, got)
    mine = jnp.concatenate([first, second], axis=2)
    mine = mine.transpose(1, 0, 2).reshape(part, 8 * columns)
    small_pair = jnp.stack([small, small_high])
    small_near = swap(small_pair, *sizes, 0, 1)
    first, second = pick(core, small_pair, small_near)
    by_core = jnp.stack([first, second], axis=1)
    first, second = pick(high, by_core[0], by_core[1])
    smalls = jnp.stack([first, second]).reshape(4, 2, columns)
    norm_rows = jnp.pad(smalls[:, 0, :rows], ((0, 0), (0, 128 - rows)))
    tile = jnp.concatenate([norm_rows, smalls[:, 1].reshape(-1, 128)], axis=0)
    tile = jnp.pad(tile, ((0, part - tile.shape[0]), (0, 0)))
    held = jnp.concatenate([mine[:, : 6 * columns], tile], axis=1)[None]
    out_own = mine[:, 6 * columns :]
    for step in range(sizes[0].bit_length() - 1):
        got = lax.ppermute(held, AXES, step_pairs(*sizes, step))
        if step == 0:
            out_high = swap(out_own, *sizes, 0, 2)
            got, out_high, along = lax.optimization_barrier((got, out_high, prepare(*along)))
        held = jnp.concatenate([held, got], axis=0)
    out_block = jnp.concatenate([out_own, out_high], axis=1)[None]
    return held, out_block, along


def gather_weights_plain(qkv_weight, out_weight, router, norm_params):
    qkv = lax.all_gather(qkv_weight, "dp", axis=1, tiled=True)
    qkv = lax.all_gather(qkv, "tensor", axis=2, tiled=True)
    out_w, router, norms = (
        lax.all_gather(lax.all_gather(w, "dp", axis=1, tiled=True), "tensor", axis=0, tiled=True)
        for w in (out_weight, router, norm_params)
    )
    width = qkv.shape[1]
    half = width // 2
    one = qkv[:, :, :half].transpose(1, 0, 2).reshape(width, 3 * half)
    two = qkv[:, :, half:].transpose(1, 0, 2).reshape(width, 3 * half)
    return one, two, out_w.T, norms.astype(F32), router.T


def sum_small(values, sizes):
    dp_size, tensor_size = sizes
    mask = 1
    while mask < tensor_size:
        values = values + swap(values, dp_size, tensor_size, 0, mask)
        mask *= 2
    mask = 1
    while mask < dp_size:
        values = values + swap(values, dp_size, tensor_size, mask, 0)
        mask *= 2
    return values


def scatter_weights(own_one, got_core, got_high, small, sizes, ids, place, rows, columns, along):
    core, tensor_index = ids
    part = rows // 2
    held = merge(place, own_one, got_core, got_high, small)
    output = None
    for step in range(sizes[0].bit_length() - 1)[::-1]:
        half = 1 << step
        got = lax.ppermute(held[half:], AXES, step_pairs(*sizes, step))
        if output is None:
            got, output = lax.optimization_barrier((got, block_output(*along)))
        held = (held[:half].astype(F32) + got.astype(F32)).astype(BF)
    mine = held[0]
    span = mine.shape[1] - 128
    tile = mine[:, span:]
    norm_grad = lax.dynamic_slice(tile, (tensor_index, 0), (1, rows)).astype(F32)
    router_grad = lax.dynamic_slice(
        tile[4 : 4 + tensor_count(span, columns) * columns // 128].reshape(-1), (tensor_index * columns,), (columns,)
    )
    by_core = mine[:, :span].reshape(part, 4, 2, columns)
    keep, give = pick(core, by_core[:, :, 0], by_core[:, :, 1])
    got = swap(give, *sizes, 0, 1)
    top, bottom = pick(core, keep, got)
    both = jnp.concatenate([top, bottom], axis=0).astype(F32).transpose(1, 0, 2)
    return both[:3], both[3].T, router_grad.astype(F32).reshape(columns, 1), norm_grad, output


def tensor_count(span, columns):
    return span // (2 * columns)


def on_device(
    sizes, tokens, qkv_weight, out_weight, router, norm_params, expert_in, expert_out, cotangent
):
    dp_size, tensor_size = sizes
    dp_index = lax.axis_index("dp")
    tensor_index = lax.axis_index("tensor")
    core = tensor_index % 2
    high = tensor_index // 2
    width = tokens.shape[1]
    half = width // 2
    rows = qkv_weight.shape[1]
    columns = qkv_weight.shape[2]
    experts = dp_size * router.shape[1]
    stepwise = rows % 32 == 0 and tensor_size == 4
    tables = ()
    if stepwise:
        tables = (core.reshape(1).astype(jnp.int32),) + places(dp_size, dp_index, core)
        held, out_block, (x_img, g_img, unit, inv_std) = gather_first(
            qkv_weight, out_weight, router, norm_params, sizes, (core, high), (tokens, cotangent)
        )
        held, out_block = lax.optimization_barrier((held, out_block))
        held_high = swap(held, *sizes, 0, 2)
        near = swap(held, *sizes, 0, 1)
        normed, qkv_one, mixed_one, probs_one, weight_one, norms, router_t = attend_first(
            unit, tables, (held, near), half, experts
        )
        got = lax.ppermute(out_block, AXES, step_pairs(*sizes, 0))
        out_block = jnp.concatenate([out_block, got], axis=0)
        normed, out_block = lax.optimization_barrier((normed, out_block))
        for step in range(1, dp_size.bit_length() - 1):
            got = lax.ppermute(out_block, AXES, step_pairs(*sizes, step))
            out_block = jnp.concatenate([out_block, got], axis=0)
        out_near = swap(out_block, *sizes, 0, 1)
        near_high = swap(held_high, *sizes, 0, 1)
        qkv_two, mixed_two, probs_two, weight_two, out_w = attend_second(
            normed, tables, (held_high, near_high, out_block, out_near), half
        )
    else:
        x_img, g_img, unit, inv_std = prepare(tokens, cotangent)
        weight_one, weight_two, out_w, norms, router_t = gather_weights_plain(
            qkv_weight, out_weight, router, norm_params
        )
        normed, qkv_one, mixed_one, probs_one = attend_first(unit, (), (weight_one, norms), half, experts)
        qkv_two, mixed_two, probs_two = attend_second(normed, (), (weight_two,), half)
    y, normed_two, logits, outgoing = route(x_img, mixed_one, mixed_two, out_w, norms, router_t, g_img)

    outgoing = outgoing.reshape(experts, SLOT_ROWS, width)
    arrived = lax.all_to_all(outgoing, "dp", split_axis=0, concat_axis=0, tiled=True)
    across = swap(arrived, *sizes, 0, 2)
    pair = jnp.concatenate([arrived, across], axis=0)
    near = swap(pair, *sizes, 0, 1)
    keep, away, *kept = run_expert(pair, near, expert_in[0], expert_out[0])
    got = swap(away, *sizes, 0, 1)
    summed = (keep.astype(F32) + got.astype(F32)).astype(BF)
    got = swap(summed[dp_size:], *sizes, 0, 2)
    got, (first_grad, second_grad) = lax.optimization_barrier((got, expert_grads(*kept)))
    summed = (summed[:dp_size].astype(F32) + got.astype(F32)).astype(BF)
    back = lax.all_to_all(summed, "dp", split_axis=0, concat_axis=0, tiled=True)
    back = back.reshape(experts * SLOT_ROWS, width)

    grad_y, grad_mixed, out_grad_t, small_two = moe_back(
        y, normed_two, g_img, logits, back, norms, router_t, out_w, mixed_one, mixed_two
    )
    grads_two, *dealt = attend_back(
        normed, qkv_two, probs_two, mixed_two, grad_mixed, out_grad_t, 1, tables, sizes
    )
    if stepwise:
        own, sib = dealt
        got = swap(sib, *sizes, 0, 1)
        paired = (own.astype(F32) + got.astype(F32)).astype(BF)
        paired, grad_mixed = lax.optimization_barrier((paired, grad_mixed))
        got_high = swap(paired, *sizes, 0, 2)
    grads_one, *dealt_one = attend_back(
        normed, qkv_one, probs_one, mixed_one, grad_mixed, out_grad_t, 0, tables, sizes
    )
    if stepwise:
        own, sib = dealt_one
        got_core = swap(sib, *sizes, 0, 1)
    input_grad, small_one = input_back(
        unit, inv_std, grad_y, grads_one, grads_two, weight_one, weight_two, norms
    )
    small = jnp.concatenate([small_one[0:2], small_two[0:2], small_two[8:]], axis=0)
    if stepwise:
        small = small + swap(small, *sizes, 0, 1)
        small = small + swap(small, *sizes, 0, 2)
        small = jnp.concatenate(
            [small[:4], jnp.zeros((12, width), F32), small[4:], jnp.zeros((-experts % 16, width), F32)], axis=0
        )
        qkv_grad, out_grad, router_grad, norm_grad, output = scatter_weights(
            own, got_core, got_high, small, sizes, (core, tensor_index), tables[1], rows, columns, (y, logits, back)
        )
    else:
        output = block_output(y, logits, back)
        small = sum_small(small, sizes)
        norm_grad = lax.dynamic_slice(small, (tensor_index, dp_index * rows), (1, rows))
        router_grad = lax.dynamic_slice(
            small, (4 + dp_index, tensor_index * columns), (1, columns)
        ).reshape(columns, 1)
        full = jnp.concatenate(
            [dealt_one[0].reshape(width, 3, half), dealt[0].reshape(width, 3, half)], axis=2
        ).transpose(1, 0, 2)
        qkv_grad = lax.psum_scatter(full, "dp", scatter_dimension=1, tiled=True)
        qkv_grad = lax.psum_scatter(qkv_grad, "tensor", scatter_dimension=2, tiled=True)
        out_grad = lax.psum_scatter(out_grad_t.T, "dp", scatter_dimension=1, tiled=True)
        out_grad = lax.psum_scatter(out_grad, "tensor", scatter_dimension=0, tiled=True)
    return (
        output,
        input_grad,
        qkv_grad,
        out_grad,
        router_grad,
        norm_grad,
        first_grad[None],
        second_grad[None],
    )


def solution(mesh):
    sizes = (mesh.shape["dp"], mesh.shape["tensor"])
    return jax.shard_map(
        functools.partial(on_device, sizes),
        mesh=mesh,
        in_specs=(
            P(("dp", "tensor"), None),
            P(None, "dp", "tensor"),
            P("tensor", "dp"),
            P("tensor", "dp"),
            P("tensor", "dp"),
            P("dp", None, "tensor"),
            P("dp", "tensor", None),
            P(("dp", "tensor"), None),
        ),
        out_specs=(
            P(("dp", "tensor"), None),
            P(("dp", "tensor"), None),
            P(None, "dp", "tensor"),
            P("tensor", "dp"),
            P("tensor", "dp"),
            P("tensor", "dp"),
            P("dp", None, "tensor"),
            P("dp", "tensor", None),
        ),
        check_vma=False,
    )
```

```python
import functools

import jax
import jax.numpy as jnp
from jax import lax
from jax.experimental import pallas as pl
from jax.experimental.pallas import tpu as pltpu
from jax.sharding import PartitionSpec as P

HEAD_DIM = 64
SEQ = 197
PAD = 208
SLOT_ROWS = 16
AXES = ("dp", "tensor")
BF = jnp.bfloat16
F32 = jnp.float32
LAST = (((1,), (1,)), ((), ()))
FIRST = (((0,), (0,)), ((), ()))
MIDDLE = (((1,), (0,)), ((), ()))
MIB = 1024 * 1024


def dot(a, b, dims=MIDDLE):
    return lax.dot_general(a, b, dims, preferred_element_type=F32)


def shape_of(shape, dtype):
    return jax.ShapeDtypeStruct(shape, dtype)


def run(kernel, name, operands, results, limit, scratch=(), scalars=0):
    memory = [pltpu.SMEM] * scalars + [pltpu.VMEM] * (len(operands) - scalars)
    return pl.pallas_call(
        kernel,
        in_specs=[pl.BlockSpec(memory_space=m) for m in memory],
        out_specs=[pl.BlockSpec(memory_space=pltpu.VMEM) for _ in results],
        out_shape=list(results),
        scratch_shapes=list(scratch),
        compiler_params=pltpu.CompilerParams(vmem_limit_bytes=limit * MIB),
        cost_estimate=pl.CostEstimate(flops=1, bytes_accessed=1, transcendentals=0),
        name=name,
    )(*operands)


def layer_stats(values):
    centre = jnp.mean(values, axis=-1, keepdims=True)
    centred = values - centre
    spread = jnp.mean(centred * centred, axis=-1, keepdims=True)
    inv_std = lax.rsqrt(spread + 1e-06)
    return centred * inv_std, inv_std


def lane_ids(shape):
    return lax.broadcasted_iota(jnp.int32, shape, len(shape) - 1)


def row_ids(shape):
    return lax.broadcasted_iota(jnp.int32, shape, len(shape) - 2)


def flat(ref):
    images, rows, columns = ref.shape
    return ref[...].reshape(images * rows, columns)


def prepare_kernel(x_ref, g_ref, x_out, g_out, unit_out, inv_out, wide):
    count, width = x_ref.shape
    real = row_ids((PAD, width)) < SEQ
    wide[count:, :] = jnp.zeros((wide.shape[0] - count, width), F32)
    for ref, out in ((x_ref, x_out), (g_ref, g_out)):
        wide[0:count, :] = ref[...].astype(F32)
        for i in range(out.shape[0]):
            rows = jnp.where(real, wide[SEQ * i : SEQ * i + PAD, :], 0.0)
            out[i] = rows.astype(BF)
            if ref is x_ref:
                unit, inv_std = layer_stats(rows)
                unit_out[i] = unit
                inv_out[i] = inv_std


def prepare(tokens, cotangent):
    count, width = tokens.shape
    images = count // SEQ
    rows = shape_of((images, PAD, width), BF)
    return run(
        prepare_kernel,
        "prepare",
        (tokens, cotangent),
        (rows, rows, shape_of((images, PAD, width), F32), shape_of((images, PAD, 1), F32)),
        14,
        scratch=[pltpu.VMEM((-(-count // 8) * 8 + 16, width), F32)],
    )


def attend_rows(normed, w_ref, qkv_ref, mixed_ref, probs_ref):
    images, rows, span = mixed_ref.shape
    low = lane_ids((rows, 128)) < HEAD_DIM
    key_ok = row_ids((rows, rows)) < SEQ
    zero = jnp.zeros((rows, 128), BF)
    proj = dot(normed, w_ref[...])
    qkv_ref[:, :, 0:span] = (proj[:, 0:span] * HEAD_DIM ** (-0.5)).astype(BF).reshape(images, rows, span)
    qkv_ref[:, :, span:] = proj[:, span:].astype(BF).reshape(images, rows, 2 * span)

    def image(i, carry):
        for p in range(span // 128):
            at = slice(p * 128, (p + 1) * 128)
            q = qkv_ref[i, :, at]
            k = qkv_ref[i, :, span + p * 128 : span + (p + 1) * 128]
            v = qkv_ref[i, :, 2 * span + p * 128 : 2 * span + (p + 1) * 128]
            mixed = []
            for h in range(2):
                q_one = jnp.where(low, q, zero) if h == 0 else jnp.where(low, zero, q)
                scores = jnp.where(key_ok, dot(k, q_one, LAST), -1e30)
                scaled = jnp.exp(scores - jnp.max(scores, axis=0, keepdims=True))
                weights = (scaled * (1.0 / jnp.sum(scaled, axis=0, keepdims=True))).astype(BF)
                probs_ref[i, 2 * p + h] = weights
                mixed.append(dot(weights, v, FIRST))
            mixed_ref[i, :, at] = jnp.where(low, mixed[0], mixed[1]).astype(BF)
        return carry

    lax.fori_loop(0, images, image, 0, unroll=3 if images % 3 == 0 else 1)


def block_refs(refs):
    return [(ref, i) for ref in refs for i in range(ref.shape[0])]


def assemble_rows(owners, parts, kinds, out_ref, lane, columns):
    for side, (owner, refs) in enumerate(zip(owners, parts, strict=True)):
        for p, (ref, i) in enumerate(block_refs(refs)):
            count = ref.shape[1]
            row = pl.multiple_of(count * owner[p], 16)
            for at, kind in enumerate(kinds):
                out_ref[pl.ds(row, count), lane + (2 * at + side) * columns : lane + (2 * at + side + 1) * columns] = (
                    ref[i, :, kind * columns : (kind + 1) * columns]
                )


def attend_first_kernel(counts, *refs):
    if counts:
        own, sib = counts
        owners, refs = refs[:2], refs[2:]
        unit_ref, norms_ref, refs = refs[0], refs[1], refs[2:]
        parts, refs = (refs[:own], refs[own : own + sib]), refs[own + sib :]
        n_ref, qkv_ref, mixed_ref, probs_ref, w_ref, out_w_ref = refs
        columns = mixed_ref.shape[2] // 2
        assemble_rows(owners, parts, range(3), w_ref, 0, columns)
        assemble_rows(owners, parts, [3], out_w_ref, 0, columns)
    else:
        unit_ref, norms_ref, w_ref, n_ref, qkv_ref, mixed_ref, probs_ref = refs
    normed = (flat(unit_ref) * norms_ref[0:1, :] + norms_ref[1:2, :]).astype(BF)
    n_ref[...] = normed.reshape(n_ref.shape)
    attend_rows(normed, w_ref, qkv_ref, mixed_ref, probs_ref)


def attend_second_kernel(counts, *refs):
    if counts:
        own, sib = counts
        owners, refs = refs[:2], refs[2:]
        n_ref, refs = refs[0], refs[1:]
        parts, refs = (refs[:own], refs[own : own + sib]), refs[own + sib :]
        qkv_ref, mixed_ref, probs_ref, w_ref, out_w_ref = refs
        columns = mixed_ref.shape[2] // 2
        assemble_rows(owners, parts, range(3), w_ref, 0, columns)
        assemble_rows(owners, parts, [3], out_w_ref, 0, columns)
    else:
        n_ref, w_ref, qkv_ref, mixed_ref, probs_ref = refs
    attend_rows(flat(n_ref), w_ref, qkv_ref, mixed_ref, probs_ref)


def attend_results(images, rows, span):
    return (
        shape_of((images, rows, 3 * span), BF),
        shape_of((images, rows, span), BF),
        shape_of((images, span // HEAD_DIM, rows, rows), BF),
    )


def attend(kernel, name, results, rows_in, span, owners, weights):
    images, rows, width = rows_in[0].shape
    results = results + attend_results(images, rows, span)
    counts = None
    if owners:
        counts = tuple(map(len, weights))
        weights = sum(weights, ())
        results += (shape_of((width, 3 * span), BF), shape_of((width, span), BF))
    return run(
        functools.partial(kernel, counts),
        name,
        owners + rows_in + weights,
        results,
        16,
        scalars=len(owners),
    )


def attend_first(unit, norms, span, owners, weights):
    normed = (shape_of(unit.shape, BF),)
    return attend(attend_first_kernel, "attend_first", normed, (unit, norms), span, owners, weights)


def attend_second(normed, span, owners, weights):
    return attend(attend_second_kernel, "attend_second", (), (normed,), span, owners, weights)


def softmaxes(logits):
    ok = lane_ids(logits.shape) < SEQ
    masked = jnp.where(ok, logits, -1e30)
    up = jnp.exp(masked - jnp.max(masked, axis=1, keepdims=True))
    dispatch = up / jnp.sum(up, axis=1, keepdims=True)
    up = jnp.exp(logits - jnp.max(logits, axis=0, keepdims=True))
    combine = up / jnp.sum(up, axis=0, keepdims=True)
    return dispatch, combine


def place_rows(experts, image, offset):
    shape = (experts * SLOT_ROWS, experts)
    return (row_ids(shape) == lane_ids(shape) * SLOT_ROWS + offset + image).astype(BF)


def pick_rows(experts, image, offset):
    shape = (experts, experts * SLOT_ROWS)
    return (lane_ids(shape) == row_ids(shape) * SLOT_ROWS + offset + image).astype(BF)


def route_kernel(
    x_ref, m1_ref, m2_ref, o1_ref, o2_ref, norms_ref, router_ref, g_ref, y_ref, n_ref, logits_ref, send_ref
):
    images, rows, width = x_ref.shape
    experts = router_ref.shape[0]
    attn = dot(flat(m1_ref), o1_ref[...], LAST) + dot(flat(m2_ref), o2_ref[...], LAST)
    y = flat(x_ref).astype(F32) + attn
    y_ref[...] = y.reshape(y_ref.shape)
    unit, _ = layer_stats(y)
    normed = (unit * norms_ref[2:3, :] + norms_ref[3:4, :]).astype(BF)
    n_ref[...] = normed.reshape(n_ref.shape)
    placed = 0.0
    for i in range(images):
        logits = dot(router_ref[...], n_ref[i], LAST)
        logits_ref[i] = logits
        dispatch, combine = softmaxes(logits)
        slots = dot(dispatch.astype(BF), n_ref[i]).astype(BF)
        grad_returned = dot(combine.astype(BF), g_ref[i]).astype(BF)
        placed = placed + dot(place_rows(experts, i, 0), slots)
        placed = placed + dot(place_rows(experts, i, SLOT_ROWS // 2), grad_returned)
    send_ref[...] = placed.astype(BF)


def route(x_img, mixed_one, mixed_two, out_one, out_two, norms, router, g_img):
    images, rows, width = x_img.shape
    experts = router.shape[0]
    return run(
        route_kernel,
        "route",
        (x_img, mixed_one, mixed_two, out_one, out_two, norms, router, g_img),
        (
            shape_of((images, rows, width), F32),
            shape_of((images, rows, width), BF),
            shape_of((images, experts, rows), F32),
            shape_of((experts * SLOT_ROWS, width), BF),
        ),
        16,
    )


def split_rows(blocks):
    wide = blocks.astype(F32)
    half = SLOT_ROWS // 2
    shape = (blocks.shape[0] * half, blocks.shape[2])
    return wide[:, :half].reshape(shape).astype(BF), wide[:, half:].reshape(shape).astype(BF)


def join_rows(ones, twos):
    half = SLOT_ROWS // 2
    shape = (ones.shape[0] // half, half, ones.shape[1])
    return jnp.concatenate([ones.reshape(shape), twos.reshape(shape)], axis=1).astype(BF)


def gelu_parts(pre):
    cdf = 0.5 * (1.0 + lax.erf(pre * (0.5**0.5)))
    density = jnp.exp(-0.5 * pre * pre) * 0.3989422804014327
    return pre * cdf, cdf + pre * density


def expert_kernel(
    own_ref, near_ref, w1_ref, w2_ref, keep_ref, send_ref, slots_ref, grads_ref, hidden_ref, pre_ref
):
    count = own_ref.shape[0]
    blocks = jnp.concatenate([own_ref[...], near_ref[...]], axis=0)
    slots, grads = split_rows(blocks)
    pre = dot(slots, w1_ref[...])
    hidden, slope = gelu_parts(pre)
    hidden = hidden.astype(BF)
    returned = dot(hidden, w2_ref[...])
    grad_pre = (dot(grads, w2_ref[...], LAST) * slope).astype(BF)
    grad_slots = dot(grad_pre, w1_ref[...], LAST)
    joined = join_rows(returned, grad_slots)
    keep_ref[...] = joined[:count]
    send_ref[...] = joined[count:]
    slots_ref[...] = slots
    grads_ref[...] = grads
    hidden_ref[...] = hidden
    pre_ref[...] = grad_pre


def run_expert(own, near, first_weight, second_weight):
    width, units = first_weight.shape
    rows = (own.shape[0] + near.shape[0]) * SLOT_ROWS // 2
    return run(
        expert_kernel,
        "expert",
        (own, near, first_weight, second_weight),
        (
            shape_of(own.shape, BF),
            shape_of(near.shape, BF),
            shape_of((rows, width), BF),
            shape_of((rows, width), BF),
            shape_of((rows, units), BF),
            shape_of((rows, units), BF),
        ),
        16 if rows <= 512 else 48,
    )


def expert_grad_kernel(slots_ref, grads_ref, hidden_ref, pre_ref, d1_ref, d2_ref):
    d1_ref[...] = dot(slots_ref[...], pre_ref[...], FIRST)
    d2_ref[...] = dot(hidden_ref[...], grads_ref[...], FIRST)


def expert_grads(slots, grads, hidden, grad_pre):
    rows, width = slots.shape
    units = hidden.shape[1]
    return run(
        expert_grad_kernel,
        "expert_grads",
        (slots, grads, hidden, grad_pre),
        (shape_of((width, units), F32), shape_of((units, width), F32)),
        16 if rows <= 512 else 32,
    )


def moe_back_kernel(
    y_ref,
    n_ref,
    g_ref,
    logits_ref,
    back_ref,
    norms_ref,
    router_ref,
    o1_ref,
    o2_ref,
    m1_ref,
    m2_ref,
    grad_y_ref,
    grad_mixed_ref,
    out_grad_ref,
    small_ref,
    attn_ref,
):
    images, rows, width = y_ref.shape
    experts = router_ref.shape[0]
    half = m1_ref.shape[2]
    gain = norms_ref[2:3, :]
    router_grad, gain_grad, shift_grad = 0.0, 0.0, 0.0
    for i in range(images):
        returned = dot(pick_rows(experts, i, 0), back_ref[...]).astype(BF)
        grad_slots = dot(pick_rows(experts, i, SLOT_ROWS // 2), back_ref[...]).astype(BF)
        dispatch, combine = softmaxes(logits_ref[i])
        grad_combine = dot(returned, g_ref[i], LAST)
        grad_dispatch = dot(grad_slots, n_ref[i], LAST)
        grad_logits = dispatch * (
            grad_dispatch - jnp.sum(grad_dispatch * dispatch, axis=1, keepdims=True)
        ) + combine * (grad_combine - jnp.sum(grad_combine * combine, axis=0, keepdims=True))
        grad_logits = grad_logits.astype(BF)
        router_grad = router_grad + dot(grad_logits, n_ref[i])
        grad_two = dot(dispatch.astype(BF), grad_slots, FIRST) + dot(grad_logits, router_ref[...], FIRST)
        unit, inv_std = layer_stats(y_ref[i])
        gain_grad = gain_grad + jnp.sum(grad_two * unit, axis=0, keepdims=True)
        shift_grad = shift_grad + jnp.sum(grad_two, axis=0, keepdims=True)
        scaled = grad_two * gain
        mean_one = jnp.mean(scaled, axis=-1, keepdims=True)
        mean_two = jnp.mean(scaled * unit, axis=-1, keepdims=True)
        grad_y = g_ref[i].astype(F32) + inv_std * (scaled - mean_one - unit * mean_two)
        grad_y_ref[i] = grad_y
        attn_ref[i] = grad_y.astype(BF)
    small_ref[...] = jnp.zeros_like(small_ref)
    small_ref[0:1, :] = gain_grad
    small_ref[1:2, :] = shift_grad
    small_ref[8 : 8 + experts, :] = router_grad
    grad_attn = flat(attn_ref)
    shape = m1_ref.shape
    grad_mixed_ref[:, :, :half] = dot(grad_attn, o1_ref[...]).astype(BF).reshape(shape)
    grad_mixed_ref[:, :, half:] = dot(grad_attn, o2_ref[...]).astype(BF).reshape(shape)
    out_grad_ref[:, :half] = dot(grad_attn, flat(m1_ref), FIRST)
    out_grad_ref[:, half:] = dot(grad_attn, flat(m2_ref), FIRST)


def moe_back(y, normed, g_img, logits, back, norms, router, out_one, out_two, mixed_one, mixed_two):
    images, rows, width = y.shape
    experts = router.shape[0]
    return run(
        moe_back_kernel,
        "moe_back",
        (y, normed, g_img, logits, back, norms, router, out_one, out_two, mixed_one, mixed_two),
        (
            shape_of((images, rows, width), F32),
            shape_of((images, rows, width), BF),
            shape_of((width, width), F32),
            shape_of((8 + experts, width), F32),
        ),
        16,
        scratch=[pltpu.VMEM((images, rows, width), BF)],
    )


def output_kernel(y_ref, logits_ref, back_ref, out_ref, wide):
    images, experts, _ = logits_ref.shape
    for i in range(images):
        returned = dot(pick_rows(experts, i, 0), back_ref[...]).astype(BF)
        _, combine = softmaxes(logits_ref[i])
        total = y_ref[i] + dot(combine.astype(BF), returned, FIRST)
        wide[SEQ * i : SEQ * (i + 1), :] = total[0:SEQ]
    out_ref[...] = wide[...].astype(BF)


def block_output(y, logits, back):
    images, rows, width = y.shape
    count = images * SEQ
    return run(
        output_kernel,
        "block_output",
        (y, logits, back),
        (shape_of((count, width), BF),),
        12,
        scratch=[pltpu.VMEM((count, width), F32)],
    )[0]


def deal_rows(owners, full_ref, first, kinds, refs, columns):
    for side, (owner, ref) in enumerate(zip(owners, refs, strict=True)):
        blocks, count, _ = ref.shape
        for p in range(blocks):
            row = pl.multiple_of(count * owner[p], 16)
            for at, kind in enumerate(kinds):
                lane = first + (2 * at + side) * columns
                ref[p, :, kind * columns : (kind + 1) * columns] = full_ref[
                    pl.ds(row, count), lane : lane + columns
                ].astype(BF)


def attend_back_kernel(stepwise, piece, *refs):
    if stepwise:
        owners, refs = refs[:2], refs[2:]
        n_ref, qkv_ref, probs_ref, mixed_ref, gm_ref, og_ref, grads_ref, own_ref, sib_ref, dw_ref = refs
    else:
        n_ref, qkv_ref, probs_ref, mixed_ref, gm_ref, grads_ref, dw_ref = refs
    images, rows, span = mixed_ref.shape
    low = lane_ids((rows, 128)) < HEAD_DIM
    zero = jnp.zeros((rows, 128), BF)
    minus = jnp.full((rows, 128), -1.0, BF)

    def image(i, carry):
        for p in range(span // 128):
            at = slice(p * 128, (p + 1) * 128)
            at_k = slice(span + p * 128, span + (p + 1) * 128)
            at_v = slice(2 * span + p * 128, 2 * span + (p + 1) * 128)
            q, k, v = qkv_ref[i, :, at], qkv_ref[i, :, at_k], qkv_ref[i, :, at_v]
            gm = gm_ref[i, :, piece * span + p * 128 : piece * span + (p + 1) * 128]
            inner = pltpu.roll(gm.astype(F32) * mixed_ref[i, :, at].astype(F32), HEAD_DIM, 1).astype(BF)
            grad_q, grad_k, grad_v = 0.0, 0.0, 0.0
            for h in range(2):
                mine = low if h == 0 else jnp.logical_not(low)
                weights = probs_ref[i, 2 * p + h]
                centred = dot(jnp.where(mine, v, minus), jnp.where(mine, gm, inner), LAST)
                grad_scores = (weights.astype(F32) * centred).astype(BF)
                grad_v = grad_v + dot(weights, jnp.where(mine, gm, zero))
                grad_k = grad_k + dot(grad_scores, jnp.where(mine, q, zero))
                grad_q = grad_q + dot(grad_scores, jnp.where(mine, k, zero), FIRST)
            grads_ref[i, :, at] = (grad_q * HEAD_DIM ** (-0.5)).astype(BF)
            grads_ref[i, :, at_k] = grad_k.astype(BF)
            grads_ref[i, :, at_v] = grad_v.astype(BF)
        return carry

    lax.fori_loop(0, images, image, 0, unroll=3 if images % 3 == 0 else 1)
    dw_ref[...] = dot(flat(n_ref), flat(grads_ref), FIRST)
    if stepwise:
        deal_rows(owners, dw_ref, 0, range(3), (own_ref, sib_ref), span // 2)
        deal_rows(owners, og_ref, piece * span, [3], (own_ref, sib_ref), span // 2)


def attend_back(normed, qkv, probs, mixed, grad_mixed, out_grad_t, piece, owners, sizes):
    images, rows, width = normed.shape
    span = mixed.shape[2]
    operands = (normed, qkv, probs, mixed, grad_mixed)
    results = (shape_of((images, rows, 3 * span), BF),)
    scratch = ()
    if owners:
        operands += (out_grad_t,)
        results += (shape_of((sizes[0], width // sizes[0], 2 * span), BF),) * 2
        scratch = (pltpu.VMEM((width, 3 * span), F32),)
    else:
        results += (shape_of((width, 3 * span), F32),)
    return run(
        functools.partial(attend_back_kernel, bool(owners), piece),
        "attend_back",
        owners + operands,
        results,
        16,
        scratch,
        scalars=len(owners),
    )


def input_back_kernel(unit_ref, inv_ref, gy_ref, p1_ref, p2_ref, w1_ref, w2_ref, norms_ref, out_ref, small_ref):
    images, rows, width = unit_ref.shape
    gain = norms_ref[0:1, :]
    grad_all = dot(flat(p1_ref), w1_ref[...], LAST) + dot(flat(p2_ref), w2_ref[...], LAST)
    gain_grad, shift_grad = 0.0, 0.0
    for i in range(images):
        grad_one = grad_all[i * rows : (i + 1) * rows]
        unit = unit_ref[i]
        gain_grad = gain_grad + jnp.sum(grad_one * unit, axis=0, keepdims=True)
        shift_grad = shift_grad + jnp.sum(grad_one, axis=0, keepdims=True)
        scaled = grad_one * gain
        mean_one = jnp.mean(scaled, axis=-1, keepdims=True)
        mean_two = jnp.mean(scaled * unit, axis=-1, keepdims=True)
        total = gy_ref[i] + inv_ref[i] * (scaled - mean_one - unit * mean_two)
        out_ref[SEQ * i : SEQ * (i + 1), :] = total[0:SEQ]
    small_ref[...] = jnp.zeros_like(small_ref)
    small_ref[0:1, :] = gain_grad
    small_ref[1:2, :] = shift_grad


def input_back(unit, inv_std, grad_y, grads_one, grads_two, weight_one, weight_two, norms):
    images, rows, width = unit.shape
    return run(
        input_back_kernel,
        "input_back",
        (unit, inv_std, grad_y, grads_one, grads_two, weight_one, weight_two, norms),
        (shape_of((images * SEQ, width), F32), shape_of((8, width), F32)),
        16,
    )


def pack_kernel(qkv_ref, out_ref, block_ref):
    kinds, _, columns = qkv_ref.shape
    for kind in range(kinds):
        block_ref[0, :, kind * columns : (kind + 1) * columns] = qkv_ref[kind]
    block_ref[0, :, kinds * columns :] = out_ref[...].T


def pack(qkv_weight, out_weight):
    kinds, rows, columns = qkv_weight.shape
    return run(
        pack_kernel,
        "pack",
        (qkv_weight, out_weight),
        (shape_of((1, rows, (kinds + 1) * columns), BF),),
        4,
    )[0]


def unpack_kernel(own_ref, got_ref, qkv_ref, out_ref):
    kinds, _, columns = qkv_ref.shape
    total = own_ref[0].astype(F32) + got_ref[0].astype(F32)
    for kind in range(kinds):
        qkv_ref[kind] = total[:, kind * columns : (kind + 1) * columns]
    out_ref[...] = total[:, kinds * columns :].T


def unpack(own, got, columns):
    _, rows, lanes = own.shape
    kinds = lanes // columns - 1
    return run(
        unpack_kernel,
        "unpack",
        (own, got),
        (shape_of((kinds, rows, columns), F32), shape_of((columns, rows), F32)),
        4,
    )


def swap(value, dp_size, tensor_size, dp_mask, tensor_mask):
    pairs = [
        (d * tensor_size + t, (d ^ dp_mask) * tensor_size + (t ^ tensor_mask))
        for d in range(dp_size)
        for t in range(tensor_size)
    ]
    return lax.ppermute(value, AXES, pairs)


def steps_of(dp_size):
    bits = dp_size.bit_length() - 1
    down = list(range(bits))[::-1]
    return [down, down[-1:] + down[:-1]]


def step_pairs(dp_size, tensor_size, step):
    orders = steps_of(dp_size)
    return [
        (d * tensor_size + t, (d ^ (1 << orders[t % 2][step])) * tensor_size + t)
        for d in range(dp_size)
        for t in range(tensor_size)
    ]


def owners_of(dp_size, dp_index, core):
    both = []
    for order in steps_of(dp_size):
        place = jnp.arange(dp_size, dtype=jnp.int32)
        away = jnp.zeros_like(place)
        for step, bit in enumerate(order):
            away = away | (((place >> step) & 1) << bit)
        both.append(away ^ dp_index)
    return jnp.where(core == 0, both[0], both[1]), jnp.where(core == 0, both[1], both[0])


def gather_smalls(router, norm_params, sizes, ids):
    dp_index, tensor_index = ids
    rows, columns = norm_params.shape[1], router.shape[0]
    experts = sizes[0] * router.shape[1]
    width = rows * sizes[0]
    held = jnp.zeros((-(-(sizes[1] + experts) // 16) * 16, width), BF)
    held = lax.dynamic_update_slice(held, norm_params, (tensor_index, dp_index * rows))
    held = lax.dynamic_update_slice(held, router.T, (sizes[1] + dp_index, tensor_index * columns))
    held = sum_small(held, sizes)
    return held[: sizes[1]].astype(F32), held[sizes[1] : sizes[1] + experts]


def gather_first(qkv_weight, out_weight, sizes, along):
    held = pack(qkv_weight, out_weight)
    own, sib, own_high, sib_high = [], [], [], []
    steps = sizes[0].bit_length() - 1
    for step in range(steps):
        got = lax.ppermute(held, AXES, step_pairs(*sizes, step))
        if step == 1:
            got, along = lax.optimization_barrier((got, prepare(*along)))
        fresh = [held, got] if step == 0 else [got]
        if step < steps - 1:
            held = jnp.concatenate([held, got], axis=0)
            fresh = [held] if step == 0 else fresh
        own += fresh
        for block in fresh:
            sib.append(swap(block, *sizes, 0, 1))
            own_high.append(swap(block, *sizes, 0, 2))
            sib_high.append(swap(own_high[-1], *sizes, 0, 1))
    return (tuple(own), tuple(sib)), (tuple(own_high), tuple(sib_high)), along


def gather_weights_plain(qkv_weight, out_weight, router, norm_params):
    qkv = lax.all_gather(qkv_weight, "dp", axis=1, tiled=True)
    qkv = lax.all_gather(qkv, "tensor", axis=2, tiled=True)
    out_w, router, norms = (
        lax.all_gather(lax.all_gather(w, "dp", axis=1, tiled=True), "tensor", axis=0, tiled=True)
        for w in (out_weight, router, norm_params)
    )
    width = qkv.shape[1]
    half = width // 2
    one = qkv[:, :, :half].transpose(1, 0, 2).reshape(width, 3 * half)
    two = qkv[:, :, half:].transpose(1, 0, 2).reshape(width, 3 * half)
    return one, two, out_w[:half].T, out_w[half:].T, norms.astype(F32), router.T


def add_low(*values):
    return sum(v.astype(F32) for v in values).astype(BF)


def core_sum(own, sib, sizes):
    got = swap(sib, *sizes, 0, 1)
    middle = own.shape[0] // 2
    return add_low(own[:middle], got[:middle]), add_low(own[middle:], got[middle:])


def sum_small(values, sizes):
    dp_size, tensor_size = sizes
    mask = 1
    while mask < tensor_size:
        values = values + swap(values, dp_size, tensor_size, 0, mask)
        mask *= 2
    mask = 1
    while mask < dp_size:
        values = values + swap(values, dp_size, tensor_size, mask, 0)
        mask *= 2
    return values


def on_device(
    sizes, tokens, qkv_weight, out_weight, router, norm_params, expert_in, expert_out, cotangent
):
    dp_size, tensor_size = sizes
    dp_index = lax.axis_index("dp")
    tensor_index = lax.axis_index("tensor")
    core = tensor_index % 2
    high = tensor_index // 2
    width = tokens.shape[1]
    half = width // 2
    rows = qkv_weight.shape[1]
    columns = qkv_weight.shape[2]
    experts = dp_size * router.shape[1]
    stepwise = rows % 16 == 0 and tensor_size == 4
    owners = ()
    if stepwise:
        owners = owners_of(dp_size, dp_index, core)
        norms, router_t = gather_smalls(router, norm_params, sizes, (dp_index, tensor_index))
        weights, weights_high, (x_img, g_img, unit, inv_std) = gather_first(
            qkv_weight, out_weight, sizes, (tokens, cotangent)
        )
        normed, qkv_one, mixed_one, probs_one, weight_one, out_one = attend_first(
            unit, norms, half, owners, weights
        )
        qkv_two, mixed_two, probs_two, weight_two, out_two = attend_second(normed, half, owners, weights_high)
    else:
        x_img, g_img, unit, inv_std = prepare(tokens, cotangent)
        weight_one, weight_two, out_one, out_two, norms, router_t = gather_weights_plain(
            qkv_weight, out_weight, router, norm_params
        )
        normed, qkv_one, mixed_one, probs_one = attend_first(unit, norms, half, (), (weight_one,))
        qkv_two, mixed_two, probs_two = attend_second(normed, half, (), (weight_two,))
    y, normed_two, logits, outgoing = route(
        x_img, mixed_one, mixed_two, out_one, out_two, norms, router_t, g_img
    )

    outgoing = outgoing.reshape(experts, SLOT_ROWS, width)
    arrived = lax.all_to_all(outgoing, "dp", split_axis=0, concat_axis=0, tiled=True)
    across = swap(arrived, *sizes, 0, 2)
    pair = jnp.concatenate([arrived, across], axis=0)
    near = swap(pair, *sizes, 0, 1)
    keep, away, *kept = run_expert(pair, near, expert_in[0], expert_out[0])
    got = swap(away, *sizes, 0, 1)
    summed = (keep.astype(F32) + got.astype(F32)).astype(BF)
    got = swap(summed[dp_size:], *sizes, 0, 2)
    got, (first_grad, second_grad) = lax.optimization_barrier((got, expert_grads(*kept)))
    summed = (summed[:dp_size].astype(F32) + got.astype(F32)).astype(BF)
    back = lax.all_to_all(summed, "dp", split_axis=0, concat_axis=0, tiled=True)
    back = back.reshape(experts * SLOT_ROWS, width)

    grad_y, grad_mixed, out_grad_t, small_two = moe_back(
        y, normed_two, g_img, logits, back, norms, router_t, out_one, out_two, mixed_one, mixed_two
    )
    grads_two, *dealt_two = attend_back(
        normed, qkv_two, probs_two, mixed_two, grad_mixed, out_grad_t, 1, owners, sizes
    )
    if stepwise:
        last = dp_size.bit_length() - 2
        middle = dp_size // 2
        kept, sent = core_sum(*dealt_two, sizes)
        kept, sent, grad_mixed = lax.optimization_barrier((kept, sent, grad_mixed))
        got = lax.ppermute(sent, AXES, step_pairs(*sizes, last))
    grads_one, *dealt_one = attend_back(
        normed, qkv_one, probs_one, mixed_one, grad_mixed, out_grad_t, 0, owners, sizes
    )
    if stepwise:
        got, grads_one = lax.optimization_barrier((got, grads_one))
        crossed = swap(add_low(kept, got), *sizes, 0, 2)
        kept, sent = core_sum(*dealt_one, sizes)
        kept, sent, grads_one = lax.optimization_barrier((kept, sent, grads_one))
        got = lax.ppermute(sent, AXES, step_pairs(*sizes, last))
    input_grad, small_one = input_back(
        unit, inv_std, grad_y, grads_one, grads_two, weight_one, weight_two, norms
    )
    small = jnp.concatenate([small_one[0:2], small_two[0:2], small_two[8:]], axis=0)
    if stepwise:
        got, small = lax.optimization_barrier((got, small))
        held = add_low(kept, got, crossed)
        output = block_output(y, logits, back)
        for step in range(last)[::-1]:
            middle = 1 << step
            got = lax.ppermute(held[middle:], AXES, step_pairs(*sizes, step))
            if step == last - 1:
                got, output = lax.optimization_barrier((got, output))
            if step > 0:
                held = add_low(held[:middle], got)
        qkv_grad, out_grad = unpack(held[:1], got, columns)
    else:
        output = block_output(y, logits, back)
        full = jnp.concatenate(
            [dealt_one[0].reshape(width, 3, half), dealt_two[0].reshape(width, 3, half)], axis=2
        ).transpose(1, 0, 2)
        qkv_grad = lax.psum_scatter(full, "dp", scatter_dimension=1, tiled=True)
        qkv_grad = lax.psum_scatter(qkv_grad, "tensor", scatter_dimension=2, tiled=True)
        out_grad = lax.psum_scatter(out_grad_t.T, "dp", scatter_dimension=1, tiled=True)
        out_grad = lax.psum_scatter(out_grad, "tensor", scatter_dimension=0, tiled=True)
    small = sum_small(small, sizes)
    norm_grad = lax.dynamic_slice(small, (tensor_index, dp_index * rows), (1, rows))
    router_grad = lax.dynamic_slice(
        small, (tensor_size + dp_index, tensor_index * columns), (1, columns)
    ).reshape(columns, 1)
    return (
        output,
        input_grad,
        qkv_grad,
        out_grad,
        router_grad,
        norm_grad,
        first_grad[None],
        second_grad[None],
    )


def solution(mesh):
    sizes = (mesh.shape["dp"], mesh.shape["tensor"])
    return jax.shard_map(
        functools.partial(on_device, sizes),
        mesh=mesh,
        in_specs=(
            P(("dp", "tensor"), None),
            P(None, "dp", "tensor"),
            P("tensor", "dp"),
            P("tensor", "dp"),
            P("tensor", "dp"),
            P("dp", None, "tensor"),
            P("dp", "tensor", None),
            P(("dp", "tensor"), None),
        ),
        out_specs=(
            P(("dp", "tensor"), None),
            P(("dp", "tensor"), None),
            P(None, "dp", "tensor"),
            P("tensor", "dp"),
            P("tensor", "dp"),
            P("tensor", "dp"),
            P("dp", None, "tensor"),
            P("dp", "tensor", None),
        ),
        check_vma=False,
    )
```

```python
import functools

import jax
import jax.numpy as jnp
from jax import lax
from jax.experimental import pallas as pl
from jax.experimental.pallas import tpu as pltpu
from jax.sharding import PartitionSpec as P

HEAD_DIM = 64
SEQ = 197
PAD = 208
SLOT_ROWS = 16
AXES = ("dp", "tensor")
BF = jnp.bfloat16
F32 = jnp.float32
LAST = (((1,), (1,)), ((), ()))
FIRST = (((0,), (0,)), ((), ()))
MIDDLE = (((1,), (0,)), ((), ()))
MIB = 1024 * 1024


def dot(a, b, dims=MIDDLE):
    return lax.dot_general(a, b, dims, preferred_element_type=F32)


def shape_of(shape, dtype):
    return jax.ShapeDtypeStruct(shape, dtype)


def run(kernel, name, operands, results, limit, scratch=(), scalars=0):
    memory = [pltpu.SMEM] * scalars + [pltpu.VMEM] * (len(operands) - scalars)
    return pl.pallas_call(
        kernel,
        in_specs=[pl.BlockSpec(memory_space=m) for m in memory],
        out_specs=[pl.BlockSpec(memory_space=pltpu.VMEM) for _ in results],
        out_shape=list(results),
        scratch_shapes=list(scratch),
        compiler_params=pltpu.CompilerParams(vmem_limit_bytes=limit * MIB),
        cost_estimate=pl.CostEstimate(flops=1, bytes_accessed=1, transcendentals=0),
        name=name,
    )(*operands)


def layer_stats(values):
    centre = jnp.mean(values, axis=-1, keepdims=True)
    centred = values - centre
    spread = jnp.mean(centred * centred, axis=-1, keepdims=True)
    inv_std = lax.rsqrt(spread + 1e-06)
    return centred * inv_std, inv_std


def lane_ids(shape):
    return lax.broadcasted_iota(jnp.int32, shape, len(shape) - 1)


def row_ids(shape):
    return lax.broadcasted_iota(jnp.int32, shape, len(shape) - 2)


def flat(ref):
    images, rows, columns = ref.shape
    return ref[...].reshape(images * rows, columns)


def prepare_kernel(x_ref, g_ref, x_out, g_out, unit_out, wide):
    count, width = x_ref.shape
    real = row_ids((PAD, width)) < SEQ
    wide[count:, :] = jnp.zeros((wide.shape[0] - count, width), F32)
    for ref, out in ((x_ref, x_out), (g_ref, g_out)):
        wide[0:count, :] = ref[...].astype(F32)
        for i in range(out.shape[0]):
            rows = jnp.where(real, wide[SEQ * i : SEQ * i + PAD, :], 0.0)
            out[i] = rows.astype(BF)
            if ref is x_ref:
                unit_out[i], _ = layer_stats(rows)


def prepare(tokens, cotangent):
    count, width = tokens.shape
    images = count // SEQ
    rows = shape_of((images, PAD, width), BF)
    return run(
        prepare_kernel,
        "prepare",
        (tokens, cotangent),
        (rows, rows, shape_of((images, PAD, width), F32)),
        14,
        scratch=[pltpu.VMEM((-(-count // 8) * 8 + 16, width), F32)],
    )


def attend_rows(normed, w_ref, qkv_ref, mixed_ref, probs_ref):
    images, rows, span = mixed_ref.shape
    low = lane_ids((rows, 128)) < HEAD_DIM
    key_ok = row_ids((rows, rows)) < SEQ
    zero = jnp.zeros((rows, 128), BF)
    proj = dot(normed, w_ref[...])
    qkv_ref[:, :, 0:span] = (proj[:, 0:span] * HEAD_DIM ** (-0.5)).astype(BF).reshape(images, rows, span)
    qkv_ref[:, :, span:] = proj[:, span:].astype(BF).reshape(images, rows, 2 * span)

    def image(i, carry):
        for p in range(span // 128):
            at = slice(p * 128, (p + 1) * 128)
            q = qkv_ref[i, :, at]
            k = qkv_ref[i, :, span + p * 128 : span + (p + 1) * 128]
            v = qkv_ref[i, :, 2 * span + p * 128 : 2 * span + (p + 1) * 128]
            mixed = []
            for h in range(2):
                q_one = jnp.where(low, q, zero) if h == 0 else jnp.where(low, zero, q)
                scores = jnp.where(key_ok, dot(k, q_one, LAST), -1e30)
                scaled = jnp.exp(scores - jnp.max(scores, axis=0, keepdims=True))
                weights = (scaled * (1.0 / jnp.sum(scaled, axis=0, keepdims=True))).astype(BF)
                probs_ref[i, 2 * p + h] = weights
                mixed.append(dot(weights, v, FIRST))
            mixed_ref[i, :, at] = jnp.where(low, mixed[0], mixed[1]).astype(BF)
        return carry

    lax.fori_loop(0, images, image, 0, unroll=3 if images % 3 == 0 else 1)


def assemble_rows(owners, parts, kinds, out_ref, columns):
    for side, (owner, refs) in enumerate(zip(owners, parts, strict=True)):
        count = out_ref.shape[0] // owner.shape[0]
        blocks = [ref[i * count : (i + 1) * count] for ref in refs for i in range(ref.shape[0] // count)]
        for p, block in enumerate(blocks):
            row = pl.multiple_of(count * owner[p], 16)
            for at, kind in enumerate(kinds):
                out_ref[pl.ds(row, count), (2 * at + side) * columns : (2 * at + side + 1) * columns] = block[
                    :, kind * columns : (kind + 1) * columns
                ]


def attend_first_kernel(counts, *refs):
    if counts:
        own, sib = counts
        owners, refs = refs[:2], refs[2:]
        unit_ref, norms_ref, refs = refs[0], refs[1], refs[2:]
        parts, refs = (refs[:own], refs[own : own + sib]), refs[own + sib :]
        n_ref, qkv_ref, mixed_ref, probs_ref, w_ref, out_w_ref = refs
        columns = mixed_ref.shape[2] // 2
        assemble_rows(owners, parts, range(3), w_ref, columns)
        assemble_rows(owners, parts, [3], out_w_ref, columns)
    else:
        unit_ref, norms_ref, w_ref, n_ref, qkv_ref, mixed_ref, probs_ref = refs
    normed = (flat(unit_ref) * norms_ref[0:1, :] + norms_ref[1:2, :]).astype(BF)
    n_ref[...] = normed.reshape(n_ref.shape)
    attend_rows(normed, w_ref, qkv_ref, mixed_ref, probs_ref)


def attend_second_kernel(counts, *refs):
    if counts:
        own, sib = counts
        owners, refs = refs[:2], refs[2:]
        n_ref, refs = refs[0], refs[1:]
        parts, refs = (refs[:own], refs[own : own + sib]), refs[own + sib :]
        qkv_ref, mixed_ref, probs_ref, w_ref, out_w_ref = refs
        columns = mixed_ref.shape[2] // 2
        assemble_rows(owners, parts, range(3), w_ref, columns)
        assemble_rows(owners, parts, [3], out_w_ref, columns)
    else:
        n_ref, w_ref, qkv_ref, mixed_ref, probs_ref = refs
    attend_rows(flat(n_ref), w_ref, qkv_ref, mixed_ref, probs_ref)


def attend_results(images, rows, span):
    return (
        shape_of((images, rows, 3 * span), BF),
        shape_of((images, rows, span), BF),
        shape_of((images, span // HEAD_DIM, rows, rows), BF),
    )


def attend(kernel, name, results, rows_in, span, owners, weights):
    images, rows, width = rows_in[0].shape
    results = results + attend_results(images, rows, span)
    counts = None
    if owners:
        counts = tuple(map(len, weights))
        weights = sum(weights, ())
        results += (shape_of((width, 3 * span), BF), shape_of((width, span), BF))
    return run(
        functools.partial(kernel, counts),
        name,
        owners + rows_in + weights,
        results,
        16,
        scalars=len(owners),
    )


def attend_first(unit, norms, span, owners, weights):
    normed = (shape_of(unit.shape, BF),)
    return attend(attend_first_kernel, "attend_first", normed, (unit, norms), span, owners, weights)


def attend_second(normed, span, owners, weights):
    return attend(attend_second_kernel, "attend_second", (), (normed,), span, owners, weights)


def softmaxes(logits):
    ok = lane_ids(logits.shape) < SEQ
    masked = jnp.where(ok, logits, -1e30)
    up = jnp.exp(masked - jnp.max(masked, axis=1, keepdims=True))
    dispatch = up / jnp.sum(up, axis=1, keepdims=True)
    up = jnp.exp(logits - jnp.max(logits, axis=0, keepdims=True))
    combine = up / jnp.sum(up, axis=0, keepdims=True)
    return dispatch, combine


def place_rows(experts, image, offset):
    shape = (experts * SLOT_ROWS, experts)
    return (row_ids(shape) == lane_ids(shape) * SLOT_ROWS + offset + image).astype(BF)


def pick_rows(experts, image, offset):
    shape = (experts, experts * SLOT_ROWS)
    return (lane_ids(shape) == row_ids(shape) * SLOT_ROWS + offset + image).astype(BF)


def route_kernel(
    x_ref, m1_ref, m2_ref, o1_ref, o2_ref, norms_ref, router_ref, g_ref, y_ref, n_ref, logits_ref, send_ref
):
    images, rows, width = x_ref.shape
    experts = router_ref.shape[0]
    attn = dot(flat(m1_ref), o1_ref[...], LAST) + dot(flat(m2_ref), o2_ref[...], LAST)
    y = flat(x_ref).astype(F32) + attn
    y_ref[...] = y.reshape(y_ref.shape)
    unit, _ = layer_stats(y)
    normed = (unit * norms_ref[2:3, :] + norms_ref[3:4, :]).astype(BF)
    n_ref[...] = normed.reshape(n_ref.shape)
    placed = 0.0
    for i in range(images):
        logits = dot(router_ref[...], n_ref[i], LAST)
        logits_ref[i] = logits
        dispatch, combine = softmaxes(logits)
        slots = dot(dispatch.astype(BF), n_ref[i]).astype(BF)
        grad_returned = dot(combine.astype(BF), g_ref[i]).astype(BF)
        placed = placed + dot(place_rows(experts, i, 0), slots)
        placed = placed + dot(place_rows(experts, i, SLOT_ROWS // 2), grad_returned)
    send_ref[...] = placed.astype(BF)


def route(x_img, mixed_one, mixed_two, out_one, out_two, norms, router, g_img):
    images, rows, width = x_img.shape
    experts = router.shape[0]
    return run(
        route_kernel,
        "route",
        (x_img, mixed_one, mixed_two, out_one, out_two, norms, router, g_img),
        (
            shape_of((images, rows, width), F32),
            shape_of((images, rows, width), BF),
            shape_of((images, experts, rows), F32),
            shape_of((experts * SLOT_ROWS, width), BF),
        ),
        16,
    )


def split_rows(blocks):
    wide = blocks.astype(F32)
    half = SLOT_ROWS // 2
    shape = (blocks.shape[0] * half, blocks.shape[2])
    return wide[:, :half].reshape(shape).astype(BF), wide[:, half:].reshape(shape).astype(BF)


def join_rows(ones, twos):
    half = SLOT_ROWS // 2
    shape = (ones.shape[0] // half, half, ones.shape[1])
    return jnp.concatenate([ones.reshape(shape), twos.reshape(shape)], axis=1).astype(BF)


def gelu_parts(pre):
    cdf = 0.5 * (1.0 + lax.erf(pre * (0.5**0.5)))
    density = jnp.exp(-0.5 * pre * pre) * 0.3989422804014327
    return pre * cdf, cdf + pre * density


def expert_kernel(
    own_ref, near_ref, w1_ref, w2_ref, keep_ref, send_ref, slots_ref, grads_ref, hidden_ref, pre_ref
):
    count = own_ref.shape[0]
    blocks = jnp.concatenate([own_ref[...], near_ref[...]], axis=0)
    slots, grads = split_rows(blocks)
    pre = dot(slots, w1_ref[...])
    hidden, slope = gelu_parts(pre)
    hidden = hidden.astype(BF)
    returned = dot(hidden, w2_ref[...])
    grad_pre = (dot(grads, w2_ref[...], LAST) * slope).astype(BF)
    grad_slots = dot(grad_pre, w1_ref[...], LAST)
    joined = join_rows(returned, grad_slots)
    keep_ref[...] = joined[:count]
    send_ref[...] = joined[count:]
    slots_ref[...] = slots
    grads_ref[...] = grads
    hidden_ref[...] = hidden
    pre_ref[...] = grad_pre


def run_expert(own, near, first_weight, second_weight):
    width, units = first_weight.shape
    rows = (own.shape[0] + near.shape[0]) * SLOT_ROWS // 2
    return run(
        expert_kernel,
        "expert",
        (own, near, first_weight, second_weight),
        (
            shape_of(own.shape, BF),
            shape_of(near.shape, BF),
            shape_of((rows, width), BF),
            shape_of((rows, width), BF),
            shape_of((rows, units), BF),
            shape_of((rows, units), BF),
        ),
        16 if rows <= 512 else 48,
    )


def expert_grad_kernel(slots_ref, grads_ref, hidden_ref, pre_ref, d1_ref, d2_ref):
    d1_ref[...] = dot(slots_ref[...], pre_ref[...], FIRST)
    d2_ref[...] = dot(hidden_ref[...], grads_ref[...], FIRST)


def expert_grads(slots, grads, hidden, grad_pre):
    rows, width = slots.shape
    units = hidden.shape[1]
    return run(
        expert_grad_kernel,
        "expert_grads",
        (slots, grads, hidden, grad_pre),
        (shape_of((width, units), F32), shape_of((units, width), F32)),
        16 if rows <= 512 else 32,
    )


def moe_back_kernel(
    y_ref,
    n_ref,
    g_ref,
    logits_ref,
    back_ref,
    norms_ref,
    router_ref,
    o1_ref,
    o2_ref,
    m1_ref,
    m2_ref,
    grad_y_ref,
    grad_mixed_ref,
    out_grad_ref,
    small_ref,
    attn_ref,
):
    images, rows, width = y_ref.shape
    experts = router_ref.shape[0]
    half = m1_ref.shape[2]
    gain = norms_ref[2:3, :]
    router_grad, gain_grad, shift_grad = 0.0, 0.0, 0.0
    for i in range(images):
        returned = dot(pick_rows(experts, i, 0), back_ref[...]).astype(BF)
        grad_slots = dot(pick_rows(experts, i, SLOT_ROWS // 2), back_ref[...]).astype(BF)
        dispatch, combine = softmaxes(logits_ref[i])
        grad_combine = dot(returned, g_ref[i], LAST)
        grad_dispatch = dot(grad_slots, n_ref[i], LAST)
        grad_logits = dispatch * (
            grad_dispatch - jnp.sum(grad_dispatch * dispatch, axis=1, keepdims=True)
        ) + combine * (grad_combine - jnp.sum(grad_combine * combine, axis=0, keepdims=True))
        grad_logits = grad_logits.astype(BF)
        router_grad = router_grad + dot(grad_logits, n_ref[i])
        grad_two = dot(dispatch.astype(BF), grad_slots, FIRST) + dot(grad_logits, router_ref[...], FIRST)
        unit, inv_std = layer_stats(y_ref[i])
        gain_grad = gain_grad + jnp.sum(grad_two * unit, axis=0, keepdims=True)
        shift_grad = shift_grad + jnp.sum(grad_two, axis=0, keepdims=True)
        scaled = grad_two * gain
        mean_one = jnp.mean(scaled, axis=-1, keepdims=True)
        mean_two = jnp.mean(scaled * unit, axis=-1, keepdims=True)
        grad_y = g_ref[i].astype(F32) + inv_std * (scaled - mean_one - unit * mean_two)
        grad_y_ref[i] = grad_y
        attn_ref[i] = grad_y.astype(BF)
    small_ref[...] = jnp.zeros_like(small_ref)
    small_ref[0:1, :] = gain_grad
    small_ref[1:2, :] = shift_grad
    small_ref[8 : 8 + experts, :] = router_grad
    grad_attn = flat(attn_ref)
    shape = m1_ref.shape
    grad_mixed_ref[:, :, :half] = dot(grad_attn, o1_ref[...]).astype(BF).reshape(shape)
    grad_mixed_ref[:, :, half:] = dot(grad_attn, o2_ref[...]).astype(BF).reshape(shape)
    out_grad_ref[:, :half] = dot(grad_attn, flat(m1_ref), FIRST)
    out_grad_ref[:, half:] = dot(grad_attn, flat(m2_ref), FIRST)


def moe_back(y, normed, g_img, logits, back, norms, router, out_one, out_two, mixed_one, mixed_two):
    images, rows, width = y.shape
    experts = router.shape[0]
    return run(
        moe_back_kernel,
        "moe_back",
        (y, normed, g_img, logits, back, norms, router, out_one, out_two, mixed_one, mixed_two),
        (
            shape_of((images, rows, width), F32),
            shape_of((images, rows, width), BF),
            shape_of((width, width), F32),
            shape_of((8 + experts, width), F32),
        ),
        16,
        scratch=[pltpu.VMEM((images, rows, width), BF)],
    )


def output_kernel(y_ref, logits_ref, back_ref, out_ref, wide):
    images, experts, _ = logits_ref.shape
    for i in range(images):
        returned = dot(pick_rows(experts, i, 0), back_ref[...]).astype(BF)
        _, combine = softmaxes(logits_ref[i])
        total = y_ref[i] + dot(combine.astype(BF), returned, FIRST)
        wide[SEQ * i : SEQ * (i + 1), :] = total[0:SEQ]
    out_ref[...] = wide[...].astype(BF)


def block_output(y, logits, back):
    images, rows, width = y.shape
    count = images * SEQ
    return run(
        output_kernel,
        "block_output",
        (y, logits, back),
        (shape_of((count, width), BF),),
        12,
        scratch=[pltpu.VMEM((count, width), F32)],
    )[0]


def deal_rows(owners, full_ref, first, kinds, refs, columns):
    for side, (owner, ref) in enumerate(zip(owners, refs, strict=True)):
        blocks, count, _ = ref.shape
        for p in range(blocks):
            row = pl.multiple_of(count * owner[p], 16)
            for at, kind in enumerate(kinds):
                lane = first + (2 * at + side) * columns
                ref[p, :, kind * columns : (kind + 1) * columns] = full_ref[
                    pl.ds(row, count), lane : lane + columns
                ].astype(BF)


def attend_back_kernel(stepwise, piece, *refs):
    if stepwise:
        owners, refs = refs[:2], refs[2:]
        n_ref, qkv_ref, probs_ref, mixed_ref, gm_ref, og_ref, grads_ref, own_ref, sib_ref, dw_ref = refs
    else:
        n_ref, qkv_ref, probs_ref, mixed_ref, gm_ref, grads_ref, dw_ref = refs
    images, rows, span = mixed_ref.shape
    low = lane_ids((rows, 128)) < HEAD_DIM
    zero = jnp.zeros((rows, 128), BF)
    minus = jnp.full((rows, 128), -1.0, BF)

    def image(i, carry):
        for p in range(span // 128):
            at = slice(p * 128, (p + 1) * 128)
            at_k = slice(span + p * 128, span + (p + 1) * 128)
            at_v = slice(2 * span + p * 128, 2 * span + (p + 1) * 128)
            q, k, v = qkv_ref[i, :, at], qkv_ref[i, :, at_k], qkv_ref[i, :, at_v]
            gm = gm_ref[i, :, piece * span + p * 128 : piece * span + (p + 1) * 128]
            inner = pltpu.roll(gm.astype(F32) * mixed_ref[i, :, at].astype(F32), HEAD_DIM, 1).astype(BF)
            grad_q, grad_k, grad_v = 0.0, 0.0, 0.0
            for h in range(2):
                mine = low if h == 0 else jnp.logical_not(low)
                weights = probs_ref[i, 2 * p + h]
                centred = dot(jnp.where(mine, v, minus), jnp.where(mine, gm, inner), LAST)
                grad_scores = (weights.astype(F32) * centred).astype(BF)
                grad_v = grad_v + dot(weights, jnp.where(mine, gm, zero))
                grad_k = grad_k + dot(grad_scores, jnp.where(mine, q, zero))
                grad_q = grad_q + dot(grad_scores, jnp.where(mine, k, zero), FIRST)
            grads_ref[i, :, at] = (grad_q * HEAD_DIM ** (-0.5)).astype(BF)
            grads_ref[i, :, at_k] = grad_k.astype(BF)
            grads_ref[i, :, at_v] = grad_v.astype(BF)
        return carry

    lax.fori_loop(0, images, image, 0, unroll=3 if images % 3 == 0 else 1)
    dw_ref[...] = dot(flat(n_ref), flat(grads_ref), FIRST)
    if stepwise:
        deal_rows(owners, dw_ref, 0, range(3), (own_ref, sib_ref), span // 2)
        deal_rows(owners, og_ref, piece * span, [3], (own_ref, sib_ref), span // 2)


def attend_back(normed, qkv, probs, mixed, grad_mixed, out_grad_t, piece, owners, sizes):
    images, rows, width = normed.shape
    span = mixed.shape[2]
    operands = (normed, qkv, probs, mixed, grad_mixed)
    results = (shape_of((images, rows, 3 * span), BF),)
    scratch = ()
    if owners:
        operands += (out_grad_t,)
        results += (shape_of((sizes[0], width // sizes[0], 2 * span), BF),) * 2
        scratch = (pltpu.VMEM((width, 3 * span), F32),)
    else:
        results += (shape_of((width, 3 * span), F32),)
    return run(
        functools.partial(attend_back_kernel, bool(owners), piece),
        "attend_back",
        owners + operands,
        results,
        16,
        scratch,
        scalars=len(owners),
    )


def input_back_kernel(x_ref, gy_ref, p1_ref, p2_ref, w1_ref, w2_ref, norms_ref, out_ref, small_ref):
    images, rows, width = x_ref.shape
    gain = norms_ref[0:1, :]
    grad_all = dot(flat(p1_ref), w1_ref[...], LAST) + dot(flat(p2_ref), w2_ref[...], LAST)
    gain_grad, shift_grad = 0.0, 0.0
    for i in range(images):
        grad_one = grad_all[i * rows : (i + 1) * rows]
        unit, inv_std = layer_stats(x_ref[i].astype(F32))
        gain_grad = gain_grad + jnp.sum(grad_one * unit, axis=0, keepdims=True)
        shift_grad = shift_grad + jnp.sum(grad_one, axis=0, keepdims=True)
        scaled = grad_one * gain
        mean_one = jnp.mean(scaled, axis=-1, keepdims=True)
        mean_two = jnp.mean(scaled * unit, axis=-1, keepdims=True)
        total = gy_ref[i] + inv_std * (scaled - mean_one - unit * mean_two)
        out_ref[SEQ * i : SEQ * (i + 1), :] = total[0:SEQ]
    small_ref[...] = jnp.zeros_like(small_ref)
    small_ref[0:1, :] = gain_grad
    small_ref[1:2, :] = shift_grad


def input_back(x_img, grad_y, grads_one, grads_two, weight_one, weight_two, norms):
    images, rows, width = x_img.shape
    return run(
        input_back_kernel,
        "input_back",
        (x_img, grad_y, grads_one, grads_two, weight_one, weight_two, norms),
        (shape_of((images * SEQ, width), F32), shape_of((8, width), F32)),
        16,
    )


def pack_kernel(qkv_ref, out_ref, block_ref):
    kinds, _, columns = qkv_ref.shape
    for kind in range(kinds):
        block_ref[:, kind * columns : (kind + 1) * columns] = qkv_ref[kind]
    block_ref[:, kinds * columns :] = out_ref[...].T


def pack(qkv_weight, out_weight):
    kinds, rows, columns = qkv_weight.shape
    return run(
        pack_kernel,
        "pack",
        (qkv_weight, out_weight),
        (shape_of((rows, (kinds + 1) * columns), BF),),
        4,
    )[0]


def unpack_kernel(own_ref, got_ref, qkv_ref, out_ref):
    kinds, _, columns = qkv_ref.shape
    total = own_ref[0].astype(F32) + got_ref[0].astype(F32)
    for kind in range(kinds):
        qkv_ref[kind] = total[:, kind * columns : (kind + 1) * columns]
    out_ref[...] = total[:, kinds * columns :].T


def unpack(own, got, columns):
    _, rows, lanes = own.shape
    kinds = lanes // columns - 1
    return run(
        unpack_kernel,
        "unpack",
        (own, got),
        (shape_of((kinds, rows, columns), F32), shape_of((columns, rows), F32)),
        4,
    )


def swap(value, dp_size, tensor_size, dp_mask, tensor_mask):
    pairs = [
        (d * tensor_size + t, (d ^ dp_mask) * tensor_size + (t ^ tensor_mask))
        for d in range(dp_size)
        for t in range(tensor_size)
    ]
    return lax.ppermute(value, AXES, pairs)


def steps_of(dp_size):
    bits = dp_size.bit_length() - 1
    down = list(range(bits))[::-1]
    return [down, down[-1:] + down[:-1]]


def step_pairs(dp_size, tensor_size, step):
    orders = steps_of(dp_size)
    return [
        (d * tensor_size + t, (d ^ (1 << orders[t % 2][step])) * tensor_size + t)
        for d in range(dp_size)
        for t in range(tensor_size)
    ]


def owners_of(dp_size, dp_index, core):
    both = []
    for order in steps_of(dp_size):
        place = jnp.arange(dp_size, dtype=jnp.int32)
        away = jnp.zeros_like(place)
        for step, bit in enumerate(order):
            away = away | (((place >> step) & 1) << bit)
        both.append(away ^ dp_index)
    return jnp.where(core == 0, both[0], both[1]), jnp.where(core == 0, both[1], both[0])


def place_smalls(router, norm_params, sizes, ids):
    dp_index, tensor_index = ids
    rows, columns = norm_params.shape[1], router.shape[0]
    experts = sizes[0] * router.shape[1]
    held = jnp.zeros((-(-(sizes[1] + experts) // 16) * 16, rows * sizes[0]), BF)
    held = lax.dynamic_update_slice(held, norm_params, (tensor_index, dp_index * rows))
    return lax.dynamic_update_slice(held, router.T, (sizes[1] + dp_index, tensor_index * columns))


def together(*values):
    return lax.optimization_barrier(values)


def send(value, sizes, step):
    return lax.ppermute(value, AXES, step_pairs(*sizes, step))


def across_core(value, sizes):
    return swap(value, *sizes, 0, 1)


def across_high(value, sizes):
    return swap(value, *sizes, 0, 2)


def gather_first(qkv_weight, out_weight, small, sizes, along):
    block = pack(qkv_weight, out_weight)
    rows = block.shape[0]
    extra = small.shape[0]
    small = small + across_high(small, sizes)
    small = small + across_core(small, sizes)
    small = small + send(small, sizes, 0)
    got, small = together(send(block, sizes, 0), small)
    held = jnp.concatenate([block, got, small], axis=0)

    got, near, high, along = together(
        send(held, sizes, 1), across_core(held, sizes), across_high(held, sizes), prepare(*along)
    )
    small = held[2 * rows :] + got[2 * rows :]
    four = jnp.concatenate([held[: 2 * rows], got[: 2 * rows], small], axis=0)

    last, near_two, high_two, high_near = together(
        send(four, sizes, 2), across_core(got, sizes), across_high(got, sizes), across_core(high, sizes)
    )
    small = four[4 * rows :] + last[4 * rows :]
    own = (four, last), (near, near_two, across_core(last, sizes))
    return own, ((high, high_two), (high_near,)), small, along


def gather_second(own, high, sizes, rows):
    (first, second), (first_near,) = high
    _, last = own
    along = send(first, sizes, 2)
    across = across_high(last[2 * rows : 4 * rows], sizes)
    return (first, second, along, across), first_near, across_core(second, sizes)


def gather_weights_plain(qkv_weight, out_weight, router, norm_params):
    qkv = lax.all_gather(qkv_weight, "dp", axis=1, tiled=True)
    qkv = lax.all_gather(qkv, "tensor", axis=2, tiled=True)
    out_w, router, norms = (
        lax.all_gather(lax.all_gather(w, "dp", axis=1, tiled=True), "tensor", axis=0, tiled=True)
        for w in (out_weight, router, norm_params)
    )
    width = qkv.shape[1]
    half = width // 2
    one = qkv[:, :, :half].transpose(1, 0, 2).reshape(width, 3 * half)
    two = qkv[:, :, half:].transpose(1, 0, 2).reshape(width, 3 * half)
    return one, two, out_w[:half].T, out_w[half:].T, norms.astype(F32), router.T


def add_low(*values):
    return sum(v.astype(F32) for v in values).astype(BF)


def sum_small(values, sizes):
    dp_size, tensor_size = sizes
    mask = 1
    while mask < tensor_size:
        values = values + swap(values, dp_size, tensor_size, 0, mask)
        mask *= 2
    mask = 1
    while mask < dp_size:
        values = values + swap(values, dp_size, tensor_size, mask, 0)
        mask *= 2
    return values


def on_device(
    sizes, tokens, qkv_weight, out_weight, router, norm_params, expert_in, expert_out, cotangent
):
    dp_size, tensor_size = sizes
    dp_index = lax.axis_index("dp")
    tensor_index = lax.axis_index("tensor")
    core = tensor_index % 2
    high = tensor_index // 2
    width = tokens.shape[1]
    half = width // 2
    rows = qkv_weight.shape[1]
    columns = qkv_weight.shape[2]
    experts = dp_size * router.shape[1]
    stepwise = rows % 16 == 0 and sizes == (8, 4)
    owners = ()
    if stepwise:
        owners = owners_of(dp_size, dp_index, core)
        small = place_smalls(router, norm_params, sizes, (dp_index, tensor_index))
        (own, near), high, small, (x_img, g_img, unit) = gather_first(
            qkv_weight, out_weight, small, sizes, (tokens, cotangent)
        )
        norms, router_t = small[:tensor_size].astype(F32), small[tensor_size : tensor_size + experts]
        (first, second, third, fourth), near_first, near_second = gather_second(own, high, sizes, rows)
        (third, fourth, near_second), (normed, qkv_one, mixed_one, probs_one, weight_one, out_one) = together(
            (third, fourth, near_second), attend_first(unit, norms, half, owners, (own, near))
        )
        near_third, near_fourth = across_core(third, sizes), across_core(fourth, sizes)
        qkv_two, mixed_two, probs_two, weight_two, out_two = attend_second(
            normed,
            half,
            owners,
            ((first, second, third, fourth), (near_first, near_second, near_third, near_fourth)),
        )
    else:
        x_img, g_img, unit = prepare(tokens, cotangent)
        weight_one, weight_two, out_one, out_two, norms, router_t = gather_weights_plain(
            qkv_weight, out_weight, router, norm_params
        )
        normed, qkv_one, mixed_one, probs_one = attend_first(unit, norms, half, (), (weight_one,))
        qkv_two, mixed_two, probs_two = attend_second(normed, half, (), (weight_two,))
    y, normed_two, logits, outgoing = route(
        x_img, mixed_one, mixed_two, out_one, out_two, norms, router_t, g_img
    )

    outgoing = outgoing.reshape(experts, SLOT_ROWS, width)
    arrived = lax.all_to_all(outgoing, "dp", split_axis=0, concat_axis=0, tiled=True)
    across = swap(arrived, *sizes, 0, 2)
    pair = jnp.concatenate([arrived, across], axis=0)
    near = swap(pair, *sizes, 0, 1)
    keep, away, *kept = run_expert(pair, near, expert_in[0], expert_out[0])
    got = swap(away, *sizes, 0, 1)
    summed = (keep.astype(F32) + got.astype(F32)).astype(BF)
    got = swap(summed[dp_size:], *sizes, 0, 2)
    summed = (summed[:dp_size].astype(F32) + got.astype(F32)).astype(BF)
    back = lax.all_to_all(summed, "dp", split_axis=0, concat_axis=0, tiled=True)
    back = back.reshape(experts * SLOT_ROWS, width)

    grad_y, grad_mixed, out_grad_t, small_two = moe_back(
        y, normed_two, g_img, logits, back, norms, router_t, out_one, out_two, mixed_one, mixed_two
    )
    grads_two, *dealt_two = attend_back(
        normed, qkv_two, probs_two, mixed_two, grad_mixed, out_grad_t, 1, owners, sizes
    )
    if stepwise:
        mine, got = dealt_two[0], across_core(dealt_two[1], sizes)
        low, along, across = (add_low(mine[a:b], got[a:b]) for a, b in ((0, 4), (4, 6), (6, 8)))
        low, along, across, grad_mixed = together(low, along, across, grad_mixed)
        along, across = send(along, sizes, 2), across_high(across, sizes)
    grads_one, *dealt_one = attend_back(
        normed, qkv_one, probs_one, mixed_one, grad_mixed, out_grad_t, 0, owners, sizes
    )
    if stepwise:
        along, across, grads_one, dealt_one = together(along, across, grads_one, dealt_one)
        low = jnp.concatenate([add_low(low[:2], along), low[2:]], axis=0)
        mine, got = dealt_one[0], across_core(dealt_one[1], sizes)
        mine_low, mine_high = add_low(mine[:4], got[:4]), add_low(mine[4:], got[4:])
        mine_high = jnp.concatenate([mine_high[:2], add_low(mine_high[2:], across)], axis=0)
        low, mine_high, grads_one = together(low, mine_high, grads_one)
        got, across = send(mine_high, sizes, 2), across_high(low, sizes)
    input_grad, small_one = input_back(x_img, grad_y, grads_one, grads_two, weight_one, weight_two, norms)
    output = block_output(y, logits, back)
    first_grad, second_grad = expert_grads(*kept)
    small = jnp.concatenate([small_one[0:2], small_two[0:2], small_two[8:]], axis=0)
    if stepwise:
        got, across, input_grad, output, small, first_grad, second_grad = together(
            got, across, input_grad, output, small, first_grad, second_grad
        )
        held = add_low(mine_low, got, across)
        small = small + across_core(small, sizes)
        small = small + across_high(small, sizes)
        small = small + swap(small, *sizes, 1, 0)
        got, small = together(send(held[2:], sizes, 1), small)
        held = add_low(held[:2], got)
        small = small + swap(small, *sizes, 2, 0)
        small = small + swap(small, *sizes, 4, 0)
        qkv_grad, out_grad = unpack(held[:1], send(held[1:], sizes, 0), columns)
    else:
        small = sum_small(small, sizes)
        full = jnp.concatenate(
            [dealt_one[0].reshape(width, 3, half), dealt_two[0].reshape(width, 3, half)], axis=2
        ).transpose(1, 0, 2)
        qkv_grad = lax.psum_scatter(full, "dp", scatter_dimension=1, tiled=True)
        qkv_grad = lax.psum_scatter(qkv_grad, "tensor", scatter_dimension=2, tiled=True)
        out_grad = lax.psum_scatter(out_grad_t.T, "dp", scatter_dimension=1, tiled=True)
        out_grad = lax.psum_scatter(out_grad, "tensor", scatter_dimension=0, tiled=True)
    norm_grad = lax.dynamic_slice(small, (tensor_index, dp_index * rows), (1, rows))
    router_grad = lax.dynamic_slice(
        small, (tensor_size + dp_index, tensor_index * columns), (1, columns)
    ).reshape(columns, 1)
    return (
        output,
        input_grad,
        qkv_grad,
        out_grad,
        router_grad,
        norm_grad,
        first_grad[None],
        second_grad[None],
    )


def solution(mesh):
    sizes = (mesh.shape["dp"], mesh.shape["tensor"])
    return jax.shard_map(
        functools.partial(on_device, sizes),
        mesh=mesh,
        in_specs=(
            P(("dp", "tensor"), None),
            P(None, "dp", "tensor"),
            P("tensor", "dp"),
            P("tensor", "dp"),
            P("tensor", "dp"),
            P("dp", None, "tensor"),
            P("dp", "tensor", None),
            P(("dp", "tensor"), None),
        ),
        out_specs=(
            P(("dp", "tensor"), None),
            P(("dp", "tensor"), None),
            P(None, "dp", "tensor"),
            P("tensor", "dp"),
            P("tensor", "dp"),
            P("tensor", "dp"),
            P("dp", None, "tensor"),
            P("dp", "tensor", None),
        ),
        check_vma=False,
    )
```

```python
import functools

import jax
import jax.numpy as jnp
from jax import lax
from jax.experimental import pallas as pl
from jax.experimental.pallas import tpu as pltpu
from jax.sharding import PartitionSpec as P

HEAD_DIM = 64
SEQ = 197
PAD = 208
SLOT_ROWS = 16
AXES = ("dp", "tensor")
BF = jnp.bfloat16
F32 = jnp.float32
LAST = (((1,), (1,)), ((), ()))
FIRST = (((0,), (0,)), ((), ()))
MIDDLE = (((1,), (0,)), ((), ()))
MIB = 1024 * 1024


def dot(a, b, dims=MIDDLE):
    return lax.dot_general(a, b, dims, preferred_element_type=F32)


def shape_of(shape, dtype):
    return jax.ShapeDtypeStruct(shape, dtype)


def run(kernel, name, operands, results, limit, scratch=(), scalars=0):
    memory = [pltpu.SMEM] * scalars + [pltpu.VMEM] * (len(operands) - scalars)
    return pl.pallas_call(
        kernel,
        in_specs=[pl.BlockSpec(memory_space=m) for m in memory],
        out_specs=[pl.BlockSpec(memory_space=pltpu.VMEM) for _ in results],
        out_shape=list(results),
        scratch_shapes=list(scratch),
        compiler_params=pltpu.CompilerParams(vmem_limit_bytes=limit * MIB),
        cost_estimate=pl.CostEstimate(flops=1, bytes_accessed=1, transcendentals=0),
        name=name,
    )(*operands)


def layer_stats(values):
    centre = jnp.mean(values, axis=-1, keepdims=True)
    centred = values - centre
    spread = jnp.mean(centred * centred, axis=-1, keepdims=True)
    inv_std = lax.rsqrt(spread + 1e-06)
    return centred * inv_std, inv_std


def lane_ids(shape):
    return lax.broadcasted_iota(jnp.int32, shape, len(shape) - 1)


def row_ids(shape):
    return lax.broadcasted_iota(jnp.int32, shape, len(shape) - 2)


def flat(ref):
    images, rows, columns = ref.shape
    return ref[...].reshape(images * rows, columns)


def prepare_kernel(x_ref, g_ref, x_out, g_out, unit_out, wide):
    count, width = x_ref.shape
    real = row_ids((PAD, width)) < SEQ
    wide[count:, :] = jnp.zeros((wide.shape[0] - count, width), F32)
    for ref, out in ((x_ref, x_out), (g_ref, g_out)):
        wide[0:count, :] = ref[...].astype(F32)
        for i in range(out.shape[0]):
            rows = jnp.where(real, wide[SEQ * i : SEQ * i + PAD, :], 0.0)
            out[i] = rows.astype(BF)
            if ref is x_ref:
                unit_out[i], _ = layer_stats(rows)


def prepare(tokens, cotangent):
    count, width = tokens.shape
    images = count // SEQ
    rows = shape_of((images, PAD, width), BF)
    return run(
        prepare_kernel,
        "prepare",
        (tokens, cotangent),
        (rows, rows, shape_of((images, PAD, width), F32)),
        14,
        scratch=[pltpu.VMEM((-(-count // 8) * 8 + 16, width), F32)],
    )


def attend_rows(normed, w_ref, qkv_ref, mixed_ref, probs_ref):
    images, rows, span = mixed_ref.shape
    low = lane_ids((rows, 128)) < HEAD_DIM
    key_ok = row_ids((rows, rows)) < SEQ
    zero = jnp.zeros((rows, 128), BF)
    proj = dot(normed, w_ref[...])
    qkv_ref[:, :, 0:span] = (proj[:, 0:span] * HEAD_DIM ** (-0.5)).astype(BF).reshape(images, rows, span)
    qkv_ref[:, :, span:] = proj[:, span:].astype(BF).reshape(images, rows, 2 * span)

    def image(i, carry):
        for p in range(span // 128):
            at = slice(p * 128, (p + 1) * 128)
            q = qkv_ref[i, :, at]
            k = qkv_ref[i, :, span + p * 128 : span + (p + 1) * 128]
            v = qkv_ref[i, :, 2 * span + p * 128 : 2 * span + (p + 1) * 128]
            mixed = []
            for h in range(2):
                q_one = jnp.where(low, q, zero) if h == 0 else jnp.where(low, zero, q)
                scores = jnp.where(key_ok, dot(k, q_one, LAST), -1e30)
                scaled = jnp.exp(scores - jnp.max(scores, axis=0, keepdims=True))
                weights = (scaled * (1.0 / jnp.sum(scaled, axis=0, keepdims=True))).astype(BF)
                probs_ref[i, 2 * p + h] = weights
                mixed.append(dot(weights, v, FIRST))
            mixed_ref[i, :, at] = jnp.where(low, mixed[0], mixed[1]).astype(BF)
        return carry

    lax.fori_loop(0, images, image, 0, unroll=3 if images % 3 == 0 else 1)


def assemble_rows(owners, parts, kinds, out_ref, columns):
    for side, (owner, refs) in enumerate(zip(owners, parts, strict=True)):
        count = out_ref.shape[0] // owner.shape[0]
        blocks = [ref[i * count : (i + 1) * count] for ref in refs for i in range(ref.shape[0] // count)]
        for p, block in enumerate(blocks):
            row = pl.multiple_of(count * owner[p], 16)
            for at, kind in enumerate(kinds):
                out_ref[pl.ds(row, count), (2 * at + side) * columns : (2 * at + side + 1) * columns] = block[
                    :, kind * columns : (kind + 1) * columns
                ]


def attend_first_kernel(counts, *refs):
    if counts:
        own, sib = counts
        owners, refs = refs[:2], refs[2:]
        unit_ref, norms_ref, refs = refs[0], refs[1], refs[2:]
        parts, refs = (refs[:own], refs[own : own + sib]), refs[own + sib :]
        n_ref, qkv_ref, mixed_ref, probs_ref, w_ref, out_w_ref = refs
        columns = mixed_ref.shape[2] // 2
        assemble_rows(owners, parts, range(3), w_ref, columns)
        assemble_rows(owners, parts, [3], out_w_ref, columns)
    else:
        unit_ref, norms_ref, w_ref, n_ref, qkv_ref, mixed_ref, probs_ref = refs
    normed = (flat(unit_ref) * norms_ref[0:1, :] + norms_ref[1:2, :]).astype(BF)
    n_ref[...] = normed.reshape(n_ref.shape)
    attend_rows(normed, w_ref, qkv_ref, mixed_ref, probs_ref)


def attend_second_kernel(counts, *refs):
    if counts:
        own, sib = counts
        owners, refs = refs[:2], refs[2:]
        n_ref, refs = refs[0], refs[1:]
        parts, refs = (refs[:own], refs[own : own + sib]), refs[own + sib :]
        qkv_ref, mixed_ref, probs_ref, w_ref, out_w_ref = refs
        columns = mixed_ref.shape[2] // 2
        assemble_rows(owners, parts, range(3), w_ref, columns)
        assemble_rows(owners, parts, [3], out_w_ref, columns)
    else:
        n_ref, w_ref, qkv_ref, mixed_ref, probs_ref = refs
    attend_rows(flat(n_ref), w_ref, qkv_ref, mixed_ref, probs_ref)


def attend_results(images, rows, span):
    return (
        shape_of((images, rows, 3 * span), BF),
        shape_of((images, rows, span), BF),
        shape_of((images, span // HEAD_DIM, rows, rows), BF),
    )


def attend(kernel, name, results, rows_in, span, owners, weights):
    images, rows, width = rows_in[0].shape
    results = results + attend_results(images, rows, span)
    counts = None
    if owners:
        counts = tuple(map(len, weights))
        weights = sum(weights, ())
        results += (shape_of((width, 3 * span), BF), shape_of((width, span), BF))
    return run(
        functools.partial(kernel, counts),
        name,
        owners + rows_in + weights,
        results,
        16,
        scalars=len(owners),
    )


def attend_first(unit, norms, span, owners, weights):
    normed = (shape_of(unit.shape, BF),)
    return attend(attend_first_kernel, "attend_first", normed, (unit, norms), span, owners, weights)


def attend_second(normed, span, owners, weights):
    return attend(attend_second_kernel, "attend_second", (), (normed,), span, owners, weights)


def softmaxes(logits):
    ok = lane_ids(logits.shape) < SEQ
    masked = jnp.where(ok, logits, -1e30)
    up = jnp.exp(masked - jnp.max(masked, axis=1, keepdims=True))
    dispatch = up / jnp.sum(up, axis=1, keepdims=True)
    up = jnp.exp(logits - jnp.max(logits, axis=0, keepdims=True))
    combine = up / jnp.sum(up, axis=0, keepdims=True)
    return dispatch, combine


def place_rows(experts, image, offset):
    shape = (experts * SLOT_ROWS, experts)
    return (row_ids(shape) == lane_ids(shape) * SLOT_ROWS + offset + image).astype(BF)


def pick_rows(experts, image, offset):
    shape = (experts, experts * SLOT_ROWS)
    return (lane_ids(shape) == row_ids(shape) * SLOT_ROWS + offset + image).astype(BF)


def route_kernel(
    x_ref, m1_ref, m2_ref, o1_ref, o2_ref, norms_ref, router_ref, g_ref, y_ref, n_ref, logits_ref, send_ref
):
    images, rows, width = x_ref.shape
    experts = router_ref.shape[0]
    attn = dot(flat(m1_ref), o1_ref[...], LAST) + dot(flat(m2_ref), o2_ref[...], LAST)
    y = flat(x_ref).astype(F32) + attn
    y_ref[...] = y.reshape(y_ref.shape)
    unit, _ = layer_stats(y)
    normed = (unit * norms_ref[2:3, :] + norms_ref[3:4, :]).astype(BF)
    n_ref[...] = normed.reshape(n_ref.shape)
    placed = 0.0
    for i in range(images):
        logits = dot(router_ref[...], n_ref[i], LAST)
        logits_ref[i] = logits
        dispatch, combine = softmaxes(logits)
        slots = dot(dispatch.astype(BF), n_ref[i]).astype(BF)
        grad_returned = dot(combine.astype(BF), g_ref[i]).astype(BF)
        placed = placed + dot(place_rows(experts, i, 0), slots)
        placed = placed + dot(place_rows(experts, i, SLOT_ROWS // 2), grad_returned)
    send_ref[...] = placed.astype(BF)


def route(x_img, mixed_one, mixed_two, out_one, out_two, norms, router, g_img):
    images, rows, width = x_img.shape
    experts = router.shape[0]
    return run(
        route_kernel,
        "route",
        (x_img, mixed_one, mixed_two, out_one, out_two, norms, router, g_img),
        (
            shape_of((images, rows, width), F32),
            shape_of((images, rows, width), BF),
            shape_of((images, experts, rows), F32),
            shape_of((experts * SLOT_ROWS, width), BF),
        ),
        16,
    )


def split_rows(blocks):
    wide = blocks.astype(F32)
    half = SLOT_ROWS // 2
    shape = (blocks.shape[0] * half, blocks.shape[2])
    return wide[:, :half].reshape(shape).astype(BF), wide[:, half:].reshape(shape).astype(BF)


def join_rows(ones, twos):
    half = SLOT_ROWS // 2
    shape = (ones.shape[0] // half, half, ones.shape[1])
    return jnp.concatenate([ones.reshape(shape), twos.reshape(shape)], axis=1).astype(BF)


def gelu_parts(pre):
    cdf = 0.5 * (1.0 + lax.erf(pre * (0.5**0.5)))
    density = jnp.exp(-0.5 * pre * pre) * 0.3989422804014327
    return pre * cdf, cdf + pre * density


def expert_kernel(
    own_ref, near_ref, w1_ref, w2_ref, keep_ref, send_ref, slots_ref, grads_ref, hidden_ref, pre_ref
):
    count = own_ref.shape[0]
    blocks = jnp.concatenate([own_ref[...], near_ref[...]], axis=0)
    slots, grads = split_rows(blocks)
    pre = dot(slots, w1_ref[...])
    hidden, slope = gelu_parts(pre)
    hidden = hidden.astype(BF)
    returned = dot(hidden, w2_ref[...])
    grad_pre = (dot(grads, w2_ref[...], LAST) * slope).astype(BF)
    grad_slots = dot(grad_pre, w1_ref[...], LAST)
    joined = join_rows(returned, grad_slots)
    keep_ref[...] = joined[:count]
    send_ref[...] = joined[count:]
    slots_ref[...] = slots
    grads_ref[...] = grads
    hidden_ref[...] = hidden
    pre_ref[...] = grad_pre


def run_expert(own, near, first_weight, second_weight):
    width, units = first_weight.shape
    rows = (own.shape[0] + near.shape[0]) * SLOT_ROWS // 2
    return run(
        expert_kernel,
        "expert",
        (own, near, first_weight, second_weight),
        (
            shape_of(own.shape, BF),
            shape_of(near.shape, BF),
            shape_of((rows, width), BF),
            shape_of((rows, width), BF),
            shape_of((rows, units), BF),
            shape_of((rows, units), BF),
        ),
        16 if rows <= 512 else 48,
    )


def expert_grad_kernel(slots_ref, grads_ref, hidden_ref, pre_ref, d1_ref, d2_ref):
    d1_ref[...] = dot(slots_ref[...], pre_ref[...], FIRST)
    d2_ref[...] = dot(hidden_ref[...], grads_ref[...], FIRST)


def expert_grads(slots, grads, hidden, grad_pre):
    rows, width = slots.shape
    units = hidden.shape[1]
    return run(
        expert_grad_kernel,
        "expert_grads",
        (slots, grads, hidden, grad_pre),
        (shape_of((width, units), F32), shape_of((units, width), F32)),
        16 if rows <= 512 else 32,
    )


def moe_back_kernel(
    y_ref,
    n_ref,
    g_ref,
    logits_ref,
    back_ref,
    norms_ref,
    router_ref,
    o1_ref,
    o2_ref,
    m1_ref,
    m2_ref,
    grad_y_ref,
    grad_mixed_ref,
    out_grad_ref,
    small_ref,
    attn_ref,
):
    images, rows, width = y_ref.shape
    experts = router_ref.shape[0]
    half = m1_ref.shape[2]
    gain = norms_ref[2:3, :]
    router_grad, gain_grad, shift_grad = 0.0, 0.0, 0.0
    for i in range(images):
        returned = dot(pick_rows(experts, i, 0), back_ref[...]).astype(BF)
        grad_slots = dot(pick_rows(experts, i, SLOT_ROWS // 2), back_ref[...]).astype(BF)
        dispatch, combine = softmaxes(logits_ref[i])
        grad_combine = dot(returned, g_ref[i], LAST)
        grad_dispatch = dot(grad_slots, n_ref[i], LAST)
        grad_logits = dispatch * (
            grad_dispatch - jnp.sum(grad_dispatch * dispatch, axis=1, keepdims=True)
        ) + combine * (grad_combine - jnp.sum(grad_combine * combine, axis=0, keepdims=True))
        grad_logits = grad_logits.astype(BF)
        router_grad = router_grad + dot(grad_logits, n_ref[i])
        grad_two = dot(dispatch.astype(BF), grad_slots, FIRST) + dot(grad_logits, router_ref[...], FIRST)
        unit, inv_std = layer_stats(y_ref[i])
        gain_grad = gain_grad + jnp.sum(grad_two * unit, axis=0, keepdims=True)
        shift_grad = shift_grad + jnp.sum(grad_two, axis=0, keepdims=True)
        scaled = grad_two * gain
        mean_one = jnp.mean(scaled, axis=-1, keepdims=True)
        mean_two = jnp.mean(scaled * unit, axis=-1, keepdims=True)
        grad_y = g_ref[i].astype(F32) + inv_std * (scaled - mean_one - unit * mean_two)
        grad_y_ref[i] = grad_y
        attn_ref[i] = grad_y.astype(BF)
    small_ref[...] = jnp.zeros_like(small_ref)
    small_ref[0:1, :] = gain_grad
    small_ref[1:2, :] = shift_grad
    small_ref[8 : 8 + experts, :] = router_grad
    grad_attn = flat(attn_ref)
    shape = m1_ref.shape
    grad_mixed_ref[:, :, :half] = dot(grad_attn, o1_ref[...]).astype(BF).reshape(shape)
    grad_mixed_ref[:, :, half:] = dot(grad_attn, o2_ref[...]).astype(BF).reshape(shape)
    out_grad_ref[:, :half] = dot(grad_attn, flat(m1_ref), FIRST)
    out_grad_ref[:, half:] = dot(grad_attn, flat(m2_ref), FIRST)


def moe_back(y, normed, g_img, logits, back, norms, router, out_one, out_two, mixed_one, mixed_two):
    images, rows, width = y.shape
    experts = router.shape[0]
    return run(
        moe_back_kernel,
        "moe_back",
        (y, normed, g_img, logits, back, norms, router, out_one, out_two, mixed_one, mixed_two),
        (
            shape_of((images, rows, width), F32),
            shape_of((images, rows, width), BF),
            shape_of((width, width), F32),
            shape_of((8 + experts, width), F32),
        ),
        16,
        scratch=[pltpu.VMEM((images, rows, width), BF)],
    )


def output_kernel(y_ref, logits_ref, back_ref, out_ref, wide):
    images, experts, _ = logits_ref.shape
    for i in range(images):
        returned = dot(pick_rows(experts, i, 0), back_ref[...]).astype(BF)
        _, combine = softmaxes(logits_ref[i])
        total = y_ref[i] + dot(combine.astype(BF), returned, FIRST)
        wide[SEQ * i : SEQ * (i + 1), :] = total[0:SEQ]
    out_ref[...] = wide[...].astype(BF)


def block_output(y, logits, back):
    images, rows, width = y.shape
    count = images * SEQ
    return run(
        output_kernel,
        "block_output",
        (y, logits, back),
        (shape_of((count, width), BF),),
        12,
        scratch=[pltpu.VMEM((count, width), F32)],
    )[0]


def deal_rows(owners, full_ref, first, kinds, refs, columns):
    for side, (owner, ref) in enumerate(zip(owners, refs, strict=True)):
        blocks, count, _ = ref.shape
        for p in range(blocks):
            row = pl.multiple_of(count * owner[p], 16)
            for at, kind in enumerate(kinds):
                lane = first + (2 * at + side) * columns
                ref[p, :, kind * columns : (kind + 1) * columns] = full_ref[
                    pl.ds(row, count), lane : lane + columns
                ].astype(BF)


def attend_back_kernel(stepwise, piece, *refs):
    if stepwise:
        owners, refs = refs[:2], refs[2:]
        n_ref, qkv_ref, probs_ref, mixed_ref, gm_ref, og_ref, grads_ref, own_ref, sib_ref, dw_ref = refs
    else:
        n_ref, qkv_ref, probs_ref, mixed_ref, gm_ref, grads_ref, dw_ref = refs
    images, rows, span = mixed_ref.shape
    low = lane_ids((rows, 128)) < HEAD_DIM
    zero = jnp.zeros((rows, 128), BF)
    minus = jnp.full((rows, 128), -1.0, BF)

    def image(i, carry):
        for p in range(span // 128):
            at = slice(p * 128, (p + 1) * 128)
            at_k = slice(span + p * 128, span + (p + 1) * 128)
            at_v = slice(2 * span + p * 128, 2 * span + (p + 1) * 128)
            q, k, v = qkv_ref[i, :, at], qkv_ref[i, :, at_k], qkv_ref[i, :, at_v]
            gm = gm_ref[i, :, piece * span + p * 128 : piece * span + (p + 1) * 128]
            inner = pltpu.roll(gm.astype(F32) * mixed_ref[i, :, at].astype(F32), HEAD_DIM, 1).astype(BF)
            grad_q, grad_k, grad_v = 0.0, 0.0, 0.0
            for h in range(2):
                mine = low if h == 0 else jnp.logical_not(low)
                weights = probs_ref[i, 2 * p + h]
                centred = dot(jnp.where(mine, v, minus), jnp.where(mine, gm, inner), LAST)
                grad_scores = (weights.astype(F32) * centred).astype(BF)
                grad_v = grad_v + dot(weights, jnp.where(mine, gm, zero))
                grad_k = grad_k + dot(grad_scores, jnp.where(mine, q, zero))
                grad_q = grad_q + dot(grad_scores, jnp.where(mine, k, zero), FIRST)
            grads_ref[i, :, at] = (grad_q * HEAD_DIM ** (-0.5)).astype(BF)
            grads_ref[i, :, at_k] = grad_k.astype(BF)
            grads_ref[i, :, at_v] = grad_v.astype(BF)
        return carry

    lax.fori_loop(0, images, image, 0, unroll=3 if images % 3 == 0 else 1)
    dw_ref[...] = dot(flat(n_ref), flat(grads_ref), FIRST)
    if stepwise:
        deal_rows(owners, dw_ref, 0, range(3), (own_ref, sib_ref), span // 2)
        deal_rows(owners, og_ref, piece * span, [3], (own_ref, sib_ref), span // 2)


def attend_back(normed, qkv, probs, mixed, grad_mixed, out_grad_t, piece, owners, sizes):
    images, rows, width = normed.shape
    span = mixed.shape[2]
    operands = (normed, qkv, probs, mixed, grad_mixed)
    results = (shape_of((images, rows, 3 * span), BF),)
    scratch = ()
    if owners:
        operands += (out_grad_t,)
        results += (shape_of((sizes[0], width // sizes[0], 2 * span), BF),) * 2
        scratch = (pltpu.VMEM((width, 3 * span), F32),)
    else:
        results += (shape_of((width, 3 * span), F32),)
    return run(
        functools.partial(attend_back_kernel, bool(owners), piece),
        "attend_back",
        owners + operands,
        results,
        16,
        scratch,
        scalars=len(owners),
    )


def input_part_kernel(p_ref, w_ref, out_ref):
    out_ref[...] = dot(flat(p_ref), w_ref[...], LAST).reshape(out_ref.shape)


def input_part(grads, weight):
    images, rows, _ = grads.shape
    return run(
        input_part_kernel, "input_part", (grads, weight), (shape_of((images, rows, weight.shape[0]), F32),), 16
    )[0]


def input_back_kernel(x_ref, gy_ref, p1_ref, part_ref, w1_ref, norms_ref, out_ref, small_ref):
    images, rows, width = x_ref.shape
    gain = norms_ref[0:1, :]
    grad_all = dot(flat(p1_ref), w1_ref[...], LAST) + flat(part_ref)
    gain_grad, shift_grad = 0.0, 0.0
    for i in range(images):
        grad_one = grad_all[i * rows : (i + 1) * rows]
        unit, inv_std = layer_stats(x_ref[i].astype(F32))
        gain_grad = gain_grad + jnp.sum(grad_one * unit, axis=0, keepdims=True)
        shift_grad = shift_grad + jnp.sum(grad_one, axis=0, keepdims=True)
        scaled = grad_one * gain
        mean_one = jnp.mean(scaled, axis=-1, keepdims=True)
        mean_two = jnp.mean(scaled * unit, axis=-1, keepdims=True)
        total = gy_ref[i] + inv_std * (scaled - mean_one - unit * mean_two)
        out_ref[SEQ * i : SEQ * (i + 1), :] = total[0:SEQ]
    small_ref[...] = jnp.zeros_like(small_ref)
    small_ref[0:1, :] = gain_grad
    small_ref[1:2, :] = shift_grad


def input_back(x_img, grad_y, grads_one, grad_part, weight_one, norms):
    images, rows, width = x_img.shape
    return run(
        input_back_kernel,
        "input_back",
        (x_img, grad_y, grads_one, grad_part, weight_one, norms),
        (shape_of((images * SEQ, width), F32), shape_of((8, width), F32)),
        16,
    )


def spot(shape, start):
    return (lane_ids(shape) == row_ids(shape) + start).astype(BF)


def place_kernel(index_ref, norm_ref, router_ref, small_ref):
    rows, columns = norm_ref.shape[1], router_ref.shape[1]
    width = small_ref.shape[1]
    dp_index, tensor_index = index_ref[0], index_ref[1]
    norm = dot(jnp.broadcast_to(norm_ref[...], (16, rows)), spot((rows, width), dp_index * rows))
    router = dot(jnp.broadcast_to(router_ref[...], (16, columns)), spot((columns, width), tensor_index * columns))
    row = row_ids(small_ref.shape)
    small_ref[...] = jnp.where(
        row == tensor_index, norm[0:1], jnp.where(row == width // columns + dp_index, router[0:1], 0.0)
    ).astype(BF)


def place(index, norm_params, router, experts):
    rows, columns = norm_params.shape[1], router.shape[0]
    width = rows * experts
    return run(
        place_kernel,
        "place",
        (index, norm_params, router.T),
        (shape_of((-(-(width // columns + experts) // 16) * 16, width), BF),),
        4,
        scalars=1,
    )[0]


def pack_kernel(qkv_ref, out_ref, block_ref):
    kinds, _, columns = qkv_ref.shape
    for kind in range(kinds):
        block_ref[:, kind * columns : (kind + 1) * columns] = qkv_ref[kind]
    block_ref[:, kinds * columns :] = out_ref[...].T


def pack(qkv_weight, out_weight):
    kinds, rows, columns = qkv_weight.shape
    return run(
        pack_kernel,
        "pack",
        (qkv_weight, out_weight),
        (shape_of((rows, (kinds + 1) * columns), BF),),
        4,
    )[0]


def unpack_kernel(index_ref, own_ref, got_ref, *refs):
    smalls, (qkv_ref, out_ref, norm_ref, router_ref) = refs[:-4], refs[-4:]
    kinds, rows, columns = qkv_ref.shape
    total = own_ref[...].astype(F32) + got_ref[...].astype(F32)
    for kind in range(kinds):
        qkv_ref[kind] = total[:, kind * columns : (kind + 1) * columns]
    out_ref[...] = total[:, kinds * columns :].T
    small = smalls[0][...]
    for ref in smalls[1:]:
        small = small + ref[...]
    dp_index, tensor_index = index_ref[0], index_ref[1]
    tensor_size = small.shape[1] // columns
    row = row_ids(small.shape)
    norm = jnp.sum(jnp.where(row == tensor_index, small, 0.0), axis=0, keepdims=True)
    router = jnp.sum(jnp.where(row == tensor_size + dp_index, small, 0.0), axis=0, keepdims=True)
    norm_out, router_out = 0.0, 0.0
    for _ in range(3):
        part = norm.astype(BF)
        norm = norm - part.astype(F32)
        part = jnp.broadcast_to(part, (16, small.shape[1]))
        norm_out = norm_out + dot(part, spot((rows, small.shape[1]), dp_index * rows), LAST)
        part = router.astype(BF)
        router = router - part.astype(F32)
        part = jnp.broadcast_to(part, (16, small.shape[1]))
        router_out = router_out + dot(part, spot((columns, small.shape[1]), tensor_index * columns), LAST)
    norm_ref[...] = norm_out[0:1]
    router_ref[...] = router_out[0:1]


def unpack(index, own, got, smalls, columns):
    rows, lanes = own.shape
    kinds = lanes // columns - 1
    return run(
        unpack_kernel,
        "unpack",
        (index, own, got) + smalls,
        (
            shape_of((kinds, rows, columns), F32),
            shape_of((columns, rows), F32),
            shape_of((1, rows), F32),
            shape_of((1, columns), F32),
        ),
        4,
        scalars=1,
    )


def swap(value, dp_size, tensor_size, dp_mask, tensor_mask):
    pairs = [
        (d * tensor_size + t, (d ^ dp_mask) * tensor_size + (t ^ tensor_mask))
        for d in range(dp_size)
        for t in range(tensor_size)
    ]
    return lax.ppermute(value, AXES, pairs)


def steps_of(dp_size):
    bits = dp_size.bit_length() - 1
    down = list(range(bits))[::-1]
    return [down, down[-1:] + down[:-1]]


def step_pairs(dp_size, tensor_size, step):
    orders = steps_of(dp_size)
    return [
        (d * tensor_size + t, (d ^ (1 << orders[t % 2][step])) * tensor_size + t)
        for d in range(dp_size)
        for t in range(tensor_size)
    ]


def owners_of(dp_size, dp_index, core):
    both = []
    for order in steps_of(dp_size):
        place = jnp.arange(dp_size, dtype=jnp.int32)
        away = jnp.zeros_like(place)
        for step, bit in enumerate(order):
            away = away | (((place >> step) & 1) << bit)
        both.append(away ^ dp_index)
    return jnp.where(core == 0, both[0], both[1]), jnp.where(core == 0, both[1], both[0])


def together(*values):
    return lax.optimization_barrier(values)


def send(value, sizes, step):
    return lax.ppermute(value, AXES, step_pairs(*sizes, step))


def across_core(value, sizes):
    return swap(value, *sizes, 0, 1)


def across_high(value, sizes):
    return swap(value, *sizes, 0, 2)


def sums_over(value, sizes, first, second):
    both = (first[0] ^ second[0], first[1] ^ second[1])
    return (value,) + tuple(swap(value, *sizes, *mask) for mask in (first, second, both))


def gather_first(block, small, sizes, along):
    rows = block.shape[0]
    small_high, block = together(across_high(small, sizes), block)
    small = small + small_high
    small = small + across_core(small, sizes)
    first = jnp.concatenate([block, small], axis=0)
    (got,) = together(send(first, sizes, 0))
    held = jnp.concatenate([block, got[:rows], small + got[rows:]], axis=0)

    got, near, high = together(send(held, sizes, 1), across_core(held, sizes), across_high(held, sizes))
    small = held[2 * rows :] + got[2 * rows :]
    four = jnp.concatenate([held[: 2 * rows], got[: 2 * rows], small], axis=0)

    last, near_two, high_two, high_near, along = together(
        send(four, sizes, 2), across_core(got, sizes), across_high(got, sizes), across_core(high, sizes), prepare(*along)
    )
    small = four[4 * rows :] + last[4 * rows :]
    own = (four, last), (near, near_two, across_core(last, sizes))
    return own, ((high, high_two), (high_near,)), small, along


def gather_second(own, high, sizes, rows):
    (first, second), (first_near,) = high
    _, last = own
    along = send(first, sizes, 2)
    across = across_high(last[2 * rows : 4 * rows], sizes)
    return (first, second, along, across), first_near, across_core(second, sizes)


def gather_weights_plain(qkv_weight, out_weight, router, norm_params):
    qkv = lax.all_gather(qkv_weight, "dp", axis=1, tiled=True)
    qkv = lax.all_gather(qkv, "tensor", axis=2, tiled=True)
    out_w, router, norms = (
        lax.all_gather(lax.all_gather(w, "dp", axis=1, tiled=True), "tensor", axis=0, tiled=True)
        for w in (out_weight, router, norm_params)
    )
    width = qkv.shape[1]
    half = width // 2
    one = qkv[:, :, :half].transpose(1, 0, 2).reshape(width, 3 * half)
    two = qkv[:, :, half:].transpose(1, 0, 2).reshape(width, 3 * half)
    return one, two, out_w[:half].T, out_w[half:].T, norms.astype(F32), router.T


def add_low(*values):
    return sum(v.astype(F32) for v in values).astype(BF)


def sum_small(values, sizes):
    dp_size, tensor_size = sizes
    mask = 1
    while mask < tensor_size:
        values = values + swap(values, dp_size, tensor_size, 0, mask)
        mask *= 2
    mask = 1
    while mask < dp_size:
        values = values + swap(values, dp_size, tensor_size, mask, 0)
        mask *= 2
    return values


def on_device(
    sizes, tokens, qkv_weight, out_weight, router, norm_params, expert_in, expert_out, cotangent
):
    dp_size, tensor_size = sizes
    dp_index = lax.axis_index("dp")
    tensor_index = lax.axis_index("tensor")
    core = jnp.bitwise_and(tensor_index, 1)
    width = tokens.shape[1]
    half = width // 2
    rows = qkv_weight.shape[1]
    columns = qkv_weight.shape[2]
    experts = dp_size * router.shape[1]
    stepwise = rows % 16 == 0 and sizes == (8, 4)
    owners = ()
    if stepwise:
        owners = owners_of(dp_size, dp_index, core)
        index = jnp.stack([dp_index, tensor_index]).astype(jnp.int32)
        *owners, index, qkv_weight, out_weight, norm_params, router = together(
            *owners, index, qkv_weight, out_weight, norm_params, router
        )
        owners = tuple(owners)
        small = place(index, norm_params, router, experts)
        block = pack(qkv_weight, out_weight)
        (own, near), high, small, (x_img, g_img, unit) = gather_first(block, small, sizes, (tokens, cotangent))
        norms, router_t = small[:tensor_size].astype(F32), small[tensor_size : tensor_size + experts]
        (first, second, third, fourth), near_first, near_second = gather_second(own, high, sizes, rows)
        normed, qkv_one, mixed_one, probs_one, weight_one, out_one = attend_first(
            unit, norms, half, owners, (own, near)
        )
        third, fourth, near_second, normed = together(third, fourth, near_second, normed)
        near_third, near_fourth = across_core(third, sizes), across_core(fourth, sizes)
        qkv_two, mixed_two, probs_two, weight_two, out_two = attend_second(
            normed,
            half,
            owners,
            ((first, second, third, fourth), (near_first, near_second, near_third, near_fourth)),
        )
    else:
        x_img, g_img, unit = prepare(tokens, cotangent)
        weight_one, weight_two, out_one, out_two, norms, router_t = gather_weights_plain(
            qkv_weight, out_weight, router, norm_params
        )
        normed, qkv_one, mixed_one, probs_one = attend_first(unit, norms, half, (), (weight_one,))
        qkv_two, mixed_two, probs_two = attend_second(normed, half, (), (weight_two,))
    y, normed_two, logits, outgoing = route(
        x_img, mixed_one, mixed_two, out_one, out_two, norms, router_t, g_img
    )

    outgoing = outgoing.reshape(experts, SLOT_ROWS, width)
    arrived = lax.all_to_all(outgoing, "dp", split_axis=0, concat_axis=0, tiled=True)
    across = swap(arrived, *sizes, 0, 2)
    pair = jnp.concatenate([arrived, across], axis=0)
    near = swap(pair, *sizes, 0, 1)
    keep, away, *kept = run_expert(pair, near, expert_in[0], expert_out[0])
    got = swap(away, *sizes, 0, 1)
    summed = (keep.astype(F32) + got.astype(F32)).astype(BF)
    got = swap(summed[dp_size:], *sizes, 0, 2)
    summed = (summed[:dp_size].astype(F32) + got.astype(F32)).astype(BF)
    back = lax.all_to_all(summed, "dp", split_axis=0, concat_axis=0, tiled=True)
    back = back.reshape(experts * SLOT_ROWS, width)

    grad_y, grad_mixed, out_grad_t, small_two = moe_back(
        y, normed_two, g_img, logits, back, norms, router_t, out_one, out_two, mixed_one, mixed_two
    )
    grads_two, *dealt_two = attend_back(
        normed, qkv_two, probs_two, mixed_two, grad_mixed, out_grad_t, 1, owners, sizes
    )
    first_grad, second_grad = expert_grads(*kept)
    if stepwise:
        mine = dealt_two[0]
        got = across_core(dealt_two[1], sizes)
        low, along, across = (add_low(mine[a:b], got[a:b]) for a, b in ((0, 4), (4, 6), (6, 8)))
        low, along, across, grad_mixed = together(low, along, across, grad_mixed)
        along, across = send(along, sizes, 2), across_high(across, sizes)
    grads_one, *dealt_one = attend_back(
        normed, qkv_one, probs_one, mixed_one, grad_mixed, out_grad_t, 0, owners, sizes
    )
    if stepwise:
        along, across, mine, sent, grads_one = together(along, across, *dealt_one, grads_one)
        low = jnp.concatenate([add_low(low[:2], along), low[2:]], axis=0)
        got, grad_part = together(across_core(sent, sizes), input_part(grads_two, weight_two))
        mine_low, mine_high = add_low(mine[:4], got[:4]), add_low(mine[4:], got[4:])
        mine_high = jnp.concatenate([mine_high[:2], add_low(mine_high[2:], across)], axis=0)
        low_first, low_second, mine_high, grad_part = together(low[:2], low[2:], mine_high, grad_part)
        got = send(mine_high, sizes, 2)
        across_second, across_first = across_high(low_second, sizes), across_high(low_first, sizes)
    else:
        grad_part = input_part(grads_two, weight_two)
    input_grad, small_one = input_back(x_img, grad_y, grads_one, grad_part, weight_one, norms)
    small = jnp.concatenate([small_one[0:2], small_two[0:2], small_two[8:]], axis=0)
    output = block_output(y, logits, back)
    if stepwise:
        got, across_second, small = together(got, across_second, small)
        small = small + across_core(small, sizes)
        smalls = sums_over(small, sizes, (0, 2), (4, 0))
        got_two = send(add_low(mine_low[2:], got[2:], across_second), sizes, 1)
        got_two, across_first, smalls, output, first_grad, second_grad = together(got_two, across_first, smalls, output, first_grad, second_grad)
        held = add_low(mine_low[:2], got[:2], across_first, got_two)
        smalls = sums_over(sum(smalls), sizes, (1, 0), (2, 0))
        got, smalls = together(send(held[1], sizes, 0), smalls)
        qkv_grad, out_grad, norm_grad, router_grad = unpack(index, held[0], got, smalls, columns)
        router_grad = router_grad.reshape(columns, 1)
    else:
        small = sum_small(small, sizes)
        full = jnp.concatenate(
            [dealt_one[0].reshape(width, 3, half), dealt_two[0].reshape(width, 3, half)], axis=2
        ).transpose(1, 0, 2)
        qkv_grad = lax.psum_scatter(full, "dp", scatter_dimension=1, tiled=True)
        qkv_grad = lax.psum_scatter(qkv_grad, "tensor", scatter_dimension=2, tiled=True)
        out_grad = lax.psum_scatter(out_grad_t.T, "dp", scatter_dimension=1, tiled=True)
        out_grad = lax.psum_scatter(out_grad, "tensor", scatter_dimension=0, tiled=True)
        norm_grad = lax.dynamic_slice(small, (tensor_index, dp_index * rows), (1, rows))
        router_grad = lax.dynamic_slice(
            small, (tensor_size + dp_index, tensor_index * columns), (1, columns)
        ).reshape(columns, 1)
    return (
        output,
        input_grad,
        qkv_grad,
        out_grad,
        router_grad,
        norm_grad,
        first_grad[None],
        second_grad[None],
    )


def solution(mesh):
    sizes = (mesh.shape["dp"], mesh.shape["tensor"])
    return jax.shard_map(
        functools.partial(on_device, sizes),
        mesh=mesh,
        in_specs=(
            P(("dp", "tensor"), None),
            P(None, "dp", "tensor"),
            P("tensor", "dp"),
            P("tensor", "dp"),
            P("tensor", "dp"),
            P("dp", None, "tensor"),
            P("dp", "tensor", None),
            P(("dp", "tensor"), None),
        ),
        out_specs=(
            P(("dp", "tensor"), None),
            P(("dp", "tensor"), None),
            P(None, "dp", "tensor"),
            P("tensor", "dp"),
            P("tensor", "dp"),
            P("tensor", "dp"),
            P("dp", None, "tensor"),
            P("dp", "tensor", None),
        ),
        check_vma=False,
    )
```

```python
import functools

import jax
import jax.numpy as jnp
from jax import lax
from jax.experimental import pallas as pl
from jax.experimental.pallas import tpu as pltpu
from jax.sharding import PartitionSpec as P

HEAD_DIM = 64
SEQ = 197
PAD = 208
SLOT_ROWS = 16
AXES = ("dp", "tensor")
BF = jnp.bfloat16
F32 = jnp.float32
LAST = (((1,), (1,)), ((), ()))
FIRST = (((0,), (0,)), ((), ()))
MIDDLE = (((1,), (0,)), ((), ()))
MIB = 1024 * 1024


def dot(a, b, dims=MIDDLE):
    return lax.dot_general(a, b, dims, preferred_element_type=F32)


def shape_of(shape, dtype):
    return jax.ShapeDtypeStruct(shape, dtype)


def run(kernel, name, operands, results, limit, scratch=(), scalars=0, aliases=()):
    memory = [pltpu.SMEM] * scalars + [pltpu.VMEM] * (len(operands) - scalars)
    return pl.pallas_call(
        kernel,
        in_specs=[pl.BlockSpec(memory_space=m) for m in memory],
        out_specs=[pl.BlockSpec(memory_space=pltpu.VMEM) for _ in results],
        out_shape=list(results),
        scratch_shapes=list(scratch),
        input_output_aliases=dict(aliases),
        compiler_params=pltpu.CompilerParams(vmem_limit_bytes=limit * MIB),
        cost_estimate=pl.CostEstimate(flops=1, bytes_accessed=1, transcendentals=0),
        name=name,
    )(*operands)


def layer_stats(values):
    centre = jnp.mean(values, axis=-1, keepdims=True)
    centred = values - centre
    spread = jnp.mean(centred * centred, axis=-1, keepdims=True)
    inv_std = lax.rsqrt(spread + 1e-06)
    return centred * inv_std, inv_std


def lane_ids(shape):
    return lax.broadcasted_iota(jnp.int32, shape, len(shape) - 1)


def row_ids(shape):
    return lax.broadcasted_iota(jnp.int32, shape, len(shape) - 2)


def flat(ref):
    images, rows, columns = ref.shape
    return ref[...].reshape(images * rows, columns)


def prepare_kernel(x_ref, g_ref, x_out, g_out, unit_out, wide):
    count, width = x_ref.shape
    real = row_ids((PAD, width)) < SEQ
    wide[count:, :] = jnp.zeros((wide.shape[0] - count, width), F32)
    for ref, out in ((x_ref, x_out), (g_ref, g_out)):
        wide[0:count, :] = ref[...].astype(F32)
        for i in range(out.shape[0]):
            rows = jnp.where(real, wide[SEQ * i : SEQ * i + PAD, :], 0.0)
            out[i] = rows.astype(BF)
            if ref is x_ref:
                unit_out[i], _ = layer_stats(rows)


def prepare(tokens, cotangent):
    count, width = tokens.shape
    images = count // SEQ
    rows = shape_of((images, PAD, width), BF)
    return run(
        prepare_kernel,
        "prepare",
        (tokens, cotangent),
        (rows, rows, shape_of((images, PAD, width), F32)),
        9,
        scratch=[pltpu.VMEM((-(-count // 8) * 8 + 16, width), F32)],
    )


def attend_rows(normed, w_ref, qkv_ref, mixed_ref, probs_ref, piece):
    images, rows, width = mixed_ref.shape
    span = width // 2
    low = lane_ids((rows, 128)) < HEAD_DIM
    key_ok = row_ids((rows, rows)) < SEQ
    zero = jnp.zeros((rows, 128), BF)
    proj = dot(normed, w_ref[...])
    qkv_ref[:, :, 0:span] = (proj[:, 0:span] * HEAD_DIM ** (-0.5)).astype(BF).reshape(images, rows, span)
    qkv_ref[:, :, span:] = proj[:, span:].astype(BF).reshape(images, rows, 2 * span)

    def image(i, carry):
        for p in range(span // 128):
            at = slice(p * 128, (p + 1) * 128)
            q = qkv_ref[i, :, at]
            k = qkv_ref[i, :, span + p * 128 : span + (p + 1) * 128]
            v = qkv_ref[i, :, 2 * span + p * 128 : 2 * span + (p + 1) * 128]
            mixed = []
            for h in range(2):
                q_one = jnp.where(low, q, zero) if h == 0 else jnp.where(low, zero, q)
                scores = jnp.where(key_ok, dot(k, q_one, LAST), -1e30)
                scaled = jnp.exp(scores - jnp.max(scores, axis=0, keepdims=True))
                weights = (scaled * (1.0 / jnp.sum(scaled, axis=0, keepdims=True))).astype(BF)
                probs_ref[i, 2 * p + h] = weights
                mixed.append(dot(weights, v, FIRST))
            at = slice(piece * span + p * 128, piece * span + (p + 1) * 128)
            mixed_ref[i, :, at] = jnp.where(low, mixed[0], mixed[1]).astype(BF)
        return carry

    lax.fori_loop(0, images, image, 0, unroll=3 if images % 3 == 0 else 1)


def assemble_rows(owners, parts, kinds, out_ref, columns, lane=0):
    for side, (owner, refs) in enumerate(zip(owners, parts, strict=True)):
        count = out_ref.shape[0] // owner.shape[0]
        blocks = [ref[i * count : (i + 1) * count] for ref in refs for i in range(ref.shape[0] // count)]
        for p, block in enumerate(blocks):
            row = pl.multiple_of(count * owner[p], 16)
            for at, kind in enumerate(kinds):
                to = lane + (2 * at + side) * columns
                out_ref[pl.ds(row, count), to : to + columns] = block[:, kind * columns : (kind + 1) * columns]


def attend_first_kernel(counts, *refs):
    if counts:
        own, sib = counts
        owners, refs = refs[:2], refs[2:]
        unit_ref, norms_ref, refs = refs[0], refs[1], refs[2:]
        parts, refs = (refs[:own], refs[own : own + sib]), refs[own + sib :]
        n_ref, qkv_ref, mixed_ref, probs_ref, w_ref, out_w_ref = refs
        columns = w_ref.shape[1] // 6
        assemble_rows(owners, parts, range(3), w_ref, columns)
        assemble_rows(owners, parts, [3], out_w_ref, columns)
    else:
        unit_ref, norms_ref, w_ref, n_ref, qkv_ref, mixed_ref, probs_ref = refs
    normed = (flat(unit_ref) * norms_ref[0:1, :] + norms_ref[1:2, :]).astype(BF)
    n_ref[...] = normed.reshape(n_ref.shape)
    attend_rows(normed, w_ref, qkv_ref, mixed_ref, probs_ref, 0)


def attend_second_kernel(counts, *refs):
    if counts:
        own, sib = counts
        owners, refs = refs[:2], refs[2:]
        n_ref, refs = refs[0], refs[3:]
        parts, refs = (refs[:own], refs[own : own + sib]), refs[own + sib :]
        mixed_ref, out_w_ref, qkv_ref, probs_ref, w_ref = refs
        columns = w_ref.shape[1] // 6
        assemble_rows(owners, parts, range(3), w_ref, columns)
        assemble_rows(owners, parts, [3], out_w_ref, columns, 2 * columns)
    else:
        n_ref, _, w_ref, mixed_ref, qkv_ref, probs_ref = refs
    attend_rows(flat(n_ref), w_ref, qkv_ref, mixed_ref, probs_ref, 1)


def attend_first(unit, norms, owners, weights):
    images, rows, width = unit.shape
    span = width // 2
    results = (
        shape_of(unit.shape, BF),
        shape_of((images, rows, 3 * span), BF),
        shape_of(unit.shape, BF),
        shape_of((images, span // HEAD_DIM, rows, rows), BF),
    )
    counts = None
    if owners:
        counts = tuple(map(len, weights))
        weights = sum(weights, ())
        results += (shape_of((width, 3 * span), BF), shape_of((width, width), BF))
    return run(
        functools.partial(attend_first_kernel, counts),
        "attend_first",
        owners + (unit, norms) + weights,
        results,
        8,
        scalars=len(owners),
    )


def attend_second(normed, mixed, out_w, owners, weights):
    images, rows, width = normed.shape
    span = width // 2
    given = (mixed, out_w) if owners else (mixed,)
    results = tuple(shape_of(g.shape, BF) for g in given) + (
        shape_of((images, rows, 3 * span), BF),
        shape_of((images, span // HEAD_DIM, rows, rows), BF),
    )
    counts = None
    if owners:
        counts = tuple(map(len, weights))
        weights = sum(weights, ())
        results += (shape_of((width, 3 * span), BF),)
    return run(
        functools.partial(attend_second_kernel, counts),
        "attend_second",
        owners + (normed,) + given + weights,
        results,
        8,
        scalars=len(owners),
        aliases=[(len(owners) + 1 + i, i) for i in range(len(given))],
    )


def softmaxes(logits):
    ok = lane_ids(logits.shape) < SEQ
    masked = jnp.where(ok, logits, -1e30)
    up = jnp.exp(masked - jnp.max(masked, axis=1, keepdims=True))
    dispatch = up / jnp.sum(up, axis=1, keepdims=True)
    up = jnp.exp(logits - jnp.max(logits, axis=0, keepdims=True))
    combine = up / jnp.sum(up, axis=0, keepdims=True)
    return dispatch, combine


def place_rows(experts, image, offset):
    shape = (experts * SLOT_ROWS, experts)
    return (row_ids(shape) == lane_ids(shape) * SLOT_ROWS + offset + image).astype(BF)


def pick_rows(experts, image, offset):
    shape = (experts, experts * SLOT_ROWS)
    return (lane_ids(shape) == row_ids(shape) * SLOT_ROWS + offset + image).astype(BF)


def route_kernel(
    x_ref, mixed_ref, out_w_ref, norms_ref, router_ref, g_ref, y_ref, n_ref, logits_ref, send_ref
):
    images, rows, width = x_ref.shape
    experts = router_ref.shape[0]
    y = flat(x_ref).astype(F32) + dot(flat(mixed_ref), out_w_ref[...], LAST)
    y_ref[...] = y.reshape(y_ref.shape)
    unit, _ = layer_stats(y)
    normed = (unit * norms_ref[2:3, :] + norms_ref[3:4, :]).astype(BF)
    n_ref[...] = normed.reshape(n_ref.shape)
    placed = 0.0
    for i in range(images):
        logits = dot(router_ref[...], n_ref[i], LAST)
        logits_ref[i] = logits
        dispatch, combine = softmaxes(logits)
        slots = dot(dispatch.astype(BF), n_ref[i]).astype(BF)
        grad_returned = dot(combine.astype(BF), g_ref[i]).astype(BF)
        placed = placed + dot(place_rows(experts, i, 0), slots)
        placed = placed + dot(place_rows(experts, i, SLOT_ROWS // 2), grad_returned)
    send_ref[...] = placed.astype(BF)


def route(x_img, mixed, out_w, norms, router, g_img):
    images, rows, width = x_img.shape
    experts = router.shape[0]
    return run(
        route_kernel,
        "route",
        (x_img, mixed, out_w, norms, router, g_img),
        (
            shape_of((images, rows, width), F32),
            shape_of((images, rows, width), BF),
            shape_of((images, experts, rows), F32),
            shape_of((experts * SLOT_ROWS, width), BF),
        ),
        8,
    )


def split_rows(blocks):
    wide = blocks.astype(F32)
    half = SLOT_ROWS // 2
    shape = (blocks.shape[0] * half, blocks.shape[2])
    return wide[:, :half].reshape(shape).astype(BF), wide[:, half:].reshape(shape).astype(BF)


def join_rows(ones, twos):
    half = SLOT_ROWS // 2
    shape = (ones.shape[0] // half, half, ones.shape[1])
    return jnp.concatenate([ones.reshape(shape), twos.reshape(shape)], axis=1).astype(BF)


def gelu_parts(pre):
    cdf = 0.5 * (1.0 + lax.erf(pre * (0.5**0.5)))
    density = jnp.exp(-0.5 * pre * pre) * 0.3989422804014327
    return pre * cdf, cdf + pre * density


def expert_kernel(
    a_ref, b_ref, c_ref, d_ref, w1_ref, w2_ref, keep_ref, send_ref, slots_ref, grads_ref, hidden_ref, pre_ref
):
    count = a_ref.shape[0]
    blocks = jnp.concatenate([a_ref[...], b_ref[...], c_ref[...], d_ref[...]], axis=0)
    slots, grads = split_rows(blocks)
    pre = dot(slots, w1_ref[...])
    hidden, slope = gelu_parts(pre)
    hidden = hidden.astype(BF)
    returned = dot(hidden, w2_ref[...])
    grad_pre = (dot(grads, w2_ref[...], LAST) * slope).astype(BF)
    grad_slots = dot(grad_pre, w1_ref[...], LAST)
    joined = join_rows(returned, grad_slots)
    joined = joined.reshape((4, count) + joined.shape[1:])
    keep_ref[...] = joined[:2]
    send_ref[...] = joined[2:]
    slots_ref[...] = slots
    grads_ref[...] = grads
    hidden_ref[...] = hidden
    pre_ref[...] = grad_pre


def run_expert(own, near, first_weight, second_weight):
    width, units = first_weight.shape
    rows = 4 * own[0].shape[0] * SLOT_ROWS // 2
    half = shape_of((2,) + own[0].shape, BF)
    return run(
        expert_kernel,
        "expert",
        own + near + (first_weight, second_weight),
        (
            half,
            half,
            shape_of((rows, width), BF),
            shape_of((rows, width), BF),
            shape_of((rows, units), BF),
            shape_of((rows, units), BF),
        ),
        8 if rows <= 512 else 48,
    )


def expert_grad_kernel(slots_ref, grads_ref, hidden_ref, pre_ref, d1_ref, d2_ref):
    d1_ref[...] = dot(slots_ref[...], pre_ref[...], FIRST)
    d2_ref[...] = dot(hidden_ref[...], grads_ref[...], FIRST)


def expert_grads(slots, grads, hidden, grad_pre):
    rows, width = slots.shape
    units = hidden.shape[1]
    return run(
        expert_grad_kernel,
        "expert_grads",
        (slots, grads, hidden, grad_pre),
        (shape_of((width, units), F32), shape_of((units, width), F32)),
        16 if rows <= 512 else 32,
    )


def moe_ready_kernel(y_ref, logits_ref, unit_ref, inv_ref, dispatch_ref, combine_ref):
    unit, inv_std = layer_stats(flat(y_ref))
    unit_ref[...] = unit.reshape(unit_ref.shape)
    inv_ref[...] = inv_std.reshape(inv_ref.shape)
    for i in range(y_ref.shape[0]):
        dispatch_ref[i], combine_ref[i] = softmaxes(logits_ref[i])


def moe_ready(y, logits):
    images, rows, width = y.shape
    return run(
        moe_ready_kernel,
        "moe_ready",
        (y, logits),
        (
            shape_of((images, rows, width), F32),
            shape_of((images, rows, 1), F32),
            shape_of(logits.shape, F32),
            shape_of(logits.shape, F32),
        ),
        8,
    )


def moe_back_kernel(
    unit_ref,
    inv_ref,
    dispatch_ref,
    combine_ref,
    n_ref,
    g_ref,
    back_ref,
    norms_ref,
    router_ref,
    out_w_ref,
    mixed_ref,
    grad_y_ref,
    grad_mixed_ref,
    out_grad_ref,
    small_ref,
    attn_ref,
):
    images, rows, width = unit_ref.shape
    experts = router_ref.shape[0]
    gain = norms_ref[2:3, :]
    router_grad, gain_grad, shift_grad = 0.0, 0.0, 0.0
    for i in range(images):
        returned = dot(pick_rows(experts, i, 0), back_ref[...]).astype(BF)
        grad_slots = dot(pick_rows(experts, i, SLOT_ROWS // 2), back_ref[...]).astype(BF)
        dispatch, combine = dispatch_ref[i], combine_ref[i]
        grad_combine = dot(returned, g_ref[i], LAST)
        grad_dispatch = dot(grad_slots, n_ref[i], LAST)
        grad_logits = dispatch * (
            grad_dispatch - jnp.sum(grad_dispatch * dispatch, axis=1, keepdims=True)
        ) + combine * (grad_combine - jnp.sum(grad_combine * combine, axis=0, keepdims=True))
        grad_logits = grad_logits.astype(BF)
        router_grad = router_grad + dot(grad_logits, n_ref[i])
        grad_two = dot(dispatch.astype(BF), grad_slots, FIRST) + dot(grad_logits, router_ref[...], FIRST)
        unit, inv_std = unit_ref[i], inv_ref[i]
        gain_grad = gain_grad + jnp.sum(grad_two * unit, axis=0, keepdims=True)
        shift_grad = shift_grad + jnp.sum(grad_two, axis=0, keepdims=True)
        scaled = grad_two * gain
        mean_one = jnp.mean(scaled, axis=-1, keepdims=True)
        mean_two = jnp.mean(scaled * unit, axis=-1, keepdims=True)
        grad_y = g_ref[i].astype(F32) + inv_std * (scaled - mean_one - unit * mean_two)
        grad_y_ref[i] = grad_y
        attn_ref[i] = grad_y.astype(BF)
    small_ref[...] = jnp.zeros_like(small_ref)
    small_ref[0:1, :] = gain_grad
    small_ref[1:2, :] = shift_grad
    small_ref[8 : 8 + experts, :] = router_grad
    grad_attn = flat(attn_ref)
    grad_mixed_ref[...] = dot(grad_attn, out_w_ref[...]).astype(BF).reshape(grad_mixed_ref.shape)
    out_grad_ref[...] = dot(grad_attn, flat(mixed_ref), FIRST).astype(out_grad_ref.dtype)


def moe_back(ready, normed, g_img, back, norms, router, out_w, mixed, dtype):
    images, rows, width = normed.shape
    experts = router.shape[0]
    return run(
        moe_back_kernel,
        "moe_back",
        ready + (normed, g_img, back, norms, router, out_w, mixed),
        (
            shape_of((images, rows, width), F32),
            shape_of((images, rows, width), BF),
            shape_of((width, width), dtype),
            shape_of((8 + experts, width), F32),
        ),
        12,
        scratch=[pltpu.VMEM((images, rows, width), BF)],
    )


def output_kernel(y_ref, logits_ref, back_ref, out_ref, wide):
    images, experts, _ = logits_ref.shape
    for i in range(images):
        returned = dot(pick_rows(experts, i, 0), back_ref[...]).astype(BF)
        _, combine = softmaxes(logits_ref[i])
        total = y_ref[i] + dot(combine.astype(BF), returned, FIRST)
        wide[SEQ * i : SEQ * (i + 1), :] = total[0:SEQ]
    out_ref[...] = wide[...].astype(BF)


def block_output(y, logits, back):
    images, rows, width = y.shape
    count = images * SEQ
    return run(
        output_kernel,
        "block_output",
        (y, logits, back),
        (shape_of((count, width), BF),),
        12,
        scratch=[pltpu.VMEM((count, width), F32)],
    )[0]


def deal_rows(owners, full_ref, first, kinds, refs, columns):
    for side, (owner, ref) in enumerate(zip(owners, refs, strict=True)):
        blocks, count, _ = ref.shape
        for p in range(blocks):
            row = pl.multiple_of(count * owner[p], 16)
            for at, kind in enumerate(kinds):
                lane = first + (2 * at + side) * columns
                ref[p, :, kind * columns : (kind + 1) * columns] = full_ref[pl.ds(row, count), lane : lane + columns]


def attend_back_kernel(stepwise, piece, *refs):
    if stepwise:
        owners, refs = refs[:2], refs[2:]
        n_ref, qkv_ref, probs_ref, mixed_ref, gm_ref, og_ref, grads_ref, own_ref, sib_ref, dw_ref = refs
    else:
        n_ref, qkv_ref, probs_ref, mixed_ref, gm_ref, grads_ref, dw_ref = refs
    images, rows, width = mixed_ref.shape
    span = width // 2
    low = lane_ids((rows, 128)) < HEAD_DIM
    zero = jnp.zeros((rows, 128), BF)
    minus = jnp.full((rows, 128), -1.0, BF)

    def image(i, carry):
        for p in range(span // 128):
            at = slice(p * 128, (p + 1) * 128)
            at_k = slice(span + p * 128, span + (p + 1) * 128)
            at_v = slice(2 * span + p * 128, 2 * span + (p + 1) * 128)
            q, k, v = qkv_ref[i, :, at], qkv_ref[i, :, at_k], qkv_ref[i, :, at_v]
            here = slice(piece * span + p * 128, piece * span + (p + 1) * 128)
            gm = gm_ref[i, :, here]
            inner = pltpu.roll(gm.astype(F32) * mixed_ref[i, :, here].astype(F32), HEAD_DIM, 1).astype(BF)
            grad_q, grad_k, grad_v = 0.0, 0.0, 0.0
            for h in range(2):
                mine = low if h == 0 else jnp.logical_not(low)
                weights = probs_ref[i, 2 * p + h]
                centred = dot(jnp.where(mine, v, minus), jnp.where(mine, gm, inner), LAST)
                grad_scores = (weights.astype(F32) * centred).astype(BF)
                grad_v = grad_v + dot(weights, jnp.where(mine, gm, zero))
                grad_k = grad_k + dot(grad_scores, jnp.where(mine, q, zero))
                grad_q = grad_q + dot(grad_scores, jnp.where(mine, k, zero), FIRST)
            grads_ref[i, :, at] = (grad_q * HEAD_DIM ** (-0.5)).astype(BF)
            grads_ref[i, :, at_k] = grad_k.astype(BF)
            grads_ref[i, :, at_v] = grad_v.astype(BF)
        return carry

    lax.fori_loop(0, images, image, 0, unroll=images)
    dw_ref[...] = dot(flat(n_ref), flat(grads_ref), FIRST).astype(dw_ref.dtype)
    if stepwise:
        deal_rows(owners, dw_ref, 0, range(3), (own_ref, sib_ref), span // 2)
        deal_rows(owners, og_ref, piece * span, [3], (own_ref, sib_ref), span // 2)


def attend_back(normed, qkv, probs, mixed, grad_mixed, out_grad_t, piece, owners, sizes):
    images, rows, width = normed.shape
    span = width // 2
    operands = (normed, qkv, probs, mixed, grad_mixed)
    results = (shape_of((images, rows, 3 * span), BF),)
    scratch = ()
    if owners:
        operands += (out_grad_t,)
        results += (shape_of((sizes[0], width // sizes[0], 2 * span), BF),) * 2
        scratch = (pltpu.VMEM((width, 3 * span), BF),)
    else:
        results += (shape_of((width, 3 * span), F32),)
    return run(
        functools.partial(attend_back_kernel, bool(owners), piece),
        "attend_back",
        owners + operands,
        results,
        9,
        scratch,
        scalars=len(owners),
    )


def input_part_kernel(p_ref, w_ref, out_ref):
    out_ref[...] = dot(flat(p_ref), w_ref[...], LAST).reshape(out_ref.shape)


def input_part(grads, weight):
    images, rows, _ = grads.shape
    return run(
        input_part_kernel, "input_part", (grads, weight), (shape_of((images, rows, weight.shape[0]), F32),), 16
    )[0]


def input_sum_kernel(x_ref, p1_ref, part_ref, w1_ref, grad_ref, small_ref):
    images, rows, width = x_ref.shape
    grad_ref[...] = (dot(flat(p1_ref), w1_ref[...], LAST) + flat(part_ref)).reshape(grad_ref.shape)
    gain_grad, shift_grad = 0.0, 0.0
    for i in range(images):
        unit, _ = layer_stats(x_ref[i].astype(F32))
        gain_grad = gain_grad + jnp.sum(grad_ref[i] * unit, axis=0, keepdims=True)
        shift_grad = shift_grad + jnp.sum(grad_ref[i], axis=0, keepdims=True)
    small_ref[...] = jnp.zeros_like(small_ref)
    small_ref[0:1, :] = gain_grad
    small_ref[1:2, :] = shift_grad


def input_sum(x_img, grads_one, grad_part, weight_one):
    width = x_img.shape[2]
    return run(
        input_sum_kernel,
        "input_sum",
        (x_img, grads_one, grad_part, weight_one),
        (shape_of(x_img.shape, F32), shape_of((8, width), F32)),
        8,
    )


def input_back_kernel(x_ref, gy_ref, grad_ref, norms_ref, out_ref):
    gain = norms_ref[0:1, :]
    for i in range(x_ref.shape[0]):
        unit, inv_std = layer_stats(x_ref[i].astype(F32))
        scaled = grad_ref[i] * gain
        mean_one = jnp.mean(scaled, axis=-1, keepdims=True)
        mean_two = jnp.mean(scaled * unit, axis=-1, keepdims=True)
        total = gy_ref[i] + inv_std * (scaled - mean_one - unit * mean_two)
        out_ref[SEQ * i : SEQ * (i + 1), :] = total[0:SEQ]


def input_back(x_img, grad_y, grad_one, norms):
    images, _, width = x_img.shape
    return run(
        input_back_kernel,
        "input_back",
        (x_img, grad_y, grad_one, norms),
        (shape_of((images * SEQ, width), F32),),
        8,
    )[0]


def spot(shape, start):
    return (lane_ids(shape) == row_ids(shape) + start).astype(BF)


def place_kernel(index_ref, norm_ref, router_ref, small_ref):
    rows, columns = norm_ref.shape[1], router_ref.shape[1]
    width = small_ref.shape[1]
    dp_index, tensor_index = index_ref[0], index_ref[1]
    norm = dot(jnp.broadcast_to(norm_ref[...], (16, rows)), spot((rows, width), dp_index * rows))
    router = dot(jnp.broadcast_to(router_ref[...], (16, columns)), spot((columns, width), tensor_index * columns))
    row = row_ids(small_ref.shape)
    small_ref[...] = jnp.where(
        row == tensor_index, norm[0:1], jnp.where(row == width // columns + dp_index, router[0:1], 0.0)
    ).astype(BF)


def place(index, norm_params, router, experts):
    rows, columns = norm_params.shape[1], router.shape[0]
    width = rows * experts
    return run(
        place_kernel,
        "place",
        (index, norm_params, router.T),
        (shape_of((-(-(width // columns + experts) // 16) * 16, width), BF),),
        4,
        scalars=1,
    )[0]


def pack_kernel(qkv_ref, out_ref, block_ref):
    kinds, _, columns = qkv_ref.shape
    for kind in range(kinds):
        block_ref[:, kind * columns : (kind + 1) * columns] = qkv_ref[kind]
    block_ref[:, kinds * columns :] = out_ref[...].T


def pack(qkv_weight, out_weight):
    kinds, rows, columns = qkv_weight.shape
    return run(
        pack_kernel,
        "pack",
        (qkv_weight, out_weight),
        (shape_of((rows, (kinds + 1) * columns), BF),),
        4,
    )[0]


def unpack_kernel(index_ref, own_ref, got_ref, near_ref, qkv_ref, out_ref, norm_ref, router_ref):
    kinds, rows, columns = qkv_ref.shape
    total = own_ref[...].astype(F32) + got_ref[...].astype(F32)
    for kind in range(kinds):
        qkv_ref[kind] = total[0:rows, kind * columns : (kind + 1) * columns]
    out_ref[...] = total[0:rows, kinds * columns :].T
    small = total[rows:] + near_ref[...].astype(F32)
    dp_index, tensor_index = index_ref[0], index_ref[1]
    width = small.shape[1]
    row = row_ids(small.shape)
    norm = jnp.sum(jnp.where(row == tensor_index, small, 0.0), axis=0, keepdims=True)
    router = jnp.sum(jnp.where(row == width // columns + dp_index, small, 0.0), axis=0, keepdims=True)
    norm_out, router_out = 0.0, 0.0
    for _ in range(3):
        part = norm.astype(BF)
        norm = norm - part.astype(F32)
        norm_out = norm_out + dot(
            jnp.broadcast_to(part, (16, width)), spot((rows, width), dp_index * rows), LAST
        )
        part = router.astype(BF)
        router = router - part.astype(F32)
        router_out = router_out + dot(
            jnp.broadcast_to(part, (16, width)), spot((columns, width), tensor_index * columns), LAST
        )
    norm_ref[...] = norm_out[0:1]
    router_ref[...] = router_out[0:1]


def unpack(index, own, got, near, sizes):
    width = own.shape[1]
    rows, columns = width // sizes[0], width // sizes[1]
    return run(
        unpack_kernel,
        "unpack",
        (index, own, got, near),
        (
            shape_of((width // columns - 1, rows, columns), F32),
            shape_of((columns, rows), F32),
            shape_of((1, rows), F32),
            shape_of((1, columns), F32),
        ),
        4,
        scalars=1,
    )


def swap(value, dp_size, tensor_size, dp_mask, tensor_mask):
    pairs = [
        (d * tensor_size + t, (d ^ dp_mask) * tensor_size + (t ^ tensor_mask))
        for d in range(dp_size)
        for t in range(tensor_size)
    ]
    return lax.ppermute(value, AXES, pairs)


def steps_of(dp_size):
    bits = dp_size.bit_length() - 1
    down = list(range(bits))[::-1]
    return [down, down[-1:] + down[:-1]]


def step_pairs(dp_size, tensor_size, *steps):
    masks = [functools.reduce(lambda mask, step: mask ^ (1 << order[step]), steps, 0) for order in steps_of(dp_size)]
    return [
        (d * tensor_size + t, (d ^ masks[t % 2]) * tensor_size + t)
        for d in range(dp_size)
        for t in range(tensor_size)
    ]


def owners_of(dp_size, dp_index, core):
    both = []
    for order in steps_of(dp_size):
        place = jnp.arange(dp_size, dtype=jnp.int32)
        away = jnp.zeros_like(place)
        for step, bit in enumerate(order):
            away = away | (((place >> step) & 1) << bit)
        both.append(away ^ dp_index)
    return jnp.where(core == 0, both[0], both[1]), jnp.where(core == 0, both[1], both[0])


def together(*values):
    return lax.optimization_barrier(values)


def send(value, sizes, *steps):
    return lax.ppermute(value, AXES, step_pairs(*sizes, *steps))


def across_core(value, sizes):
    return swap(value, *sizes, 0, 1)


def across_high(value, sizes, *steps):
    pairs = [(a, b ^ 2) for a, b in step_pairs(*sizes, *steps)]
    return lax.ppermute(value, AXES, pairs)


def gather_first(block, small, sizes, along):
    rows = block.shape[0]
    small_high, block = together(across_high(small, sizes), block)
    small = small + small_high
    small = small + across_core(small, sizes)
    first = jnp.concatenate([block, small], axis=0)
    got, high = together(send(first, sizes, 0), across_high(block, sizes))
    held = jnp.concatenate([block, got[:rows], small + got[rows:]], axis=0)

    got, near, high_got = together(send(held, sizes, 1), across_core(held, sizes), across_high(got[:rows], sizes))
    high = jnp.concatenate([high, high_got], axis=0)
    small = held[2 * rows :] + got[2 * rows :]
    four = jnp.concatenate([held[: 2 * rows], got[: 2 * rows], small], axis=0)

    last, near_two, high_two, high_near, along = together(
        send(four, sizes, 2), across_core(got, sizes), across_high(got, sizes), across_core(high, sizes), prepare(*along)
    )
    small = four[4 * rows :] + last[4 * rows :]
    own = (four, last), (near, near_two, across_core(last, sizes))
    return own, ((high, high_two), (high_near,)), small, along


def gather_second(own, high, sizes, rows):
    (first, second), (first_near,) = high
    _, last = own
    along = send(first, sizes, 2)
    across = across_high(last[2 * rows : 4 * rows], sizes)
    return (first, second, along, across), first_near, across_core(second, sizes)


def gather_weights_plain(qkv_weight, out_weight, router, norm_params):
    qkv = lax.all_gather(qkv_weight, "dp", axis=1, tiled=True)
    qkv = lax.all_gather(qkv, "tensor", axis=2, tiled=True)
    out_w, router, norms = (
        lax.all_gather(lax.all_gather(w, "dp", axis=1, tiled=True), "tensor", axis=0, tiled=True)
        for w in (out_weight, router, norm_params)
    )
    width = qkv.shape[1]
    half = width // 2
    one = qkv[:, :, :half].transpose(1, 0, 2).reshape(width, 3 * half)
    two = qkv[:, :, half:].transpose(1, 0, 2).reshape(width, 3 * half)
    return one, two, out_w.T, norms.astype(F32), router.T


def add_low(*values):
    return sum(v.astype(F32) for v in values).astype(BF)


def sum_small(values, sizes):
    dp_size, tensor_size = sizes
    mask = 1
    while mask < tensor_size:
        values = values + swap(values, dp_size, tensor_size, 0, mask)
        mask *= 2
    mask = 1
    while mask < dp_size:
        values = values + swap(values, dp_size, tensor_size, mask, 0)
        mask *= 2
    return values


def on_device(
    sizes, tokens, qkv_weight, out_weight, router, norm_params, expert_in, expert_out, cotangent
):
    dp_size, tensor_size = sizes
    dp_index = lax.axis_index("dp")
    tensor_index = lax.axis_index("tensor")
    core = jnp.bitwise_and(tensor_index, 1)
    width = tokens.shape[1]
    half = width // 2
    rows = qkv_weight.shape[1]
    columns = qkv_weight.shape[2]
    experts = dp_size * router.shape[1]
    stepwise = rows % 16 == 0 and sizes == (8, 4)
    owners = ()
    if stepwise:
        owners = owners_of(dp_size, dp_index, core)
        index = jnp.stack([dp_index, tensor_index]).astype(jnp.int32)
        *owners, index, qkv_weight, out_weight, norm_params, router = together(
            *owners, index, qkv_weight, out_weight, norm_params, router
        )
        owners = tuple(owners)
        small = place(index, norm_params, router, experts)
        block = pack(qkv_weight, out_weight)
        (own, near), high, small, (x_img, g_img, unit) = gather_first(block, small, sizes, (tokens, cotangent))
        norms, router_t = small[:tensor_size].astype(F32), small[tensor_size : tensor_size + experts]
        (first, second, third, fourth), near_first, near_second = gather_second(own, high, sizes, rows)
        normed, qkv_one, mixed, probs_one, weight_one, out_w = attend_first(unit, norms, owners, (own, near))
        third, fourth, near_second, normed = together(third, fourth, near_second, normed)
        near_third, near_fourth = across_core(third, sizes), across_core(fourth, sizes)
        parts = (first, second, third, fourth), (near_first, near_second, near_third, near_fourth)
        mixed, out_w, qkv_two, probs_two, weight_two = attend_second(normed, mixed, out_w, owners, parts)
    else:
        x_img, g_img, unit = prepare(tokens, cotangent)
        weight_one, weight_two, out_w, norms, router_t = gather_weights_plain(
            qkv_weight, out_weight, router, norm_params
        )
        normed, qkv_one, mixed, probs_one = attend_first(unit, norms, (), (weight_one,))
        mixed, qkv_two, probs_two = attend_second(normed, mixed, None, (), (weight_two,))
    y, normed_two, logits, outgoing = route(x_img, mixed, out_w, norms, router_t, g_img)

    outgoing = outgoing.reshape(experts, SLOT_ROWS, width)
    arrived = lax.all_to_all(outgoing, "dp", split_axis=0, concat_axis=0, tiled=True)
    across = across_high(arrived, sizes)
    near = across_core(arrived, sizes)
    across, near, ready = lax.optimization_barrier((across, near, tuple(moe_ready(y, logits))))
    keep, away, *kept = run_expert((arrived, across), (near, across_core(across, sizes)), expert_in[0], expert_out[0])
    got = across_high(add_low(keep[1], across_core(away[1], sizes)), sizes)
    got, near = lax.optimization_barrier((got, across_core(away[0], sizes)))
    summed = add_low(keep[0], near, got)
    back = lax.all_to_all(summed, "dp", split_axis=0, concat_axis=0, tiled=True)
    back = back.reshape(experts * SLOT_ROWS, width)

    grad_y, grad_mixed, out_grad_t, small_two = moe_back(
        ready, normed_two, g_img, back, norms, router_t, out_w, mixed, BF if stepwise else F32
    )
    grads_two, *dealt_two = attend_back(
        normed, qkv_two, probs_two, mixed, grad_mixed, out_grad_t, 1, owners, sizes
    )
    grad_part = input_part(grads_two, weight_two)
    if stepwise:
        mine = dealt_two[0].reshape(width, width)
        got, grad_part = together(across_core(dealt_two[1].reshape(width, width), sizes), grad_part)
        cut = [rows * place for place in range(9)]
        low, along = add_low(mine[: cut[3]], got[: cut[3]]), add_low(mine[cut[4] : cut[7]], got[cut[4] : cut[7]])
        across = [add_low(mine[at : at + rows], got[at : at + rows]) for at in (cut[3], cut[7])]
        low, along, across, grad_mixed = together(low, along, jnp.concatenate(across, axis=0), grad_mixed)
        along, across = send(along, sizes, 2), across_high(across, sizes)
    grads_one, *dealt_one = attend_back(
        normed, qkv_one, probs_one, mixed, grad_mixed, out_grad_t, 0, owners, sizes
    )
    if stepwise:
        along, across, mine, sent, grads_one = together(along, across, *dealt_one, grads_one)
        mine = mine.reshape(width, width)
        got = across_core(sent.reshape(width, width), sizes)
    grad_one, small_one = input_sum(x_img, grads_one, grad_part, weight_one)
    small = jnp.concatenate([small_one[0:2], small_two[0:2], small_two[8:]], axis=0)
    if stepwise:
        got, small, grad_one = together(got, small, grad_one)
        small = jnp.pad(small.astype(BF), ((0, -small.shape[0] % 16), (0, 0)))
        low = jnp.concatenate([add_low(low, along), small], axis=0)
        high = [
            add_low(mine[cut[4] : cut[7]], got[cut[4] : cut[7]]),
            add_low(mine[cut[7] :], got[cut[7] :], across[rows:]),
            small,
        ]
        high = jnp.concatenate(high, axis=0)
        held = [
            add_low(mine[: cut[3]], got[: cut[3]]),
            add_low(mine[cut[3] : cut[4]], got[cut[3] : cut[4]], across[:rows]),
        ]
        low, high, held, grad_one = together(low, high, held, grad_one)
        got, across, corner = send(high, sizes, 2), across_high(low, sizes), across_high(small, sizes, 2)
    input_grad = input_back(x_img, grad_y, grad_one, norms)
    output = block_output(y, logits, back)
    first_grad, second_grad = expert_grads(*kept)
    if stepwise:
        got, across, corner, input_grad = together(got, across, corner, input_grad)
        small = add_low(small, got[cut[4] :], across[cut[3] :], corner)
        low = add_low(held[0][: cut[2]], got[: cut[2]], across[: cut[2]])
        high = [
            add_low(held[0][cut[2] :], got[cut[2] : cut[3]], across[cut[2] : cut[3]]),
            add_low(held[1], got[cut[3] : cut[4]]),
            small,
        ]
        got, output = together(send(jnp.concatenate(high, axis=0), sizes, 1), output)
        low = add_low(low, got[: cut[2]])
        small = add_low(small, got[cut[2] :])
        high = jnp.concatenate([low[rows:], small], axis=0)
        got, first_grad, second_grad = together(send(high, sizes, 0), first_grad, second_grad)
        low = jnp.concatenate([low[:rows], small], axis=0)
        near = across_core(add_low(small, got[rows:]), sizes)
        qkv_grad, out_grad, norm_grad, router_grad = unpack(index, low, got, near, sizes)
        router_grad = router_grad.reshape(columns, 1)
    else:
        small = sum_small(small, sizes)
        full = jnp.concatenate(
            [dealt_one[0].reshape(width, 3, half), dealt_two[0].reshape(width, 3, half)], axis=2
        ).transpose(1, 0, 2)
        qkv_grad = lax.psum_scatter(full, "dp", scatter_dimension=1, tiled=True)
        qkv_grad = lax.psum_scatter(qkv_grad, "tensor", scatter_dimension=2, tiled=True)
        out_grad = lax.psum_scatter(out_grad_t.T, "dp", scatter_dimension=1, tiled=True)
        out_grad = lax.psum_scatter(out_grad, "tensor", scatter_dimension=0, tiled=True)
        norm_grad = lax.dynamic_slice(small, (tensor_index, dp_index * rows), (1, rows))
        router_grad = lax.dynamic_slice(
            small, (tensor_size + dp_index, tensor_index * columns), (1, columns)
        ).reshape(columns, 1)
    return (
        output,
        input_grad,
        qkv_grad,
        out_grad,
        router_grad,
        norm_grad,
        first_grad[None],
        second_grad[None],
    )


def solution(mesh):
    sizes = (mesh.shape["dp"], mesh.shape["tensor"])
    return jax.shard_map(
        functools.partial(on_device, sizes),
        mesh=mesh,
        in_specs=(
            P(("dp", "tensor"), None),
            P(None, "dp", "tensor"),
            P("tensor", "dp"),
            P("tensor", "dp"),
            P("tensor", "dp"),
            P("dp", None, "tensor"),
            P("dp", "tensor", None),
            P(("dp", "tensor"), None),
        ),
        out_specs=(
            P(("dp", "tensor"), None),
            P(("dp", "tensor"), None),
            P(None, "dp", "tensor"),
            P("tensor", "dp"),
            P("tensor", "dp"),
            P("tensor", "dp"),
            P("dp", None, "tensor"),
            P("dp", "tensor", None),
        ),
        check_vma=False,
    )
```

```python
import functools

import jax
import jax.numpy as jnp
from jax import lax
from jax.experimental import pallas as pl
from jax.experimental.pallas import tpu as pltpu
from jax.sharding import PartitionSpec as P

HEAD_DIM = 64
SEQ = 197
PAD = 208
SLOT_ROWS = 16
AXES = ("dp", "tensor")
BF = jnp.bfloat16
F32 = jnp.float32
LAST = (((1,), (1,)), ((), ()))
FIRST = (((0,), (0,)), ((), ()))
MIDDLE = (((1,), (0,)), ((), ()))
MIB = 1024 * 1024


def dot(a, b, dims=MIDDLE):
    return lax.dot_general(a, b, dims, preferred_element_type=F32)


def shape_of(shape, dtype):
    return jax.ShapeDtypeStruct(shape, dtype)


def run(kernel, name, operands, results, limit, scratch=(), scalars=0, aliases=()):
    memory = [pltpu.SMEM] * scalars + [pltpu.VMEM] * (len(operands) - scalars)
    return pl.pallas_call(
        kernel,
        in_specs=[pl.BlockSpec(memory_space=m) for m in memory],
        out_specs=[pl.BlockSpec(memory_space=pltpu.VMEM) for _ in results],
        out_shape=list(results),
        scratch_shapes=list(scratch),
        input_output_aliases=dict(aliases),
        compiler_params=pltpu.CompilerParams(vmem_limit_bytes=limit * MIB),
        cost_estimate=pl.CostEstimate(flops=1, bytes_accessed=1, transcendentals=0),
        name=name,
    )(*operands)


def layer_stats(values):
    centre = jnp.mean(values, axis=-1, keepdims=True)
    centred = values - centre
    spread = jnp.mean(centred * centred, axis=-1, keepdims=True)
    inv_std = lax.rsqrt(spread + 1e-06)
    return centred * inv_std, inv_std


def lane_ids(shape):
    return lax.broadcasted_iota(jnp.int32, shape, len(shape) - 1)


def row_ids(shape):
    return lax.broadcasted_iota(jnp.int32, shape, len(shape) - 2)


def flat(ref):
    images, rows, columns = ref.shape
    return ref[...].reshape(images * rows, columns)


def prepare_kernel(x_ref, g_ref, x_out, g_out, unit_out, wide):
    count, width = x_ref.shape
    real = row_ids((PAD, width)) < SEQ
    wide[count:, :] = jnp.zeros((wide.shape[0] - count, width), F32)
    for ref, out in ((x_ref, x_out), (g_ref, g_out)):
        wide[0:count, :] = ref[...].astype(F32)
        for i in range(out.shape[0]):
            rows = jnp.where(real, wide[SEQ * i : SEQ * i + PAD, :], 0.0)
            out[i] = rows.astype(BF)
            if ref is x_ref:
                unit_out[i], _ = layer_stats(rows)


def prepare(tokens, cotangent):
    count, width = tokens.shape
    images = count // SEQ
    rows = shape_of((images, PAD, width), BF)
    return run(
        prepare_kernel,
        "prepare",
        (tokens, cotangent),
        (rows, rows, shape_of((images, PAD, width), F32)),
        9,
        scratch=[pltpu.VMEM((-(-count // 8) * 8 + 16, width), F32)],
    )


def attend_rows(normed, w_ref, qkv_ref, mixed_ref, probs_ref, piece):
    images, rows, width = mixed_ref.shape
    span = width // 2
    low = lane_ids((rows, 128)) < HEAD_DIM
    key_ok = row_ids((rows, rows)) < SEQ
    zero = jnp.zeros((rows, 128), BF)
    proj = dot(normed, w_ref[...])
    qkv_ref[:, :, 0:span] = (proj[:, 0:span] * HEAD_DIM ** (-0.5)).astype(BF).reshape(images, rows, span)
    qkv_ref[:, :, span:] = proj[:, span:].astype(BF).reshape(images, rows, 2 * span)

    def image(i, carry):
        for p in range(span // 128):
            at = slice(p * 128, (p + 1) * 128)
            q = qkv_ref[i, :, at]
            k = qkv_ref[i, :, span + p * 128 : span + (p + 1) * 128]
            v = qkv_ref[i, :, 2 * span + p * 128 : 2 * span + (p + 1) * 128]
            mixed = []
            for h in range(2):
                q_one = jnp.where(low, q, zero) if h == 0 else jnp.where(low, zero, q)
                scores = jnp.where(key_ok, dot(k, q_one, LAST), -1e30)
                scaled = jnp.exp(scores - jnp.max(scores, axis=0, keepdims=True))
                weights = (scaled * (1.0 / jnp.sum(scaled, axis=0, keepdims=True))).astype(BF)
                probs_ref[i, 2 * p + h] = weights
                mixed.append(dot(weights, v, FIRST))
            at = slice(piece * span + p * 128, piece * span + (p + 1) * 128)
            mixed_ref[i, :, at] = jnp.where(low, mixed[0], mixed[1]).astype(BF)
        return carry

    lax.fori_loop(0, images, image, 0, unroll=3 if images % 3 == 0 else 1)


def assemble_rows(owners, parts, kinds, out_ref, columns, lane=0):
    for side, (owner, refs) in enumerate(zip(owners, parts, strict=True)):
        count = out_ref.shape[0] // owner.shape[0]
        blocks = [ref[i * count : (i + 1) * count] for ref in refs for i in range(ref.shape[0] // count)]
        for p, block in enumerate(blocks):
            row = pl.multiple_of(count * owner[p], 16)
            for at, kind in enumerate(kinds):
                to = lane + (2 * at + side) * columns
                out_ref[pl.ds(row, count), to : to + columns] = block[:, kind * columns : (kind + 1) * columns]


def attend_first_kernel(counts, *refs):
    if counts:
        own, sib = counts
        owners, refs = refs[:2], refs[2:]
        unit_ref, norms_ref, refs = refs[0], refs[1], refs[2:]
        parts, refs = (refs[:own], refs[own : own + sib]), refs[own + sib :]
        n_ref, qkv_ref, mixed_ref, probs_ref, w_ref, out_w_ref = refs
        columns = w_ref.shape[1] // 6
        assemble_rows(owners, parts, range(3), w_ref, columns)
        assemble_rows(owners, parts, [3], out_w_ref, columns)
    else:
        unit_ref, norms_ref, w_ref, n_ref, qkv_ref, mixed_ref, probs_ref = refs
    normed = (flat(unit_ref) * norms_ref[0:1, :] + norms_ref[1:2, :]).astype(BF)
    n_ref[...] = normed.reshape(n_ref.shape)
    attend_rows(normed, w_ref, qkv_ref, mixed_ref, probs_ref, 0)


def attend_second_kernel(counts, *refs):
    if counts:
        own, sib = counts
        owners, refs = refs[:2], refs[2:]
        n_ref, refs = refs[0], refs[3:]
        parts, refs = (refs[:own], refs[own : own + sib]), refs[own + sib :]
        mixed_ref, out_w_ref, qkv_ref, probs_ref, w_ref = refs
        columns = w_ref.shape[1] // 6
        assemble_rows(owners, parts, range(3), w_ref, columns)
        assemble_rows(owners, parts, [3], out_w_ref, columns, 2 * columns)
    else:
        n_ref, _, w_ref, mixed_ref, qkv_ref, probs_ref = refs
    attend_rows(flat(n_ref), w_ref, qkv_ref, mixed_ref, probs_ref, 1)


def attend_first(unit, norms, owners, weights):
    images, rows, width = unit.shape
    span = width // 2
    results = (
        shape_of(unit.shape, BF),
        shape_of((images, rows, 3 * span), BF),
        shape_of(unit.shape, BF),
        shape_of((images, span // HEAD_DIM, rows, rows), BF),
    )
    counts = None
    if owners:
        counts = tuple(map(len, weights))
        weights = sum(weights, ())
        results += (shape_of((width, 3 * span), BF), shape_of((width, width), BF))
    return run(
        functools.partial(attend_first_kernel, counts),
        "attend_first",
        owners + (unit, norms) + weights,
        results,
        5,
        scalars=len(owners),
    )


def attend_second(normed, mixed, out_w, owners, weights):
    images, rows, width = normed.shape
    span = width // 2
    given = (mixed, out_w) if owners else (mixed,)
    results = tuple(shape_of(g.shape, BF) for g in given) + (
        shape_of((images, rows, 3 * span), BF),
        shape_of((images, span // HEAD_DIM, rows, rows), BF),
    )
    counts = None
    if owners:
        counts = tuple(map(len, weights))
        weights = sum(weights, ())
        results += (shape_of((width, 3 * span), BF),)
    return run(
        functools.partial(attend_second_kernel, counts),
        "attend_second",
        owners + (normed,) + given + weights,
        results,
        5,
        scalars=len(owners),
        aliases=[(len(owners) + 1 + i, i) for i in range(len(given))],
    )


def softmaxes(logits):
    ok = lane_ids(logits.shape) < SEQ
    masked = jnp.where(ok, logits, -1e30)
    up = jnp.exp(masked - jnp.max(masked, axis=1, keepdims=True))
    dispatch = up / jnp.sum(up, axis=1, keepdims=True)
    up = jnp.exp(logits - jnp.max(logits, axis=0, keepdims=True))
    combine = up / jnp.sum(up, axis=0, keepdims=True)
    return dispatch, combine


def place_rows(experts, image, offset):
    shape = (experts * SLOT_ROWS, experts)
    return (row_ids(shape) == lane_ids(shape) * SLOT_ROWS + offset + image).astype(BF)


def pick_rows(experts, image, offset):
    shape = (experts, experts * SLOT_ROWS)
    return (lane_ids(shape) == row_ids(shape) * SLOT_ROWS + offset + image).astype(BF)


def route_kernel(
    x_ref, mixed_ref, out_w_ref, norms_ref, router_ref, g_ref, y_ref, n_ref, logits_ref, send_ref
):
    images, rows, width = x_ref.shape
    experts = router_ref.shape[0]
    y = flat(x_ref).astype(F32) + dot(flat(mixed_ref), out_w_ref[...], LAST)
    y_ref[...] = y.reshape(y_ref.shape)
    unit, _ = layer_stats(y)
    normed = (unit * norms_ref[2:3, :] + norms_ref[3:4, :]).astype(BF)
    n_ref[...] = normed.reshape(n_ref.shape)
    placed = 0.0
    for i in range(images):
        logits = dot(router_ref[...], n_ref[i], LAST)
        logits_ref[i] = logits
        dispatch, combine = softmaxes(logits)
        slots = dot(dispatch.astype(BF), n_ref[i]).astype(BF)
        grad_returned = dot(combine.astype(BF), g_ref[i]).astype(BF)
        placed = placed + dot(place_rows(experts, i, 0), slots)
        placed = placed + dot(place_rows(experts, i, SLOT_ROWS // 2), grad_returned)
    send_ref[...] = placed.astype(BF)


def route(x_img, mixed, out_w, norms, router, g_img):
    images, rows, width = x_img.shape
    experts = router.shape[0]
    return run(
        route_kernel,
        "route",
        (x_img, mixed, out_w, norms, router, g_img),
        (
            shape_of((images, rows, width), F32),
            shape_of((images, rows, width), BF),
            shape_of((images, experts, rows), F32),
            shape_of((experts * SLOT_ROWS, width), BF),
        ),
        5,
    )


def split_rows(blocks):
    wide = blocks.astype(F32)
    half = SLOT_ROWS // 2
    shape = (blocks.shape[0] * half, blocks.shape[2])
    return wide[:, :half].reshape(shape).astype(BF), wide[:, half:].reshape(shape).astype(BF)


def join_rows(ones, twos):
    half = SLOT_ROWS // 2
    shape = (ones.shape[0] // half, half, ones.shape[1])
    return jnp.concatenate([ones.reshape(shape), twos.reshape(shape)], axis=1).astype(BF)


def gelu_parts(pre):
    cdf = 0.5 * (1.0 + lax.erf(pre * (0.5**0.5)))
    density = jnp.exp(-0.5 * pre * pre) * 0.3989422804014327
    return pre * cdf, cdf + pre * density


def expert_kernel(
    a_ref, b_ref, c_ref, d_ref, w1_ref, w2_ref, keep_ref, send_ref, slots_ref, grads_ref, hidden_ref, pre_ref
):
    count = a_ref.shape[0]
    blocks = jnp.concatenate([a_ref[...], b_ref[...], c_ref[...], d_ref[...]], axis=0)
    slots, grads = split_rows(blocks)
    pre = dot(slots, w1_ref[...])
    hidden, slope = gelu_parts(pre)
    hidden = hidden.astype(BF)
    returned = dot(hidden, w2_ref[...])
    grad_pre = (dot(grads, w2_ref[...], LAST) * slope).astype(BF)
    grad_slots = dot(grad_pre, w1_ref[...], LAST)
    joined = join_rows(returned, grad_slots)
    joined = joined.reshape((4, count) + joined.shape[1:])
    keep_ref[...] = joined[:2]
    send_ref[...] = joined[2:]
    slots_ref[...] = slots
    grads_ref[...] = grads
    hidden_ref[...] = hidden
    pre_ref[...] = grad_pre


def run_expert(own, near, first_weight, second_weight):
    width, units = first_weight.shape
    rows = 4 * own[0].shape[0] * SLOT_ROWS // 2
    half = shape_of((2,) + own[0].shape, BF)
    return run(
        expert_kernel,
        "expert",
        own + near + (first_weight, second_weight),
        (
            half,
            half,
            shape_of((rows, width), BF),
            shape_of((rows, width), BF),
            shape_of((rows, units), BF),
            shape_of((rows, units), BF),
        ),
        5 if rows <= 512 else 48,
    )


def expert_grad_kernel(slots_ref, grads_ref, hidden_ref, pre_ref, d1_ref, d2_ref):
    d1_ref[...] = dot(slots_ref[...], pre_ref[...], FIRST)
    d2_ref[...] = dot(hidden_ref[...], grads_ref[...], FIRST)


def expert_grads(slots, grads, hidden, grad_pre):
    rows, width = slots.shape
    units = hidden.shape[1]
    return run(
        expert_grad_kernel,
        "expert_grads",
        (slots, grads, hidden, grad_pre),
        (shape_of((width, units), F32), shape_of((units, width), F32)),
        16 if rows <= 512 else 32,
    )


def moe_ready_kernel(y_ref, logits_ref, unit_ref, inv_ref, dispatch_ref, combine_ref):
    unit, inv_std = layer_stats(flat(y_ref))
    unit_ref[...] = unit.reshape(unit_ref.shape)
    inv_ref[...] = inv_std.reshape(inv_ref.shape)
    for i in range(y_ref.shape[0]):
        dispatch_ref[i], combine_ref[i] = softmaxes(logits_ref[i])


def moe_ready(y, logits):
    images, rows, width = y.shape
    return run(
        moe_ready_kernel,
        "moe_ready",
        (y, logits),
        (
            shape_of((images, rows, width), F32),
            shape_of((images, rows, 1), F32),
            shape_of(logits.shape, F32),
            shape_of(logits.shape, F32),
        ),
        5,
    )


def moe_back_kernel(
    unit_ref,
    inv_ref,
    dispatch_ref,
    combine_ref,
    n_ref,
    g_ref,
    back_ref,
    norms_ref,
    router_ref,
    out_w_ref,
    mixed_ref,
    grad_y_ref,
    grad_mixed_ref,
    out_grad_ref,
    small_ref,
    attn_ref,
):
    images, rows, width = unit_ref.shape
    experts = router_ref.shape[0]
    gain = norms_ref[2:3, :]
    router_grad, gain_grad, shift_grad = 0.0, 0.0, 0.0
    for i in range(images):
        returned = dot(pick_rows(experts, i, 0), back_ref[...]).astype(BF)
        grad_slots = dot(pick_rows(experts, i, SLOT_ROWS // 2), back_ref[...]).astype(BF)
        dispatch, combine = dispatch_ref[i], combine_ref[i]
        grad_combine = dot(returned, g_ref[i], LAST)
        grad_dispatch = dot(grad_slots, n_ref[i], LAST)
        grad_logits = dispatch * (
            grad_dispatch - jnp.sum(grad_dispatch * dispatch, axis=1, keepdims=True)
        ) + combine * (grad_combine - jnp.sum(grad_combine * combine, axis=0, keepdims=True))
        grad_logits = grad_logits.astype(BF)
        router_grad = router_grad + dot(grad_logits, n_ref[i])
        grad_two = dot(
            jnp.concatenate([dispatch.astype(BF), grad_logits], axis=0),
            jnp.concatenate([grad_slots, router_ref[...]], axis=0),
            FIRST,
        )
        unit, inv_std = unit_ref[i], inv_ref[i]
        gain_grad = gain_grad + jnp.sum(grad_two * unit, axis=0, keepdims=True)
        shift_grad = shift_grad + jnp.sum(grad_two, axis=0, keepdims=True)
        scaled = grad_two * gain
        mean_one = jnp.mean(scaled, axis=-1, keepdims=True)
        mean_two = jnp.mean(scaled * unit, axis=-1, keepdims=True)
        grad_y = g_ref[i].astype(F32) + inv_std * (scaled - mean_one - unit * mean_two)
        grad_y_ref[i] = grad_y
        attn_ref[i] = grad_y.astype(BF)
    small_ref[...] = jnp.zeros_like(small_ref)
    small_ref[0:1, :] = gain_grad
    small_ref[1:2, :] = shift_grad
    small_ref[8 : 8 + experts, :] = router_grad
    grad_attn = flat(attn_ref)
    grad_mixed_ref[...] = dot(grad_attn, out_w_ref[...]).astype(BF).reshape(grad_mixed_ref.shape)
    out_grad_ref[...] = dot(grad_attn, flat(mixed_ref), FIRST).astype(out_grad_ref.dtype)


def moe_back(ready, normed, g_img, back, norms, router, out_w, mixed, dtype):
    images, rows, width = normed.shape
    experts = router.shape[0]
    return run(
        moe_back_kernel,
        "moe_back",
        ready + (normed, g_img, back, norms, router, out_w, mixed),
        (
            shape_of((images, rows, width), F32),
            shape_of((images, rows, width), BF),
            shape_of((width, width), dtype),
            shape_of((8 + experts, width), F32),
        ),
        10,
        scratch=[pltpu.VMEM((images, rows, width), BF)],
    )


def output_kernel(y_ref, logits_ref, back_ref, out_ref, wide):
    images, experts, _ = logits_ref.shape
    for i in range(images):
        returned = dot(pick_rows(experts, i, 0), back_ref[...]).astype(BF)
        _, combine = softmaxes(logits_ref[i])
        total = y_ref[i] + dot(combine.astype(BF), returned, FIRST)
        wide[SEQ * i : SEQ * (i + 1), :] = total[0:SEQ]
    out_ref[...] = wide[...].astype(BF)


def block_output(y, logits, back):
    images, rows, width = y.shape
    count = images * SEQ
    return run(
        output_kernel,
        "block_output",
        (y, logits, back),
        (shape_of((count, width), BF),),
        12,
        scratch=[pltpu.VMEM((count, width), F32)],
    )[0]


def deal_rows(owners, full_ref, first, kinds, refs, columns):
    for side, (owner, ref) in enumerate(zip(owners, refs, strict=True)):
        blocks, count, _ = ref.shape
        for p in range(blocks):
            row = pl.multiple_of(count * owner[p], 16)
            for at, kind in enumerate(kinds):
                lane = first + (2 * at + side) * columns
                ref[p, :, kind * columns : (kind + 1) * columns] = full_ref[pl.ds(row, count), lane : lane + columns]


def attend_back_kernel(stepwise, piece, *refs):
    if stepwise:
        owners, refs = refs[:2], refs[2:]
        n_ref, qkv_ref, probs_ref, mixed_ref, gm_ref, og_ref, grads_ref, own_ref, sib_ref, dw_ref = refs
    else:
        n_ref, qkv_ref, probs_ref, mixed_ref, gm_ref, grads_ref, dw_ref = refs
    images, rows, width = mixed_ref.shape
    span = width // 2
    low = lane_ids((rows, 128)) < HEAD_DIM
    zero = jnp.zeros((rows, 128), BF)
    minus = jnp.full((rows, 128), -1.0, BF)

    def image(i, carry):
        for p in range(span // 128):
            at = slice(p * 128, (p + 1) * 128)
            at_k = slice(span + p * 128, span + (p + 1) * 128)
            at_v = slice(2 * span + p * 128, 2 * span + (p + 1) * 128)
            q, k, v = qkv_ref[i, :, at], qkv_ref[i, :, at_k], qkv_ref[i, :, at_v]
            here = slice(piece * span + p * 128, piece * span + (p + 1) * 128)
            gm = gm_ref[i, :, here]
            inner = pltpu.roll(gm.astype(F32) * mixed_ref[i, :, here].astype(F32), HEAD_DIM, 1).astype(BF)
            grad_q, grad_k, grad_v = 0.0, 0.0, 0.0
            for h in range(2):
                mine = low if h == 0 else jnp.logical_not(low)
                weights = probs_ref[i, 2 * p + h]
                centred = dot(jnp.where(mine, v, minus), jnp.where(mine, gm, inner), LAST)
                grad_scores = (weights.astype(F32) * centred).astype(BF)
                grad_v = grad_v + dot(weights, jnp.where(mine, gm, zero))
                grad_k = grad_k + dot(grad_scores, jnp.where(mine, q, zero))
                grad_q = grad_q + dot(grad_scores, jnp.where(mine, k, zero), FIRST)
            grads_ref[i, :, at] = (grad_q * HEAD_DIM ** (-0.5)).astype(BF)
            grads_ref[i, :, at_k] = grad_k.astype(BF)
            grads_ref[i, :, at_v] = grad_v.astype(BF)
        return carry

    lax.fori_loop(0, images, image, 0, unroll=images)
    dw_ref[...] = dot(flat(n_ref), flat(grads_ref), FIRST).astype(dw_ref.dtype)
    if stepwise:
        deal_rows(owners, dw_ref, 0, range(3), (own_ref, sib_ref), span // 2)
        deal_rows(owners, og_ref, piece * span, [3], (own_ref, sib_ref), span // 2)


def attend_back(normed, qkv, probs, mixed, grad_mixed, out_grad_t, piece, owners, sizes):
    images, rows, width = normed.shape
    span = width // 2
    operands = (normed, qkv, probs, mixed, grad_mixed)
    results = (shape_of((images, rows, 3 * span), BF),)
    scratch = ()
    if owners:
        operands += (out_grad_t,)
        results += (shape_of((sizes[0], width // sizes[0], 2 * span), BF),) * 2
        scratch = (pltpu.VMEM((width, 3 * span), BF),)
    else:
        results += (shape_of((width, 3 * span), F32),)
    return run(
        functools.partial(attend_back_kernel, bool(owners), piece),
        "attend_back",
        owners + operands,
        results,
        7,
        scratch,
        scalars=len(owners),
    )


def input_part_kernel(p_ref, w_ref, out_ref):
    out_ref[...] = dot(flat(p_ref), w_ref[...], LAST).reshape(out_ref.shape)


def input_part(grads, weight):
    images, rows, _ = grads.shape
    return run(
        input_part_kernel, "input_part", (grads, weight), (shape_of((images, rows, weight.shape[0]), F32),), 16
    )[0]


def input_sum_kernel(x_ref, p1_ref, part_ref, w1_ref, grad_ref, small_ref):
    images, rows, width = x_ref.shape
    grad_ref[...] = (dot(flat(p1_ref), w1_ref[...], LAST) + flat(part_ref)).reshape(grad_ref.shape)
    gain_grad, shift_grad = 0.0, 0.0
    for i in range(images):
        unit, _ = layer_stats(x_ref[i].astype(F32))
        gain_grad = gain_grad + jnp.sum(grad_ref[i] * unit, axis=0, keepdims=True)
        shift_grad = shift_grad + jnp.sum(grad_ref[i], axis=0, keepdims=True)
    small_ref[...] = jnp.zeros_like(small_ref)
    small_ref[0:1, :] = gain_grad
    small_ref[1:2, :] = shift_grad


def input_sum(x_img, grads_one, grad_part, weight_one):
    width = x_img.shape[2]
    return run(
        input_sum_kernel,
        "input_sum",
        (x_img, grads_one, grad_part, weight_one),
        (shape_of(x_img.shape, F32), shape_of((8, width), F32)),
        8,
    )


def input_back_kernel(x_ref, gy_ref, grad_ref, norms_ref, out_ref):
    gain = norms_ref[0:1, :]
    for i in range(x_ref.shape[0]):
        unit, inv_std = layer_stats(x_ref[i].astype(F32))
        scaled = grad_ref[i] * gain
        mean_one = jnp.mean(scaled, axis=-1, keepdims=True)
        mean_two = jnp.mean(scaled * unit, axis=-1, keepdims=True)
        total = gy_ref[i] + inv_std * (scaled - mean_one - unit * mean_two)
        out_ref[SEQ * i : SEQ * (i + 1), :] = total[0:SEQ]


def input_back(x_img, grad_y, grad_one, norms):
    images, _, width = x_img.shape
    return run(
        input_back_kernel,
        "input_back",
        (x_img, grad_y, grad_one, norms),
        (shape_of((images * SEQ, width), F32),),
        8,
    )[0]


def spot(shape, start):
    return (lane_ids(shape) == row_ids(shape) + start).astype(BF)


def place_kernel(index_ref, norm_ref, router_ref, small_ref):
    rows, columns = norm_ref.shape[1], router_ref.shape[1]
    width = small_ref.shape[1]
    dp_index, tensor_index = index_ref[0], index_ref[1]
    norm = dot(jnp.broadcast_to(norm_ref[...], (16, rows)), spot((rows, width), dp_index * rows))
    router = dot(jnp.broadcast_to(router_ref[...], (16, columns)), spot((columns, width), tensor_index * columns))
    row = row_ids(small_ref.shape)
    small_ref[...] = jnp.where(
        row == tensor_index, norm[0:1], jnp.where(row == width // columns + dp_index, router[0:1], 0.0)
    ).astype(BF)


def place(index, norm_params, router, experts):
    rows, columns = norm_params.shape[1], router.shape[0]
    width = rows * experts
    return run(
        place_kernel,
        "place",
        (index, norm_params, router.T),
        (shape_of((-(-(width // columns + experts) // 16) * 16, width), BF),),
        4,
        scalars=1,
    )[0]


def pack_kernel(qkv_ref, out_ref, block_ref):
    kinds, _, columns = qkv_ref.shape
    for kind in range(kinds):
        block_ref[:, kind * columns : (kind + 1) * columns] = qkv_ref[kind]
    block_ref[:, kinds * columns :] = out_ref[...].T


def pack(qkv_weight, out_weight):
    kinds, rows, columns = qkv_weight.shape
    return run(
        pack_kernel,
        "pack",
        (qkv_weight, out_weight),
        (shape_of((rows, (kinds + 1) * columns), BF),),
        4,
    )[0]


def unpack_kernel(index_ref, own_ref, got_ref, near_ref, corner_ref, qkv_ref, out_ref, norm_ref, router_ref):
    kinds, rows, columns = qkv_ref.shape
    total = own_ref[...].astype(F32) + got_ref[...].astype(F32)
    for kind in range(kinds):
        qkv_ref[kind] = total[0:rows, kind * columns : (kind + 1) * columns]
    out_ref[...] = total[0:rows, kinds * columns :].T
    small = total[rows:] + near_ref[...].astype(F32) + corner_ref[...].astype(F32)
    dp_index, tensor_index = index_ref[0], index_ref[1]
    width = small.shape[1]
    row = row_ids(small.shape)
    norm = jnp.sum(jnp.where(row == tensor_index, small, 0.0), axis=0, keepdims=True)
    router = jnp.sum(jnp.where(row == width // columns + dp_index, small, 0.0), axis=0, keepdims=True)
    norm_out, router_out = 0.0, 0.0
    for _ in range(2):
        part = norm.astype(BF)
        norm = norm - part.astype(F32)
        norm_out = norm_out + dot(
            jnp.broadcast_to(part, (16, width)), spot((rows, width), dp_index * rows), LAST
        )
        part = router.astype(BF)
        router = router - part.astype(F32)
        router_out = router_out + dot(
            jnp.broadcast_to(part, (16, width)), spot((columns, width), tensor_index * columns), LAST
        )
    norm_ref[...] = norm_out[0:1]
    router_ref[...] = router_out[0:1]


def unpack(index, own, got, near, corner, sizes):
    width = own.shape[1]
    rows, columns = width // sizes[0], width // sizes[1]
    return run(
        unpack_kernel,
        "unpack",
        (index, own, got, near, corner),
        (
            shape_of((width // columns - 1, rows, columns), F32),
            shape_of((columns, rows), F32),
            shape_of((1, rows), F32),
            shape_of((1, columns), F32),
        ),
        4,
        scalars=1,
    )


def swap(value, dp_size, tensor_size, dp_mask, tensor_mask):
    pairs = [
        (d * tensor_size + t, (d ^ dp_mask) * tensor_size + (t ^ tensor_mask))
        for d in range(dp_size)
        for t in range(tensor_size)
    ]
    return lax.ppermute(value, AXES, pairs)


def steps_of(dp_size):
    bits = dp_size.bit_length() - 1
    down = list(range(bits))[::-1]
    return [down, down[-1:] + down[:-1]]


def step_pairs(dp_size, tensor_size, *steps):
    masks = [functools.reduce(lambda mask, step: mask ^ (1 << order[step]), steps, 0) for order in steps_of(dp_size)]
    return [
        (d * tensor_size + t, (d ^ masks[t % 2]) * tensor_size + t)
        for d in range(dp_size)
        for t in range(tensor_size)
    ]


def owners_of(dp_size, dp_index, core):
    both = []
    for order in steps_of(dp_size):
        place = jnp.arange(dp_size, dtype=jnp.int32)
        away = jnp.zeros_like(place)
        for step, bit in enumerate(order):
            away = away | (((place >> step) & 1) << bit)
        both.append(away ^ dp_index)
    return jnp.where(core == 0, both[0], both[1]), jnp.where(core == 0, both[1], both[0])


def together(*values):
    return lax.optimization_barrier(values)


def send(value, sizes, *steps):
    return lax.ppermute(value, AXES, step_pairs(*sizes, *steps))


def across_core(value, sizes):
    return swap(value, *sizes, 0, 1)


def across_core_after(value, sizes, step):
    pairs = [(a, b ^ 1) for a, b in step_pairs(*sizes, step)]
    return lax.ppermute(value, AXES, pairs)


def across_high(value, sizes, *steps):
    pairs = [(a, b ^ 2) for a, b in step_pairs(*sizes, *steps)]
    return lax.ppermute(value, AXES, pairs)


def gather_first(block, small, sizes, along):
    rows = block.shape[0]
    small_high, block = together(across_high(small, sizes), block)
    small = small + small_high
    small = small + across_core(small, sizes)
    first = jnp.concatenate([block, small], axis=0)
    got, high = together(send(first, sizes, 0), across_high(block, sizes))
    held = jnp.concatenate([block, got[:rows], small + got[rows:]], axis=0)

    got, near, high_got = together(send(held, sizes, 1), across_core(held, sizes), across_high(got[:rows], sizes))
    high = jnp.concatenate([high, high_got], axis=0)
    small = held[2 * rows :] + got[2 * rows :]
    four = jnp.concatenate([held[: 2 * rows], got[: 2 * rows], small], axis=0)

    last, near_two, high_two, high_near, along = together(
        send(four, sizes, 2), across_core(got, sizes), across_high(got, sizes), across_core(high, sizes), prepare(*along)
    )
    small = four[4 * rows :] + last[4 * rows :]
    own = (four, last), (near, near_two, across_core(last, sizes))
    return own, ((high, high_two), (high_near,)), small, along


def gather_second(own, high, sizes, rows):
    (first, second), (first_near,) = high
    _, last = own
    along = send(first, sizes, 2)
    across = across_high(last[2 * rows : 4 * rows], sizes)
    return (first, second, along, across), first_near, across_core(second, sizes)


def gather_weights_plain(qkv_weight, out_weight, router, norm_params):
    qkv = lax.all_gather(qkv_weight, "dp", axis=1, tiled=True)
    qkv = lax.all_gather(qkv, "tensor", axis=2, tiled=True)
    out_w, router, norms = (
        lax.all_gather(lax.all_gather(w, "dp", axis=1, tiled=True), "tensor", axis=0, tiled=True)
        for w in (out_weight, router, norm_params)
    )
    width = qkv.shape[1]
    half = width // 2
    one = qkv[:, :, :half].transpose(1, 0, 2).reshape(width, 3 * half)
    two = qkv[:, :, half:].transpose(1, 0, 2).reshape(width, 3 * half)
    return one, two, out_w.T, norms.astype(F32), router.T


def add_low(*values):
    return sum(v.astype(F32) for v in values).astype(BF)


def sum_small(values, sizes):
    dp_size, tensor_size = sizes
    mask = 1
    while mask < tensor_size:
        values = values + swap(values, dp_size, tensor_size, 0, mask)
        mask *= 2
    mask = 1
    while mask < dp_size:
        values = values + swap(values, dp_size, tensor_size, mask, 0)
        mask *= 2
    return values


def on_device(
    sizes, tokens, qkv_weight, out_weight, router, norm_params, expert_in, expert_out, cotangent
):
    dp_size, tensor_size = sizes
    dp_index = lax.axis_index("dp")
    tensor_index = lax.axis_index("tensor")
    core = jnp.bitwise_and(tensor_index, 1)
    width = tokens.shape[1]
    half = width // 2
    rows = qkv_weight.shape[1]
    columns = qkv_weight.shape[2]
    experts = dp_size * router.shape[1]
    stepwise = rows % 16 == 0 and sizes == (8, 4)
    owners = ()
    if stepwise:
        owners = owners_of(dp_size, dp_index, core)
        index = jnp.stack([dp_index, tensor_index]).astype(jnp.int32)
        *owners, index, qkv_weight, out_weight, norm_params, router = together(
            *owners, index, qkv_weight, out_weight, norm_params, router
        )
        owners = tuple(owners)
        small = place(index, norm_params, router, experts)
        block = pack(qkv_weight, out_weight)
        (own, near), high, small, (x_img, g_img, unit) = gather_first(block, small, sizes, (tokens, cotangent))
        norms, router_t = small[:tensor_size].astype(F32), small[tensor_size : tensor_size + experts]
        (first, second, third, fourth), near_first, near_second = gather_second(own, high, sizes, rows)
        normed, qkv_one, mixed, probs_one, weight_one, out_w = attend_first(unit, norms, owners, (own, near))
        third, fourth, near_second, normed = together(third, fourth, near_second, normed)
        near_third, near_fourth = across_core(third, sizes), across_core(fourth, sizes)
        parts = (first, second, third, fourth), (near_first, near_second, near_third, near_fourth)
        mixed, out_w, qkv_two, probs_two, weight_two = attend_second(normed, mixed, out_w, owners, parts)
    else:
        x_img, g_img, unit = prepare(tokens, cotangent)
        weight_one, weight_two, out_w, norms, router_t = gather_weights_plain(
            qkv_weight, out_weight, router, norm_params
        )
        normed, qkv_one, mixed, probs_one = attend_first(unit, norms, (), (weight_one,))
        mixed, qkv_two, probs_two = attend_second(normed, mixed, None, (), (weight_two,))
    y, normed_two, logits, outgoing = route(x_img, mixed, out_w, norms, router_t, g_img)

    outgoing = outgoing.reshape(experts, SLOT_ROWS, width)
    arrived = lax.all_to_all(outgoing, "dp", split_axis=0, concat_axis=0, tiled=True)
    across = across_high(arrived, sizes)
    near = across_core(arrived, sizes)
    across, near, ready = lax.optimization_barrier((across, near, tuple(moe_ready(y, logits))))
    keep, away, *kept = run_expert((arrived, across), (near, across_core(across, sizes)), expert_in[0], expert_out[0])
    got = across_high(add_low(keep[1], across_core(away[1], sizes)), sizes)
    got, near = lax.optimization_barrier((got, across_core(away[0], sizes)))
    summed = add_low(keep[0], near, got)
    back = lax.all_to_all(summed, "dp", split_axis=0, concat_axis=0, tiled=True)
    back = back.reshape(experts * SLOT_ROWS, width)

    grad_y, grad_mixed, out_grad_t, small_two = moe_back(
        ready, normed_two, g_img, back, norms, router_t, out_w, mixed, BF if stepwise else F32
    )
    grads_two, *dealt_two = attend_back(
        normed, qkv_two, probs_two, mixed, grad_mixed, out_grad_t, 1, owners, sizes
    )
    grad_part = input_part(grads_two, weight_two)
    if stepwise:
        mine = dealt_two[0].reshape(width, width)
        got, grad_part = together(across_core(dealt_two[1].reshape(width, width), sizes), grad_part)
        cut = [rows * place for place in range(9)]
        low, along = add_low(mine[: cut[3]], got[: cut[3]]), add_low(mine[cut[4] : cut[7]], got[cut[4] : cut[7]])
        across = [add_low(mine[at : at + rows], got[at : at + rows]) for at in (cut[3], cut[7])]
        low, along, across, grad_mixed = together(low, along, jnp.concatenate(across, axis=0), grad_mixed)
        along, across = send(along, sizes, 2), across_high(across, sizes)
    grads_one, *dealt_one = attend_back(
        normed, qkv_one, probs_one, mixed, grad_mixed, out_grad_t, 0, owners, sizes
    )
    if stepwise:
        along, across, mine, sent, grads_one = together(along, across, *dealt_one, grads_one)
        mine, sent = mine.reshape(width, width), sent.reshape(width, width)
        got = across_core(sent[cut[4] :], sizes)
        high = [
            add_low(mine[cut[4] : cut[7]], got[: cut[3]]),
            add_low(mine[cut[7] :], got[cut[3] :], across[rows:]),
        ]
        low = add_low(low, along)
        high, low, grads_one, sent = together(jnp.concatenate(high, axis=0), low, grads_one, sent)
        got, got_high, near = send(high, sizes, 2), across_high(low, sizes), across_core(sent[: cut[4]], sizes)
    grad_one, small_one = input_sum(x_img, grads_one, grad_part, weight_one)
    small = jnp.concatenate([small_one[0:2], small_two[0:2], small_two[8:]], axis=0)
    if stepwise:
        small = jnp.pad(small.astype(BF), ((0, -small.shape[0] % 16), (0, 0)))
        smalls = across_high(small, sizes), send(small, sizes, 2), across_high(small, sizes, 2)
        got, got_high, near, smalls = together(got, got_high, near, smalls)
        small = add_low(small, *smalls)
        held = mine[: cut[4]], near, got
        low = add_low(*(h[: cut[2]] for h in held), got_high[: cut[2]])
        high = [
            add_low(*(h[cut[2] : cut[3]] for h in held), got_high[cut[2] :]),
            add_low(*(h[cut[3] : cut[4]] for h in held), across[:rows]),
            small,
        ]
        low, high, grad_one = together(low, jnp.concatenate(high, axis=0), grad_one)
    input_grad = input_back(x_img, grad_y, grad_one, norms)
    output = block_output(y, logits, back)
    first_grad, second_grad = expert_grads(*kept)
    if stepwise:
        got, output, input_grad = together(send(high, sizes, 1), output, input_grad)
        low = add_low(low, got[: cut[2]])
        small = add_low(small, got[cut[2] :])
        near, corner = across_core(small, sizes), across_core_after(small, sizes, 0)
        got, first_grad, second_grad, near, corner = together(
            send(jnp.concatenate([low[rows:], small], axis=0), sizes, 0), first_grad, second_grad, near, corner
        )
        low = jnp.concatenate([low[:rows], small], axis=0)
        qkv_grad, out_grad, norm_grad, router_grad = unpack(index, low, got, near, corner, sizes)
        router_grad = router_grad.reshape(columns, 1)
    else:
        small = sum_small(small, sizes)
        full = jnp.concatenate(
            [dealt_one[0].reshape(width, 3, half), dealt_two[0].reshape(width, 3, half)], axis=2
        ).transpose(1, 0, 2)
        qkv_grad = lax.psum_scatter(full, "dp", scatter_dimension=1, tiled=True)
        qkv_grad = lax.psum_scatter(qkv_grad, "tensor", scatter_dimension=2, tiled=True)
        out_grad = lax.psum_scatter(out_grad_t.T, "dp", scatter_dimension=1, tiled=True)
        out_grad = lax.psum_scatter(out_grad, "tensor", scatter_dimension=0, tiled=True)
        norm_grad = lax.dynamic_slice(small, (tensor_index, dp_index * rows), (1, rows))
        router_grad = lax.dynamic_slice(
            small, (tensor_size + dp_index, tensor_index * columns), (1, columns)
        ).reshape(columns, 1)
    return (
        output,
        input_grad,
        qkv_grad,
        out_grad,
        router_grad,
        norm_grad,
        first_grad[None],
        second_grad[None],
    )


def solution(mesh):
    sizes = (mesh.shape["dp"], mesh.shape["tensor"])
    return jax.shard_map(
        functools.partial(on_device, sizes),
        mesh=mesh,
        in_specs=(
            P(("dp", "tensor"), None),
            P(None, "dp", "tensor"),
            P("tensor", "dp"),
            P("tensor", "dp"),
            P("tensor", "dp"),
            P("dp", None, "tensor"),
            P("dp", "tensor", None),
            P(("dp", "tensor"), None),
        ),
        out_specs=(
            P(("dp", "tensor"), None),
            P(("dp", "tensor"), None),
            P(None, "dp", "tensor"),
            P("tensor", "dp"),
            P("tensor", "dp"),
            P("tensor", "dp"),
            P("dp", None, "tensor"),
            P("dp", "tensor", None),
        ),
        check_vma=False,
    )
```

```python
import functools

import jax
import jax.numpy as jnp
from jax import lax
from jax.experimental import pallas as pl
from jax.experimental.pallas import tpu as pltpu
from jax.sharding import PartitionSpec as P

HEAD_DIM = 64
SEQ = 197
PAD = 208
BLOCK = 8
AXES = ("dp", "tensor")
BF = jnp.bfloat16
F32 = jnp.float32
LAST = (((1,), (1,)), ((), ()))
FIRST = (((0,), (0,)), ((), ()))
MIDDLE = (((1,), (0,)), ((), ()))
MIB = 1024 * 1024


def dot(a, b, dims=MIDDLE):
    return lax.dot_general(a, b, dims, preferred_element_type=F32)


def shape_of(shape, dtype):
    return jax.ShapeDtypeStruct(shape, dtype)


def run(kernel, name, operands, results, limit, scratch=(), scalars=0, aliases=()):
    memory = [pltpu.SMEM] * scalars + [pltpu.VMEM] * (len(operands) - scalars)
    return pl.pallas_call(
        kernel,
        in_specs=[pl.BlockSpec(memory_space=m) for m in memory],
        out_specs=[pl.BlockSpec(memory_space=pltpu.VMEM) for _ in results],
        out_shape=list(results),
        scratch_shapes=list(scratch),
        input_output_aliases=dict(aliases),
        compiler_params=pltpu.CompilerParams(vmem_limit_bytes=limit * MIB),
        cost_estimate=pl.CostEstimate(flops=1, bytes_accessed=1, transcendentals=0),
        name=name,
    )(*operands)


def layer_stats(values):
    centre = jnp.mean(values, axis=-1, keepdims=True)
    centred = values - centre
    spread = jnp.mean(centred * centred, axis=-1, keepdims=True)
    inv_std = lax.rsqrt(spread + 1e-06)
    return centred * inv_std, inv_std


def lane_ids(shape):
    return lax.broadcasted_iota(jnp.int32, shape, len(shape) - 1)


def row_ids(shape):
    return lax.broadcasted_iota(jnp.int32, shape, len(shape) - 2)


def flat(ref):
    images, rows, columns = ref.shape
    return ref[...].reshape(images * rows, columns)


def prepare_kernel(x_ref, g_ref, x_out, g_out, unit_out, wide):
    count, width = x_ref.shape
    real = row_ids((PAD, width)) < SEQ
    wide[count:, :] = jnp.zeros((wide.shape[0] - count, width), F32)
    for ref, out in ((x_ref, x_out), (g_ref, g_out)):
        wide[0:count, :] = ref[...].astype(F32)
        for i in range(out.shape[0]):
            rows = jnp.where(real, wide[SEQ * i : SEQ * i + PAD, :], 0.0)
            out[i] = rows.astype(BF)
            if ref is x_ref:
                unit_out[i], _ = layer_stats(rows)


def prepare(tokens, cotangent):
    count, width = tokens.shape
    images = count // SEQ
    rows = shape_of((images, PAD, width), BF)
    return run(
        prepare_kernel,
        "prepare",
        (tokens, cotangent),
        (rows, rows, shape_of((images, PAD, width), F32)),
        9,
        scratch=[pltpu.VMEM((-(-count // 8) * 8 + 16, width), F32)],
    )


def attend_rows(normed, w_ref, qkv_ref, mixed_ref, probs_ref, piece):
    images, rows, width = mixed_ref.shape
    span = width // 2
    low = lane_ids((rows, 128)) < HEAD_DIM
    key_ok = row_ids((rows, rows)) < SEQ
    zero = jnp.zeros((rows, 128), BF)
    proj = dot(normed, w_ref[...])
    qkv_ref[:, :, 0:span] = (proj[:, 0:span] * HEAD_DIM ** (-0.5)).astype(BF).reshape(images, rows, span)
    qkv_ref[:, :, span:] = proj[:, span:].astype(BF).reshape(images, rows, 2 * span)

    def image(i, carry):
        for p in range(span // 128):
            at = slice(p * 128, (p + 1) * 128)
            q = qkv_ref[i, :, at]
            k = qkv_ref[i, :, span + p * 128 : span + (p + 1) * 128]
            v = qkv_ref[i, :, 2 * span + p * 128 : 2 * span + (p + 1) * 128]
            mixed = []
            for h in range(2):
                q_one = jnp.where(low, q, zero) if h == 0 else jnp.where(low, zero, q)
                scores = jnp.where(key_ok, dot(k, q_one, LAST), -1e30)
                scaled = jnp.exp(scores - jnp.max(scores, axis=0, keepdims=True))
                weights = (scaled * (1.0 / jnp.sum(scaled, axis=0, keepdims=True))).astype(BF)
                probs_ref[i, 2 * p + h] = weights
                mixed.append(dot(weights, v, FIRST))
            at = slice(piece * span + p * 128, piece * span + (p + 1) * 128)
            mixed_ref[i, :, at] = jnp.where(low, mixed[0], mixed[1]).astype(BF)
        return carry

    lax.fori_loop(0, images, image, 0, unroll=3 if images % 3 == 0 else 1)


def assemble_rows(owners, parts, kinds, out_ref, columns, lane=0):
    for side, (owner, refs) in enumerate(zip(owners, parts, strict=True)):
        count = out_ref.shape[0] // owner.shape[0]
        blocks = [ref[i * count : (i + 1) * count] for ref in refs for i in range(ref.shape[0] // count)]
        for p, block in enumerate(blocks):
            row = pl.multiple_of(count * owner[p], 16)
            for at, kind in enumerate(kinds):
                to = lane + (2 * at + side) * columns
                out_ref[pl.ds(row, count), to : to + columns] = block[:, kind * columns : (kind + 1) * columns]


def attend_first_kernel(counts, *refs):
    if counts:
        own, sib = counts
        owners, refs = refs[:2], refs[2:]
        unit_ref, norms_ref, refs = refs[0], refs[1], refs[2:]
        parts, refs = (refs[:own], refs[own : own + sib]), refs[own + sib :]
        n_ref, qkv_ref, mixed_ref, probs_ref, w_ref, out_w_ref = refs
        columns = w_ref.shape[1] // 6
        assemble_rows(owners, parts, range(3), w_ref, columns)
        assemble_rows(owners, parts, [3], out_w_ref, columns)
    else:
        unit_ref, norms_ref, w_ref, n_ref, qkv_ref, mixed_ref, probs_ref = refs
    normed = (flat(unit_ref) * norms_ref[0:1, :] + norms_ref[1:2, :]).astype(BF)
    n_ref[...] = normed.reshape(n_ref.shape)
    attend_rows(normed, w_ref, qkv_ref, mixed_ref, probs_ref, 0)


def attend_second_kernel(counts, *refs):
    if counts:
        own, sib = counts
        owners, refs = refs[:2], refs[2:]
        n_ref, refs = refs[0], refs[3:]
        parts, refs = (refs[:own], refs[own : own + sib]), refs[own + sib :]
        mixed_ref, out_w_ref, qkv_ref, probs_ref, w_ref = refs
        columns = w_ref.shape[1] // 6
        assemble_rows(owners, parts, range(3), w_ref, columns)
        assemble_rows(owners, parts, [3], out_w_ref, columns, 2 * columns)
    else:
        n_ref, _, w_ref, mixed_ref, qkv_ref, probs_ref = refs
    attend_rows(flat(n_ref), w_ref, qkv_ref, mixed_ref, probs_ref, 1)


def attend_first(unit, norms, owners, weights):
    images, rows, width = unit.shape
    span = width // 2
    results = (
        shape_of(unit.shape, BF),
        shape_of((images, rows, 3 * span), BF),
        shape_of(unit.shape, BF),
        shape_of((images, span // HEAD_DIM, rows, rows), BF),
    )
    counts = None
    if owners:
        counts = tuple(map(len, weights))
        weights = sum(weights, ())
        results += (shape_of((width, 3 * span), BF), shape_of((width, width), BF))
    return run(
        functools.partial(attend_first_kernel, counts),
        "attend_first",
        owners + (unit, norms) + weights,
        results,
        5,
        scalars=len(owners),
    )


def attend_second(normed, mixed, out_w, owners, weights):
    images, rows, width = normed.shape
    span = width // 2
    given = (mixed, out_w) if owners else (mixed,)
    results = tuple(shape_of(g.shape, BF) for g in given) + (
        shape_of((images, rows, 3 * span), BF),
        shape_of((images, span // HEAD_DIM, rows, rows), BF),
    )
    counts = None
    if owners:
        counts = tuple(map(len, weights))
        weights = sum(weights, ())
        results += (shape_of((width, 3 * span), BF),)
    return run(
        functools.partial(attend_second_kernel, counts),
        "attend_second",
        owners + (normed,) + given + weights,
        results,
        5,
        scalars=len(owners),
        aliases=[(len(owners) + 1 + i, i) for i in range(len(given))],
    )


def softmaxes(logits):
    ok = lane_ids(logits.shape) < SEQ
    masked = jnp.where(ok, logits, -1e30)
    up = jnp.exp(masked - jnp.max(masked, axis=1, keepdims=True))
    dispatch = up / jnp.sum(up, axis=1, keepdims=True)
    up = jnp.exp(logits - jnp.max(logits, axis=0, keepdims=True))
    combine = up / jnp.sum(up, axis=0, keepdims=True)
    return dispatch, combine


def by_image(experts, places, low, back=False):
    shape = (experts * BLOCK, places * experts)
    shape = shape[::-1] if back else shape
    blocked, other = (lane_ids(shape), row_ids(shape)) if back else (row_ids(shape), lane_ids(shape))
    place = jnp.bitwise_and(blocked, BLOCK - 1) - low
    inside = jnp.logical_and(place >= 0, place < places)
    return jnp.logical_and(inside, other == place * experts + lax.div(blocked, BLOCK)).astype(BF)


def to_blocks(first, second):
    experts, width = first[0].shape
    half = width // 2
    head = dot(by_image(experts, BLOCK, 0), jnp.concatenate(first + second[:2], axis=0))
    rest = jnp.concatenate(second[2:], axis=0)
    rest = dot(by_image(experts, 4, 0), rest[:, :half]) + dot(by_image(experts, 4, 4), rest[:, half:])
    return head.astype(BF), rest.astype(BF)


def from_blocks(blocks, experts, width):
    head = dot(by_image(experts, BLOCK, 0, True), blocks[:, :width])
    rest = [dot(by_image(experts, 4, low, True), blocks[:, width:]) for low in (0, 4)]
    rest = jnp.concatenate(rest, axis=1)
    head, rest = ([v[at : at + experts].astype(BF) for at in range(0, v.shape[0], experts)] for v in (head, rest))
    return head[:6], head[6:] + rest


def route_kernel(
    x_ref, mixed_ref, out_w_ref, norms_ref, router_ref, g_ref, y_ref, n_ref, logits_ref, send_ref
):
    images, rows, width = x_ref.shape
    experts = router_ref.shape[0]
    y = flat(x_ref).astype(F32) + dot(flat(mixed_ref), out_w_ref[...], LAST)
    y_ref[...] = y.reshape(y_ref.shape)
    unit, _ = layer_stats(y)
    normed = (unit * norms_ref[2:3, :] + norms_ref[3:4, :]).astype(BF)
    n_ref[...] = normed.reshape(n_ref.shape)
    first, second = [], []
    for i in range(images):
        logits = dot(router_ref[...], n_ref[i], LAST)
        logits_ref[i] = logits
        dispatch, combine = softmaxes(logits)
        first.append(dot(dispatch.astype(BF), n_ref[i]).astype(BF))
        second.append(dot(combine.astype(BF), g_ref[i]).astype(BF))
    send_ref[:, :width], send_ref[:, width:] = to_blocks(first, second)


def route(x_img, mixed, out_w, norms, router, g_img):
    images, rows, width = x_img.shape
    experts = router.shape[0]
    return run(
        route_kernel,
        "route",
        (x_img, mixed, out_w, norms, router, g_img),
        (
            shape_of((images, rows, width), F32),
            shape_of((images, rows, width), BF),
            shape_of((images, experts, rows), F32),
            shape_of((experts * BLOCK, width + width // 2), BF),
        ),
        5,
    )


def chosen(rows, low, high, shift):
    shape = (rows, rows)
    place = jnp.bitwise_and(row_ids(shape), BLOCK - 1)
    inside = jnp.logical_and(place >= low, place < high)
    return jnp.logical_and(inside, lane_ids(shape) == row_ids(shape) + shift).astype(BF)


def split_rows(blocks):
    rows, lanes = blocks.shape
    width = lanes // 3 * 2
    half = width // 2
    place = jnp.bitwise_and(row_ids((rows, width)), BLOCK - 1)
    first = jnp.where(place < 6, blocks[:, :width], jnp.zeros((rows, width), BF))
    second = dot(chosen(rows, 0, 2, 6), blocks[:, :width])
    left = second[:, :half] + dot(chosen(rows, 2, 6, -2), blocks[:, width:])
    right = second[:, half:] + dot(chosen(rows, 2, 6, 2), blocks[:, width:])
    return first, jnp.concatenate([left, right], axis=1).astype(BF)


def join_rows(first, second):
    rows, width = first.shape
    half = width // 2
    place = jnp.bitwise_and(row_ids((rows, width)), BLOCK - 1)
    second = second.astype(BF)
    head = jnp.where(place < 6, first, dot(chosen(rows, 6, 8, -6), second))
    rest = dot(chosen(rows, 0, 4, 2), second[:, :half]) + dot(chosen(rows, 4, 8, -2), second[:, half:])
    return head.astype(BF), rest.astype(BF)


def gelu_parts(pre):
    cdf = 0.5 * (1.0 + lax.erf(pre * (0.5**0.5)))
    density = jnp.exp(-0.5 * pre * pre) * 0.3989422804014327
    return pre * cdf, cdf + pre * density


def expert_kernel(a_ref, b_ref, c_ref, d_ref, w1_ref, w2_ref, *refs):
    outs, (slots_ref, grads_ref, hidden_ref, pre_ref) = refs[:4], refs[4:]
    width = w1_ref.shape[0]
    count = a_ref.shape[0]
    blocks = jnp.concatenate([a_ref[...], b_ref[...], c_ref[...], d_ref[...]], axis=0)
    step = min(4 * count, 256)
    for at in range(0, 4 * count, step):
        slots_ref[at : at + step], grads_ref[at : at + step] = split_rows(blocks[at : at + step])
    slots, grads = slots_ref[...], grads_ref[...]
    pre = dot(slots, w1_ref[...])
    hidden, slope = gelu_parts(pre)
    hidden = hidden.astype(BF)
    returned = dot(hidden, w2_ref[...])
    grad_pre = (dot(grads, w2_ref[...], LAST) * slope).astype(BF)
    grad_slots = dot(grad_pre, w1_ref[...], LAST)
    parts = [join_rows(returned[at : at + step], grad_slots[at : at + step]) for at in range(0, 4 * count, step)]
    head, rest = (jnp.concatenate(p, axis=0) for p in zip(*parts, strict=True))
    for i, ref in enumerate(outs):
        ref[:, :width] = head[i * count : (i + 1) * count]
        ref[:, width:] = rest[i * count : (i + 1) * count]
    hidden_ref[...] = hidden
    pre_ref[...] = grad_pre


def run_expert(own, near, first_weight, second_weight):
    width, units = first_weight.shape
    rows = 4 * own[0].shape[0]
    return run(
        expert_kernel,
        "expert",
        own + near + (first_weight, second_weight),
        (shape_of(own[0].shape, BF),) * 4
        + (
            shape_of((rows, width), BF),
            shape_of((rows, width), BF),
            shape_of((rows, units), BF),
            shape_of((rows, units), BF),
        ),
        8 if rows <= 512 else 48,
    )


def expert_grad_kernel(slots_ref, grads_ref, hidden_ref, pre_ref, d1_ref, d2_ref):
    d1_ref[...] = dot(slots_ref[...], pre_ref[...], FIRST)
    d2_ref[...] = dot(hidden_ref[...], grads_ref[...], FIRST)


def expert_grads(slots, grads, hidden, grad_pre):
    rows, width = slots.shape
    units = hidden.shape[1]
    return run(
        expert_grad_kernel,
        "expert_grads",
        (slots, grads, hidden, grad_pre),
        (shape_of((width, units), F32), shape_of((units, width), F32)),
        16 if rows <= 512 else 32,
    )


def moe_ready_kernel(y_ref, logits_ref, unit_ref, inv_ref, dispatch_ref, combine_ref):
    unit, inv_std = layer_stats(flat(y_ref))
    unit_ref[...] = unit.reshape(unit_ref.shape)
    inv_ref[...] = inv_std.reshape(inv_ref.shape)
    for i in range(y_ref.shape[0]):
        dispatch_ref[i], combine_ref[i] = softmaxes(logits_ref[i])


def moe_ready(y, logits):
    images, rows, width = y.shape
    return run(
        moe_ready_kernel,
        "moe_ready",
        (y, logits),
        (
            shape_of((images, rows, width), F32),
            shape_of((images, rows, 1), F32),
            shape_of(logits.shape, F32),
            shape_of(logits.shape, F32),
        ),
        5,
    )


def moe_back_kernel(
    unit_ref,
    inv_ref,
    dispatch_ref,
    combine_ref,
    n_ref,
    g_ref,
    back_ref,
    norms_ref,
    router_ref,
    out_w_ref,
    mixed_ref,
    grad_y_ref,
    grad_mixed_ref,
    out_grad_ref,
    small_ref,
    attn_ref,
):
    images, rows, width = unit_ref.shape
    experts = router_ref.shape[0]
    gain = norms_ref[2:3, :]
    all_returned, all_slots = from_blocks(back_ref[...], experts, width)
    router_grad, gain_grad, shift_grad = 0.0, 0.0, 0.0
    for i in range(images):
        returned, grad_slots = all_returned[i], all_slots[i]
        dispatch, combine = dispatch_ref[i], combine_ref[i]
        grad_combine = dot(returned, g_ref[i], LAST)
        grad_dispatch = dot(grad_slots, n_ref[i], LAST)
        grad_logits = dispatch * (
            grad_dispatch - jnp.sum(grad_dispatch * dispatch, axis=1, keepdims=True)
        ) + combine * (grad_combine - jnp.sum(grad_combine * combine, axis=0, keepdims=True))
        grad_logits = grad_logits.astype(BF)
        router_grad = router_grad + dot(grad_logits, n_ref[i])
        grad_two = dot(
            jnp.concatenate([dispatch.astype(BF), grad_logits], axis=0),
            jnp.concatenate([grad_slots, router_ref[...]], axis=0),
            FIRST,
        )
        unit, inv_std = unit_ref[i], inv_ref[i]
        gain_grad = gain_grad + jnp.sum(grad_two * unit, axis=0, keepdims=True)
        shift_grad = shift_grad + jnp.sum(grad_two, axis=0, keepdims=True)
        scaled = grad_two * gain
        mean_one = jnp.mean(scaled, axis=-1, keepdims=True)
        mean_two = jnp.mean(scaled * unit, axis=-1, keepdims=True)
        grad_y = g_ref[i].astype(F32) + inv_std * (scaled - mean_one - unit * mean_two)
        grad_y_ref[i] = grad_y
        attn_ref[i] = grad_y.astype(BF)
    small_ref[...] = jnp.zeros_like(small_ref)
    small_ref[0:1, :] = gain_grad
    small_ref[1:2, :] = shift_grad
    small_ref[8 : 8 + experts, :] = router_grad
    grad_attn = flat(attn_ref)
    grad_mixed_ref[...] = dot(grad_attn, out_w_ref[...]).astype(BF).reshape(grad_mixed_ref.shape)
    out_grad_ref[...] = dot(grad_attn, flat(mixed_ref), FIRST).astype(out_grad_ref.dtype)


def moe_back(ready, normed, g_img, back, norms, router, out_w, mixed, dtype):
    images, rows, width = normed.shape
    experts = router.shape[0]
    return run(
        moe_back_kernel,
        "moe_back",
        ready + (normed, g_img, back, norms, router, out_w, mixed),
        (
            shape_of((images, rows, width), F32),
            shape_of((images, rows, width), BF),
            shape_of((width, width), dtype),
            shape_of((8 + experts, width), F32),
        ),
        10,
        scratch=[pltpu.VMEM((images, rows, width), BF)],
    )


def output_kernel(y_ref, logits_ref, back_ref, out_ref, wide):
    images, experts, _ = logits_ref.shape
    all_returned, _ = from_blocks(back_ref[...], experts, y_ref.shape[2])
    for i in range(images):
        returned = all_returned[i]
        _, combine = softmaxes(logits_ref[i])
        total = y_ref[i] + dot(combine.astype(BF), returned, FIRST)
        wide[SEQ * i : SEQ * (i + 1), :] = total[0:SEQ]
    out_ref[...] = wide[...].astype(BF)


def block_output(y, logits, back):
    images, rows, width = y.shape
    count = images * SEQ
    return run(
        output_kernel,
        "block_output",
        (y, logits, back),
        (shape_of((count, width), BF),),
        12,
        scratch=[pltpu.VMEM((count, width), F32)],
    )[0]


def deal_rows(owners, full_ref, first, kinds, refs, columns):
    for side, (owner, ref) in enumerate(zip(owners, refs, strict=True)):
        blocks, count, _ = ref.shape
        for p in range(blocks):
            row = pl.multiple_of(count * owner[p], 16)
            for at, kind in enumerate(kinds):
                lane = first + (2 * at + side) * columns
                ref[p, :, kind * columns : (kind + 1) * columns] = full_ref[pl.ds(row, count), lane : lane + columns]


def attend_back_kernel(stepwise, piece, *refs):
    if stepwise:
        owners, refs = refs[:2], refs[2:]
        n_ref, qkv_ref, probs_ref, mixed_ref, gm_ref, og_ref, grads_ref, own_ref, sib_ref, dw_ref = refs
    else:
        n_ref, qkv_ref, probs_ref, mixed_ref, gm_ref, grads_ref, dw_ref = refs
    images, rows, width = mixed_ref.shape
    span = width // 2
    low = lane_ids((rows, 128)) < HEAD_DIM
    zero = jnp.zeros((rows, 128), BF)
    minus = jnp.full((rows, 128), -1.0, BF)

    def image(i, carry):
        for p in range(span // 128):
            at = slice(p * 128, (p + 1) * 128)
            at_k = slice(span + p * 128, span + (p + 1) * 128)
            at_v = slice(2 * span + p * 128, 2 * span + (p + 1) * 128)
            q, k, v = qkv_ref[i, :, at], qkv_ref[i, :, at_k], qkv_ref[i, :, at_v]
            here = slice(piece * span + p * 128, piece * span + (p + 1) * 128)
            gm = gm_ref[i, :, here]
            inner = pltpu.roll(gm.astype(F32) * mixed_ref[i, :, here].astype(F32), HEAD_DIM, 1).astype(BF)
            grad_q, grad_k, grad_v = 0.0, 0.0, 0.0
            for h in range(2):
                mine = low if h == 0 else jnp.logical_not(low)
                weights = probs_ref[i, 2 * p + h]
                centred = dot(jnp.where(mine, v, minus), jnp.where(mine, gm, inner), LAST)
                grad_scores = (weights.astype(F32) * centred).astype(BF)
                grad_v = grad_v + dot(weights, jnp.where(mine, gm, zero))
                grad_k = grad_k + dot(grad_scores, jnp.where(mine, q, zero))
                grad_q = grad_q + dot(grad_scores, jnp.where(mine, k, zero), FIRST)
            grads_ref[i, :, at] = (grad_q * HEAD_DIM ** (-0.5)).astype(BF)
            grads_ref[i, :, at_k] = grad_k.astype(BF)
            grads_ref[i, :, at_v] = grad_v.astype(BF)
        return carry

    lax.fori_loop(0, images, image, 0, unroll=images)
    dw_ref[...] = dot(flat(n_ref), flat(grads_ref), FIRST).astype(dw_ref.dtype)
    if stepwise:
        deal_rows(owners, dw_ref, 0, range(3), (own_ref, sib_ref), span // 2)
        deal_rows(owners, og_ref, piece * span, [3], (own_ref, sib_ref), span // 2)


def attend_back(normed, qkv, probs, mixed, grad_mixed, out_grad_t, piece, owners, sizes):
    images, rows, width = normed.shape
    span = width // 2
    operands = (normed, qkv, probs, mixed, grad_mixed)
    results = (shape_of((images, rows, 3 * span), BF),)
    scratch = ()
    if owners:
        operands += (out_grad_t,)
        results += (shape_of((sizes[0], width // sizes[0], 2 * span), BF),) * 2
        scratch = (pltpu.VMEM((width, 3 * span), BF),)
    else:
        results += (shape_of((width, 3 * span), F32),)
    return run(
        functools.partial(attend_back_kernel, bool(owners), piece),
        "attend_back",
        owners + operands,
        results,
        7,
        scratch,
        scalars=len(owners),
    )


def input_part_kernel(p_ref, w_ref, out_ref):
    out_ref[...] = dot(flat(p_ref), w_ref[...], LAST).reshape(out_ref.shape)


def input_part(grads, weight):
    images, rows, _ = grads.shape
    return run(
        input_part_kernel, "input_part", (grads, weight), (shape_of((images, rows, weight.shape[0]), F32),), 16
    )[0]


def input_sum_kernel(x_ref, p1_ref, part_ref, w1_ref, grad_ref, small_ref):
    images, rows, width = x_ref.shape
    grad_ref[...] = (dot(flat(p1_ref), w1_ref[...], LAST) + flat(part_ref)).reshape(grad_ref.shape)
    gain_grad, shift_grad = 0.0, 0.0
    for i in range(images):
        unit, _ = layer_stats(x_ref[i].astype(F32))
        gain_grad = gain_grad + jnp.sum(grad_ref[i] * unit, axis=0, keepdims=True)
        shift_grad = shift_grad + jnp.sum(grad_ref[i], axis=0, keepdims=True)
    small_ref[...] = jnp.zeros_like(small_ref)
    small_ref[0:1, :] = gain_grad
    small_ref[1:2, :] = shift_grad


def input_sum(x_img, grads_one, grad_part, weight_one):
    width = x_img.shape[2]
    return run(
        input_sum_kernel,
        "input_sum",
        (x_img, grads_one, grad_part, weight_one),
        (shape_of(x_img.shape, F32), shape_of((8, width), F32)),
        8,
    )


def input_back_kernel(x_ref, gy_ref, grad_ref, norms_ref, out_ref):
    gain = norms_ref[0:1, :]
    for i in range(x_ref.shape[0]):
        unit, inv_std = layer_stats(x_ref[i].astype(F32))
        scaled = grad_ref[i] * gain
        mean_one = jnp.mean(scaled, axis=-1, keepdims=True)
        mean_two = jnp.mean(scaled * unit, axis=-1, keepdims=True)
        total = gy_ref[i] + inv_std * (scaled - mean_one - unit * mean_two)
        out_ref[SEQ * i : SEQ * (i + 1), :] = total[0:SEQ]


def input_back(x_img, grad_y, grad_one, norms):
    images, _, width = x_img.shape
    return run(
        input_back_kernel,
        "input_back",
        (x_img, grad_y, grad_one, norms),
        (shape_of((images * SEQ, width), F32),),
        8,
    )[0]


def spot(shape, start):
    return (lane_ids(shape) == row_ids(shape) + start).astype(BF)


def place_kernel(index_ref, norm_ref, router_ref, small_ref):
    rows, columns = norm_ref.shape[1], router_ref.shape[1]
    width = small_ref.shape[1]
    dp_index, tensor_index = index_ref[0], index_ref[1]
    norm = dot(jnp.broadcast_to(norm_ref[...], (16, rows)), spot((rows, width), dp_index * rows))
    router = dot(jnp.broadcast_to(router_ref[...], (16, columns)), spot((columns, width), tensor_index * columns))
    row = row_ids(small_ref.shape)
    small_ref[...] = jnp.where(
        row == tensor_index, norm[0:1], jnp.where(row == width // columns + dp_index, router[0:1], 0.0)
    ).astype(BF)


def place(index, norm_params, router, experts):
    rows, columns = norm_params.shape[1], router.shape[0]
    width = rows * experts
    return run(
        place_kernel,
        "place",
        (index, norm_params, router.T),
        (shape_of((-(-(width // columns + experts) // 16) * 16, width), BF),),
        4,
        scalars=1,
    )[0]


def pack_kernel(qkv_ref, out_ref, block_ref):
    kinds, _, columns = qkv_ref.shape
    for kind in range(kinds):
        block_ref[:, kind * columns : (kind + 1) * columns] = qkv_ref[kind]
    block_ref[:, kinds * columns :] = out_ref[...].T


def pack(qkv_weight, out_weight):
    kinds, rows, columns = qkv_weight.shape
    return run(
        pack_kernel,
        "pack",
        (qkv_weight, out_weight),
        (shape_of((rows, (kinds + 1) * columns), BF),),
        4,
    )[0]


def unpack_kernel(index_ref, own_ref, got_ref, near_ref, corner_ref, qkv_ref, out_ref, norm_ref, router_ref):
    kinds, rows, columns = qkv_ref.shape
    total = own_ref[...].astype(F32) + got_ref[...].astype(F32)
    for kind in range(kinds):
        qkv_ref[kind] = total[0:rows, kind * columns : (kind + 1) * columns]
    out_ref[...] = total[0:rows, kinds * columns :].T
    small = total[rows:] + near_ref[...].astype(F32) + corner_ref[...].astype(F32)
    dp_index, tensor_index = index_ref[0], index_ref[1]
    width = small.shape[1]
    row = row_ids(small.shape)
    norm = jnp.sum(jnp.where(row == tensor_index, small, 0.0), axis=0, keepdims=True)
    router = jnp.sum(jnp.where(row == width // columns + dp_index, small, 0.0), axis=0, keepdims=True)
    norm_out, router_out = 0.0, 0.0
    for _ in range(2):
        part = norm.astype(BF)
        norm = norm - part.astype(F32)
        norm_out = norm_out + dot(
            jnp.broadcast_to(part, (16, width)), spot((rows, width), dp_index * rows), LAST
        )
        part = router.astype(BF)
        router = router - part.astype(F32)
        router_out = router_out + dot(
            jnp.broadcast_to(part, (16, width)), spot((columns, width), tensor_index * columns), LAST
        )
    norm_ref[...] = norm_out[0:1]
    router_ref[...] = router_out[0:1]


def unpack(index, own, got, near, corner, sizes):
    width = own.shape[1]
    rows, columns = width // sizes[0], width // sizes[1]
    return run(
        unpack_kernel,
        "unpack",
        (index, own, got, near, corner),
        (
            shape_of((width // columns - 1, rows, columns), F32),
            shape_of((columns, rows), F32),
            shape_of((1, rows), F32),
            shape_of((1, columns), F32),
        ),
        4,
        scalars=1,
    )


def swap(value, dp_size, tensor_size, dp_mask, tensor_mask):
    pairs = [
        (d * tensor_size + t, (d ^ dp_mask) * tensor_size + (t ^ tensor_mask))
        for d in range(dp_size)
        for t in range(tensor_size)
    ]
    return lax.ppermute(value, AXES, pairs)


def steps_of(dp_size):
    bits = dp_size.bit_length() - 1
    down = list(range(bits))[::-1]
    return [down, down[-1:] + down[:-1]]


def step_pairs(dp_size, tensor_size, *steps):
    masks = [functools.reduce(lambda mask, step: mask ^ (1 << order[step]), steps, 0) for order in steps_of(dp_size)]
    return [
        (d * tensor_size + t, (d ^ masks[t % 2]) * tensor_size + t)
        for d in range(dp_size)
        for t in range(tensor_size)
    ]


def owners_of(dp_size, dp_index, core):
    both = []
    for order in steps_of(dp_size):
        place = jnp.arange(dp_size, dtype=jnp.int32)
        away = jnp.zeros_like(place)
        for step, bit in enumerate(order):
            away = away | (((place >> step) & 1) << bit)
        both.append(away ^ dp_index)
    return jnp.where(core == 0, both[0], both[1]), jnp.where(core == 0, both[1], both[0])


def exchange(blocks, dp_size):
    shape = blocks.shape
    blocks = blocks.reshape(dp_size, shape[0] // dp_size, shape[1])
    return lax.all_to_all(blocks, "dp", split_axis=0, concat_axis=0, tiled=True).reshape(shape)


def together(*values):
    return lax.optimization_barrier(values)


def send(value, sizes, *steps):
    return lax.ppermute(value, AXES, step_pairs(*sizes, *steps))


def across_core(value, sizes):
    return swap(value, *sizes, 0, 1)


def across_core_after(value, sizes, step):
    pairs = [(a, b ^ 1) for a, b in step_pairs(*sizes, step)]
    return lax.ppermute(value, AXES, pairs)


def across_high(value, sizes, *steps):
    pairs = [(a, b ^ 2) for a, b in step_pairs(*sizes, *steps)]
    return lax.ppermute(value, AXES, pairs)


def gather_first(block, small, sizes, along):
    rows = block.shape[0]
    small_high, block = together(across_high(small, sizes), block)
    small = small + small_high
    small = small + across_core(small, sizes)
    first = jnp.concatenate([block, small], axis=0)
    got, high = together(send(first, sizes, 0), across_high(block, sizes))
    held = jnp.concatenate([block, got[:rows], small + got[rows:]], axis=0)

    got, near, high_got = together(send(held, sizes, 1), across_core(held, sizes), across_high(got[:rows], sizes))
    high = jnp.concatenate([high, high_got], axis=0)
    small = held[2 * rows :] + got[2 * rows :]
    four = jnp.concatenate([held[: 2 * rows], got[: 2 * rows], small], axis=0)

    last, near_two, high_two, high_near, along = together(
        send(four, sizes, 2), across_core(got, sizes), across_high(got[: 2 * rows], sizes), across_core(high, sizes), prepare(*along)
    )
    small = four[4 * rows :] + last[4 * rows :]
    own = (four, last), (near, near_two, across_core(last, sizes))
    high = jnp.concatenate([high, high_two], axis=0)
    return own, (high, high_near, across_core(high_two, sizes)), small, along


def gather_weights_plain(qkv_weight, out_weight, router, norm_params):
    qkv = lax.all_gather(qkv_weight, "dp", axis=1, tiled=True)
    qkv = lax.all_gather(qkv, "tensor", axis=2, tiled=True)
    out_w, router, norms = (
        lax.all_gather(lax.all_gather(w, "dp", axis=1, tiled=True), "tensor", axis=0, tiled=True)
        for w in (out_weight, router, norm_params)
    )
    width = qkv.shape[1]
    half = width // 2
    one = qkv[:, :, :half].transpose(1, 0, 2).reshape(width, 3 * half)
    two = qkv[:, :, half:].transpose(1, 0, 2).reshape(width, 3 * half)
    return one, two, out_w.T, norms.astype(F32), router.T


def add_low(*values):
    return sum(v.astype(F32) for v in values).astype(BF)


def sum_small(values, sizes):
    dp_size, tensor_size = sizes
    mask = 1
    while mask < tensor_size:
        values = values + swap(values, dp_size, tensor_size, 0, mask)
        mask *= 2
    mask = 1
    while mask < dp_size:
        values = values + swap(values, dp_size, tensor_size, mask, 0)
        mask *= 2
    return values


def on_device(
    sizes, tokens, qkv_weight, out_weight, router, norm_params, expert_in, expert_out, cotangent
):
    dp_size, tensor_size = sizes
    dp_index = lax.axis_index("dp")
    tensor_index = lax.axis_index("tensor")
    core = jnp.bitwise_and(tensor_index, 1)
    width = tokens.shape[1]
    half = width // 2
    rows = qkv_weight.shape[1]
    columns = qkv_weight.shape[2]
    experts = dp_size * router.shape[1]
    stepwise = rows % 16 == 0 and sizes == (8, 4)
    owners = ()
    if stepwise:
        owners = owners_of(dp_size, dp_index, core)
        index = jnp.stack([dp_index, tensor_index]).astype(jnp.int32)
        *owners, index, qkv_weight, out_weight, norm_params, router = together(
            *owners, index, qkv_weight, out_weight, norm_params, router
        )
        owners = tuple(owners)
        small = place(index, norm_params, router, experts)
        block = pack(qkv_weight, out_weight)
        (own, near), high, small, (x_img, g_img, unit) = gather_first(block, small, sizes, (tokens, cotangent))
        norms, router_t = small[:tensor_size].astype(F32), small[tensor_size : tensor_size + experts]
        high, near_first, near_second = high
        last_high = send(high, sizes, 2)
        normed, qkv_one, mixed, probs_one, weight_one, out_w = attend_first(unit, norms, owners, (own, near))
        last_high, near_second, normed = together(last_high, near_second, normed)
        parts = (high, last_high), (near_first, near_second, across_core(last_high, sizes))
        mixed, out_w, qkv_two, probs_two, weight_two = attend_second(normed, mixed, out_w, owners, parts)
    else:
        x_img, g_img, unit = prepare(tokens, cotangent)
        weight_one, weight_two, out_w, norms, router_t = gather_weights_plain(
            qkv_weight, out_weight, router, norm_params
        )
        normed, qkv_one, mixed, probs_one = attend_first(unit, norms, (), (weight_one,))
        mixed, qkv_two, probs_two = attend_second(normed, mixed, None, (), (weight_two,))
    y, normed_two, logits, outgoing = route(x_img, mixed, out_w, norms, router_t, g_img)

    arrived = exchange(outgoing, dp_size)
    across = across_high(arrived, sizes)
    near = across_core(arrived, sizes)
    across, near, ready = lax.optimization_barrier((across, near, tuple(moe_ready(y, logits))))
    keep, keep_high, away, away_high, *kept = run_expert(
        (arrived, across), (near, across_core(across, sizes)), expert_in[0], expert_out[0]
    )
    got = across_high(add_low(keep_high, across_core(away_high, sizes)), sizes)
    got, near = lax.optimization_barrier((got, across_core(away, sizes)))
    back = exchange(add_low(keep, near, got), dp_size)

    grad_y, grad_mixed, out_grad_t, small_two = moe_back(
        ready, normed_two, g_img, back, norms, router_t, out_w, mixed, BF if stepwise else F32
    )
    grads_two, *dealt_two = attend_back(
        normed, qkv_two, probs_two, mixed, grad_mixed, out_grad_t, 1, owners, sizes
    )
    grad_part = input_part(grads_two, weight_two)
    if stepwise:
        mine = dealt_two[0].reshape(width, width)
        got, grad_part = together(across_core(dealt_two[1].reshape(width, width), sizes), grad_part)
        cut = [rows * place for place in range(9)]
        low, along = add_low(mine[: cut[3]], got[: cut[3]]), add_low(mine[cut[4] : cut[7]], got[cut[4] : cut[7]])
        across = [add_low(mine[at : at + rows], got[at : at + rows]) for at in (cut[3], cut[7])]
        low, along, across, grad_mixed = together(low, along, jnp.concatenate(across, axis=0), grad_mixed)
        along, across = send(along, sizes, 2), across_high(across, sizes)
    grads_one, *dealt_one = attend_back(
        normed, qkv_one, probs_one, mixed, grad_mixed, out_grad_t, 0, owners, sizes
    )
    if stepwise:
        along, across, mine, sent, grads_one = together(along, across, *dealt_one, grads_one)
        mine, sent = mine.reshape(width, width), sent.reshape(width, width)
        got = across_core(sent[cut[4] :], sizes)
        high = [
            add_low(mine[cut[4] : cut[7]], got[: cut[3]]),
            add_low(mine[cut[7] :], got[cut[3] :], across[rows:]),
        ]
        low = add_low(low, along)
        high, low, grads_one, sent = together(jnp.concatenate(high, axis=0), low, grads_one, sent)
        got, got_high, near = send(high, sizes, 2), across_high(low, sizes), across_core(sent[: cut[4]], sizes)
    grad_one, small_one = input_sum(x_img, grads_one, grad_part, weight_one)
    small = jnp.concatenate([small_one[0:2], small_two[0:2], small_two[8:]], axis=0)
    if stepwise:
        near, small = together(near, small)
        small = jnp.pad(small.astype(BF), ((0, -small.shape[0] % 16), (0, 0)))
        smalls = across_high(small, sizes), send(small, sizes, 2), across_high(small, sizes, 2)
        got, got_high, near, smalls = together(got, got_high, near, smalls)
        small = add_low(small, *smalls)
        held = mine[: cut[4]], near, got
        low = add_low(*(h[: cut[2]] for h in held), got_high[: cut[2]])
        high = [
            add_low(*(h[cut[2] : cut[3]] for h in held), got_high[cut[2] :]),
            add_low(*(h[cut[3] : cut[4]] for h in held), across[:rows]),
            small,
        ]
        low, high, grad_one = together(low, jnp.concatenate(high, axis=0), grad_one)
    input_grad = input_back(x_img, grad_y, grad_one, norms)
    output = block_output(y, logits, back)
    first_grad, second_grad = expert_grads(*kept)
    if stepwise:
        got, output, input_grad = together(send(high, sizes, 1), output, input_grad)
        low = add_low(low, got[: cut[2]])
        small = add_low(small, got[cut[2] :])
        near, corner = across_core(small, sizes), across_core_after(small, sizes, 0)
        got, first_grad, second_grad, near, corner = together(
            send(jnp.concatenate([low[rows:], small], axis=0), sizes, 0), first_grad, second_grad, near, corner
        )
        low = jnp.concatenate([low[:rows], small], axis=0)
        qkv_grad, out_grad, norm_grad, router_grad = unpack(index, low, got, near, corner, sizes)
        router_grad = router_grad.reshape(columns, 1)
    else:
        small = sum_small(small, sizes)
        full = jnp.concatenate(
            [dealt_one[0].reshape(width, 3, half), dealt_two[0].reshape(width, 3, half)], axis=2
        ).transpose(1, 0, 2)
        qkv_grad = lax.psum_scatter(full, "dp", scatter_dimension=1, tiled=True)
        qkv_grad = lax.psum_scatter(qkv_grad, "tensor", scatter_dimension=2, tiled=True)
        out_grad = lax.psum_scatter(out_grad_t.T, "dp", scatter_dimension=1, tiled=True)
        out_grad = lax.psum_scatter(out_grad, "tensor", scatter_dimension=0, tiled=True)
        norm_grad = lax.dynamic_slice(small, (tensor_index, dp_index * rows), (1, rows))
        router_grad = lax.dynamic_slice(
            small, (tensor_size + dp_index, tensor_index * columns), (1, columns)
        ).reshape(columns, 1)
    return (
        output,
        input_grad,
        qkv_grad,
        out_grad,
        router_grad,
        norm_grad,
        first_grad[None],
        second_grad[None],
    )


def solution(mesh):
    sizes = (mesh.shape["dp"], mesh.shape["tensor"])
    return jax.shard_map(
        functools.partial(on_device, sizes),
        mesh=mesh,
        in_specs=(
            P(("dp", "tensor"), None),
            P(None, "dp", "tensor"),
            P("tensor", "dp"),
            P("tensor", "dp"),
            P("tensor", "dp"),
            P("dp", None, "tensor"),
            P("dp", "tensor", None),
            P(("dp", "tensor"), None),
        ),
        out_specs=(
            P(("dp", "tensor"), None),
            P(("dp", "tensor"), None),
            P(None, "dp", "tensor"),
            P("tensor", "dp"),
            P("tensor", "dp"),
            P("tensor", "dp"),
            P("dp", None, "tensor"),
            P("dp", "tensor", None),
        ),
        check_vma=False,
    )
```

```python
import functools

import jax
import jax.numpy as jnp
from jax import lax
from jax.experimental import pallas as pl
from jax.experimental.pallas import tpu as pltpu
from jax.sharding import PartitionSpec as P

HEAD_DIM = 64
SEQ = 197
PAD = 208
BLOCK = 8
AXES = ("dp", "tensor")
BF = jnp.bfloat16
F32 = jnp.float32
LAST = (((1,), (1,)), ((), ()))
FIRST = (((0,), (0,)), ((), ()))
MIDDLE = (((1,), (0,)), ((), ()))
MIB = 1024 * 1024


def dot(a, b, dims=MIDDLE):
    return lax.dot_general(a, b, dims, preferred_element_type=F32)


def shape_of(shape, dtype):
    return jax.ShapeDtypeStruct(shape, dtype)


def run(kernel, name, operands, results, limit, scratch=(), scalars=0, aliases=()):
    memory = [pltpu.SMEM] * scalars + [pltpu.VMEM] * (len(operands) - scalars)
    return pl.pallas_call(
        kernel,
        in_specs=[pl.BlockSpec(memory_space=m) for m in memory],
        out_specs=[pl.BlockSpec(memory_space=pltpu.VMEM) for _ in results],
        out_shape=list(results),
        scratch_shapes=list(scratch),
        input_output_aliases=dict(aliases),
        compiler_params=pltpu.CompilerParams(vmem_limit_bytes=limit * MIB),
        cost_estimate=pl.CostEstimate(flops=1, bytes_accessed=1, transcendentals=0),
        name=name,
    )(*operands)


def layer_stats(values):
    centre = jnp.mean(values, axis=-1, keepdims=True)
    centred = values - centre
    spread = jnp.mean(centred * centred, axis=-1, keepdims=True)
    inv_std = lax.rsqrt(spread + 1e-06)
    return centred * inv_std, inv_std


def lane_ids(shape):
    return lax.broadcasted_iota(jnp.int32, shape, len(shape) - 1)


def row_ids(shape):
    return lax.broadcasted_iota(jnp.int32, shape, len(shape) - 2)


def flat(ref):
    images, rows, columns = ref.shape
    return ref[...].reshape(images * rows, columns)


def prepare_kernel(x_ref, g_ref, x_out, g_out, unit_out, wide):
    count, width = x_ref.shape
    real = row_ids((PAD, width)) < SEQ
    wide[count:, :] = jnp.zeros((wide.shape[0] - count, width), F32)
    for ref, out in ((x_ref, x_out), (g_ref, g_out)):
        wide[0:count, :] = ref[...].astype(F32)
        for i in range(out.shape[0]):
            rows = jnp.where(real, wide[SEQ * i : SEQ * i + PAD, :], 0.0)
            out[i] = rows.astype(BF)
            if ref is x_ref:
                unit_out[i], _ = layer_stats(rows)


def prepare(tokens, cotangent):
    count, width = tokens.shape
    images = count // SEQ
    rows = shape_of((images, PAD, width), BF)
    return run(
        prepare_kernel,
        "prepare",
        (tokens, cotangent),
        (rows, rows, shape_of((images, PAD, width), F32)),
        9,
        scratch=[pltpu.VMEM((-(-count // 8) * 8 + 16, width), F32)],
    )


def attend_rows(normed, w_ref, qkv_ref, mixed_ref, probs_ref, piece):
    images, rows, width = mixed_ref.shape
    span = width // 2
    low = lane_ids((rows, 128)) < HEAD_DIM
    key_ok = row_ids((rows, rows)) < SEQ
    zero = jnp.zeros((rows, 128), BF)
    proj = dot(normed, w_ref[...])
    qkv_ref[:, :, 0:span] = (proj[:, 0:span] * HEAD_DIM ** (-0.5)).astype(BF).reshape(images, rows, span)
    qkv_ref[:, :, span:] = proj[:, span:].astype(BF).reshape(images, rows, 2 * span)

    def image(i, carry):
        for p in range(span // 128):
            at = slice(p * 128, (p + 1) * 128)
            q = qkv_ref[i, :, at]
            k = qkv_ref[i, :, span + p * 128 : span + (p + 1) * 128]
            v = qkv_ref[i, :, 2 * span + p * 128 : 2 * span + (p + 1) * 128]
            mixed = []
            for h in range(2):
                q_one = jnp.where(low, q, zero) if h == 0 else jnp.where(low, zero, q)
                scores = jnp.where(key_ok, dot(k, q_one, LAST), -1e30)
                scaled = jnp.exp(scores - jnp.max(scores, axis=0, keepdims=True))
                weights = (scaled * (1.0 / jnp.sum(scaled, axis=0, keepdims=True))).astype(BF)
                probs_ref[i, 2 * p + h] = weights
                mixed.append(dot(weights, v, FIRST))
            at = slice(piece * span + p * 128, piece * span + (p + 1) * 128)
            mixed_ref[i, :, at] = jnp.where(low, mixed[0], mixed[1]).astype(BF)
        return carry

    lax.fori_loop(0, images, image, 0, unroll=3 if images % 3 == 0 else 1)


def assemble_rows(owners, parts, kinds, out_ref, columns, lane=0):
    for side, (owner, refs) in enumerate(zip(owners, parts, strict=True)):
        count = out_ref.shape[0] // owner.shape[0]
        blocks = [ref[i * count : (i + 1) * count] for ref in refs for i in range(ref.shape[0] // count)]
        for p, block in enumerate(blocks):
            row = pl.multiple_of(count * owner[p], 16)
            for at, kind in enumerate(kinds):
                to = lane + (2 * at + side) * columns
                out_ref[pl.ds(row, count), to : to + columns] = block[:, kind * columns : (kind + 1) * columns]


def attend_first_kernel(counts, *refs):
    if counts:
        own, sib = counts
        owners, refs = refs[:2], refs[2:]
        unit_ref, norms_ref, refs = refs[0], refs[1], refs[2:]
        parts, refs = (refs[:own], refs[own : own + sib]), refs[own + sib :]
        n_ref, qkv_ref, mixed_ref, probs_ref, w_ref, out_w_ref = refs
        columns = w_ref.shape[1] // 6
        assemble_rows(owners, parts, range(3), w_ref, columns)
        assemble_rows(owners, parts, [3], out_w_ref, columns)
    else:
        unit_ref, norms_ref, w_ref, n_ref, qkv_ref, mixed_ref, probs_ref = refs
    normed = (flat(unit_ref) * norms_ref[0:1, :] + norms_ref[1:2, :]).astype(BF)
    n_ref[...] = normed.reshape(n_ref.shape)
    attend_rows(normed, w_ref, qkv_ref, mixed_ref, probs_ref, 0)


def attend_second_kernel(counts, *refs):
    if counts:
        own, sib = counts
        owners, refs = refs[:2], refs[2:]
        n_ref, refs = refs[0], refs[3:]
        parts, refs = (refs[:own], refs[own : own + sib]), refs[own + sib :]
        mixed_ref, out_w_ref, qkv_ref, probs_ref, w_ref = refs
        columns = w_ref.shape[1] // 6
        assemble_rows(owners, parts, range(3), w_ref, columns)
        assemble_rows(owners, parts, [3], out_w_ref, columns, 2 * columns)
    else:
        n_ref, _, w_ref, mixed_ref, qkv_ref, probs_ref = refs
    attend_rows(flat(n_ref), w_ref, qkv_ref, mixed_ref, probs_ref, 1)


def attend_first(unit, norms, owners, weights):
    images, rows, width = unit.shape
    span = width // 2
    results = (
        shape_of(unit.shape, BF),
        shape_of((images, rows, 3 * span), BF),
        shape_of(unit.shape, BF),
        shape_of((images, span // HEAD_DIM, rows, rows), BF),
    )
    counts = None
    if owners:
        counts = tuple(map(len, weights))
        weights = sum(weights, ())
        results += (shape_of((width, 3 * span), BF), shape_of((width, width), BF))
    return run(
        functools.partial(attend_first_kernel, counts),
        "attend_first",
        owners + (unit, norms) + weights,
        results,
        5,
        scalars=len(owners),
    )


def attend_second(normed, mixed, out_w, owners, weights):
    images, rows, width = normed.shape
    span = width // 2
    given = (mixed, out_w) if owners else (mixed,)
    results = tuple(shape_of(g.shape, BF) for g in given) + (
        shape_of((images, rows, 3 * span), BF),
        shape_of((images, span // HEAD_DIM, rows, rows), BF),
    )
    counts = None
    if owners:
        counts = tuple(map(len, weights))
        weights = sum(weights, ())
        results += (shape_of((width, 3 * span), BF),)
    return run(
        functools.partial(attend_second_kernel, counts),
        "attend_second",
        owners + (normed,) + given + weights,
        results,
        5,
        scalars=len(owners),
        aliases=[(len(owners) + 1 + i, i) for i in range(len(given))],
    )


def softmaxes(logits):
    ok = lane_ids(logits.shape) < SEQ
    masked = jnp.where(ok, logits, -1e30)
    up = jnp.exp(masked - jnp.max(masked, axis=1, keepdims=True))
    dispatch = up / jnp.sum(up, axis=1, keepdims=True)
    up = jnp.exp(logits - jnp.max(logits, axis=0, keepdims=True))
    combine = up / jnp.sum(up, axis=0, keepdims=True)
    return dispatch, combine


def by_image(experts, places, low, back=False):
    shape = (experts * BLOCK, places * experts)
    shape = shape[::-1] if back else shape
    blocked, other = (lane_ids(shape), row_ids(shape)) if back else (row_ids(shape), lane_ids(shape))
    place = jnp.bitwise_and(blocked, BLOCK - 1) - low
    inside = jnp.logical_and(place >= 0, place < places)
    return jnp.logical_and(inside, other == place * experts + lax.div(blocked, BLOCK)).astype(BF)


def to_blocks(first, second):
    experts, width = first[0].shape
    half = width // 2
    head = dot(by_image(experts, BLOCK, 0), jnp.concatenate(first + second[:2], axis=0))
    rest = jnp.concatenate(second[2:], axis=0)
    rest = dot(by_image(experts, 4, 0), rest[:, :half]) + dot(by_image(experts, 4, 4), rest[:, half:])
    return head.astype(BF), rest.astype(BF)


def from_blocks(blocks, experts, width):
    head = dot(by_image(experts, BLOCK, 0, True), blocks[:, :width])
    rest = [dot(by_image(experts, 4, low, True), blocks[:, width:]) for low in (0, 4)]
    rest = jnp.concatenate(rest, axis=1)
    head, rest = ([v[at : at + experts].astype(BF) for at in range(0, v.shape[0], experts)] for v in (head, rest))
    return head[:6], head[6:] + rest


def route_kernel(
    x_ref, mixed_ref, out_w_ref, norms_ref, router_ref, g_ref, y_ref, n_ref, logits_ref, send_ref
):
    images, rows, width = x_ref.shape
    experts = router_ref.shape[0]
    for at in range(0, images, 2):
        some = slice(at, min(at + 2, images))
        y = flat(x_ref.at[some]).astype(F32) + dot(flat(mixed_ref.at[some]), out_w_ref[...], LAST)
        y_ref[some] = y.reshape(-1, rows, width)
        unit, _ = layer_stats(y)
        n_ref[some] = (unit * norms_ref[2:3, :] + norms_ref[3:4, :]).astype(BF).reshape(-1, rows, width)
    first, second = [], []
    for i in range(images):
        logits = dot(router_ref[...], n_ref[i], LAST)
        logits_ref[i] = logits
        dispatch, combine = softmaxes(logits)
        first.append(dot(dispatch.astype(BF), n_ref[i]).astype(BF))
        second.append(dot(combine.astype(BF), g_ref[i]).astype(BF))
    send_ref[:, :width], send_ref[:, width:] = to_blocks(first, second)


def route(x_img, mixed, out_w, norms, router, g_img):
    images, rows, width = x_img.shape
    experts = router.shape[0]
    return run(
        route_kernel,
        "route",
        (x_img, mixed, out_w, norms, router, g_img),
        (
            shape_of((images, rows, width), F32),
            shape_of((images, rows, width), BF),
            shape_of((images, experts, rows), F32),
            shape_of((experts * BLOCK, width + width // 2), BF),
        ),
        5,
    )


def chosen(rows, low, high, shift):
    shape = (rows, rows)
    place = jnp.bitwise_and(row_ids(shape), BLOCK - 1)
    inside = jnp.logical_and(place >= low, place < high)
    return jnp.logical_and(inside, lane_ids(shape) == row_ids(shape) + shift).astype(BF)


def split_rows(blocks):
    rows, lanes = blocks.shape
    width = lanes // 3 * 2
    half = width // 2
    place = jnp.bitwise_and(row_ids((rows, width)), BLOCK - 1)
    first = jnp.where(place < 6, blocks[:, :width], jnp.zeros((rows, width), BF))
    second = dot(chosen(rows, 0, 2, 6), blocks[:, :width])
    left = second[:, :half] + dot(chosen(rows, 2, 6, -2), blocks[:, width:])
    right = second[:, half:] + dot(chosen(rows, 2, 6, 2), blocks[:, width:])
    return first, jnp.concatenate([left, right], axis=1).astype(BF)


def join_rows(first, second):
    rows, width = first.shape
    half = width // 2
    place = jnp.bitwise_and(row_ids((rows, width)), BLOCK - 1)
    second = second.astype(BF)
    head = jnp.where(place < 6, first, dot(chosen(rows, 6, 8, -6), second))
    rest = dot(chosen(rows, 0, 4, 2), second[:, :half]) + dot(chosen(rows, 4, 8, -2), second[:, half:])
    return head.astype(BF), rest.astype(BF)


def gelu_parts(pre):
    cdf = 0.5 * (1.0 + lax.erf(pre * (0.5**0.5)))
    density = jnp.exp(-0.5 * pre * pre) * 0.3989422804014327
    return pre * cdf, cdf + pre * density


def expert_kernel(a_ref, b_ref, c_ref, d_ref, w1_ref, w2_ref, *refs):
    outs, (slots_ref, grads_ref, hidden_ref, pre_ref) = refs[:4], refs[4:]
    width = w1_ref.shape[0]
    count = a_ref.shape[0]
    blocks = jnp.concatenate([a_ref[...], b_ref[...], c_ref[...], d_ref[...]], axis=0)
    step = min(4 * count, 256)
    for at in range(0, 4 * count, step):
        slots_ref[at : at + step], grads_ref[at : at + step] = split_rows(blocks[at : at + step])
    slots, grads = slots_ref[...], grads_ref[...]
    pre = dot(slots, w1_ref[...])
    hidden, slope = gelu_parts(pre)
    hidden = hidden.astype(BF)
    returned = dot(hidden, w2_ref[...])
    grad_pre = (dot(grads, w2_ref[...], LAST) * slope).astype(BF)
    grad_slots = dot(grad_pre, w1_ref[...], LAST)
    parts = [join_rows(returned[at : at + step], grad_slots[at : at + step]) for at in range(0, 4 * count, step)]
    head, rest = (jnp.concatenate(p, axis=0) for p in zip(*parts, strict=True))
    for i, ref in enumerate(outs):
        ref[:, :width] = head[i * count : (i + 1) * count]
        ref[:, width:] = rest[i * count : (i + 1) * count]
    hidden_ref[...] = hidden
    pre_ref[...] = grad_pre


def run_expert(own, near, first_weight, second_weight):
    width, units = first_weight.shape
    rows = 4 * own[0].shape[0]
    return run(
        expert_kernel,
        "expert",
        own + near + (first_weight, second_weight),
        (shape_of(own[0].shape, BF),) * 4
        + (
            shape_of((rows, width), BF),
            shape_of((rows, width), BF),
            shape_of((rows, units), BF),
            shape_of((rows, units), BF),
        ),
        8 if rows <= 512 else 48,
    )


def expert_grad_kernel(slots_ref, grads_ref, hidden_ref, pre_ref, d1_ref, d2_ref):
    d1_ref[...] = dot(slots_ref[...], pre_ref[...], FIRST)
    d2_ref[...] = dot(hidden_ref[...], grads_ref[...], FIRST)


def expert_grads(slots, grads, hidden, grad_pre):
    rows, width = slots.shape
    units = hidden.shape[1]
    return run(
        expert_grad_kernel,
        "expert_grads",
        (slots, grads, hidden, grad_pre),
        (shape_of((width, units), F32), shape_of((units, width), F32)),
        16 if rows <= 512 else 32,
    )


def moe_ready_kernel(y_ref, logits_ref, unit_ref, inv_ref, dispatch_ref, combine_ref):
    unit, inv_std = layer_stats(flat(y_ref))
    unit_ref[...] = unit.reshape(unit_ref.shape)
    inv_ref[...] = inv_std.reshape(inv_ref.shape)
    for i in range(y_ref.shape[0]):
        dispatch_ref[i], combine_ref[i] = softmaxes(logits_ref[i])


def moe_ready(y, logits):
    images, rows, width = y.shape
    return run(
        moe_ready_kernel,
        "moe_ready",
        (y, logits),
        (
            shape_of((images, rows, width), F32),
            shape_of((images, rows, 1), F32),
            shape_of(logits.shape, F32),
            shape_of(logits.shape, F32),
        ),
        5,
    )


def moe_back_kernel(
    unit_ref,
    inv_ref,
    dispatch_ref,
    combine_ref,
    n_ref,
    g_ref,
    back_ref,
    norms_ref,
    router_ref,
    out_w_ref,
    mixed_ref,
    grad_y_ref,
    grad_mixed_ref,
    out_grad_ref,
    small_ref,
    attn_ref,
):
    images, rows, width = unit_ref.shape
    experts = router_ref.shape[0]
    gain = norms_ref[2:3, :]
    all_returned, all_slots = from_blocks(back_ref[...], experts, width)
    router_grad, gain_grad, shift_grad = 0.0, 0.0, 0.0
    for i in range(images):
        returned, grad_slots = all_returned[i], all_slots[i]
        dispatch, combine = dispatch_ref[i], combine_ref[i]
        grad_combine = dot(returned, g_ref[i], LAST)
        grad_dispatch = dot(grad_slots, n_ref[i], LAST)
        grad_logits = dispatch * (
            grad_dispatch - jnp.sum(grad_dispatch * dispatch, axis=1, keepdims=True)
        ) + combine * (grad_combine - jnp.sum(grad_combine * combine, axis=0, keepdims=True))
        grad_logits = grad_logits.astype(BF)
        router_grad = router_grad + dot(grad_logits, n_ref[i])
        grad_two = dot(
            jnp.concatenate([dispatch.astype(BF), grad_logits], axis=0),
            jnp.concatenate([grad_slots, router_ref[...]], axis=0),
            FIRST,
        )
        unit, inv_std = unit_ref[i], inv_ref[i]
        gain_grad = gain_grad + jnp.sum(grad_two * unit, axis=0, keepdims=True)
        shift_grad = shift_grad + jnp.sum(grad_two, axis=0, keepdims=True)
        scaled = grad_two * gain
        mean_one = jnp.mean(scaled, axis=-1, keepdims=True)
        mean_two = jnp.mean(scaled * unit, axis=-1, keepdims=True)
        grad_y = g_ref[i].astype(F32) + inv_std * (scaled - mean_one - unit * mean_two)
        grad_y_ref[i] = grad_y
        attn_ref[i] = grad_y.astype(BF)
    small_ref[...] = jnp.zeros_like(small_ref)
    small_ref[0:1, :] = gain_grad
    small_ref[1:2, :] = shift_grad
    small_ref[8 : 8 + experts, :] = router_grad
    grad_attn = flat(attn_ref)
    grad_mixed_ref[...] = dot(grad_attn, out_w_ref[...]).astype(BF).reshape(grad_mixed_ref.shape)
    out_grad_ref[...] = dot(grad_attn, flat(mixed_ref), FIRST).astype(out_grad_ref.dtype)


def moe_back(ready, normed, g_img, back, norms, router, out_w, mixed, dtype):
    images, rows, width = normed.shape
    experts = router.shape[0]
    return run(
        moe_back_kernel,
        "moe_back",
        ready + (normed, g_img, back, norms, router, out_w, mixed),
        (
            shape_of((images, rows, width), F32),
            shape_of((images, rows, width), BF),
            shape_of((width, width), dtype),
            shape_of((8 + experts, width), F32),
        ),
        10,
        scratch=[pltpu.VMEM((images, rows, width), BF)],
    )


def output_kernel(y_ref, logits_ref, back_ref, out_ref, wide):
    images, experts, _ = logits_ref.shape
    all_returned, _ = from_blocks(back_ref[...], experts, y_ref.shape[2])
    for i in range(images):
        returned = all_returned[i]
        _, combine = softmaxes(logits_ref[i])
        total = y_ref[i] + dot(combine.astype(BF), returned, FIRST)
        wide[SEQ * i : SEQ * (i + 1), :] = total[0:SEQ]
    out_ref[...] = wide[...].astype(BF)


def block_output(y, logits, back):
    images, rows, width = y.shape
    count = images * SEQ
    return run(
        output_kernel,
        "block_output",
        (y, logits, back),
        (shape_of((count, width), BF),),
        12,
        scratch=[pltpu.VMEM((count, width), F32)],
    )[0]


def deal_rows(owners, full_ref, first, kinds, refs, columns):
    for side, (owner, ref) in enumerate(zip(owners, refs, strict=True)):
        blocks, count, _ = ref.shape
        for p in range(blocks):
            row = pl.multiple_of(count * owner[p], 16)
            for at, kind in enumerate(kinds):
                lane = first + (2 * at + side) * columns
                ref[p, :, kind * columns : (kind + 1) * columns] = full_ref[pl.ds(row, count), lane : lane + columns]


def attend_back_kernel(stepwise, piece, *refs):
    if stepwise:
        owners, refs = refs[:2], refs[2:]
        n_ref, qkv_ref, probs_ref, mixed_ref, gm_ref, og_ref, grads_ref, own_ref, sib_ref, dw_ref = refs
    else:
        n_ref, qkv_ref, probs_ref, mixed_ref, gm_ref, grads_ref, dw_ref = refs
    images, rows, width = mixed_ref.shape
    span = width // 2
    low = lane_ids((rows, 128)) < HEAD_DIM
    zero = jnp.zeros((rows, 128), BF)
    minus = jnp.full((rows, 128), -1.0, BF)

    def image(i, carry):
        for p in range(span // 128):
            at = slice(p * 128, (p + 1) * 128)
            at_k = slice(span + p * 128, span + (p + 1) * 128)
            at_v = slice(2 * span + p * 128, 2 * span + (p + 1) * 128)
            q, k, v = qkv_ref[i, :, at], qkv_ref[i, :, at_k], qkv_ref[i, :, at_v]
            here = slice(piece * span + p * 128, piece * span + (p + 1) * 128)
            gm = gm_ref[i, :, here]
            inner = pltpu.roll(gm.astype(F32) * mixed_ref[i, :, here].astype(F32), HEAD_DIM, 1).astype(BF)
            grad_q, grad_k, grad_v = 0.0, 0.0, 0.0
            for h in range(2):
                mine = low if h == 0 else jnp.logical_not(low)
                weights = probs_ref[i, 2 * p + h]
                centred = dot(jnp.where(mine, v, minus), jnp.where(mine, gm, inner), LAST)
                grad_scores = (weights.astype(F32) * centred).astype(BF)
                grad_v = grad_v + dot(weights, jnp.where(mine, gm, zero))
                grad_k = grad_k + dot(grad_scores, jnp.where(mine, q, zero))
                grad_q = grad_q + dot(grad_scores, jnp.where(mine, k, zero), FIRST)
            grads_ref[i, :, at] = (grad_q * HEAD_DIM ** (-0.5)).astype(BF)
            grads_ref[i, :, at_k] = grad_k.astype(BF)
            grads_ref[i, :, at_v] = grad_v.astype(BF)
        return carry

    lax.fori_loop(0, images, image, 0, unroll=images)
    dw_ref[...] = dot(flat(n_ref), flat(grads_ref), FIRST).astype(dw_ref.dtype)
    if stepwise:
        deal_rows(owners, dw_ref, 0, range(3), (own_ref, sib_ref), span // 2)
        deal_rows(owners, og_ref, piece * span, [3], (own_ref, sib_ref), span // 2)


def attend_back(normed, qkv, probs, mixed, grad_mixed, out_grad_t, piece, owners, sizes):
    images, rows, width = normed.shape
    span = width // 2
    operands = (normed, qkv, probs, mixed, grad_mixed)
    results = (shape_of((images, rows, 3 * span), BF),)
    scratch = ()
    if owners:
        operands += (out_grad_t,)
        results += (shape_of((sizes[0], width // sizes[0], 2 * span), BF),) * 2
        scratch = (pltpu.VMEM((width, 3 * span), BF),)
    else:
        results += (shape_of((width, 3 * span), F32),)
    return run(
        functools.partial(attend_back_kernel, bool(owners), piece),
        "attend_back",
        owners + operands,
        results,
        7,
        scratch,
        scalars=len(owners),
    )


def input_part_kernel(p_ref, w_ref, out_ref):
    out_ref[...] = dot(flat(p_ref), w_ref[...], LAST).reshape(out_ref.shape)


def input_part(grads, weight):
    images, rows, _ = grads.shape
    return run(
        input_part_kernel, "input_part", (grads, weight), (shape_of((images, rows, weight.shape[0]), F32),), 16
    )[0]


def input_sum_kernel(x_ref, p1_ref, part_ref, w1_ref, grad_ref, small_ref):
    images, rows, width = x_ref.shape
    gain_grad, shift_grad = 0.0, 0.0
    for i in range(images):
        if i % 2 == 0:
            some = slice(i, min(i + 2, images))
            grad = dot(flat(p1_ref.at[some]), w1_ref[...], LAST) + flat(part_ref.at[some])
            grad_ref[some] = grad.reshape(-1, rows, width)
        unit, _ = layer_stats(x_ref[i].astype(F32))
        gain_grad = gain_grad + jnp.sum(grad_ref[i] * unit, axis=0, keepdims=True)
        shift_grad = shift_grad + jnp.sum(grad_ref[i], axis=0, keepdims=True)
    small_ref[...] = jnp.zeros_like(small_ref)
    small_ref[0:1, :] = gain_grad
    small_ref[1:2, :] = shift_grad


def input_sum(x_img, grads_one, grad_part, weight_one):
    width = x_img.shape[2]
    return run(
        input_sum_kernel,
        "input_sum",
        (x_img, grads_one, grad_part, weight_one),
        (shape_of(x_img.shape, F32), shape_of((8, width), F32)),
        8,
    )


def input_back_kernel(x_ref, gy_ref, grad_ref, norms_ref, out_ref):
    gain = norms_ref[0:1, :]
    for i in range(x_ref.shape[0]):
        unit, inv_std = layer_stats(x_ref[i].astype(F32))
        scaled = grad_ref[i] * gain
        mean_one = jnp.mean(scaled, axis=-1, keepdims=True)
        mean_two = jnp.mean(scaled * unit, axis=-1, keepdims=True)
        total = gy_ref[i] + inv_std * (scaled - mean_one - unit * mean_two)
        out_ref[SEQ * i : SEQ * (i + 1), :] = total[0:SEQ]


def input_back(x_img, grad_y, grad_one, norms):
    images, _, width = x_img.shape
    return run(
        input_back_kernel,
        "input_back",
        (x_img, grad_y, grad_one, norms),
        (shape_of((images * SEQ, width), F32),),
        8,
    )[0]


def spot(shape, start):
    return (lane_ids(shape) == row_ids(shape) + start).astype(BF)


def place_kernel(index_ref, norm_ref, router_ref, small_ref):
    rows, columns = norm_ref.shape[1], router_ref.shape[1]
    width = small_ref.shape[1]
    dp_index, tensor_index = index_ref[0], index_ref[1]
    norm = dot(jnp.broadcast_to(norm_ref[...], (16, rows)), spot((rows, width), dp_index * rows))
    router = dot(jnp.broadcast_to(router_ref[...], (16, columns)), spot((columns, width), tensor_index * columns))
    row = row_ids(small_ref.shape)
    small_ref[...] = jnp.where(
        row == tensor_index, norm[0:1], jnp.where(row == width // columns + dp_index, router[0:1], 0.0)
    ).astype(BF)


def place(index, norm_params, router, experts):
    rows, columns = norm_params.shape[1], router.shape[0]
    width = rows * experts
    return run(
        place_kernel,
        "place",
        (index, norm_params, router.T),
        (shape_of((-(-(width // columns + experts) // 16) * 16, width), BF),),
        4,
        scalars=1,
    )[0]


def pack_kernel(qkv_ref, out_ref, block_ref):
    kinds, _, columns = qkv_ref.shape
    for kind in range(kinds):
        block_ref[:, kind * columns : (kind + 1) * columns] = qkv_ref[kind]
    block_ref[:, kinds * columns :] = out_ref[...].T


def pack(qkv_weight, out_weight):
    kinds, rows, columns = qkv_weight.shape
    return run(
        pack_kernel,
        "pack",
        (qkv_weight, out_weight),
        (shape_of((rows, (kinds + 1) * columns), BF),),
        4,
    )[0]


def unpack_kernel(index_ref, own_ref, got_ref, near_ref, corner_ref, qkv_ref, out_ref, norm_ref, router_ref):
    kinds, rows, columns = qkv_ref.shape
    total = own_ref[...].astype(F32) + got_ref[...].astype(F32)
    for kind in range(kinds):
        qkv_ref[kind] = total[0:rows, kind * columns : (kind + 1) * columns]
    out_ref[...] = total[0:rows, kinds * columns :].T
    small = total[rows:] + near_ref[...].astype(F32) + corner_ref[...].astype(F32)
    dp_index, tensor_index = index_ref[0], index_ref[1]
    width = small.shape[1]
    row = row_ids(small.shape)
    norm = jnp.sum(jnp.where(row == tensor_index, small, 0.0), axis=0, keepdims=True)
    router = jnp.sum(jnp.where(row == width // columns + dp_index, small, 0.0), axis=0, keepdims=True)
    norm_out, router_out = 0.0, 0.0
    for _ in range(2):
        part = norm.astype(BF)
        norm = norm - part.astype(F32)
        norm_out = norm_out + dot(
            jnp.broadcast_to(part, (16, width)), spot((rows, width), dp_index * rows), LAST
        )
        part = router.astype(BF)
        router = router - part.astype(F32)
        router_out = router_out + dot(
            jnp.broadcast_to(part, (16, width)), spot((columns, width), tensor_index * columns), LAST
        )
    norm_ref[...] = norm_out[0:1]
    router_ref[...] = router_out[0:1]


def unpack(index, own, got, near, corner, sizes):
    width = own.shape[1]
    rows, columns = width // sizes[0], width // sizes[1]
    return run(
        unpack_kernel,
        "unpack",
        (index, own, got, near, corner),
        (
            shape_of((width // columns - 1, rows, columns), F32),
            shape_of((columns, rows), F32),
            shape_of((1, rows), F32),
            shape_of((1, columns), F32),
        ),
        4,
        scalars=1,
    )


def swap(value, dp_size, tensor_size, dp_mask, tensor_mask):
    pairs = [
        (d * tensor_size + t, (d ^ dp_mask) * tensor_size + (t ^ tensor_mask))
        for d in range(dp_size)
        for t in range(tensor_size)
    ]
    return lax.ppermute(value, AXES, pairs)


def steps_of(dp_size):
    bits = dp_size.bit_length() - 1
    down = list(range(bits))[::-1]
    return [down, down[-1:] + down[:-1]]


def step_pairs(dp_size, tensor_size, *steps):
    masks = [functools.reduce(lambda mask, step: mask ^ (1 << order[step]), steps, 0) for order in steps_of(dp_size)]
    return [
        (d * tensor_size + t, (d ^ masks[t % 2]) * tensor_size + t)
        for d in range(dp_size)
        for t in range(tensor_size)
    ]


def owners_of(dp_size, dp_index, core):
    both = []
    for order in steps_of(dp_size):
        place = jnp.arange(dp_size, dtype=jnp.int32)
        away = jnp.zeros_like(place)
        for step, bit in enumerate(order):
            away = away | (((place >> step) & 1) << bit)
        both.append(away ^ dp_index)
    return jnp.where(core == 0, both[0], both[1]), jnp.where(core == 0, both[1], both[0])


def exchange(blocks, dp_size):
    shape = blocks.shape
    blocks = blocks.reshape(dp_size, shape[0] // dp_size, shape[1])
    return lax.all_to_all(blocks, "dp", split_axis=0, concat_axis=0, tiled=True).reshape(shape)


def together(*values):
    return lax.optimization_barrier(values)


def send(value, sizes, *steps):
    return lax.ppermute(value, AXES, step_pairs(*sizes, *steps))


def across_core(value, sizes):
    return swap(value, *sizes, 0, 1)


def across_core_after(value, sizes, step):
    pairs = [(a, b ^ 1) for a, b in step_pairs(*sizes, step)]
    return lax.ppermute(value, AXES, pairs)


def across_high(value, sizes, *steps):
    pairs = [(a, b ^ 2) for a, b in step_pairs(*sizes, *steps)]
    return lax.ppermute(value, AXES, pairs)


def gather_first(block, small, sizes, along):
    rows = block.shape[0]
    small_high, block = together(across_high(small, sizes), block)
    small = small + small_high
    small = small + across_core(small, sizes)
    first = jnp.concatenate([block, small], axis=0)
    got, high = together(send(first, sizes, 0), across_high(block, sizes))
    held = jnp.concatenate([block, got[:rows], small + got[rows:]], axis=0)

    got, near, high_got = together(send(held, sizes, 1), across_core(held, sizes), across_high(got[:rows], sizes))
    high = jnp.concatenate([high, high_got], axis=0)
    small = held[2 * rows :] + got[2 * rows :]
    four = jnp.concatenate([held[: 2 * rows], got[: 2 * rows], small], axis=0)

    last, near_two, high_two, high_near, along = together(
        send(four, sizes, 2), across_core(got, sizes), across_high(got[: 2 * rows], sizes), across_core(high, sizes), prepare(*along)
    )
    small = four[4 * rows :] + last[4 * rows :]
    own = (four, last), (near, near_two, across_core(last, sizes))
    high = jnp.concatenate([high, high_two], axis=0)
    return own, (high, high_near, across_core(high_two, sizes)), small, along


def gather_weights_plain(qkv_weight, out_weight, router, norm_params):
    qkv = lax.all_gather(qkv_weight, "dp", axis=1, tiled=True)
    qkv = lax.all_gather(qkv, "tensor", axis=2, tiled=True)
    out_w, router, norms = (
        lax.all_gather(lax.all_gather(w, "dp", axis=1, tiled=True), "tensor", axis=0, tiled=True)
        for w in (out_weight, router, norm_params)
    )
    width = qkv.shape[1]
    half = width // 2
    one = qkv[:, :, :half].transpose(1, 0, 2).reshape(width, 3 * half)
    two = qkv[:, :, half:].transpose(1, 0, 2).reshape(width, 3 * half)
    return one, two, out_w.T, norms.astype(F32), router.T


def add_low(*values):
    return sum(v.astype(F32) for v in values).astype(BF)


def sum_small(values, sizes):
    dp_size, tensor_size = sizes
    mask = 1
    while mask < tensor_size:
        values = values + swap(values, dp_size, tensor_size, 0, mask)
        mask *= 2
    mask = 1
    while mask < dp_size:
        values = values + swap(values, dp_size, tensor_size, mask, 0)
        mask *= 2
    return values


def on_device(
    sizes, tokens, qkv_weight, out_weight, router, norm_params, expert_in, expert_out, cotangent
):
    dp_size, tensor_size = sizes
    dp_index = lax.axis_index("dp")
    tensor_index = lax.axis_index("tensor")
    core = jnp.bitwise_and(tensor_index, 1)
    width = tokens.shape[1]
    half = width // 2
    rows = qkv_weight.shape[1]
    columns = qkv_weight.shape[2]
    experts = dp_size * router.shape[1]
    stepwise = rows % 16 == 0 and sizes == (8, 4)
    owners = ()
    if stepwise:
        owners = owners_of(dp_size, dp_index, core)
        index = jnp.stack([dp_index, tensor_index]).astype(jnp.int32)
        *owners, index, qkv_weight, out_weight, norm_params, router = together(
            *owners, index, qkv_weight, out_weight, norm_params, router
        )
        owners = tuple(owners)
        small = place(index, norm_params, router, experts)
        block = pack(qkv_weight, out_weight)
        (own, near), high, small, (x_img, g_img, unit) = gather_first(block, small, sizes, (tokens, cotangent))
        norms, router_t = small[:tensor_size].astype(F32), small[tensor_size : tensor_size + experts]
        high, near_first, near_second = high
        last_high = send(high, sizes, 2)
        normed, qkv_one, mixed, probs_one, weight_one, out_w = attend_first(unit, norms, owners, (own, near))
        last_high, near_second, normed = together(last_high, near_second, normed)
        parts = (high, last_high), (near_first, near_second, across_core(last_high, sizes))
        mixed, out_w, qkv_two, probs_two, weight_two = attend_second(normed, mixed, out_w, owners, parts)
    else:
        x_img, g_img, unit = prepare(tokens, cotangent)
        weight_one, weight_two, out_w, norms, router_t = gather_weights_plain(
            qkv_weight, out_weight, router, norm_params
        )
        normed, qkv_one, mixed, probs_one = attend_first(unit, norms, (), (weight_one,))
        mixed, qkv_two, probs_two = attend_second(normed, mixed, None, (), (weight_two,))
    y, normed_two, logits, outgoing = route(x_img, mixed, out_w, norms, router_t, g_img)

    arrived = exchange(outgoing, dp_size)
    across = across_high(arrived, sizes)
    near = across_core(arrived, sizes)
    across, near, ready = lax.optimization_barrier((across, near, tuple(moe_ready(y, logits))))
    keep, keep_high, away, away_high, *kept = run_expert(
        (arrived, across), (near, across_core(across, sizes)), expert_in[0], expert_out[0]
    )
    got = across_high(add_low(keep_high, across_core(away_high, sizes)), sizes)
    got, near, (first_grad, second_grad) = lax.optimization_barrier(
        (got, across_core(away, sizes), tuple(expert_grads(*kept)))
    )
    back = exchange(add_low(keep, near, got), dp_size)

    grad_y, grad_mixed, out_grad_t, small_two = moe_back(
        ready, normed_two, g_img, back, norms, router_t, out_w, mixed, BF if stepwise else F32
    )
    grads_two, *dealt_two = attend_back(
        normed, qkv_two, probs_two, mixed, grad_mixed, out_grad_t, 1, owners, sizes
    )
    grad_part = input_part(grads_two, weight_two)
    if stepwise:
        mine = dealt_two[0].reshape(width, width)
        got, grad_part = together(across_core(dealt_two[1].reshape(width, width), sizes), grad_part)
        cut = [rows * place for place in range(9)]
        low, along = add_low(mine[: cut[3]], got[: cut[3]]), add_low(mine[cut[4] : cut[7]], got[cut[4] : cut[7]])
        across = [add_low(mine[at : at + rows], got[at : at + rows]) for at in (cut[3], cut[7])]
        low, along, across, grad_mixed = together(low, along, jnp.concatenate(across, axis=0), grad_mixed)
        along, across = send(along, sizes, 2), across_high(across, sizes)
    grads_one, *dealt_one = attend_back(
        normed, qkv_one, probs_one, mixed, grad_mixed, out_grad_t, 0, owners, sizes
    )
    if stepwise:
        along, across, mine, sent, grads_one = together(along, across, *dealt_one, grads_one)
        mine, sent = mine.reshape(width, width), sent.reshape(width, width)
        got = across_core(sent[cut[4] :], sizes)
        high = [
            add_low(mine[cut[4] : cut[7]], got[: cut[3]]),
            add_low(mine[cut[7] :], got[cut[3] :], across[rows:]),
        ]
        low = add_low(low, along)
        high, low, grads_one, sent = together(jnp.concatenate(high, axis=0), low, grads_one, sent)
        got, near = send(high, sizes, 2), across_core(sent[: cut[4]], sizes)
        got_high, got_low = across_high(low[cut[2] :], sizes), across_high(low[: cut[2]], sizes)
    grad_one, small_one = input_sum(x_img, grads_one, grad_part, weight_one)
    small = jnp.concatenate([small_one[0:2], small_two[0:2], small_two[8:]], axis=0)
    if stepwise:
        near, small = together(near, small)
        small = jnp.pad(small.astype(BF), ((0, -small.shape[0] % 16), (0, 0)))
        smalls = across_high(small, sizes), send(small, sizes, 2), across_high(small, sizes, 2)
        got, got_high, near, smalls = together(got, got_high, near, smalls)
        small = add_low(small, *smalls)
        held = mine[: cut[4]], near, got
        low = add_low(*(h[: cut[2]] for h in held))
        high = [
            add_low(*(h[cut[2] : cut[3]] for h in held), got_high),
            add_low(*(h[cut[3] : cut[4]] for h in held), across[:rows]),
            small,
        ]
        low, high, grad_one = together(low, jnp.concatenate(high, axis=0), grad_one)
    input_grad = input_back(x_img, grad_y, grad_one, norms)
    output = block_output(y, logits, back)
    if stepwise:
        got, got_low, input_grad = together(send(high, sizes, 1), got_low, input_grad)
        low = add_low(low, got[: cut[2]], got_low)
        small = add_low(small, got[cut[2] :])
        near, corner = across_core(small, sizes), across_core_after(small, sizes, 0)
        got, output, near, corner = together(
            send(jnp.concatenate([low[rows:], small], axis=0), sizes, 0), output, near, corner
        )
        low = jnp.concatenate([low[:rows], small], axis=0)
        qkv_grad, out_grad, norm_grad, router_grad = unpack(index, low, got, near, corner, sizes)
        router_grad = router_grad.reshape(columns, 1)
    else:
        small = sum_small(small, sizes)
        full = jnp.concatenate(
            [dealt_one[0].reshape(width, 3, half), dealt_two[0].reshape(width, 3, half)], axis=2
        ).transpose(1, 0, 2)
        qkv_grad = lax.psum_scatter(full, "dp", scatter_dimension=1, tiled=True)
        qkv_grad = lax.psum_scatter(qkv_grad, "tensor", scatter_dimension=2, tiled=True)
        out_grad = lax.psum_scatter(out_grad_t.T, "dp", scatter_dimension=1, tiled=True)
        out_grad = lax.psum_scatter(out_grad, "tensor", scatter_dimension=0, tiled=True)
        norm_grad = lax.dynamic_slice(small, (tensor_index, dp_index * rows), (1, rows))
        router_grad = lax.dynamic_slice(
            small, (tensor_size + dp_index, tensor_index * columns), (1, columns)
        ).reshape(columns, 1)
    return (
        output,
        input_grad,
        qkv_grad,
        out_grad,
        router_grad,
        norm_grad,
        first_grad[None],
        second_grad[None],
    )


def solution(mesh):
    sizes = (mesh.shape["dp"], mesh.shape["tensor"])
    return jax.shard_map(
        functools.partial(on_device, sizes),
        mesh=mesh,
        in_specs=(
            P(("dp", "tensor"), None),
            P(None, "dp", "tensor"),
            P("tensor", "dp"),
            P("tensor", "dp"),
            P("tensor", "dp"),
            P("dp", None, "tensor"),
            P("dp", "tensor", None),
            P(("dp", "tensor"), None),
        ),
        out_specs=(
            P(("dp", "tensor"), None),
            P(("dp", "tensor"), None),
            P(None, "dp", "tensor"),
            P("tensor", "dp"),
            P("tensor", "dp"),
            P("tensor", "dp"),
            P("dp", None, "tensor"),
            P("dp", "tensor", None),
        ),
        check_vma=False,
    )
```

```python
import functools

import jax
import jax.numpy as jnp
from jax import lax
from jax.experimental import pallas as pl
from jax.experimental.pallas import tpu as pltpu
from jax.sharding import PartitionSpec as P

HEAD_DIM = 64
SEQ = 197
PAD = 208
BLOCK = 8
AXES = ("dp", "tensor")
BF = jnp.bfloat16
F32 = jnp.float32
LAST = (((1,), (1,)), ((), ()))
FIRST = (((0,), (0,)), ((), ()))
MIDDLE = (((1,), (0,)), ((), ()))
MIB = 1024 * 1024


def dot(a, b, dims=MIDDLE):
    return lax.dot_general(a, b, dims, preferred_element_type=F32)


def shape_of(shape, dtype):
    return jax.ShapeDtypeStruct(shape, dtype)


def run(kernel, name, operands, results, limit, scratch=(), scalars=0, aliases=()):
    memory = [pltpu.SMEM] * scalars + [pltpu.VMEM] * (len(operands) - scalars)
    return pl.pallas_call(
        kernel,
        in_specs=[pl.BlockSpec(memory_space=m) for m in memory],
        out_specs=[pl.BlockSpec(memory_space=pltpu.VMEM) for _ in results],
        out_shape=list(results),
        scratch_shapes=list(scratch),
        input_output_aliases=dict(aliases),
        compiler_params=pltpu.CompilerParams(vmem_limit_bytes=limit * MIB),
        cost_estimate=pl.CostEstimate(flops=1, bytes_accessed=1, transcendentals=0),
        name=name,
    )(*operands)


def layer_stats(values):
    centre = jnp.mean(values, axis=-1, keepdims=True)
    centred = values - centre
    spread = jnp.mean(centred * centred, axis=-1, keepdims=True)
    inv_std = lax.rsqrt(spread + 1e-06)
    return centred * inv_std, inv_std


def lane_ids(shape):
    return lax.broadcasted_iota(jnp.int32, shape, len(shape) - 1)


def row_ids(shape):
    return lax.broadcasted_iota(jnp.int32, shape, len(shape) - 2)


def flat(ref):
    images, rows, columns = ref.shape
    return ref[...].reshape(images * rows, columns)


def prepare_kernel(x_ref, g_ref, x_out, g_out, unit_out, inv_out, wide):
    count, width = x_ref.shape
    real = row_ids((PAD, width)) < SEQ
    wide[count:, :] = jnp.zeros((wide.shape[0] - count, width), F32)
    for ref, out in ((x_ref, x_out), (g_ref, g_out)):
        wide[0:count, :] = ref[...].astype(F32)
        for i in range(out.shape[0]):
            rows = jnp.where(real, wide[SEQ * i : SEQ * i + PAD, :], 0.0)
            out[i] = rows.astype(BF)
            if ref is x_ref:
                unit_out[i], inv_out[i] = layer_stats(rows)


def prepare(tokens, cotangent):
    count, width = tokens.shape
    images = count // SEQ
    rows = shape_of((images, PAD, width), BF)
    return run(
        prepare_kernel,
        "prepare",
        (tokens, cotangent),
        (rows, rows, shape_of((images, PAD, width), F32), shape_of((images, PAD, 1), F32)),
        8,
        scratch=[pltpu.VMEM((-(-count // 8) * 8 + 16, width), F32)],
    )


def attend_rows(normed, w_ref, qkv_ref, mixed_ref, probs_ref, piece):
    images, rows, width = mixed_ref.shape
    span = width // 2
    low = lane_ids((rows, 128)) < HEAD_DIM
    key_ok = row_ids((rows, rows)) < SEQ
    zero = jnp.zeros((rows, 128), BF)
    proj = dot(normed, w_ref[...])
    qkv_ref[:, :, 0:span] = (proj[:, 0:span] * HEAD_DIM ** (-0.5)).astype(BF).reshape(images, rows, span)
    qkv_ref[:, :, span:] = proj[:, span:].astype(BF).reshape(images, rows, 2 * span)

    def image(i, carry):
        for p in range(span // 128):
            at = slice(p * 128, (p + 1) * 128)
            q = qkv_ref[i, :, at]
            k = qkv_ref[i, :, span + p * 128 : span + (p + 1) * 128]
            v = qkv_ref[i, :, 2 * span + p * 128 : 2 * span + (p + 1) * 128]
            mixed = []
            for h in range(2):
                q_one = jnp.where(low, q, zero) if h == 0 else jnp.where(low, zero, q)
                scores = jnp.where(key_ok, dot(k, q_one, LAST), -1e30)
                scaled = jnp.exp(scores - jnp.max(scores, axis=0, keepdims=True))
                weights = (scaled * (1.0 / jnp.sum(scaled, axis=0, keepdims=True))).astype(BF)
                probs_ref[i, 2 * p + h] = weights
                mixed.append(dot(weights, v, FIRST))
            at = slice(piece * span + p * 128, piece * span + (p + 1) * 128)
            mixed_ref[i, :, at] = jnp.where(low, mixed[0], mixed[1]).astype(BF)
        return carry

    lax.fori_loop(0, images, image, 0, unroll=3 if images % 3 == 0 else 1)


def assemble_rows(owners, parts, kinds, out_ref, columns, lane=0):
    for side, (owner, refs) in enumerate(zip(owners, parts, strict=True)):
        count = out_ref.shape[0] // owner.shape[0]
        blocks = [ref[i * count : (i + 1) * count] for ref in refs for i in range(ref.shape[0] // count)]
        for p, block in enumerate(blocks):
            row = pl.multiple_of(count * owner[p], 16)
            for at, kind in enumerate(kinds):
                to = lane + (2 * at + side) * columns
                out_ref[pl.ds(row, count), to : to + columns] = block[:, kind * columns : (kind + 1) * columns]


def attend_first_kernel(counts, *refs):
    if counts:
        own, sib = counts
        owners, refs = refs[:2], refs[2:]
        unit_ref, norms_ref, refs = refs[0], refs[1], refs[2:]
        parts, refs = (refs[:own], refs[own : own + sib]), refs[own + sib :]
        n_ref, qkv_ref, mixed_ref, probs_ref, w_ref, out_w_ref = refs
        columns = w_ref.shape[1] // 6
        assemble_rows(owners, parts, range(3), w_ref, columns)
        assemble_rows(owners, parts, [3], out_w_ref, columns)
    else:
        unit_ref, norms_ref, w_ref, n_ref, qkv_ref, mixed_ref, probs_ref = refs
    normed = (flat(unit_ref) * norms_ref[0:1, :] + norms_ref[1:2, :]).astype(BF)
    n_ref[...] = normed.reshape(n_ref.shape)
    attend_rows(normed, w_ref, qkv_ref, mixed_ref, probs_ref, 0)


def attend_second_kernel(counts, *refs):
    if counts:
        own, sib = counts
        owners, refs = refs[:2], refs[2:]
        n_ref, refs = refs[0], refs[3:]
        parts, refs = (refs[:own], refs[own : own + sib]), refs[own + sib :]
        mixed_ref, out_w_ref, qkv_ref, probs_ref, w_ref = refs
        columns = w_ref.shape[1] // 6
        assemble_rows(owners, parts, range(3), w_ref, columns)
        assemble_rows(owners, parts, [3], out_w_ref, columns, 2 * columns)
    else:
        n_ref, _, w_ref, mixed_ref, qkv_ref, probs_ref = refs
    attend_rows(flat(n_ref), w_ref, qkv_ref, mixed_ref, probs_ref, 1)


def attend_first(unit, norms, owners, weights):
    images, rows, width = unit.shape
    span = width // 2
    results = (
        shape_of(unit.shape, BF),
        shape_of((images, rows, 3 * span), BF),
        shape_of(unit.shape, BF),
        shape_of((images, span // HEAD_DIM, rows, rows), BF),
    )
    counts = None
    if owners:
        counts = tuple(map(len, weights))
        weights = sum(weights, ())
        results += (shape_of((width, 3 * span), BF), shape_of((width, width), BF))
    return run(
        functools.partial(attend_first_kernel, counts),
        "attend_first",
        owners + (unit, norms) + weights,
        results,
        4,
        scalars=len(owners),
    )


def attend_second(normed, mixed, out_w, owners, weights):
    images, rows, width = normed.shape
    span = width // 2
    given = (mixed, out_w) if owners else (mixed,)
    results = tuple(shape_of(g.shape, BF) for g in given) + (
        shape_of((images, rows, 3 * span), BF),
        shape_of((images, span // HEAD_DIM, rows, rows), BF),
    )
    counts = None
    if owners:
        counts = tuple(map(len, weights))
        weights = sum(weights, ())
        results += (shape_of((width, 3 * span), BF),)
    return run(
        functools.partial(attend_second_kernel, counts),
        "attend_second",
        owners + (normed,) + given + weights,
        results,
        4,
        scalars=len(owners),
        aliases=[(len(owners) + 1 + i, i) for i in range(len(given))],
    )


def softmaxes(logits):
    ok = lane_ids(logits.shape) < SEQ
    masked = jnp.where(ok, logits, -1e30)
    up = jnp.exp(masked - jnp.max(masked, axis=1, keepdims=True))
    dispatch = up / jnp.sum(up, axis=1, keepdims=True)
    up = jnp.exp(logits - jnp.max(logits, axis=0, keepdims=True))
    combine = up / jnp.sum(up, axis=0, keepdims=True)
    return dispatch, combine


def by_image(experts, places, low, back=False):
    shape = (experts * BLOCK, places * experts)
    shape = shape[::-1] if back else shape
    blocked, other = (lane_ids(shape), row_ids(shape)) if back else (row_ids(shape), lane_ids(shape))
    place = jnp.bitwise_and(blocked, BLOCK - 1) - low
    inside = jnp.logical_and(place >= 0, place < places)
    return jnp.logical_and(inside, other == place * experts + lax.div(blocked, BLOCK)).astype(BF)


def to_blocks(first, second):
    experts, width = first[0].shape
    half = width // 2
    head = dot(by_image(experts, BLOCK, 0), jnp.concatenate(first + second[:2], axis=0))
    rest = jnp.concatenate(second[2:], axis=0)
    rest = dot(by_image(experts, 4, 0), rest[:, :half]) + dot(by_image(experts, 4, 4), rest[:, half:])
    return head.astype(BF), rest.astype(BF)


def from_blocks(blocks, experts, width):
    head = dot(by_image(experts, BLOCK, 0, True), blocks[:, :width])
    rest = [dot(by_image(experts, 4, low, True), blocks[:, width:]) for low in (0, 4)]
    rest = jnp.concatenate(rest, axis=1)
    head, rest = ([v[at : at + experts].astype(BF) for at in range(0, v.shape[0], experts)] for v in (head, rest))
    return head[:6], head[6:] + rest


def route_kernel(
    x_ref, mixed_ref, out_w_ref, norms_ref, router_ref, g_ref, y_ref, n_ref, logits_ref, send_ref
):
    images, rows, width = x_ref.shape
    experts = router_ref.shape[0]
    for at in range(0, images, 2):
        some = slice(at, min(at + 2, images))
        y = flat(x_ref.at[some]).astype(F32) + dot(flat(mixed_ref.at[some]), out_w_ref[...], LAST)
        y_ref[some] = y.reshape(-1, rows, width)
        unit, _ = layer_stats(y)
        n_ref[some] = (unit * norms_ref[2:3, :] + norms_ref[3:4, :]).astype(BF).reshape(-1, rows, width)
    first, second = [], []
    for i in range(images):
        logits = dot(router_ref[...], n_ref[i], LAST)
        logits_ref[i] = logits
        dispatch, combine = softmaxes(logits)
        first.append(dot(dispatch.astype(BF), n_ref[i]).astype(BF))
        second.append(dot(combine.astype(BF), g_ref[i]).astype(BF))
    send_ref[:, :width], send_ref[:, width:] = to_blocks(first, second)


def route(x_img, mixed, out_w, norms, router, g_img):
    images, rows, width = x_img.shape
    experts = router.shape[0]
    return run(
        route_kernel,
        "route",
        (x_img, mixed, out_w, norms, router, g_img),
        (
            shape_of((images, rows, width), F32),
            shape_of((images, rows, width), BF),
            shape_of((images, experts, rows), F32),
            shape_of((experts * BLOCK, width + width // 2), BF),
        ),
        4,
    )


def turned(blocks, shift):
    return pltpu.roll(blocks, shift, 1)


def split_rows(blocks):
    rows, lanes = blocks.shape
    width = lanes // 3 * 2
    wide = blocks.astype(F32).reshape(rows // BLOCK, BLOCK, lanes)
    head, rest = wide[:, :, :width], wide[:, :, width:]
    place = row_ids(head.shape)
    first = jnp.where(place < 6, head, 0.0)
    second = jnp.concatenate([turned(rest, 2), turned(rest, BLOCK - 2)], axis=2)
    second = jnp.where(place < 2, turned(head, 2), jnp.where(place < 6, second, 0.0))
    return first.reshape(rows, width).astype(BF), second.reshape(rows, width).astype(BF)


def join_rows(first, second):
    rows, width = first.shape
    half = width // 2
    first = first.reshape(rows // BLOCK, BLOCK, width)
    second = second.reshape(rows // BLOCK, BLOCK, width)
    head = jnp.where(row_ids(first.shape) < 6, first, turned(second, 6))
    left, right = turned(second[:, :, :half], BLOCK - 2), turned(second[:, :, half:], 2)
    rest = jnp.where(row_ids(left.shape) < 4, left, right)
    return head.reshape(rows, width).astype(BF), rest.reshape(rows, half).astype(BF)


def gelu_parts(pre):
    cdf = 0.5 * (1.0 + lax.erf(pre * (0.5**0.5)))
    density = jnp.exp(-0.5 * pre * pre) * 0.3989422804014327
    return pre * cdf, cdf + pre * density


def expert_kernel(a_ref, b_ref, c_ref, d_ref, w1_ref, w2_ref, *refs):
    outs, (slots_ref, grads_ref, hidden_ref, pre_ref) = refs[:4], refs[4:]
    width = w1_ref.shape[0]
    count = a_ref.shape[0]
    blocks = jnp.concatenate([a_ref[...], b_ref[...], c_ref[...], d_ref[...]], axis=0)
    step = min(4 * count, 256)
    for at in range(0, 4 * count, step):
        slots_ref[at : at + step], grads_ref[at : at + step] = split_rows(blocks[at : at + step])
    slots, grads = slots_ref[...], grads_ref[...]
    pre = dot(slots, w1_ref[...])
    hidden, slope = gelu_parts(pre)
    hidden = hidden.astype(BF)
    returned = dot(hidden, w2_ref[...])
    grad_pre = (dot(grads, w2_ref[...], LAST) * slope).astype(BF)
    grad_slots = dot(grad_pre, w1_ref[...], LAST)
    parts = [join_rows(returned[at : at + step], grad_slots[at : at + step]) for at in range(0, 4 * count, step)]
    head, rest = (jnp.concatenate(p, axis=0) for p in zip(*parts, strict=True))
    for i, ref in enumerate(outs):
        ref[:, :width] = head[i * count : (i + 1) * count]
        ref[:, width:] = rest[i * count : (i + 1) * count]
    hidden_ref[...] = hidden
    pre_ref[...] = grad_pre


def run_expert(own, near, first_weight, second_weight):
    width, units = first_weight.shape
    rows = 4 * own[0].shape[0]
    return run(
        expert_kernel,
        "expert",
        own + near + (first_weight, second_weight),
        (shape_of(own[0].shape, BF),) * 4
        + (
            shape_of((rows, width), BF),
            shape_of((rows, width), BF),
            shape_of((rows, units), BF),
            shape_of((rows, units), BF),
        ),
        8 if rows <= 512 else 48,
    )


def expert_grad_kernel(slots_ref, grads_ref, hidden_ref, pre_ref, d1_ref, d2_ref):
    d1_ref[...] = dot(slots_ref[...], pre_ref[...], FIRST)
    d2_ref[...] = dot(hidden_ref[...], grads_ref[...], FIRST)


def expert_grads(slots, grads, hidden, grad_pre):
    rows, width = slots.shape
    units = hidden.shape[1]
    return run(
        expert_grad_kernel,
        "expert_grads",
        (slots, grads, hidden, grad_pre),
        (shape_of((width, units), F32), shape_of((units, width), F32)),
        6 if rows <= 512 else 32,
    )


def moe_ready_kernel(y_ref, logits_ref, unit_ref, inv_ref, dispatch_ref, combine_ref):
    unit, inv_std = layer_stats(flat(y_ref))
    unit_ref[...] = unit.reshape(unit_ref.shape)
    inv_ref[...] = inv_std.reshape(inv_ref.shape)
    for i in range(y_ref.shape[0]):
        dispatch_ref[i], combine_ref[i] = softmaxes(logits_ref[i])


def moe_ready(y, logits):
    images, rows, width = y.shape
    return run(
        moe_ready_kernel,
        "moe_ready",
        (y, logits),
        (
            shape_of((images, rows, width), F32),
            shape_of((images, rows, 1), F32),
            shape_of(logits.shape, F32),
            shape_of(logits.shape, F32),
        ),
        4,
    )


def moe_back_kernel(
    unit_ref,
    inv_ref,
    dispatch_ref,
    combine_ref,
    n_ref,
    g_ref,
    back_ref,
    norms_ref,
    router_ref,
    out_w_ref,
    mixed_ref,
    grad_y_ref,
    grad_mixed_ref,
    out_grad_ref,
    small_ref,
    attn_ref,
):
    images, rows, width = unit_ref.shape
    experts = router_ref.shape[0]
    gain = norms_ref[2:3, :]
    all_returned, all_slots = from_blocks(back_ref[...], experts, width)
    router_grad, gain_grad, shift_grad = 0.0, 0.0, 0.0
    for i in range(images):
        returned, grad_slots = all_returned[i], all_slots[i]
        dispatch, combine = dispatch_ref[i], combine_ref[i]
        grad_combine = dot(returned, g_ref[i], LAST)
        grad_dispatch = dot(grad_slots, n_ref[i], LAST)
        grad_logits = dispatch * (
            grad_dispatch - jnp.sum(grad_dispatch * dispatch, axis=1, keepdims=True)
        ) + combine * (grad_combine - jnp.sum(grad_combine * combine, axis=0, keepdims=True))
        grad_logits = grad_logits.astype(BF)
        router_grad = router_grad + dot(grad_logits, n_ref[i])
        grad_two = dot(
            jnp.concatenate([dispatch.astype(BF), grad_logits], axis=0),
            jnp.concatenate([grad_slots, router_ref[...]], axis=0),
            FIRST,
        )
        unit, inv_std = unit_ref[i], inv_ref[i]
        gain_grad = gain_grad + jnp.sum(grad_two * unit, axis=0, keepdims=True)
        shift_grad = shift_grad + jnp.sum(grad_two, axis=0, keepdims=True)
        scaled = grad_two * gain
        mean_one = jnp.mean(scaled, axis=-1, keepdims=True)
        mean_two = jnp.mean(scaled * unit, axis=-1, keepdims=True)
        grad_y = g_ref[i].astype(F32) + inv_std * (scaled - mean_one - unit * mean_two)
        grad_y_ref[i] = grad_y
        attn_ref[i] = grad_y.astype(BF)
    small_ref[...] = jnp.zeros_like(small_ref)
    small_ref[0:1, :] = gain_grad
    small_ref[1:2, :] = shift_grad
    small_ref[8 : 8 + experts, :] = router_grad
    grad_attn = flat(attn_ref)
    grad_mixed_ref[...] = dot(grad_attn, out_w_ref[...]).astype(BF).reshape(grad_mixed_ref.shape)
    out_grad_ref[...] = dot(grad_attn, flat(mixed_ref), FIRST).astype(out_grad_ref.dtype)


def moe_back(ready, normed, g_img, back, norms, router, out_w, mixed, dtype):
    images, rows, width = normed.shape
    experts = router.shape[0]
    return run(
        moe_back_kernel,
        "moe_back",
        ready + (normed, g_img, back, norms, router, out_w, mixed),
        (
            shape_of((images, rows, width), F32),
            shape_of((images, rows, width), BF),
            shape_of((width, width), dtype),
            shape_of((8 + experts, width), F32),
        ),
        10,
        scratch=[pltpu.VMEM((images, rows, width), BF)],
    )


def output_kernel(y_ref, logits_ref, back_ref, out_ref, wide):
    images, experts, _ = logits_ref.shape
    all_returned, _ = from_blocks(back_ref[...], experts, y_ref.shape[2])
    for i in range(images):
        returned = all_returned[i]
        _, combine = softmaxes(logits_ref[i])
        total = y_ref[i] + dot(combine.astype(BF), returned, FIRST)
        wide[SEQ * i : SEQ * (i + 1), :] = total[0:SEQ]
    out_ref[...] = wide[...].astype(BF)


def block_output(y, logits, back):
    images, rows, width = y.shape
    count = images * SEQ
    return run(
        output_kernel,
        "block_output",
        (y, logits, back),
        (shape_of((count, width), BF),),
        7,
        scratch=[pltpu.VMEM((count, width), F32)],
    )[0]


def deal_rows(owners, full_ref, first, kinds, refs, columns):
    for side, (owner, ref) in enumerate(zip(owners, refs, strict=True)):
        blocks, count, _ = ref.shape
        for p in range(blocks):
            row = pl.multiple_of(count * owner[p], 16)
            for at, kind in enumerate(kinds):
                lane = first + (2 * at + side) * columns
                ref[p, :, kind * columns : (kind + 1) * columns] = full_ref[pl.ds(row, count), lane : lane + columns]


def attend_back_kernel(stepwise, piece, *refs):
    if stepwise:
        owners, refs = refs[:2], refs[2:]
        n_ref, qkv_ref, probs_ref, mixed_ref, gm_ref, og_ref, grads_ref, own_ref, sib_ref, dw_ref = refs
    else:
        n_ref, qkv_ref, probs_ref, mixed_ref, gm_ref, grads_ref, dw_ref = refs
    images, rows, width = mixed_ref.shape
    span = width // 2
    low = lane_ids((rows, 128)) < HEAD_DIM
    zero = jnp.zeros((rows, 128), BF)
    minus = jnp.full((rows, 128), -1.0, BF)

    def image(i, carry):
        for p in range(span // 128):
            at = slice(p * 128, (p + 1) * 128)
            at_k = slice(span + p * 128, span + (p + 1) * 128)
            at_v = slice(2 * span + p * 128, 2 * span + (p + 1) * 128)
            q, k, v = qkv_ref[i, :, at], qkv_ref[i, :, at_k], qkv_ref[i, :, at_v]
            here = slice(piece * span + p * 128, piece * span + (p + 1) * 128)
            gm = gm_ref[i, :, here]
            inner = pltpu.roll(gm.astype(F32) * mixed_ref[i, :, here].astype(F32), HEAD_DIM, 1).astype(BF)
            grad_q, grad_k, grad_v = 0.0, 0.0, 0.0
            for h in range(2):
                mine = low if h == 0 else jnp.logical_not(low)
                weights = probs_ref[i, 2 * p + h]
                centred = dot(jnp.where(mine, v, minus), jnp.where(mine, gm, inner), LAST)
                grad_scores = (weights.astype(F32) * centred).astype(BF)
                grad_v = grad_v + dot(weights, jnp.where(mine, gm, zero))
                grad_k = grad_k + dot(grad_scores, jnp.where(mine, q, zero))
                grad_q = grad_q + dot(grad_scores, jnp.where(mine, k, zero), FIRST)
            grads_ref[i, :, at] = (grad_q * HEAD_DIM ** (-0.5)).astype(BF)
            grads_ref[i, :, at_k] = grad_k.astype(BF)
            grads_ref[i, :, at_v] = grad_v.astype(BF)
        return carry

    lax.fori_loop(0, images, image, 0, unroll=images)
    dw_ref[...] = dot(flat(n_ref), flat(grads_ref), FIRST).astype(dw_ref.dtype)
    if stepwise:
        deal_rows(owners, dw_ref, 0, range(3), (own_ref, sib_ref), span // 2)
        deal_rows(owners, og_ref, piece * span, [3], (own_ref, sib_ref), span // 2)


def attend_back(normed, qkv, probs, mixed, grad_mixed, out_grad_t, piece, owners, sizes):
    images, rows, width = normed.shape
    span = width // 2
    operands = (normed, qkv, probs, mixed, grad_mixed)
    results = (shape_of((images, rows, 3 * span), BF),)
    scratch = ()
    if owners:
        operands += (out_grad_t,)
        results += (shape_of((sizes[0], width // sizes[0], 2 * span), BF),) * 2
        scratch = (pltpu.VMEM((width, 3 * span), BF),)
    else:
        results += (shape_of((width, 3 * span), F32),)
    return run(
        functools.partial(attend_back_kernel, bool(owners), piece),
        "attend_back",
        owners + operands,
        results,
        7,
        scratch,
        scalars=len(owners),
    )


def input_part_kernel(p_ref, w_ref, out_ref):
    out_ref[...] = dot(flat(p_ref), w_ref[...], LAST).reshape(out_ref.shape)


def input_part(grads, weight):
    images, rows, _ = grads.shape
    return run(
        input_part_kernel, "input_part", (grads, weight), (shape_of((images, rows, weight.shape[0]), F32),), 6
    )[0]


def input_sum_kernel(unit_ref, p1_ref, part_ref, w1_ref, grad_ref, small_ref):
    images, rows, width = unit_ref.shape
    gain_grad, shift_grad = 0.0, 0.0
    for i in range(images):
        if i % 2 == 0:
            some = slice(i, min(i + 2, images))
            grad = dot(flat(p1_ref.at[some]), w1_ref[...], LAST) + flat(part_ref.at[some])
            grad_ref[some] = grad.reshape(-1, rows, width)
        gain_grad = gain_grad + jnp.sum(grad_ref[i] * unit_ref[i], axis=0, keepdims=True)
        shift_grad = shift_grad + jnp.sum(grad_ref[i], axis=0, keepdims=True)
    small_ref[...] = jnp.zeros_like(small_ref)
    small_ref[0:1, :] = gain_grad
    small_ref[1:2, :] = shift_grad


def input_sum(unit, grads_one, grad_part, weight_one):
    width = unit.shape[2]
    return run(
        input_sum_kernel,
        "input_sum",
        (unit, grads_one, grad_part, weight_one),
        (shape_of(unit.shape, F32), shape_of((8, width), F32)),
        7,
    )


def input_back_kernel(unit_ref, inv_ref, gy_ref, grad_ref, norms_ref, out_ref):
    gain = norms_ref[0:1, :]
    for i in range(unit_ref.shape[0]):
        unit, inv_std = unit_ref[i], inv_ref[i]
        scaled = grad_ref[i] * gain
        mean_one = jnp.mean(scaled, axis=-1, keepdims=True)
        mean_two = jnp.mean(scaled * unit, axis=-1, keepdims=True)
        total = gy_ref[i] + inv_std * (scaled - mean_one - unit * mean_two)
        out_ref[SEQ * i : SEQ * (i + 1), :] = total[0:SEQ]


def input_back(unit, inv_std, grad_y, grad_one, norms):
    images, _, width = unit.shape
    return run(
        input_back_kernel,
        "input_back",
        (unit, inv_std, grad_y, grad_one, norms),
        (shape_of((images * SEQ, width), F32),),
        9,
    )[0]


def spot(shape, start):
    return (lane_ids(shape) == row_ids(shape) + start).astype(BF)


def place_kernel(index_ref, norm_ref, router_ref, small_ref):
    rows, columns = norm_ref.shape[1], router_ref.shape[1]
    width = small_ref.shape[1]
    dp_index, tensor_index = index_ref[0], index_ref[1]
    norm = dot(jnp.broadcast_to(norm_ref[...], (16, rows)), spot((rows, width), dp_index * rows))
    router = dot(jnp.broadcast_to(router_ref[...], (16, columns)), spot((columns, width), tensor_index * columns))
    row = row_ids(small_ref.shape)
    small_ref[...] = jnp.where(
        row == tensor_index, norm[0:1], jnp.where(row == width // columns + dp_index, router[0:1], 0.0)
    ).astype(BF)


def place(index, norm_params, router, experts):
    rows, columns = norm_params.shape[1], router.shape[0]
    width = rows * experts
    return run(
        place_kernel,
        "place",
        (index, norm_params, router.T),
        (shape_of((-(-(width // columns + experts) // 16) * 16, width), BF),),
        4,
        scalars=1,
    )[0]


def pack_kernel(qkv_ref, out_ref, block_ref):
    kinds, _, columns = qkv_ref.shape
    for kind in range(kinds):
        block_ref[:, kind * columns : (kind + 1) * columns] = qkv_ref[kind]
    block_ref[:, kinds * columns :] = out_ref[...].T


def pack(qkv_weight, out_weight):
    kinds, rows, columns = qkv_weight.shape
    return run(
        pack_kernel,
        "pack",
        (qkv_weight, out_weight),
        (shape_of((rows, (kinds + 1) * columns), BF),),
        4,
    )[0]


def unpack_kernel(index_ref, own_ref, got_ref, near_ref, corner_ref, qkv_ref, out_ref, norm_ref, router_ref):
    kinds, rows, columns = qkv_ref.shape
    total = own_ref[...].astype(F32) + got_ref[...].astype(F32)
    for kind in range(kinds):
        qkv_ref[kind] = total[0:rows, kind * columns : (kind + 1) * columns]
    out_ref[...] = total[0:rows, kinds * columns :].T
    small = total[rows:] + near_ref[...].astype(F32) + corner_ref[...].astype(F32)
    dp_index, tensor_index = index_ref[0], index_ref[1]
    width = small.shape[1]
    row = row_ids(small.shape)
    norm = jnp.sum(jnp.where(row == tensor_index, small, 0.0), axis=0, keepdims=True)
    router = jnp.sum(jnp.where(row == width // columns + dp_index, small, 0.0), axis=0, keepdims=True)
    norm_out, router_out = 0.0, 0.0
    for _ in range(2):
        part = norm.astype(BF)
        norm = norm - part.astype(F32)
        norm_out = norm_out + dot(
            jnp.broadcast_to(part, (16, width)), spot((rows, width), dp_index * rows), LAST
        )
        part = router.astype(BF)
        router = router - part.astype(F32)
        router_out = router_out + dot(
            jnp.broadcast_to(part, (16, width)), spot((columns, width), tensor_index * columns), LAST
        )
    norm_ref[...] = norm_out[0:1]
    router_ref[...] = router_out[0:1]


def unpack(index, own, got, near, corner, sizes):
    width = own.shape[1]
    rows, columns = width // sizes[0], width // sizes[1]
    return run(
        unpack_kernel,
        "unpack",
        (index, own, got, near, corner),
        (
            shape_of((width // columns - 1, rows, columns), F32),
            shape_of((columns, rows), F32),
            shape_of((1, rows), F32),
            shape_of((1, columns), F32),
        ),
        4,
        scalars=1,
    )


def swap(value, dp_size, tensor_size, dp_mask, tensor_mask):
    pairs = [
        (d * tensor_size + t, (d ^ dp_mask) * tensor_size + (t ^ tensor_mask))
        for d in range(dp_size)
        for t in range(tensor_size)
    ]
    return lax.ppermute(value, AXES, pairs)


def steps_of(dp_size):
    bits = dp_size.bit_length() - 1
    down = list(range(bits))[::-1]
    return [down, down[-1:] + down[:-1]]


def step_pairs(dp_size, tensor_size, *steps):
    masks = [functools.reduce(lambda mask, step: mask ^ (1 << order[step]), steps, 0) for order in steps_of(dp_size)]
    return [
        (d * tensor_size + t, (d ^ masks[t % 2]) * tensor_size + t)
        for d in range(dp_size)
        for t in range(tensor_size)
    ]


def owners_of(dp_size, dp_index, core):
    both = []
    for order in steps_of(dp_size):
        place = jnp.arange(dp_size, dtype=jnp.int32)
        away = jnp.zeros_like(place)
        for step, bit in enumerate(order):
            away = away | (((place >> step) & 1) << bit)
        both.append(away ^ dp_index)
    return jnp.where(core == 0, both[0], both[1]), jnp.where(core == 0, both[1], both[0])


def exchange(blocks, dp_size):
    shape = blocks.shape
    blocks = blocks.reshape(dp_size, shape[0] // dp_size, shape[1])
    return lax.all_to_all(blocks, "dp", split_axis=0, concat_axis=0, tiled=True).reshape(shape)


def together(*values):
    return lax.optimization_barrier(values)


def send(value, sizes, *steps):
    return lax.ppermute(value, AXES, step_pairs(*sizes, *steps))


def across_core(value, sizes):
    return swap(value, *sizes, 0, 1)


def across_core_after(value, sizes, step):
    pairs = [(a, b ^ 1) for a, b in step_pairs(*sizes, step)]
    return lax.ppermute(value, AXES, pairs)


def across_high(value, sizes, *steps):
    pairs = [(a, b ^ 2) for a, b in step_pairs(*sizes, *steps)]
    return lax.ppermute(value, AXES, pairs)


def gather_first(block, small, sizes, along):
    rows = block.shape[0]
    small_high, block = together(across_high(small, sizes), block)
    small = small + small_high
    small = small + across_core(small, sizes)
    first = jnp.concatenate([block, small], axis=0)
    got, high = together(send(first, sizes, 0), across_high(block, sizes))
    held = jnp.concatenate([block, got[:rows], small + got[rows:]], axis=0)

    got, near, high_got = together(send(held, sizes, 1), across_core(held, sizes), across_high(got[:rows], sizes))
    high = jnp.concatenate([high, high_got], axis=0)
    small = held[2 * rows :] + got[2 * rows :]
    four = jnp.concatenate([held[: 2 * rows], got[: 2 * rows], small], axis=0)

    last, near_two, high_two, high_near, along = together(
        send(four, sizes, 2), across_core(got, sizes), across_high(got[: 2 * rows], sizes), across_core(high, sizes), prepare(*along)
    )
    small = four[4 * rows :] + last[4 * rows :]
    own = (four, last), (near, near_two, across_core(last, sizes))
    high = jnp.concatenate([high, high_two], axis=0)
    return own, (high, high_near, across_core(high_two, sizes)), small, along


def gather_weights_plain(qkv_weight, out_weight, router, norm_params):
    qkv = lax.all_gather(qkv_weight, "dp", axis=1, tiled=True)
    qkv = lax.all_gather(qkv, "tensor", axis=2, tiled=True)
    out_w, router, norms = (
        lax.all_gather(lax.all_gather(w, "dp", axis=1, tiled=True), "tensor", axis=0, tiled=True)
        for w in (out_weight, router, norm_params)
    )
    width = qkv.shape[1]
    half = width // 2
    one = qkv[:, :, :half].transpose(1, 0, 2).reshape(width, 3 * half)
    two = qkv[:, :, half:].transpose(1, 0, 2).reshape(width, 3 * half)
    return one, two, out_w.T, norms.astype(F32), router.T


def add_low(*values):
    return sum(v.astype(F32) for v in values).astype(BF)


def sum_small(values, sizes):
    dp_size, tensor_size = sizes
    mask = 1
    while mask < tensor_size:
        values = values + swap(values, dp_size, tensor_size, 0, mask)
        mask *= 2
    mask = 1
    while mask < dp_size:
        values = values + swap(values, dp_size, tensor_size, mask, 0)
        mask *= 2
    return values


def on_device(
    sizes, tokens, qkv_weight, out_weight, router, norm_params, expert_in, expert_out, cotangent
):
    dp_size, tensor_size = sizes
    dp_index = lax.axis_index("dp")
    tensor_index = lax.axis_index("tensor")
    core = jnp.bitwise_and(tensor_index, 1)
    width = tokens.shape[1]
    half = width // 2
    rows = qkv_weight.shape[1]
    columns = qkv_weight.shape[2]
    experts = dp_size * router.shape[1]
    stepwise = rows % 16 == 0 and sizes == (8, 4)
    owners = ()
    if stepwise:
        owners = owners_of(dp_size, dp_index, core)
        index = jnp.stack([dp_index, tensor_index]).astype(jnp.int32)
        *owners, index, qkv_weight, out_weight, norm_params, router = together(
            *owners, index, qkv_weight, out_weight, norm_params, router
        )
        owners = tuple(owners)
        small = place(index, norm_params, router, experts)
        block = pack(qkv_weight, out_weight)
        (own, near), high, small, (x_img, g_img, unit, inv_std) = gather_first(block, small, sizes, (tokens, cotangent))
        norms, router_t = small[:tensor_size].astype(F32), small[tensor_size : tensor_size + experts]
        high, near_first, near_second = high
        last_high = send(high, sizes, 2)
        normed, qkv_one, mixed, probs_one, weight_one, out_w = attend_first(unit, norms, owners, (own, near))
        last_high, near_second, normed = together(last_high, near_second, normed)
        parts = (high, last_high), (near_first, near_second, across_core(last_high, sizes))
        mixed, out_w, qkv_two, probs_two, weight_two = attend_second(normed, mixed, out_w, owners, parts)
    else:
        x_img, g_img, unit, inv_std = prepare(tokens, cotangent)
        weight_one, weight_two, out_w, norms, router_t = gather_weights_plain(
            qkv_weight, out_weight, router, norm_params
        )
        normed, qkv_one, mixed, probs_one = attend_first(unit, norms, (), (weight_one,))
        mixed, qkv_two, probs_two = attend_second(normed, mixed, None, (), (weight_two,))
    y, normed_two, logits, outgoing = route(x_img, mixed, out_w, norms, router_t, g_img)

    arrived = exchange(outgoing, dp_size)
    across = across_high(arrived, sizes)
    near = across_core(arrived, sizes)
    across, near, ready = lax.optimization_barrier((across, near, tuple(moe_ready(y, logits))))
    keep, keep_high, away, away_high, *kept = run_expert(
        (arrived, across), (near, across_core(across, sizes)), expert_in[0], expert_out[0]
    )
    got = across_high(add_low(keep_high, across_core(away_high, sizes)), sizes)
    got, near, (first_grad, second_grad) = lax.optimization_barrier(
        (got, across_core(away, sizes), tuple(expert_grads(*kept)))
    )
    back = exchange(add_low(keep, near, got), dp_size)

    grad_y, grad_mixed, out_grad_t, small_two = moe_back(
        ready, normed_two, g_img, back, norms, router_t, out_w, mixed, BF if stepwise else F32
    )
    grads_two, *dealt_two = attend_back(
        normed, qkv_two, probs_two, mixed, grad_mixed, out_grad_t, 1, owners, sizes
    )
    grad_part = input_part(grads_two, weight_two)
    if stepwise:
        mine = dealt_two[0].reshape(width, width)
        got, grad_part = together(across_core(dealt_two[1].reshape(width, width), sizes), grad_part)
        cut = [rows * place for place in range(9)]
        low, along = add_low(mine[: cut[3]], got[: cut[3]]), add_low(mine[cut[4] : cut[7]], got[cut[4] : cut[7]])
        across = [add_low(mine[at : at + rows], got[at : at + rows]) for at in (cut[3], cut[7])]
        low, along, across, grad_mixed = together(low, along, jnp.concatenate(across, axis=0), grad_mixed)
        along, across = send(along, sizes, 2), across_high(across, sizes)
    grads_one, *dealt_one = attend_back(
        normed, qkv_one, probs_one, mixed, grad_mixed, out_grad_t, 0, owners, sizes
    )
    if stepwise:
        along, across, mine, sent, grads_one = together(along, across, *dealt_one, grads_one)
        mine, sent = mine.reshape(width, width), sent.reshape(width, width)
        got = across_core(sent[cut[4] :], sizes)
        high = [
            add_low(mine[cut[4] : cut[7]], got[: cut[3]]),
            add_low(mine[cut[7] :], got[cut[3] :], across[rows:]),
        ]
        low = add_low(low, along)
        high, low, grads_one, sent = together(jnp.concatenate(high, axis=0), low, grads_one, sent)
        got, near = send(high, sizes, 2), across_core(sent[: cut[4]], sizes)
        got_high, got_low = across_high(low[cut[2] :], sizes), across_high(low[: cut[2]], sizes)
    grad_one, small_one = input_sum(unit, grads_one, grad_part, weight_one)
    small = jnp.concatenate([small_one[0:2], small_two[0:2], small_two[8:]], axis=0)
    if stepwise:
        near, small = together(near, small)
        small = jnp.pad(small.astype(BF), ((0, -small.shape[0] % 16), (0, 0)))
        smalls = across_high(small, sizes), send(small, sizes, 2), across_high(small, sizes, 2)
        got, got_high, near, smalls = together(got, got_high, near, smalls)
        small = add_low(small, *smalls)
        held = mine[: cut[4]], near, got
        low = add_low(*(h[: cut[2]] for h in held))
        high = [
            add_low(*(h[cut[2] : cut[3]] for h in held), got_high),
            add_low(*(h[cut[3] : cut[4]] for h in held), across[:rows]),
            small,
        ]
        low, high, grad_one = together(low, jnp.concatenate(high, axis=0), grad_one)
    input_grad = input_back(unit, inv_std, grad_y, grad_one, norms)
    output = block_output(y, logits, back)
    if stepwise:
        got, got_low, input_grad = together(send(high, sizes, 1), got_low, input_grad)
        low = add_low(low, got[: cut[2]], got_low)
        small = add_low(small, got[cut[2] :])
        near, corner = across_core(small, sizes), across_core_after(small, sizes, 0)
        got, output, near, corner = together(
            send(jnp.concatenate([low[rows:], small], axis=0), sizes, 0), output, near, corner
        )
        low = jnp.concatenate([low[:rows], small], axis=0)
        qkv_grad, out_grad, norm_grad, router_grad = unpack(index, low, got, near, corner, sizes)
        router_grad = router_grad.reshape(columns, 1)
    else:
        small = sum_small(small, sizes)
        full = jnp.concatenate(
            [dealt_one[0].reshape(width, 3, half), dealt_two[0].reshape(width, 3, half)], axis=2
        ).transpose(1, 0, 2)
        qkv_grad = lax.psum_scatter(full, "dp", scatter_dimension=1, tiled=True)
        qkv_grad = lax.psum_scatter(qkv_grad, "tensor", scatter_dimension=2, tiled=True)
        out_grad = lax.psum_scatter(out_grad_t.T, "dp", scatter_dimension=1, tiled=True)
        out_grad = lax.psum_scatter(out_grad, "tensor", scatter_dimension=0, tiled=True)
        norm_grad = lax.dynamic_slice(small, (tensor_index, dp_index * rows), (1, rows))
        router_grad = lax.dynamic_slice(
            small, (tensor_size + dp_index, tensor_index * columns), (1, columns)
        ).reshape(columns, 1)
    return (
        output,
        input_grad,
        qkv_grad,
        out_grad,
        router_grad,
        norm_grad,
        first_grad[None],
        second_grad[None],
    )


def solution(mesh):
    sizes = (mesh.shape["dp"], mesh.shape["tensor"])
    return jax.shard_map(
        functools.partial(on_device, sizes),
        mesh=mesh,
        in_specs=(
            P(("dp", "tensor"), None),
            P(None, "dp", "tensor"),
            P("tensor", "dp"),
            P("tensor", "dp"),
            P("tensor", "dp"),
            P("dp", None, "tensor"),
            P("dp", "tensor", None),
            P(("dp", "tensor"), None),
        ),
        out_specs=(
            P(("dp", "tensor"), None),
            P(("dp", "tensor"), None),
            P(None, "dp", "tensor"),
            P("tensor", "dp"),
            P("tensor", "dp"),
            P("tensor", "dp"),
            P("dp", None, "tensor"),
            P("dp", "tensor", None),
        ),
        check_vma=False,
    )
```

```python
import functools

import jax
import jax.numpy as jnp
from jax import lax
from jax.experimental import pallas as pl
from jax.experimental.pallas import tpu as pltpu
from jax.sharding import PartitionSpec as P

HEAD_DIM = 64
SEQ = 197
PAD = 208
BLOCK = 8
AXES = ("dp", "tensor")
BF = jnp.bfloat16
F32 = jnp.float32
LAST = (((1,), (1,)), ((), ()))
FIRST = (((0,), (0,)), ((), ()))
MIDDLE = (((1,), (0,)), ((), ()))
MIB = 1024 * 1024


def dot(a, b, dims=MIDDLE):
    return lax.dot_general(a, b, dims, preferred_element_type=F32)


def shape_of(shape, dtype):
    return jax.ShapeDtypeStruct(shape, dtype)


def run(kernel, name, operands, results, limit, scratch=(), scalars=0, aliases=()):
    memory = [pltpu.SMEM] * scalars + [pltpu.VMEM] * (len(operands) - scalars)
    return pl.pallas_call(
        kernel,
        in_specs=[pl.BlockSpec(memory_space=m) for m in memory],
        out_specs=[pl.BlockSpec(memory_space=pltpu.VMEM) for _ in results],
        out_shape=list(results),
        scratch_shapes=list(scratch),
        input_output_aliases=dict(aliases),
        compiler_params=pltpu.CompilerParams(vmem_limit_bytes=limit * MIB),
        cost_estimate=pl.CostEstimate(flops=1, bytes_accessed=1, transcendentals=0),
        name=name,
    )(*operands)


def layer_stats(values):
    centre = jnp.mean(values, axis=-1, keepdims=True)
    centred = values - centre
    spread = jnp.mean(centred * centred, axis=-1, keepdims=True)
    inv_std = lax.rsqrt(spread + 1e-06)
    return centred * inv_std, inv_std


def lane_ids(shape):
    return lax.broadcasted_iota(jnp.int32, shape, len(shape) - 1)


def row_ids(shape):
    return lax.broadcasted_iota(jnp.int32, shape, len(shape) - 2)


def flat(ref):
    images, rows, columns = ref.shape
    return ref[...].reshape(images * rows, columns)


def prepare_kernel(x_ref, g_ref, x_out, g_out, unit_out, inv_out, wide):
    count, width = x_ref.shape
    real = row_ids((PAD, width)) < SEQ
    wide[count:, :] = jnp.zeros((wide.shape[0] - count, width), F32)
    for ref, out in ((x_ref, x_out), (g_ref, g_out)):
        wide[0:count, :] = ref[...].astype(F32)
        for i in range(out.shape[0]):
            rows = jnp.where(real, wide[SEQ * i : SEQ * i + PAD, :], 0.0)
            out[i] = rows.astype(BF)
            if ref is x_ref:
                unit_out[i], inv_out[i] = layer_stats(rows)


def prepare(tokens, cotangent):
    count, width = tokens.shape
    images = count // SEQ
    rows = shape_of((images, PAD, width), BF)
    return run(
        prepare_kernel,
        "prepare",
        (tokens, cotangent),
        (rows, rows, shape_of((images, PAD, width), F32), shape_of((images, PAD, 1), F32)),
        8,
        scratch=[pltpu.VMEM((-(-count // 8) * 8 + 16, width), F32)],
    )


def attend_rows(normed, w_ref, qkv_ref, mixed_ref, probs_ref, piece):
    images, rows, width = mixed_ref.shape
    span = width // 2
    low = lane_ids((rows, 128)) < HEAD_DIM
    key_ok = row_ids((rows, rows)) < SEQ
    zero = jnp.zeros((rows, 128), BF)
    proj = dot(normed, w_ref[...])
    qkv_ref[:, :, 0:span] = (proj[:, 0:span] * HEAD_DIM ** (-0.5)).astype(BF).reshape(images, rows, span)
    qkv_ref[:, :, span:] = proj[:, span:].astype(BF).reshape(images, rows, 2 * span)

    def image(i, carry):
        for p in range(span // 128):
            at = slice(p * 128, (p + 1) * 128)
            q = qkv_ref[i, :, at]
            k = qkv_ref[i, :, span + p * 128 : span + (p + 1) * 128]
            v = qkv_ref[i, :, 2 * span + p * 128 : 2 * span + (p + 1) * 128]
            mixed = []
            for h in range(2):
                q_one = jnp.where(low, q, zero) if h == 0 else jnp.where(low, zero, q)
                scores = jnp.where(key_ok, dot(k, q_one, LAST), -1e30)
                scaled = jnp.exp(scores - jnp.max(scores, axis=0, keepdims=True))
                weights = (scaled * (1.0 / jnp.sum(scaled, axis=0, keepdims=True))).astype(BF)
                probs_ref[i, 2 * p + h] = weights
                mixed.append(dot(weights, v, FIRST))
            at = slice(piece * span + p * 128, piece * span + (p + 1) * 128)
            mixed_ref[i, :, at] = jnp.where(low, mixed[0], mixed[1]).astype(BF)
        return carry

    lax.fori_loop(0, images, image, 0, unroll=3 if images % 3 == 0 else 1)


def assemble_rows(owners, parts, kinds, out_ref, columns, lane=0):
    for side, (owner, refs) in enumerate(zip(owners, parts, strict=True)):
        count = out_ref.shape[0] // owner.shape[0]
        blocks = [ref[i * count : (i + 1) * count] for ref in refs for i in range(ref.shape[0] // count)]
        for p, block in enumerate(blocks):
            row = pl.multiple_of(count * owner[p], 16)
            for at, kind in enumerate(kinds):
                to = lane + (2 * at + side) * columns
                out_ref[pl.ds(row, count), to : to + columns] = block[:, kind * columns : (kind + 1) * columns]


def attend_first_kernel(counts, *refs):
    if counts:
        own, sib = counts
        owners, refs = refs[:2], refs[2:]
        unit_ref, norms_ref, refs = refs[0], refs[1], refs[2:]
        parts, refs = (refs[:own], refs[own : own + sib]), refs[own + sib :]
        n_ref, qkv_ref, mixed_ref, probs_ref, w_ref, out_w_ref = refs
        columns = w_ref.shape[1] // 6
        assemble_rows(owners, parts, range(3), w_ref, columns)
        assemble_rows(owners, parts, [3], out_w_ref, columns)
    else:
        unit_ref, norms_ref, w_ref, n_ref, qkv_ref, mixed_ref, probs_ref = refs
    normed = (flat(unit_ref) * norms_ref[0:1, :] + norms_ref[1:2, :]).astype(BF)
    n_ref[...] = normed.reshape(n_ref.shape)
    attend_rows(normed, w_ref, qkv_ref, mixed_ref, probs_ref, 0)


def attend_second_kernel(counts, *refs):
    if counts:
        own, sib = counts
        owners, refs = refs[:2], refs[2:]
        n_ref, refs = refs[0], refs[3:]
        parts, refs = (refs[:own], refs[own : own + sib]), refs[own + sib :]
        mixed_ref, out_w_ref, qkv_ref, probs_ref, w_ref = refs
        columns = w_ref.shape[1] // 6
        assemble_rows(owners, parts, range(3), w_ref, columns)
        assemble_rows(owners, parts, [3], out_w_ref, columns, 2 * columns)
    else:
        n_ref, _, w_ref, mixed_ref, qkv_ref, probs_ref = refs
    attend_rows(flat(n_ref), w_ref, qkv_ref, mixed_ref, probs_ref, 1)


def attend_first(unit, norms, owners, weights):
    images, rows, width = unit.shape
    span = width // 2
    results = (
        shape_of(unit.shape, BF),
        shape_of((images, rows, 3 * span), BF),
        shape_of(unit.shape, BF),
        shape_of((images, span // HEAD_DIM, rows, rows), BF),
    )
    counts = None
    if owners:
        counts = tuple(map(len, weights))
        weights = sum(weights, ())
        results += (shape_of((width, 3 * span), BF), shape_of((width, width), BF))
    return run(
        functools.partial(attend_first_kernel, counts),
        "attend_first",
        owners + (unit, norms) + weights,
        results,
        4,
        scalars=len(owners),
    )


def attend_second(normed, mixed, out_w, owners, weights):
    images, rows, width = normed.shape
    span = width // 2
    given = (mixed, out_w) if owners else (mixed,)
    results = tuple(shape_of(g.shape, BF) for g in given) + (
        shape_of((images, rows, 3 * span), BF),
        shape_of((images, span // HEAD_DIM, rows, rows), BF),
    )
    counts = None
    if owners:
        counts = tuple(map(len, weights))
        weights = sum(weights, ())
        results += (shape_of((width, 3 * span), BF),)
    return run(
        functools.partial(attend_second_kernel, counts),
        "attend_second",
        owners + (normed,) + given + weights,
        results,
        4,
        scalars=len(owners),
        aliases=[(len(owners) + 1 + i, i) for i in range(len(given))],
    )


def softmaxes(logits):
    ok = lane_ids(logits.shape) < SEQ
    masked = jnp.where(ok, logits, -1e30)
    up = jnp.exp(masked - jnp.max(masked, axis=1, keepdims=True))
    dispatch = up / jnp.sum(up, axis=1, keepdims=True)
    up = jnp.exp(logits - jnp.max(logits, axis=0, keepdims=True))
    combine = up / jnp.sum(up, axis=0, keepdims=True)
    return dispatch, combine


def by_image(experts, places, low, back=False):
    shape = (experts * BLOCK, places * experts)
    shape = shape[::-1] if back else shape
    blocked, other = (lane_ids(shape), row_ids(shape)) if back else (row_ids(shape), lane_ids(shape))
    place = jnp.bitwise_and(blocked, BLOCK - 1) - low
    inside = jnp.logical_and(place >= 0, place < places)
    return jnp.logical_and(inside, other == place * experts + lax.div(blocked, BLOCK)).astype(BF)


def to_blocks(first, second):
    experts, width = first[0].shape
    half = width // 2
    head = dot(by_image(experts, BLOCK, 0), jnp.concatenate(first + second[:2], axis=0))
    rest = jnp.concatenate(second[2:], axis=0)
    rest = dot(by_image(experts, 4, 0), rest[:, :half]) + dot(by_image(experts, 4, 4), rest[:, half:])
    return head.astype(BF), rest.astype(BF)


def from_blocks(blocks, experts, width):
    head = dot(by_image(experts, BLOCK, 0, True), blocks[:, :width])
    rest = [dot(by_image(experts, 4, low, True), blocks[:, width:]) for low in (0, 4)]
    rest = jnp.concatenate(rest, axis=1)
    head, rest = ([v[at : at + experts].astype(BF) for at in range(0, v.shape[0], experts)] for v in (head, rest))
    return head[:6], head[6:] + rest


def route_kernel(
    x_ref, mixed_ref, out_w_ref, norms_ref, router_ref, g_ref, y_ref, n_ref, logits_ref, send_ref
):
    images, rows, width = x_ref.shape
    experts = router_ref.shape[0]
    for at in range(0, images, 2):
        some = slice(at, min(at + 2, images))
        y = flat(x_ref.at[some]).astype(F32) + dot(flat(mixed_ref.at[some]), out_w_ref[...], LAST)
        y_ref[some] = y.reshape(-1, rows, width)
        unit, _ = layer_stats(y)
        n_ref[some] = (unit * norms_ref[2:3, :] + norms_ref[3:4, :]).astype(BF).reshape(-1, rows, width)
    first, second = [], []
    for i in range(images):
        logits = dot(router_ref[...], n_ref[i], LAST)
        logits_ref[i] = logits
        dispatch, combine = softmaxes(logits)
        first.append(dot(dispatch.astype(BF), n_ref[i]).astype(BF))
        second.append(dot(combine.astype(BF), g_ref[i]).astype(BF))
    send_ref[:, :width], send_ref[:, width:] = to_blocks(first, second)


def route(x_img, mixed, out_w, norms, router, g_img):
    images, rows, width = x_img.shape
    experts = router.shape[0]
    return run(
        route_kernel,
        "route",
        (x_img, mixed, out_w, norms, router, g_img),
        (
            shape_of((images, rows, width), F32),
            shape_of((images, rows, width), BF),
            shape_of((images, experts, rows), F32),
            shape_of((experts * BLOCK, width + width // 2), BF),
        ),
        4,
    )


def turned(blocks, shift):
    return pltpu.roll(blocks, shift, 1)


def split_rows(blocks):
    rows, lanes = blocks.shape
    width = lanes // 3 * 2
    wide = blocks.astype(F32).reshape(rows // BLOCK, BLOCK, lanes)
    head, rest = wide[:, :, :width], wide[:, :, width:]
    place = row_ids(head.shape)
    first = jnp.where(place < 6, head, 0.0)
    second = jnp.concatenate([turned(rest, 2), turned(rest, BLOCK - 2)], axis=2)
    second = jnp.where(place < 2, turned(head, 2), jnp.where(place < 6, second, 0.0))
    return first.reshape(rows, width).astype(BF), second.reshape(rows, width).astype(BF)


def join_rows(first, second):
    rows, width = first.shape
    half = width // 2
    first = first.reshape(rows // BLOCK, BLOCK, width)
    second = second.reshape(rows // BLOCK, BLOCK, width)
    head = jnp.where(row_ids(first.shape) < 6, first, turned(second, 6))
    left, right = turned(second[:, :, :half], BLOCK - 2), turned(second[:, :, half:], 2)
    rest = jnp.where(row_ids(left.shape) < 4, left, right)
    return head.reshape(rows, width).astype(BF), rest.reshape(rows, half).astype(BF)


def gelu_parts(pre):
    cdf = 0.5 * (1.0 + lax.erf(pre * (0.5**0.5)))
    density = jnp.exp(-0.5 * pre * pre) * 0.3989422804014327
    return pre * cdf, cdf + pre * density


def expert_kernel(a_ref, b_ref, c_ref, d_ref, w1_ref, w2_ref, *refs):
    outs, (slots_ref, grads_ref, hidden_ref, pre_ref) = refs[:4], refs[4:]
    width = w1_ref.shape[0]
    count = a_ref.shape[0]
    blocks = jnp.concatenate([a_ref[...], b_ref[...], c_ref[...], d_ref[...]], axis=0)
    step = min(4 * count, 256)
    for at in range(0, 4 * count, step):
        slots_ref[at : at + step], grads_ref[at : at + step] = split_rows(blocks[at : at + step])
    slots, grads = slots_ref[...], grads_ref[...]
    pre = dot(slots, w1_ref[...])
    hidden, slope = gelu_parts(pre)
    hidden = hidden.astype(BF)
    returned = dot(hidden, w2_ref[...])
    grad_pre = (dot(grads, w2_ref[...], LAST) * slope).astype(BF)
    grad_slots = dot(grad_pre, w1_ref[...], LAST)
    parts = [join_rows(returned[at : at + step], grad_slots[at : at + step]) for at in range(0, 4 * count, step)]
    head, rest = (jnp.concatenate(p, axis=0) for p in zip(*parts, strict=True))
    for i, ref in enumerate(outs):
        ref[:, :width] = head[i * count : (i + 1) * count]
        ref[:, width:] = rest[i * count : (i + 1) * count]
    hidden_ref[...] = hidden
    pre_ref[...] = grad_pre


def run_expert(own, near, first_weight, second_weight):
    width, units = first_weight.shape
    rows = 4 * own[0].shape[0]
    return run(
        expert_kernel,
        "expert",
        own + near + (first_weight, second_weight),
        (shape_of(own[0].shape, BF),) * 4
        + (
            shape_of((rows, width), BF),
            shape_of((rows, width), BF),
            shape_of((rows, units), BF),
            shape_of((rows, units), BF),
        ),
        8 if rows <= 512 else 48,
    )


def expert_grad_kernel(slots_ref, grads_ref, hidden_ref, pre_ref, d1_ref, d2_ref):
    d1_ref[...] = dot(slots_ref[...], pre_ref[...], FIRST)
    d2_ref[...] = dot(hidden_ref[...], grads_ref[...], FIRST)


def expert_grads(slots, grads, hidden, grad_pre):
    rows, width = slots.shape
    units = hidden.shape[1]
    return run(
        expert_grad_kernel,
        "expert_grads",
        (slots, grads, hidden, grad_pre),
        (shape_of((width, units), F32), shape_of((units, width), F32)),
        6 if rows <= 512 else 32,
    )


def moe_ready_kernel(y_ref, logits_ref, unit_ref, inv_ref, dispatch_ref, combine_ref):
    unit, inv_std = layer_stats(flat(y_ref))
    unit_ref[...] = unit.reshape(unit_ref.shape)
    inv_ref[...] = inv_std.reshape(inv_ref.shape)
    for i in range(y_ref.shape[0]):
        dispatch_ref[i], combine_ref[i] = softmaxes(logits_ref[i])


def moe_ready(y, logits):
    images, rows, width = y.shape
    return run(
        moe_ready_kernel,
        "moe_ready",
        (y, logits),
        (
            shape_of((images, rows, width), F32),
            shape_of((images, rows, 1), F32),
            shape_of(logits.shape, F32),
            shape_of(logits.shape, F32),
        ),
        4,
    )


def moe_back_kernel(
    unit_ref,
    inv_ref,
    dispatch_ref,
    combine_ref,
    n_ref,
    g_ref,
    back_ref,
    norms_ref,
    router_ref,
    out_w_ref,
    mixed_ref,
    grad_y_ref,
    grad_mixed_ref,
    out_grad_ref,
    small_ref,
    attn_ref,
):
    images, rows, width = unit_ref.shape
    experts = router_ref.shape[0]
    gain = norms_ref[2:3, :]
    all_returned, all_slots = from_blocks(back_ref[...], experts, width)
    router_grad, gain_grad, shift_grad = 0.0, 0.0, 0.0
    for i in range(images):
        returned, grad_slots = all_returned[i], all_slots[i]
        dispatch, combine = dispatch_ref[i], combine_ref[i]
        grad_combine = dot(returned, g_ref[i], LAST)
        grad_dispatch = dot(grad_slots, n_ref[i], LAST)
        grad_logits = dispatch * (
            grad_dispatch - jnp.sum(grad_dispatch * dispatch, axis=1, keepdims=True)
        ) + combine * (grad_combine - jnp.sum(grad_combine * combine, axis=0, keepdims=True))
        grad_logits = grad_logits.astype(BF)
        router_grad = router_grad + dot(grad_logits, n_ref[i])
        grad_two = dot(
            jnp.concatenate([dispatch.astype(BF), grad_logits], axis=0),
            jnp.concatenate([grad_slots, router_ref[...]], axis=0),
            FIRST,
        )
        unit, inv_std = unit_ref[i], inv_ref[i]
        gain_grad = gain_grad + jnp.sum(grad_two * unit, axis=0, keepdims=True)
        shift_grad = shift_grad + jnp.sum(grad_two, axis=0, keepdims=True)
        scaled = grad_two * gain
        mean_one = jnp.mean(scaled, axis=-1, keepdims=True)
        mean_two = jnp.mean(scaled * unit, axis=-1, keepdims=True)
        grad_y = g_ref[i].astype(F32) + inv_std * (scaled - mean_one - unit * mean_two)
        grad_y_ref[i] = grad_y
        attn_ref[i] = grad_y.astype(BF)
    small_ref[...] = jnp.zeros_like(small_ref)
    small_ref[0:1, :] = gain_grad
    small_ref[1:2, :] = shift_grad
    small_ref[8 : 8 + experts, :] = router_grad
    grad_attn = flat(attn_ref)
    grad_mixed_ref[...] = dot(grad_attn, out_w_ref[...]).astype(BF).reshape(grad_mixed_ref.shape)
    out_grad_ref[...] = dot(grad_attn, flat(mixed_ref), FIRST).astype(out_grad_ref.dtype)


def moe_back(ready, normed, g_img, back, norms, router, out_w, mixed, dtype):
    images, rows, width = normed.shape
    experts = router.shape[0]
    return run(
        moe_back_kernel,
        "moe_back",
        ready + (normed, g_img, back, norms, router, out_w, mixed),
        (
            shape_of((images, rows, width), F32),
            shape_of((images, rows, width), BF),
            shape_of((width, width), dtype),
            shape_of((8 + experts, width), F32),
        ),
        10,
        scratch=[pltpu.VMEM((images, rows, width), BF)],
    )


def output_kernel(y_ref, logits_ref, back_ref, out_ref, wide):
    images, experts, _ = logits_ref.shape
    all_returned, _ = from_blocks(back_ref[...], experts, y_ref.shape[2])
    for i in range(images):
        returned = all_returned[i]
        _, combine = softmaxes(logits_ref[i])
        total = y_ref[i] + dot(combine.astype(BF), returned, FIRST)
        wide[SEQ * i : SEQ * (i + 1), :] = total[0:SEQ]
    out_ref[...] = wide[...].astype(BF)


def block_output(y, logits, back):
    images, rows, width = y.shape
    count = images * SEQ
    return run(
        output_kernel,
        "block_output",
        (y, logits, back),
        (shape_of((count, width), BF),),
        7,
        scratch=[pltpu.VMEM((count, width), F32)],
    )[0]


def deal_rows(owners, full_ref, first, kinds, refs, columns):
    for side, (owner, ref) in enumerate(zip(owners, refs, strict=True)):
        blocks, count, _ = ref.shape
        for p in range(blocks):
            row = pl.multiple_of(count * owner[p], 16)
            for at, kind in enumerate(kinds):
                lane = first + (2 * at + side) * columns
                ref[p, :, kind * columns : (kind + 1) * columns] = full_ref[pl.ds(row, count), lane : lane + columns]


def attend_back_kernel(stepwise, piece, *refs):
    if stepwise:
        owners, refs = refs[:2], refs[2:]
        n_ref, qkv_ref, probs_ref, mixed_ref, gm_ref, og_ref, grads_ref, own_ref, sib_ref, dw_ref = refs
    else:
        n_ref, qkv_ref, probs_ref, mixed_ref, gm_ref, grads_ref, dw_ref = refs
    images, rows, width = mixed_ref.shape
    span = width // 2
    low = lane_ids((rows, 128)) < HEAD_DIM
    zero = jnp.zeros((rows, 128), BF)
    minus = jnp.full((rows, 128), -1.0, BF)

    def image(i, carry):
        for p in range(span // 128):
            at = slice(p * 128, (p + 1) * 128)
            at_k = slice(span + p * 128, span + (p + 1) * 128)
            at_v = slice(2 * span + p * 128, 2 * span + (p + 1) * 128)
            q, k, v = qkv_ref[i, :, at], qkv_ref[i, :, at_k], qkv_ref[i, :, at_v]
            here = slice(piece * span + p * 128, piece * span + (p + 1) * 128)
            gm = gm_ref[i, :, here]
            inner = pltpu.roll(gm.astype(F32) * mixed_ref[i, :, here].astype(F32), HEAD_DIM, 1).astype(BF)
            grad_q, grad_k, grad_v = 0.0, 0.0, 0.0
            for h in range(2):
                mine = low if h == 0 else jnp.logical_not(low)
                weights = probs_ref[i, 2 * p + h]
                centred = dot(jnp.where(mine, v, minus), jnp.where(mine, gm, inner), LAST)
                grad_scores = (weights.astype(F32) * centred).astype(BF)
                grad_v = grad_v + dot(weights, jnp.where(mine, gm, zero))
                grad_k = grad_k + dot(grad_scores, jnp.where(mine, q, zero))
                grad_q = grad_q + dot(grad_scores, jnp.where(mine, k, zero), FIRST)
            grads_ref[i, :, at] = (grad_q * HEAD_DIM ** (-0.5)).astype(BF)
            grads_ref[i, :, at_k] = grad_k.astype(BF)
            grads_ref[i, :, at_v] = grad_v.astype(BF)
        return carry

    lax.fori_loop(0, images, image, 0, unroll=images)
    dw_ref[...] = dot(flat(n_ref), flat(grads_ref), FIRST).astype(dw_ref.dtype)
    if stepwise:
        deal_rows(owners, dw_ref, 0, range(3), (own_ref, sib_ref), span // 2)
        deal_rows(owners, og_ref, piece * span, [3], (own_ref, sib_ref), span // 2)


def attend_back(normed, qkv, probs, mixed, grad_mixed, out_grad_t, piece, owners, sizes):
    images, rows, width = normed.shape
    span = width // 2
    operands = (normed, qkv, probs, mixed, grad_mixed)
    results = (shape_of((images, rows, 3 * span), BF),)
    scratch = ()
    if owners:
        operands += (out_grad_t,)
        results += (shape_of((sizes[0], width // sizes[0], 2 * span), BF),) * 2
        scratch = (pltpu.VMEM((width, 3 * span), BF),)
    else:
        results += (shape_of((width, 3 * span), F32),)
    return run(
        functools.partial(attend_back_kernel, bool(owners), piece),
        "attend_back",
        owners + operands,
        results,
        7,
        scratch,
        scalars=len(owners),
    )


def input_part_kernel(p_ref, w_ref, out_ref):
    out_ref[...] = dot(flat(p_ref), w_ref[...], LAST).reshape(out_ref.shape)


def input_part(grads, weight):
    images, rows, _ = grads.shape
    return run(
        input_part_kernel, "input_part", (grads, weight), (shape_of((images, rows, weight.shape[0]), F32),), 6
    )[0]


def input_sum_kernel(unit_ref, p1_ref, part_ref, w1_ref, grad_ref, small_ref):
    images, rows, width = unit_ref.shape
    gain_grad, shift_grad = 0.0, 0.0
    for i in range(images):
        if i % 2 == 0:
            some = slice(i, min(i + 2, images))
            grad = dot(flat(p1_ref.at[some]), w1_ref[...], LAST) + flat(part_ref.at[some])
            grad_ref[some] = grad.reshape(-1, rows, width)
        gain_grad = gain_grad + jnp.sum(grad_ref[i] * unit_ref[i], axis=0, keepdims=True)
        shift_grad = shift_grad + jnp.sum(grad_ref[i], axis=0, keepdims=True)
    small_ref[...] = jnp.zeros_like(small_ref)
    small_ref[0:1, :] = gain_grad
    small_ref[1:2, :] = shift_grad


def input_sum(unit, grads_one, grad_part, weight_one):
    width = unit.shape[2]
    return run(
        input_sum_kernel,
        "input_sum",
        (unit, grads_one, grad_part, weight_one),
        (shape_of(unit.shape, F32), shape_of((8, width), F32)),
        7,
    )


def input_back_kernel(unit_ref, inv_ref, gy_ref, grad_ref, norms_ref, out_ref):
    gain = norms_ref[0:1, :]
    for i in range(unit_ref.shape[0]):
        unit, inv_std = unit_ref[i], inv_ref[i]
        scaled = grad_ref[i] * gain
        mean_one = jnp.mean(scaled, axis=-1, keepdims=True)
        mean_two = jnp.mean(scaled * unit, axis=-1, keepdims=True)
        total = gy_ref[i] + inv_std * (scaled - mean_one - unit * mean_two)
        out_ref[SEQ * i : SEQ * (i + 1), :] = total[0:SEQ]


def input_back(unit, inv_std, grad_y, grad_one, norms):
    images, _, width = unit.shape
    return run(
        input_back_kernel,
        "input_back",
        (unit, inv_std, grad_y, grad_one, norms),
        (shape_of((images * SEQ, width), F32),),
        9,
    )[0]


def spot(shape, start):
    return (lane_ids(shape) == row_ids(shape) + start).astype(BF)


def place_kernel(rows, index_ref, pair_ref, small_ref):
    columns, width = pair_ref.shape[1], small_ref.shape[1]
    dp_index, tensor_index = index_ref[0], index_ref[1]
    shape = (columns, width)
    inside = jnp.logical_and(lane_ids(shape) == row_ids(shape) + dp_index * rows, row_ids(shape) < rows)
    norm = dot(jnp.broadcast_to(pair_ref[0:1], (16, columns)), inside.astype(BF))
    router = dot(jnp.broadcast_to(pair_ref[1:2], (16, columns)), spot(shape, tensor_index * columns))
    row = row_ids(small_ref.shape)
    small_ref[...] = jnp.where(
        row == tensor_index, norm[0:1], jnp.where(row == width // columns + dp_index, router[0:1], 0.0)
    ).astype(BF)


def place(index, norm_params, router, experts):
    rows, columns = norm_params.shape[1], router.shape[0]
    width = rows * experts
    pair = jnp.concatenate([jnp.pad(norm_params, ((0, 0), (0, columns - rows))), router.T], axis=0)
    return run(
        functools.partial(place_kernel, rows),
        "place",
        (index, pair),
        (shape_of((-(-(width // columns + experts) // 16) * 16, width), BF),),
        4,
        scalars=1,
    )[0]


def pack_kernel(qkv_ref, out_ref, block_ref):
    kinds, _, columns = qkv_ref.shape
    for kind in range(kinds):
        block_ref[:, kind * columns : (kind + 1) * columns] = qkv_ref[kind]
    block_ref[:, kinds * columns :] = out_ref[...].T


def pack(qkv_weight, out_weight):
    kinds, rows, columns = qkv_weight.shape
    return run(
        pack_kernel,
        "pack",
        (qkv_weight, out_weight),
        (shape_of((rows, (kinds + 1) * columns), BF),),
        4,
    )[0]


def unpack_kernel(index_ref, own_ref, got_ref, near_ref, corner_ref, qkv_ref, out_ref, norm_ref, router_ref):
    kinds, rows, columns = qkv_ref.shape
    total = own_ref[...].astype(F32) + got_ref[...].astype(F32)
    for kind in range(kinds):
        qkv_ref[kind] = total[0:rows, kind * columns : (kind + 1) * columns]
    out_ref[...] = total[0:rows, kinds * columns :].T
    small = total[rows:] + near_ref[...].astype(F32) + corner_ref[...].astype(F32)
    dp_index, tensor_index = index_ref[0], index_ref[1]
    width = small.shape[1]
    row = row_ids(small.shape)
    norm = jnp.sum(jnp.where(row == tensor_index, small, 0.0), axis=0, keepdims=True)
    router = jnp.sum(jnp.where(row == width // columns + dp_index, small, 0.0), axis=0, keepdims=True)
    pair = jnp.concatenate([norm, router, jnp.zeros((6, width), F32)], axis=0)
    high = pair.astype(BF)
    parts = jnp.concatenate([high, (pair - high.astype(F32)).astype(BF)], axis=0)
    spots = [spot((rows, width), dp_index * rows), spot((columns, width), tensor_index * columns)]
    moved = [dot(parts, at, LAST) for at in spots]
    norm_ref[...] = moved[0][0:1] + moved[0][8:9]
    router_ref[...] = moved[1][1:2] + moved[1][9:10]


def unpack(index, own, got, near, corner, sizes):
    width = own.shape[1]
    rows, columns = width // sizes[0], width // sizes[1]
    return run(
        unpack_kernel,
        "unpack",
        (index, own, got, near, corner),
        (
            shape_of((width // columns - 1, rows, columns), F32),
            shape_of((columns, rows), F32),
            shape_of((1, rows), F32),
            shape_of((1, columns), F32),
        ),
        4,
        scalars=1,
    )


def swap(value, dp_size, tensor_size, dp_mask, tensor_mask):
    pairs = [
        (d * tensor_size + t, (d ^ dp_mask) * tensor_size + (t ^ tensor_mask))
        for d in range(dp_size)
        for t in range(tensor_size)
    ]
    return lax.ppermute(value, AXES, pairs)


def steps_of(dp_size):
    bits = dp_size.bit_length() - 1
    down = list(range(bits))[::-1]
    return [down, down[-1:] + down[:-1]]


def step_pairs(dp_size, tensor_size, *steps):
    masks = [functools.reduce(lambda mask, step: mask ^ (1 << order[step]), steps, 0) for order in steps_of(dp_size)]
    return [
        (d * tensor_size + t, (d ^ masks[t % 2]) * tensor_size + t)
        for d in range(dp_size)
        for t in range(tensor_size)
    ]


def owners_of(dp_size, dp_index, core):
    both = []
    for order in steps_of(dp_size):
        place = jnp.arange(dp_size, dtype=jnp.int32)
        away = jnp.zeros_like(place)
        for step, bit in enumerate(order):
            away = away | (((place >> step) & 1) << bit)
        both.append(away ^ dp_index)
    return jnp.where(core == 0, both[0], both[1]), jnp.where(core == 0, both[1], both[0])


def exchange(blocks, dp_size):
    shape = blocks.shape
    blocks = blocks.reshape(dp_size, shape[0] // dp_size, shape[1])
    return lax.all_to_all(blocks, "dp", split_axis=0, concat_axis=0, tiled=True).reshape(shape)


def together(*values):
    return lax.optimization_barrier(values)


def send(value, sizes, *steps):
    return lax.ppermute(value, AXES, step_pairs(*sizes, *steps))


def across_core(value, sizes):
    return swap(value, *sizes, 0, 1)


def across_core_after(value, sizes, step):
    pairs = [(a, b ^ 1) for a, b in step_pairs(*sizes, step)]
    return lax.ppermute(value, AXES, pairs)


def high_pairs(dp_size, tensor_size, *steps):
    return [(a, b ^ 2) for a, b in step_pairs(dp_size, tensor_size, *steps)]


def across_high(value, sizes, *steps):
    return lax.ppermute(value, AXES, high_pairs(*sizes, *steps))


def gather_first(block, small, sizes, along):
    rows = block.shape[0]
    far = lax.ppermute(small, AXES, [(p, q ^ 1) for p, q in high_pairs(*sizes)])
    *smalls, block = together(across_core(small, sizes), across_high(small, sizes), far, block)
    small = sum(smalls, small)
    first = jnp.concatenate([block, small], axis=0)
    got, high = together(send(first, sizes, 0), across_high(block, sizes))
    held = jnp.concatenate([block, got[:rows], small + got[rows:]], axis=0)

    got, near, high_got = together(send(held, sizes, 1), across_core(held, sizes), across_high(got[:rows], sizes))
    high = jnp.concatenate([high, high_got], axis=0)
    small = held[2 * rows :] + got[2 * rows :]
    four = jnp.concatenate([held[: 2 * rows], got[: 2 * rows], small], axis=0)

    last, near_two, high_two, high_near, along = together(
        send(four, sizes, 2), across_core(got, sizes), across_high(got[: 2 * rows], sizes), across_core(high, sizes), prepare(*along)
    )
    small = four[4 * rows :] + last[4 * rows :]
    own = (four, last), (near, near_two, across_core(last, sizes))
    high = jnp.concatenate([high, high_two], axis=0)
    return own, (high, high_near, across_core(high_two, sizes)), small, along


def gather_weights_plain(qkv_weight, out_weight, router, norm_params):
    qkv = lax.all_gather(qkv_weight, "dp", axis=1, tiled=True)
    qkv = lax.all_gather(qkv, "tensor", axis=2, tiled=True)
    out_w, router, norms = (
        lax.all_gather(lax.all_gather(w, "dp", axis=1, tiled=True), "tensor", axis=0, tiled=True)
        for w in (out_weight, router, norm_params)
    )
    width = qkv.shape[1]
    half = width // 2
    one = qkv[:, :, :half].transpose(1, 0, 2).reshape(width, 3 * half)
    two = qkv[:, :, half:].transpose(1, 0, 2).reshape(width, 3 * half)
    return one, two, out_w.T, norms.astype(F32), router.T


def add_low(*values):
    return sum(v.astype(F32) for v in values).astype(BF)


def sum_small(values, sizes):
    dp_size, tensor_size = sizes
    mask = 1
    while mask < tensor_size:
        values = values + swap(values, dp_size, tensor_size, 0, mask)
        mask *= 2
    mask = 1
    while mask < dp_size:
        values = values + swap(values, dp_size, tensor_size, mask, 0)
        mask *= 2
    return values


def on_device(
    sizes, tokens, qkv_weight, out_weight, router, norm_params, expert_in, expert_out, cotangent
):
    dp_size, tensor_size = sizes
    dp_index = lax.axis_index("dp")
    tensor_index = lax.axis_index("tensor")
    core = jnp.bitwise_and(tensor_index, 1)
    width = tokens.shape[1]
    half = width // 2
    rows = qkv_weight.shape[1]
    columns = qkv_weight.shape[2]
    experts = dp_size * router.shape[1]
    stepwise = rows % 16 == 0 and sizes == (8, 4)
    owners = ()
    if stepwise:
        owners = owners_of(dp_size, dp_index, core)
        index = jnp.stack([dp_index, tensor_index]).astype(jnp.int32)
        *owners, index, qkv_weight, out_weight, norm_params, router = together(
            *owners, index, qkv_weight, out_weight, norm_params, router
        )
        owners = tuple(owners)
        small = place(index, norm_params, router, experts)
        block = pack(qkv_weight, out_weight)
        (own, near), high, small, (x_img, g_img, unit, inv_std) = gather_first(block, small, sizes, (tokens, cotangent))
        norms, router_t = small[:tensor_size].astype(F32), small[tensor_size : tensor_size + experts]
        high, near_first, near_second = high
        last_high = send(high, sizes, 2)
        normed, qkv_one, mixed, probs_one, weight_one, out_w = attend_first(unit, norms, owners, (own, near))
        last_high, near_second, normed = together(last_high, near_second, normed)
        parts = (high, last_high), (near_first, near_second, across_core(last_high, sizes))
        mixed, out_w, qkv_two, probs_two, weight_two = attend_second(normed, mixed, out_w, owners, parts)
    else:
        x_img, g_img, unit, inv_std = prepare(tokens, cotangent)
        weight_one, weight_two, out_w, norms, router_t = gather_weights_plain(
            qkv_weight, out_weight, router, norm_params
        )
        normed, qkv_one, mixed, probs_one = attend_first(unit, norms, (), (weight_one,))
        mixed, qkv_two, probs_two = attend_second(normed, mixed, None, (), (weight_two,))
    y, normed_two, logits, outgoing = route(x_img, mixed, out_w, norms, router_t, g_img)

    arrived = exchange(outgoing, dp_size)
    across = across_high(arrived, sizes)
    near = across_core(arrived, sizes)
    across, near, ready = lax.optimization_barrier((across, near, tuple(moe_ready(y, logits))))
    keep, keep_high, away, away_high, *kept = run_expert(
        (arrived, across), (near, across_core(across, sizes)), expert_in[0], expert_out[0]
    )
    got = across_high(add_low(keep_high, across_core(away_high, sizes)), sizes)
    got, near, (first_grad, second_grad) = lax.optimization_barrier(
        (got, across_core(away, sizes), tuple(expert_grads(*kept)))
    )
    back = exchange(add_low(keep, near, got), dp_size)

    grad_y, grad_mixed, out_grad_t, small_two = moe_back(
        ready, normed_two, g_img, back, norms, router_t, out_w, mixed, BF if stepwise else F32
    )
    grads_two, *dealt_two = attend_back(
        normed, qkv_two, probs_two, mixed, grad_mixed, out_grad_t, 1, owners, sizes
    )
    grad_part = input_part(grads_two, weight_two)
    if stepwise:
        mine = dealt_two[0].reshape(width, width)
        got, grad_part = together(across_core(dealt_two[1].reshape(width, width), sizes), grad_part)
        cut = [rows * place for place in range(9)]
        low, along = add_low(mine[: cut[3]], got[: cut[3]]), add_low(mine[cut[4] : cut[7]], got[cut[4] : cut[7]])
        across = [add_low(mine[at : at + rows], got[at : at + rows]) for at in (cut[3], cut[7])]
        low, along, across, grad_mixed = together(low, along, jnp.concatenate(across, axis=0), grad_mixed)
        along, across = send(along, sizes, 2), across_high(across, sizes)
    grads_one, *dealt_one = attend_back(
        normed, qkv_one, probs_one, mixed, grad_mixed, out_grad_t, 0, owners, sizes
    )
    if stepwise:
        along, across, mine, sent, grads_one = together(along, across, *dealt_one, grads_one)
        mine, sent = mine.reshape(width, width), sent.reshape(width, width)
        got = across_core(sent[cut[4] :], sizes)
        high = [
            add_low(mine[cut[4] : cut[7]], got[: cut[3]]),
            add_low(mine[cut[7] :], got[cut[3] :], across[rows:]),
        ]
        low = add_low(low, along)
        high, low, grads_one, sent = together(jnp.concatenate(high, axis=0), low, grads_one, sent)
        got, near = send(high, sizes, 2), across_core(sent[: cut[4]], sizes)
        got_high, got_low = across_high(low[cut[2] :], sizes), across_high(low[: cut[2]], sizes)
    grad_one, small_one = input_sum(unit, grads_one, grad_part, weight_one)
    small = jnp.concatenate([small_one[0:2], small_two[0:2], small_two[8:]], axis=0)
    if stepwise:
        near, small = together(near, small)
        small = jnp.pad(small.astype(BF), ((0, -small.shape[0] % 16), (0, 0)))
        smalls = across_high(small, sizes), send(small, sizes, 2), across_high(small, sizes, 2)
        got, got_high, near, smalls = together(got, got_high, near, smalls)
        small = add_low(small, *smalls)
        held = mine[: cut[4]], near, got
        low = add_low(*(h[: cut[2]] for h in held))
        high = [
            add_low(*(h[cut[2] : cut[3]] for h in held), got_high),
            add_low(*(h[cut[3] : cut[4]] for h in held), across[:rows]),
            small,
        ]
        low, high, grad_one = together(low, jnp.concatenate(high, axis=0), grad_one)
    input_grad = input_back(unit, inv_std, grad_y, grad_one, norms)
    output = block_output(y, logits, back)
    if stepwise:
        got, got_low, input_grad = together(send(high, sizes, 1), got_low, input_grad)
        low = add_low(low, got[: cut[2]], got_low)
        small = add_low(small, got[cut[2] :])
        near, corner = across_core(small, sizes), across_core_after(small, sizes, 0)
        got, output, near, corner = together(
            send(jnp.concatenate([low[rows:], small], axis=0), sizes, 0), output, near, corner
        )
        low = jnp.concatenate([low[:rows], small], axis=0)
        qkv_grad, out_grad, norm_grad, router_grad = unpack(index, low, got, near, corner, sizes)
        router_grad = router_grad.reshape(columns, 1)
    else:
        small = sum_small(small, sizes)
        full = jnp.concatenate(
            [dealt_one[0].reshape(width, 3, half), dealt_two[0].reshape(width, 3, half)], axis=2
        ).transpose(1, 0, 2)
        qkv_grad = lax.psum_scatter(full, "dp", scatter_dimension=1, tiled=True)
        qkv_grad = lax.psum_scatter(qkv_grad, "tensor", scatter_dimension=2, tiled=True)
        out_grad = lax.psum_scatter(out_grad_t.T, "dp", scatter_dimension=1, tiled=True)
        out_grad = lax.psum_scatter(out_grad, "tensor", scatter_dimension=0, tiled=True)
        norm_grad = lax.dynamic_slice(small, (tensor_index, dp_index * rows), (1, rows))
        router_grad = lax.dynamic_slice(
            small, (tensor_size + dp_index, tensor_index * columns), (1, columns)
        ).reshape(columns, 1)
    return (
        output,
        input_grad,
        qkv_grad,
        out_grad,
        router_grad,
        norm_grad,
        first_grad[None],
        second_grad[None],
    )


def solution(mesh):
    sizes = (mesh.shape["dp"], mesh.shape["tensor"])
    return jax.shard_map(
        functools.partial(on_device, sizes),
        mesh=mesh,
        in_specs=(
            P(("dp", "tensor"), None),
            P(None, "dp", "tensor"),
            P("tensor", "dp"),
            P("tensor", "dp"),
            P("tensor", "dp"),
            P("dp", None, "tensor"),
            P("dp", "tensor", None),
            P(("dp", "tensor"), None),
        ),
        out_specs=(
            P(("dp", "tensor"), None),
            P(("dp", "tensor"), None),
            P(None, "dp", "tensor"),
            P("tensor", "dp"),
            P("tensor", "dp"),
            P("tensor", "dp"),
            P("dp", None, "tensor"),
            P("dp", "tensor", None),
        ),
        check_vma=False,
    )
```

```python
import functools

import jax
import jax.numpy as jnp
from jax import lax
from jax.experimental import pallas as pl
from jax.experimental.pallas import tpu as pltpu
from jax.sharding import PartitionSpec as P

HEAD_DIM = 64
SEQ = 197
PAD = 208
BLOCK = 8
AXES = ("dp", "tensor")
BF = jnp.bfloat16
F32 = jnp.float32
LAST = (((1,), (1,)), ((), ()))
FIRST = (((0,), (0,)), ((), ()))
MIDDLE = (((1,), (0,)), ((), ()))
MIB = 1024 * 1024


def dot(a, b, dims=MIDDLE):
    return lax.dot_general(a, b, dims, preferred_element_type=F32)


def shape_of(shape, dtype):
    return jax.ShapeDtypeStruct(shape, dtype)


def run(kernel, name, operands, results, limit, scratch=(), scalars=0, aliases=()):
    memory = [pltpu.SMEM] * scalars + [pltpu.VMEM] * (len(operands) - scalars)
    return pl.pallas_call(
        kernel,
        in_specs=[pl.BlockSpec(memory_space=m) for m in memory],
        out_specs=[pl.BlockSpec(memory_space=pltpu.VMEM) for _ in results],
        out_shape=list(results),
        scratch_shapes=list(scratch),
        input_output_aliases=dict(aliases),
        compiler_params=pltpu.CompilerParams(vmem_limit_bytes=limit * MIB),
        cost_estimate=pl.CostEstimate(flops=1, bytes_accessed=1, transcendentals=0),
        name=name,
    )(*operands)


def layer_stats(values):
    centre = jnp.mean(values, axis=-1, keepdims=True)
    centred = values - centre
    spread = jnp.mean(centred * centred, axis=-1, keepdims=True)
    inv_std = lax.rsqrt(spread + 1e-06)
    return centred * inv_std, inv_std


def lane_ids(shape):
    return lax.broadcasted_iota(jnp.int32, shape, len(shape) - 1)


def row_ids(shape):
    return lax.broadcasted_iota(jnp.int32, shape, len(shape) - 2)


def flat(ref):
    images, rows, columns = ref.shape
    return ref[...].reshape(images * rows, columns)


def prepare_kernel(x_ref, g_ref, x_out, g_out, unit_out, inv_out, wide):
    count, width = x_ref.shape
    real = row_ids((PAD, width)) < SEQ
    wide[count:, :] = jnp.zeros((wide.shape[0] - count, width), F32)
    for ref, out in ((x_ref, x_out), (g_ref, g_out)):
        wide[0:count, :] = ref[...].astype(F32)
        for i in range(out.shape[0]):
            rows = jnp.where(real, wide[SEQ * i : SEQ * i + PAD, :], 0.0)
            out[i] = rows.astype(BF)
            if ref is x_ref:
                unit_out[i], inv_out[i] = layer_stats(rows)


def prepare(tokens, cotangent):
    count, width = tokens.shape
    images = count // SEQ
    rows = shape_of((images, PAD, width), BF)
    return run(
        prepare_kernel,
        "prepare",
        (tokens, cotangent),
        (rows, rows, shape_of((images, PAD, width), F32), shape_of((images, PAD, 1), F32)),
        8,
        scratch=[pltpu.VMEM((-(-count // 8) * 8 + 16, width), F32)],
    )


def attend_rows(normed, w_ref, qkv_ref, mixed_ref, probs_ref, piece):
    images, rows, width = mixed_ref.shape
    span = width // 2
    low = lane_ids((rows, 128)) < HEAD_DIM
    key_ok = row_ids((rows, rows)) < SEQ
    zero = jnp.zeros((rows, 128), BF)
    proj = dot(normed, w_ref[...])
    qkv_ref[:, :, 0:span] = (proj[:, 0:span] * HEAD_DIM ** (-0.5)).astype(BF).reshape(images, rows, span)
    qkv_ref[:, :, span:] = proj[:, span:].astype(BF).reshape(images, rows, 2 * span)

    def image(i, carry):
        for p in range(span // 128):
            at = slice(p * 128, (p + 1) * 128)
            q = qkv_ref[i, :, at]
            k = qkv_ref[i, :, span + p * 128 : span + (p + 1) * 128]
            v = qkv_ref[i, :, 2 * span + p * 128 : 2 * span + (p + 1) * 128]
            mixed = []
            for h in range(2):
                q_one = jnp.where(low, q, zero) if h == 0 else jnp.where(low, zero, q)
                scores = jnp.where(key_ok, dot(k, q_one, LAST), -1e30)
                scaled = jnp.exp(scores - jnp.max(scores, axis=0, keepdims=True))
                weights = (scaled * (1.0 / jnp.sum(scaled, axis=0, keepdims=True))).astype(BF)
                probs_ref[i, 2 * p + h] = weights
                mixed.append(dot(weights, v, FIRST))
            at = slice(piece * span + p * 128, piece * span + (p + 1) * 128)
            mixed_ref[i, :, at] = jnp.where(low, mixed[0], mixed[1]).astype(BF)
        return carry

    lax.fori_loop(0, images, image, 0, unroll=3 if images % 3 == 0 else 1)


def assemble_rows(owners, parts, kinds, out_ref, columns, lane=0):
    for side, (owner, refs) in enumerate(zip(owners, parts, strict=True)):
        count = out_ref.shape[0] // owner.shape[0]
        blocks = [ref[i * count : (i + 1) * count] for ref in refs for i in range(ref.shape[0] // count)]
        for p, block in enumerate(blocks):
            row = pl.multiple_of(count * owner[p], 16)
            for at, kind in enumerate(kinds):
                to = lane + (2 * at + side) * columns
                out_ref[pl.ds(row, count), to : to + columns] = block[:, kind * columns : (kind + 1) * columns]


def attend_first_kernel(counts, *refs):
    if counts:
        own, sib = counts
        owners, refs = refs[:2], refs[2:]
        unit_ref, norms_ref, refs = refs[0], refs[1], refs[2:]
        parts, refs = (refs[:own], refs[own : own + sib]), refs[own + sib :]
        n_ref, qkv_ref, mixed_ref, probs_ref, w_ref, out_w_ref = refs
        columns = w_ref.shape[1] // 6
        assemble_rows(owners, parts, range(3), w_ref, columns)
        assemble_rows(owners, parts, [3], out_w_ref, columns)
    else:
        unit_ref, norms_ref, w_ref, n_ref, qkv_ref, mixed_ref, probs_ref = refs
    normed = (flat(unit_ref) * norms_ref[0:1, :] + norms_ref[1:2, :]).astype(BF)
    n_ref[...] = normed.reshape(n_ref.shape)
    attend_rows(normed, w_ref, qkv_ref, mixed_ref, probs_ref, 0)


def attend_second_kernel(counts, *refs):
    if counts:
        own, sib = counts
        owners, refs = refs[:2], refs[2:]
        n_ref, refs = refs[0], refs[3:]
        parts, refs = (refs[:own], refs[own : own + sib]), refs[own + sib :]
        mixed_ref, out_w_ref, qkv_ref, probs_ref, w_ref = refs
        columns = w_ref.shape[1] // 6
        assemble_rows(owners, parts, range(3), w_ref, columns)
        assemble_rows(owners, parts, [3], out_w_ref, columns, 2 * columns)
    else:
        n_ref, _, w_ref, mixed_ref, qkv_ref, probs_ref = refs
    attend_rows(flat(n_ref), w_ref, qkv_ref, mixed_ref, probs_ref, 1)


def attend_first(unit, norms, owners, weights):
    images, rows, width = unit.shape
    span = width // 2
    results = (
        shape_of(unit.shape, BF),
        shape_of((images, rows, 3 * span), BF),
        shape_of(unit.shape, BF),
        shape_of((images, span // HEAD_DIM, rows, rows), BF),
    )
    counts = None
    if owners:
        counts = tuple(map(len, weights))
        weights = sum(weights, ())
        results += (shape_of((width, 3 * span), BF), shape_of((width, width), BF))
    return run(
        functools.partial(attend_first_kernel, counts),
        "attend_first",
        owners + (unit, norms) + weights,
        results,
        4,
        scalars=len(owners),
    )


def attend_second(normed, mixed, out_w, owners, weights):
    images, rows, width = normed.shape
    span = width // 2
    given = (mixed, out_w) if owners else (mixed,)
    results = tuple(shape_of(g.shape, BF) for g in given) + (
        shape_of((images, rows, 3 * span), BF),
        shape_of((images, span // HEAD_DIM, rows, rows), BF),
    )
    counts = None
    if owners:
        counts = tuple(map(len, weights))
        weights = sum(weights, ())
        results += (shape_of((width, 3 * span), BF),)
    return run(
        functools.partial(attend_second_kernel, counts),
        "attend_second",
        owners + (normed,) + given + weights,
        results,
        4,
        scalars=len(owners),
        aliases=[(len(owners) + 1 + i, i) for i in range(len(given))],
    )


def softmaxes(logits):
    ok = lane_ids(logits.shape) < SEQ
    masked = jnp.where(ok, logits, -1e30)
    up = jnp.exp(masked - jnp.max(masked, axis=1, keepdims=True))
    dispatch = up / jnp.sum(up, axis=1, keepdims=True)
    up = jnp.exp(logits - jnp.max(logits, axis=0, keepdims=True))
    combine = up / jnp.sum(up, axis=0, keepdims=True)
    return dispatch, combine


def by_image(experts, places, low, back=False):
    shape = (experts * BLOCK, places * experts)
    shape = shape[::-1] if back else shape
    blocked, other = (lane_ids(shape), row_ids(shape)) if back else (row_ids(shape), lane_ids(shape))
    place = jnp.bitwise_and(blocked, BLOCK - 1) - low
    inside = jnp.logical_and(place >= 0, place < places)
    return jnp.logical_and(inside, other == place * experts + lax.div(blocked, BLOCK)).astype(BF)


def to_blocks(first, second):
    experts, width = first[0].shape
    half = width // 2
    head = dot(by_image(experts, BLOCK, 0), jnp.concatenate(first + second[:2], axis=0))
    rest = jnp.concatenate(second[2:], axis=0)
    rest = dot(by_image(experts, 4, 0), rest[:, :half]) + dot(by_image(experts, 4, 4), rest[:, half:])
    return head.astype(BF), rest.astype(BF)


def from_blocks(blocks, experts, width):
    head = dot(by_image(experts, BLOCK, 0, True), blocks[:, :width])
    rest = [dot(by_image(experts, 4, low, True), blocks[:, width:]) for low in (0, 4)]
    rest = jnp.concatenate(rest, axis=1)
    head, rest = ([v[at : at + experts].astype(BF) for at in range(0, v.shape[0], experts)] for v in (head, rest))
    return head[:6], head[6:] + rest


def route_kernel(
    x_ref, mixed_ref, out_w_ref, norms_ref, router_ref, g_ref, y_ref, n_ref, logits_ref, send_ref
):
    images, rows, width = x_ref.shape
    experts = router_ref.shape[0]
    for at in range(0, images, 2):
        some = slice(at, min(at + 2, images))
        y = flat(x_ref.at[some]).astype(F32) + dot(flat(mixed_ref.at[some]), out_w_ref[...], LAST)
        y_ref[some] = y.reshape(-1, rows, width)
        unit, _ = layer_stats(y)
        n_ref[some] = (unit * norms_ref[2:3, :] + norms_ref[3:4, :]).astype(BF).reshape(-1, rows, width)
    first, second = [], []
    for i in range(images):
        logits = dot(router_ref[...], n_ref[i], LAST)
        logits_ref[i] = logits
        dispatch, combine = softmaxes(logits)
        first.append(dot(dispatch.astype(BF), n_ref[i]).astype(BF))
        second.append(dot(combine.astype(BF), g_ref[i]).astype(BF))
    send_ref[:, :width], send_ref[:, width:] = to_blocks(first, second)


def route(x_img, mixed, out_w, norms, router, g_img):
    images, rows, width = x_img.shape
    experts = router.shape[0]
    return run(
        route_kernel,
        "route",
        (x_img, mixed, out_w, norms, router, g_img),
        (
            shape_of((images, rows, width), F32),
            shape_of((images, rows, width), BF),
            shape_of((images, experts, rows), F32),
            shape_of((experts * BLOCK, width + width // 2), BF),
        ),
        4,
    )


def turned(blocks, shift):
    return pltpu.roll(blocks, shift, 1)


def split_rows(blocks):
    rows, lanes = blocks.shape
    width = lanes // 3 * 2
    wide = blocks.astype(F32).reshape(rows // BLOCK, BLOCK, lanes)
    head, rest = wide[:, :, :width], wide[:, :, width:]
    place = row_ids(head.shape)
    first = jnp.where(place < 6, head, 0.0)
    second = jnp.concatenate([turned(rest, 2), turned(rest, BLOCK - 2)], axis=2)
    second = jnp.where(place < 2, turned(head, 2), jnp.where(place < 6, second, 0.0))
    return first.reshape(rows, width).astype(BF), second.reshape(rows, width).astype(BF)


def join_rows(first, second):
    rows, width = first.shape
    half = width // 2
    first = first.reshape(rows // BLOCK, BLOCK, width)
    second = second.reshape(rows // BLOCK, BLOCK, width)
    head = jnp.where(row_ids(first.shape) < 6, first, turned(second, 6))
    left, right = turned(second[:, :, :half], BLOCK - 2), turned(second[:, :, half:], 2)
    rest = jnp.where(row_ids(left.shape) < 4, left, right)
    return head.reshape(rows, width).astype(BF), rest.reshape(rows, half).astype(BF)


def gelu_parts(pre):
    cdf = 0.5 * (1.0 + lax.erf(pre * (0.5**0.5)))
    density = jnp.exp(-0.5 * pre * pre) * 0.3989422804014327
    return pre * cdf, cdf + pre * density


def expert_kernel(a_ref, b_ref, c_ref, d_ref, w1_ref, w2_ref, *refs):
    outs, (slots_ref, grads_ref, hidden_ref, pre_ref) = refs[:4], refs[4:]
    width = w1_ref.shape[0]
    count = a_ref.shape[0]
    blocks = jnp.concatenate([a_ref[...], b_ref[...], c_ref[...], d_ref[...]], axis=0)
    step = min(4 * count, 256)
    for at in range(0, 4 * count, step):
        slots_ref[at : at + step], grads_ref[at : at + step] = split_rows(blocks[at : at + step])
    slots, grads = slots_ref[...], grads_ref[...]
    pre = dot(slots, w1_ref[...])
    hidden, slope = gelu_parts(pre)
    hidden = hidden.astype(BF)
    returned = dot(hidden, w2_ref[...])
    grad_pre = (dot(grads, w2_ref[...], LAST) * slope).astype(BF)
    grad_slots = dot(grad_pre, w1_ref[...], LAST)
    parts = [join_rows(returned[at : at + step], grad_slots[at : at + step]) for at in range(0, 4 * count, step)]
    head, rest = (jnp.concatenate(p, axis=0) for p in zip(*parts, strict=True))
    for i, ref in enumerate(outs):
        ref[:, :width] = head[i * count : (i + 1) * count]
        ref[:, width:] = rest[i * count : (i + 1) * count]
    hidden_ref[...] = hidden
    pre_ref[...] = grad_pre


def run_expert(own, near, first_weight, second_weight):
    width, units = first_weight.shape
    rows = 4 * own[0].shape[0]
    return run(
        expert_kernel,
        "expert",
        own + near + (first_weight, second_weight),
        (shape_of(own[0].shape, BF),) * 4
        + (
            shape_of((rows, width), BF),
            shape_of((rows, width), BF),
            shape_of((rows, units), BF),
            shape_of((rows, units), BF),
        ),
        8 if rows <= 512 else 48,
    )


def expert_grad_kernel(slots_ref, grads_ref, hidden_ref, pre_ref, d1_ref, d2_ref):
    d1_ref[...] = dot(slots_ref[...], pre_ref[...], FIRST)
    d2_ref[...] = dot(hidden_ref[...], grads_ref[...], FIRST)


def expert_grads(slots, grads, hidden, grad_pre):
    rows, width = slots.shape
    units = hidden.shape[1]
    return run(
        expert_grad_kernel,
        "expert_grads",
        (slots, grads, hidden, grad_pre),
        (shape_of((width, units), F32), shape_of((units, width), F32)),
        6 if rows <= 512 else 32,
    )


def moe_ready_kernel(y_ref, logits_ref, unit_ref, inv_ref, dispatch_ref, combine_ref):
    unit, inv_std = layer_stats(flat(y_ref))
    unit_ref[...] = unit.reshape(unit_ref.shape)
    inv_ref[...] = inv_std.reshape(inv_ref.shape)
    for i in range(y_ref.shape[0]):
        dispatch_ref[i], combine_ref[i] = softmaxes(logits_ref[i])


def moe_ready(y, logits):
    images, rows, width = y.shape
    return run(
        moe_ready_kernel,
        "moe_ready",
        (y, logits),
        (
            shape_of((images, rows, width), F32),
            shape_of((images, rows, 1), F32),
            shape_of(logits.shape, F32),
            shape_of(logits.shape, F32),
        ),
        4,
    )


def moe_back_kernel(
    unit_ref,
    inv_ref,
    dispatch_ref,
    combine_ref,
    n_ref,
    g_ref,
    back_ref,
    norms_ref,
    router_ref,
    out_w_ref,
    mixed_ref,
    grad_y_ref,
    grad_mixed_ref,
    out_grad_ref,
    small_ref,
    attn_ref,
):
    images, rows, width = unit_ref.shape
    experts = router_ref.shape[0]
    gain = norms_ref[2:3, :]
    all_returned, all_slots = from_blocks(back_ref[...], experts, width)
    router_grad, gain_grad, shift_grad = 0.0, 0.0, 0.0
    lefts, rights = [], []
    for i in range(images):
        returned, grad_slots = all_returned[i], all_slots[i]
        dispatch, combine = dispatch_ref[i], combine_ref[i]
        grad_combine = dot(returned, g_ref[i], LAST)
        grad_dispatch = dot(grad_slots, n_ref[i], LAST)
        grad_logits = dispatch * (
            grad_dispatch - jnp.sum(grad_dispatch * dispatch, axis=1, keepdims=True)
        ) + combine * (grad_combine - jnp.sum(grad_combine * combine, axis=0, keepdims=True))
        grad_logits = grad_logits.astype(BF)
        router_grad = router_grad + dot(grad_logits, n_ref[i])
        lefts.append(jnp.concatenate([dispatch.astype(BF), grad_logits], axis=0))
        rights.append(jnp.concatenate([grad_slots, router_ref[...]], axis=0))
    for at in range(0, images, 3):
        some = slice(at, min(at + 3, images))
        here = range(some.start, some.stop)
        grad_two = jnp.concatenate([dot(lefts[i], rights[i], FIRST) for i in here], axis=0)
        unit, inv_std = flat(unit_ref.at[some]), flat(inv_ref.at[some])
        gain_grad = gain_grad + jnp.sum(grad_two * unit, axis=0, keepdims=True)
        shift_grad = shift_grad + jnp.sum(grad_two, axis=0, keepdims=True)
        scaled = grad_two * gain
        mean_one = jnp.mean(scaled, axis=-1, keepdims=True)
        mean_two = jnp.mean(scaled * unit, axis=-1, keepdims=True)
        grad_y = flat(g_ref.at[some]).astype(F32) + inv_std * (scaled - mean_one - unit * mean_two)
        grad_y_ref[some] = grad_y.reshape(-1, rows, width)
        grad_attn = grad_y.astype(BF)
        attn_ref[some] = grad_attn.reshape(-1, rows, width)
        grad_mixed_ref[some] = dot(grad_attn, out_w_ref[...]).astype(BF).reshape(-1, rows, width)
    small_ref[...] = jnp.zeros_like(small_ref)
    small_ref[0:1, :] = gain_grad
    small_ref[1:2, :] = shift_grad
    small_ref[8 : 8 + experts, :] = router_grad
    grad_attn = flat(attn_ref)
    out_grad_ref[...] = dot(grad_attn, flat(mixed_ref), FIRST).astype(out_grad_ref.dtype)


def moe_back(ready, normed, g_img, back, norms, router, out_w, mixed, dtype):
    images, rows, width = normed.shape
    experts = router.shape[0]
    return run(
        moe_back_kernel,
        "moe_back",
        ready + (normed, g_img, back, norms, router, out_w, mixed),
        (
            shape_of((images, rows, width), F32),
            shape_of((images, rows, width), BF),
            shape_of((width, width), dtype),
            shape_of((8 + experts, width), F32),
        ),
        10,
        scratch=[pltpu.VMEM((images, rows, width), BF)],
    )


def output_kernel(y_ref, logits_ref, back_ref, out_ref, wide):
    images, experts, _ = logits_ref.shape
    all_returned, _ = from_blocks(back_ref[...], experts, y_ref.shape[2])
    for i in range(images):
        returned = all_returned[i]
        _, combine = softmaxes(logits_ref[i])
        total = y_ref[i] + dot(combine.astype(BF), returned, FIRST)
        wide[SEQ * i : SEQ * (i + 1), :] = total[0:SEQ]
    out_ref[...] = wide[...].astype(BF)


def block_output(y, logits, back):
    images, rows, width = y.shape
    count = images * SEQ
    return run(
        output_kernel,
        "block_output",
        (y, logits, back),
        (shape_of((count, width), BF),),
        7,
        scratch=[pltpu.VMEM((count, width), F32)],
    )[0]


def deal_rows(owners, full_ref, first, kinds, refs, columns):
    for side, (owner, ref) in enumerate(zip(owners, refs, strict=True)):
        blocks, count, _ = ref.shape
        for p in range(blocks):
            row = pl.multiple_of(count * owner[p], 16)
            for at, kind in enumerate(kinds):
                lane = first + (2 * at + side) * columns
                ref[p, :, kind * columns : (kind + 1) * columns] = full_ref[pl.ds(row, count), lane : lane + columns]


def attend_back_kernel(stepwise, piece, *refs):
    if stepwise:
        owners, refs = refs[:2], refs[2:]
        n_ref, qkv_ref, probs_ref, mixed_ref, gm_ref, og_ref, grads_ref, own_ref, sib_ref, dw_ref = refs
    else:
        n_ref, qkv_ref, probs_ref, mixed_ref, gm_ref, grads_ref, dw_ref = refs
    images, rows, width = mixed_ref.shape
    span = width // 2
    low = lane_ids((rows, 128)) < HEAD_DIM
    zero = jnp.zeros((rows, 128), BF)
    minus = jnp.full((rows, 128), -1.0, BF)

    def image(i, carry):
        for p in range(span // 128):
            at = slice(p * 128, (p + 1) * 128)
            at_k = slice(span + p * 128, span + (p + 1) * 128)
            at_v = slice(2 * span + p * 128, 2 * span + (p + 1) * 128)
            q, k, v = qkv_ref[i, :, at], qkv_ref[i, :, at_k], qkv_ref[i, :, at_v]
            here = slice(piece * span + p * 128, piece * span + (p + 1) * 128)
            gm = gm_ref[i, :, here]
            inner = pltpu.roll(gm.astype(F32) * mixed_ref[i, :, here].astype(F32), HEAD_DIM, 1).astype(BF)
            grad_q, grad_k, grad_v = 0.0, 0.0, 0.0
            for h in range(2):
                mine = low if h == 0 else jnp.logical_not(low)
                weights = probs_ref[i, 2 * p + h]
                centred = dot(jnp.where(mine, v, minus), jnp.where(mine, gm, inner), LAST)
                grad_scores = (weights.astype(F32) * centred).astype(BF)
                grad_v = grad_v + dot(weights, jnp.where(mine, gm, zero))
                grad_k = grad_k + dot(grad_scores, jnp.where(mine, q, zero))
                grad_q = grad_q + dot(grad_scores, jnp.where(mine, k, zero), FIRST)
            grads_ref[i, :, at] = (grad_q * HEAD_DIM ** (-0.5)).astype(BF)
            grads_ref[i, :, at_k] = grad_k.astype(BF)
            grads_ref[i, :, at_v] = grad_v.astype(BF)
        return carry

    lax.fori_loop(0, images, image, 0, unroll=images)
    dw_ref[...] = dot(flat(n_ref), flat(grads_ref), FIRST).astype(dw_ref.dtype)
    if stepwise:
        deal_rows(owners, dw_ref, 0, range(3), (own_ref, sib_ref), span // 2)
        deal_rows(owners, og_ref, piece * span, [3], (own_ref, sib_ref), span // 2)


def attend_back(normed, qkv, probs, mixed, grad_mixed, out_grad_t, piece, owners, sizes):
    images, rows, width = normed.shape
    span = width // 2
    operands = (normed, qkv, probs, mixed, grad_mixed)
    results = (shape_of((images, rows, 3 * span), BF),)
    scratch = ()
    if owners:
        operands += (out_grad_t,)
        results += (shape_of((sizes[0], width // sizes[0], 2 * span), BF),) * 2
        scratch = (pltpu.VMEM((width, 3 * span), BF),)
    else:
        results += (shape_of((width, 3 * span), F32),)
    return run(
        functools.partial(attend_back_kernel, bool(owners), piece),
        "attend_back",
        owners + operands,
        results,
        7,
        scratch,
        scalars=len(owners),
    )


def input_part_kernel(p_ref, w_ref, out_ref):
    out_ref[...] = dot(flat(p_ref), w_ref[...], LAST).reshape(out_ref.shape)


def input_part(grads, weight):
    images, rows, _ = grads.shape
    return run(
        input_part_kernel, "input_part", (grads, weight), (shape_of((images, rows, weight.shape[0]), F32),), 6
    )[0]


def input_sum_kernel(unit_ref, p1_ref, part_ref, w1_ref, two_ref, grad_ref, small_ref):
    images, rows, width = unit_ref.shape
    gain_grad, shift_grad = 0.0, 0.0
    for i in range(images):
        if i % 2 == 0:
            some = slice(i, min(i + 2, images))
            grad = dot(flat(p1_ref.at[some]), w1_ref[...], LAST) + flat(part_ref.at[some])
            grad_ref[some] = grad.reshape(-1, rows, width)
        gain_grad = gain_grad + jnp.sum(grad_ref[i] * unit_ref[i], axis=0, keepdims=True)
        shift_grad = shift_grad + jnp.sum(grad_ref[i], axis=0, keepdims=True)
    rows = [gain_grad, shift_grad, two_ref[0:2, :], two_ref[8:, :]]
    count = 4 + two_ref.shape[0] - 8
    if small_ref.shape[0] > count:
        rows.append(jnp.zeros((small_ref.shape[0] - count, width), F32))
    small_ref[...] = jnp.concatenate(rows, axis=0).astype(small_ref.dtype)


def input_sum(unit, grads_one, grad_part, weight_one, small_two, low):
    width = unit.shape[2]
    count = small_two.shape[0] - 4
    small = shape_of((-(-count // 16) * 16, width), BF) if low else shape_of((count, width), F32)
    return run(
        input_sum_kernel,
        "input_sum",
        (unit, grads_one, grad_part, weight_one, small_two),
        (shape_of(unit.shape, F32), small),
        7,
    )


def input_back_kernel(unit_ref, inv_ref, gy_ref, grad_ref, norms_ref, out_ref):
    gain = norms_ref[0:1, :]
    for i in range(unit_ref.shape[0]):
        unit, inv_std = unit_ref[i], inv_ref[i]
        scaled = grad_ref[i] * gain
        mean_one = jnp.mean(scaled, axis=-1, keepdims=True)
        mean_two = jnp.mean(scaled * unit, axis=-1, keepdims=True)
        total = gy_ref[i] + inv_std * (scaled - mean_one - unit * mean_two)
        out_ref[SEQ * i : SEQ * (i + 1), :] = total[0:SEQ]


def input_back(unit, inv_std, grad_y, grad_one, norms):
    images, _, width = unit.shape
    return run(
        input_back_kernel,
        "input_back",
        (unit, inv_std, grad_y, grad_one, norms),
        (shape_of((images * SEQ, width), F32),),
        9,
    )[0]


def spot(shape, start):
    return (lane_ids(shape) == row_ids(shape) + start).astype(BF)


def place_kernel(rows, index_ref, pair_ref, small_ref):
    columns, width = pair_ref.shape[1], small_ref.shape[1]
    dp_index, tensor_index = index_ref[0], index_ref[1]
    shape = (columns, width)
    inside = jnp.logical_and(lane_ids(shape) == row_ids(shape) + dp_index * rows, row_ids(shape) < rows)
    norm = dot(jnp.broadcast_to(pair_ref[0:1], (16, columns)), inside.astype(BF))
    router = dot(jnp.broadcast_to(pair_ref[1:2], (16, columns)), spot(shape, tensor_index * columns))
    row = row_ids(small_ref.shape)
    small_ref[...] = jnp.where(
        row == tensor_index, norm[0:1], jnp.where(row == width // columns + dp_index, router[0:1], 0.0)
    ).astype(BF)


def place(index, norm_params, router, experts):
    rows, columns = norm_params.shape[1], router.shape[0]
    width = rows * experts
    pair = jnp.concatenate([jnp.pad(norm_params, ((0, 0), (0, columns - rows))), router.T], axis=0)
    return run(
        functools.partial(place_kernel, rows),
        "place",
        (index, pair),
        (shape_of((-(-(width // columns + experts) // 16) * 16, width), BF),),
        4,
        scalars=1,
    )[0]


def pack_kernel(qkv_ref, out_ref, block_ref):
    kinds, _, columns = qkv_ref.shape
    for kind in range(kinds):
        block_ref[:, kind * columns : (kind + 1) * columns] = qkv_ref[kind]
    block_ref[:, kinds * columns :] = out_ref[...].T


def pack(qkv_weight, out_weight):
    kinds, rows, columns = qkv_weight.shape
    return run(
        pack_kernel,
        "pack",
        (qkv_weight, out_weight),
        (shape_of((rows, (kinds + 1) * columns), BF),),
        4,
    )[0]


def unpack_kernel(index_ref, own_ref, got_ref, near_ref, corner_ref, qkv_ref, out_ref, norm_ref, router_ref):
    kinds, rows, columns = qkv_ref.shape
    total = own_ref[...].astype(F32) + got_ref[...].astype(F32)
    for kind in range(kinds):
        qkv_ref[kind] = total[0:rows, kind * columns : (kind + 1) * columns]
    out_ref[...] = total[0:rows, kinds * columns :].T
    small = total[rows:] + near_ref[...].astype(F32) + corner_ref[...].astype(F32)
    dp_index, tensor_index = index_ref[0], index_ref[1]
    width = small.shape[1]
    row = row_ids(small.shape)
    norm = jnp.sum(jnp.where(row == tensor_index, small, 0.0), axis=0, keepdims=True)
    router = jnp.sum(jnp.where(row == width // columns + dp_index, small, 0.0), axis=0, keepdims=True)
    pair = jnp.concatenate([norm, router, jnp.zeros((6, width), F32)], axis=0)
    high = pair.astype(BF)
    parts = jnp.concatenate([high, (pair - high.astype(F32)).astype(BF)], axis=0)
    spots = [spot((rows, width), dp_index * rows), spot((columns, width), tensor_index * columns)]
    moved = [dot(parts, at, LAST) for at in spots]
    norm_ref[...] = moved[0][0:1] + moved[0][8:9]
    router_ref[...] = moved[1][1:2] + moved[1][9:10]


def unpack(index, own, got, near, corner, sizes):
    width = own.shape[1]
    rows, columns = width // sizes[0], width // sizes[1]
    return run(
        unpack_kernel,
        "unpack",
        (index, own, got, near, corner),
        (
            shape_of((width // columns - 1, rows, columns), F32),
            shape_of((columns, rows), F32),
            shape_of((1, rows), F32),
            shape_of((1, columns), F32),
        ),
        4,
        scalars=1,
    )


def swap(value, dp_size, tensor_size, dp_mask, tensor_mask):
    pairs = [
        (d * tensor_size + t, (d ^ dp_mask) * tensor_size + (t ^ tensor_mask))
        for d in range(dp_size)
        for t in range(tensor_size)
    ]
    return lax.ppermute(value, AXES, pairs)


def steps_of(dp_size):
    bits = dp_size.bit_length() - 1
    down = list(range(bits))[::-1]
    return [down, down[-1:] + down[:-1]]


def step_pairs(dp_size, tensor_size, *steps):
    masks = [functools.reduce(lambda mask, step: mask ^ (1 << order[step]), steps, 0) for order in steps_of(dp_size)]
    return [
        (d * tensor_size + t, (d ^ masks[t % 2]) * tensor_size + t)
        for d in range(dp_size)
        for t in range(tensor_size)
    ]


def owners_of(dp_size, dp_index, core):
    both = []
    for order in steps_of(dp_size):
        place = jnp.arange(dp_size, dtype=jnp.int32)
        away = jnp.zeros_like(place)
        for step, bit in enumerate(order):
            away = away | (((place >> step) & 1) << bit)
        both.append(away ^ dp_index)
    return jnp.where(core == 0, both[0], both[1]), jnp.where(core == 0, both[1], both[0])


def exchange(blocks, dp_size):
    shape = blocks.shape
    blocks = blocks.reshape(dp_size, shape[0] // dp_size, shape[1])
    return lax.all_to_all(blocks, "dp", split_axis=0, concat_axis=0, tiled=True).reshape(shape)


def together(*values):
    return lax.optimization_barrier(values)


def send(value, sizes, *steps):
    return lax.ppermute(value, AXES, step_pairs(*sizes, *steps))


def across_core(value, sizes):
    return swap(value, *sizes, 0, 1)


def across_core_after(value, sizes, step):
    pairs = [(a, b ^ 1) for a, b in step_pairs(*sizes, step)]
    return lax.ppermute(value, AXES, pairs)


def high_pairs(dp_size, tensor_size, *steps):
    return [(a, b ^ 2) for a, b in step_pairs(dp_size, tensor_size, *steps)]


def across_high(value, sizes, *steps):
    return lax.ppermute(value, AXES, high_pairs(*sizes, *steps))


def gather_first(block, small, sizes, along):
    rows = block.shape[0]
    far = lax.ppermute(small, AXES, [(p, q ^ 1) for p, q in high_pairs(*sizes)])
    *smalls, block = together(across_core(small, sizes), across_high(small, sizes), far, block)
    small = sum(smalls, small)
    first = jnp.concatenate([block, small], axis=0)
    got, high = together(send(first, sizes, 0), across_high(block, sizes))
    held = jnp.concatenate([block, got[:rows], small + got[rows:]], axis=0)

    got, near, high_got = together(send(held, sizes, 1), across_core(held, sizes), across_high(got[:rows], sizes))
    high = jnp.concatenate([high, high_got], axis=0)
    small = held[2 * rows :] + got[2 * rows :]
    four = jnp.concatenate([held[: 2 * rows], got[: 2 * rows], small], axis=0)

    last, near_two, high_two, high_near, along = together(
        send(four, sizes, 2), across_core(got, sizes), across_high(got[: 2 * rows], sizes), across_core(high, sizes), prepare(*along)
    )
    small = four[4 * rows :] + last[4 * rows :]
    own = (four, last), (near, near_two, across_core(last, sizes))
    high = jnp.concatenate([high, high_two], axis=0)
    return own, (high, high_near, across_core(high_two, sizes)), small, along


def gather_weights_plain(qkv_weight, out_weight, router, norm_params):
    qkv = lax.all_gather(qkv_weight, "dp", axis=1, tiled=True)
    qkv = lax.all_gather(qkv, "tensor", axis=2, tiled=True)
    out_w, router, norms = (
        lax.all_gather(lax.all_gather(w, "dp", axis=1, tiled=True), "tensor", axis=0, tiled=True)
        for w in (out_weight, router, norm_params)
    )
    width = qkv.shape[1]
    half = width // 2
    one = qkv[:, :, :half].transpose(1, 0, 2).reshape(width, 3 * half)
    two = qkv[:, :, half:].transpose(1, 0, 2).reshape(width, 3 * half)
    return one, two, out_w.T, norms.astype(F32), router.T


def add_low(*values):
    return sum(v.astype(F32) for v in values).astype(BF)


def sum_small(values, sizes):
    dp_size, tensor_size = sizes
    mask = 1
    while mask < tensor_size:
        values = values + swap(values, dp_size, tensor_size, 0, mask)
        mask *= 2
    mask = 1
    while mask < dp_size:
        values = values + swap(values, dp_size, tensor_size, mask, 0)
        mask *= 2
    return values


def on_device(
    sizes, tokens, qkv_weight, out_weight, router, norm_params, expert_in, expert_out, cotangent
):
    dp_size, tensor_size = sizes
    dp_index = lax.axis_index("dp")
    tensor_index = lax.axis_index("tensor")
    core = jnp.bitwise_and(tensor_index, 1)
    width = tokens.shape[1]
    half = width // 2
    rows = qkv_weight.shape[1]
    columns = qkv_weight.shape[2]
    experts = dp_size * router.shape[1]
    stepwise = rows % 16 == 0 and sizes == (8, 4)
    owners = ()
    if stepwise:
        owners = owners_of(dp_size, dp_index, core)
        index = jnp.stack([dp_index, tensor_index]).astype(jnp.int32)
        *owners, index, qkv_weight, out_weight, norm_params, router = together(
            *owners, index, qkv_weight, out_weight, norm_params, router
        )
        owners = tuple(owners)
        small = place(index, norm_params, router, experts)
        block = pack(qkv_weight, out_weight)
        (own, near), high, small, (x_img, g_img, unit, inv_std) = gather_first(block, small, sizes, (tokens, cotangent))
        norms, router_t = small[:tensor_size].astype(F32), small[tensor_size : tensor_size + experts]
        high, near_first, near_second = high
        last_high = send(high, sizes, 2)
        normed, qkv_one, mixed, probs_one, weight_one, out_w = attend_first(unit, norms, owners, (own, near))
        last_high, near_second, normed = together(last_high, near_second, normed)
        parts = (high, last_high), (near_first, near_second, across_core(last_high, sizes))
        mixed, out_w, qkv_two, probs_two, weight_two = attend_second(normed, mixed, out_w, owners, parts)
    else:
        x_img, g_img, unit, inv_std = prepare(tokens, cotangent)
        weight_one, weight_two, out_w, norms, router_t = gather_weights_plain(
            qkv_weight, out_weight, router, norm_params
        )
        normed, qkv_one, mixed, probs_one = attend_first(unit, norms, (), (weight_one,))
        mixed, qkv_two, probs_two = attend_second(normed, mixed, None, (), (weight_two,))
    y, normed_two, logits, outgoing = route(x_img, mixed, out_w, norms, router_t, g_img)

    arrived = exchange(outgoing, dp_size)
    across = across_high(arrived, sizes)
    near = across_core(arrived, sizes)
    across, near, ready = lax.optimization_barrier((across, near, tuple(moe_ready(y, logits))))
    keep, keep_high, away, away_high, *kept = run_expert(
        (arrived, across), (near, across_core(across, sizes)), expert_in[0], expert_out[0]
    )
    got = across_high(add_low(keep_high, across_core(away_high, sizes)), sizes)
    got, near, (first_grad, second_grad) = lax.optimization_barrier(
        (got, across_core(away, sizes), tuple(expert_grads(*kept)))
    )
    back = exchange(add_low(keep, near, got), dp_size)

    grad_y, grad_mixed, out_grad_t, small_two = moe_back(
        ready, normed_two, g_img, back, norms, router_t, out_w, mixed, BF if stepwise else F32
    )
    grads_two, *dealt_two = attend_back(
        normed, qkv_two, probs_two, mixed, grad_mixed, out_grad_t, 1, owners, sizes
    )
    grad_part = input_part(grads_two, weight_two)
    if stepwise:
        mine = dealt_two[0].reshape(width, width)
        got, grad_part = together(across_core(dealt_two[1].reshape(width, width), sizes), grad_part)
        cut = [rows * place for place in range(9)]
        low, along = add_low(mine[: cut[4]], got[: cut[4]]), add_low(mine[cut[4] :], got[cut[4] :])
        low, along, grad_mixed = together(low, along, grad_mixed)
        along = send(along, sizes, 2)
    grads_one, *dealt_one = attend_back(
        normed, qkv_one, probs_one, mixed, grad_mixed, out_grad_t, 0, owners, sizes
    )
    if stepwise:
        along, mine, sent, grads_one = together(along, *dealt_one, grads_one)
        mine, sent = mine.reshape(width, width), sent.reshape(width, width)
        high = add_low(mine[cut[4] :], across_core(sent[cut[4] :], sizes))
        low = add_low(low, along)
        high, low, grads_one, sent = together(high, low, grads_one, sent)
        got, near = send(high, sizes, 2), across_core(sent[: cut[4]], sizes)
        got_high, got_low = across_high(low[cut[2] :], sizes), across_high(low[: cut[2]], sizes)
    grad_one, small = input_sum(unit, grads_one, grad_part, weight_one, small_two, stepwise)
    if stepwise:
        near, small = together(near, small)
        smalls = across_high(small, sizes), send(small, sizes, 2), across_high(small, sizes, 2)
        got, got_high, near, smalls = together(got, got_high, near, smalls)
        small = add_low(small, *smalls)
        held = mine[: cut[4]], near, got
        low = add_low(*(h[: cut[2]] for h in held))
        high = [add_low(*(h[cut[2] : cut[4]] for h in held), got_high), small]
        low, high, grad_one = together(low, jnp.concatenate(high, axis=0), grad_one)
    input_grad = input_back(unit, inv_std, grad_y, grad_one, norms)
    output = block_output(y, logits, back)
    if stepwise:
        got, got_low, input_grad = together(send(high, sizes, 1), got_low, input_grad)
        low = add_low(low, got[: cut[2]], got_low)
        small = add_low(small, got[cut[2] :])
        near, corner = across_core(small, sizes), across_core_after(small, sizes, 0)
        got, output, near, corner = together(
            send(jnp.concatenate([low[rows:], small], axis=0), sizes, 0), output, near, corner
        )
        low = jnp.concatenate([low[:rows], small], axis=0)
        qkv_grad, out_grad, norm_grad, router_grad = unpack(index, low, got, near, corner, sizes)
        router_grad = router_grad.reshape(columns, 1)
    else:
        small = sum_small(small, sizes)
        full = jnp.concatenate(
            [dealt_one[0].reshape(width, 3, half), dealt_two[0].reshape(width, 3, half)], axis=2
        ).transpose(1, 0, 2)
        qkv_grad = lax.psum_scatter(full, "dp", scatter_dimension=1, tiled=True)
        qkv_grad = lax.psum_scatter(qkv_grad, "tensor", scatter_dimension=2, tiled=True)
        out_grad = lax.psum_scatter(out_grad_t.T, "dp", scatter_dimension=1, tiled=True)
        out_grad = lax.psum_scatter(out_grad, "tensor", scatter_dimension=0, tiled=True)
        norm_grad = lax.dynamic_slice(small, (tensor_index, dp_index * rows), (1, rows))
        router_grad = lax.dynamic_slice(
            small, (tensor_size + dp_index, tensor_index * columns), (1, columns)
        ).reshape(columns, 1)
    return (
        output,
        input_grad,
        qkv_grad,
        out_grad,
        router_grad,
        norm_grad,
        first_grad[None],
        second_grad[None],
    )


def solution(mesh):
    sizes = (mesh.shape["dp"], mesh.shape["tensor"])
    return jax.shard_map(
        functools.partial(on_device, sizes),
        mesh=mesh,
        in_specs=(
            P(("dp", "tensor"), None),
            P(None, "dp", "tensor"),
            P("tensor", "dp"),
            P("tensor", "dp"),
            P("tensor", "dp"),
            P("dp", None, "tensor"),
            P("dp", "tensor", None),
            P(("dp", "tensor"), None),
        ),
        out_specs=(
            P(("dp", "tensor"), None),
            P(("dp", "tensor"), None),
            P(None, "dp", "tensor"),
            P("tensor", "dp"),
            P("tensor", "dp"),
            P("tensor", "dp"),
            P("dp", None, "tensor"),
            P("dp", "tensor", None),
        ),
        check_vma=False,
    )
```

```python
import functools

import jax
import jax.numpy as jnp
from jax import lax
from jax.experimental import pallas as pl
from jax.experimental.pallas import tpu as pltpu
from jax.sharding import PartitionSpec as P

HEAD_DIM = 64
SEQ = 197
PAD = 208
BLOCK = 8
AXES = ("dp", "tensor")
BF = jnp.bfloat16
F32 = jnp.float32
LAST = (((1,), (1,)), ((), ()))
FIRST = (((0,), (0,)), ((), ()))
MIDDLE = (((1,), (0,)), ((), ()))
MIB = 1024 * 1024


def dot(a, b, dims=MIDDLE):
    return lax.dot_general(a, b, dims, preferred_element_type=F32)


def shape_of(shape, dtype):
    return jax.ShapeDtypeStruct(shape, dtype)


def run(kernel, name, operands, results, limit, scratch=(), scalars=0, aliases=()):
    memory = [pltpu.SMEM] * scalars + [pltpu.VMEM] * (len(operands) - scalars)
    return pl.pallas_call(
        kernel,
        in_specs=[pl.BlockSpec(memory_space=m) for m in memory],
        out_specs=[pl.BlockSpec(memory_space=pltpu.VMEM) for _ in results],
        out_shape=list(results),
        scratch_shapes=list(scratch),
        input_output_aliases=dict(aliases),
        compiler_params=pltpu.CompilerParams(vmem_limit_bytes=limit * MIB),
        cost_estimate=pl.CostEstimate(flops=1, bytes_accessed=1, transcendentals=0),
        name=name,
    )(*operands)


def layer_stats(values):
    centre = jnp.mean(values, axis=-1, keepdims=True)
    centred = values - centre
    spread = jnp.mean(centred * centred, axis=-1, keepdims=True)
    inv_std = lax.rsqrt(spread + 1e-06)
    return centred * inv_std, inv_std


def lane_ids(shape):
    return lax.broadcasted_iota(jnp.int32, shape, len(shape) - 1)


def row_ids(shape):
    return lax.broadcasted_iota(jnp.int32, shape, len(shape) - 2)


def flat(ref):
    images, rows, columns = ref.shape
    return ref[...].reshape(images * rows, columns)


def prepare_kernel(x_ref, g_ref, x_out, g_out, unit_out, inv_out, wide):
    count, width = x_ref.shape
    real = row_ids((PAD, width)) < SEQ
    wide[count:, :] = jnp.zeros((wide.shape[0] - count, width), F32)
    for ref, out in ((x_ref, x_out), (g_ref, g_out)):
        wide[0:count, :] = ref[...].astype(F32)
        for i in range(out.shape[0]):
            rows = jnp.where(real, wide[SEQ * i : SEQ * i + PAD, :], 0.0)
            out[i] = rows.astype(BF)
            if ref is x_ref:
                unit_out[i], inv_out[i] = layer_stats(rows)


def prepare(tokens, cotangent):
    count, width = tokens.shape
    images = count // SEQ
    rows = shape_of((images, PAD, width), BF)
    return run(
        prepare_kernel,
        "prepare",
        (tokens, cotangent),
        (rows, rows, shape_of((images, PAD, width), F32), shape_of((images, PAD, 1), F32)),
        8,
        scratch=[pltpu.VMEM((-(-count // 8) * 8 + 16, width), F32)],
    )


def attend_rows(normed, w_ref, qkv_ref, mixed_ref, probs_ref, piece):
    images, rows, width = mixed_ref.shape
    span = width // 2
    low = lane_ids((rows, 128)) < HEAD_DIM
    key_ok = row_ids((rows, rows)) < SEQ
    zero = jnp.zeros((rows, 128), BF)
    proj = dot(normed, w_ref[...])
    qkv_ref[:, :, 0:span] = (proj[:, 0:span] * HEAD_DIM ** (-0.5)).astype(BF).reshape(images, rows, span)
    qkv_ref[:, :, span:] = proj[:, span:].astype(BF).reshape(images, rows, 2 * span)

    def image(i, carry):
        for p in range(span // 128):
            at = slice(p * 128, (p + 1) * 128)
            q = qkv_ref[i, :, at]
            k = qkv_ref[i, :, span + p * 128 : span + (p + 1) * 128]
            v = qkv_ref[i, :, 2 * span + p * 128 : 2 * span + (p + 1) * 128]
            mixed = []
            for h in range(2):
                q_one = jnp.where(low, q, zero) if h == 0 else jnp.where(low, zero, q)
                scores = jnp.where(key_ok, dot(k, q_one, LAST), -1e30)
                scaled = jnp.exp(scores - jnp.max(scores, axis=0, keepdims=True))
                weights = (scaled * (1.0 / jnp.sum(scaled, axis=0, keepdims=True))).astype(BF)
                probs_ref[i, 2 * p + h] = weights
                mixed.append(dot(weights, v, FIRST))
            at = slice(piece * span + p * 128, piece * span + (p + 1) * 128)
            mixed_ref[i, :, at] = jnp.where(low, mixed[0], mixed[1]).astype(BF)
        return carry

    lax.fori_loop(0, images, image, 0, unroll=3 if images % 3 == 0 else 1)


def assemble_rows(owners, parts, kinds, out_ref, columns, lane=0):
    for side, (owner, refs) in enumerate(zip(owners, parts, strict=True)):
        count = out_ref.shape[0] // owner.shape[0]
        blocks = [ref[i * count : (i + 1) * count] for ref in refs for i in range(ref.shape[0] // count)]
        for p, block in enumerate(blocks):
            row = pl.multiple_of(count * owner[p], 16)
            for at, kind in enumerate(kinds):
                to = lane + (2 * at + side) * columns
                out_ref[pl.ds(row, count), to : to + columns] = block[:, kind * columns : (kind + 1) * columns]


def attend_first_kernel(counts, *refs):
    if counts:
        own, sib = counts
        owners, refs = refs[:2], refs[2:]
        unit_ref, norms_ref, refs = refs[0], refs[1], refs[2:]
        parts, refs = (refs[:own], refs[own : own + sib]), refs[own + sib :]
        n_ref, qkv_ref, mixed_ref, probs_ref, w_ref, out_w_ref = refs
        columns = w_ref.shape[1] // 6
        assemble_rows(owners, parts, range(3), w_ref, columns)
        assemble_rows(owners, parts, [3], out_w_ref, columns)
    else:
        unit_ref, norms_ref, w_ref, n_ref, qkv_ref, mixed_ref, probs_ref = refs
    normed = (flat(unit_ref) * norms_ref[0:1, :] + norms_ref[1:2, :]).astype(BF)
    n_ref[...] = normed.reshape(n_ref.shape)
    attend_rows(normed, w_ref, qkv_ref, mixed_ref, probs_ref, 0)


def attend_second_kernel(counts, *refs):
    if counts:
        own, sib = counts
        owners, refs = refs[:2], refs[2:]
        n_ref, refs = refs[0], refs[3:]
        parts, refs = (refs[:own], refs[own : own + sib]), refs[own + sib :]
        mixed_ref, out_w_ref, qkv_ref, probs_ref, w_ref = refs
        columns = w_ref.shape[1] // 6
        assemble_rows(owners, parts, range(3), w_ref, columns)
        assemble_rows(owners, parts, [3], out_w_ref, columns, 2 * columns)
    else:
        n_ref, _, w_ref, mixed_ref, qkv_ref, probs_ref = refs
    attend_rows(flat(n_ref), w_ref, qkv_ref, mixed_ref, probs_ref, 1)


def attend_first(unit, norms, owners, weights):
    images, rows, width = unit.shape
    span = width // 2
    results = (
        shape_of(unit.shape, BF),
        shape_of((images, rows, 3 * span), BF),
        shape_of(unit.shape, BF),
        shape_of((images, span // HEAD_DIM, rows, rows), BF),
    )
    counts = None
    if owners:
        counts = tuple(map(len, weights))
        weights = sum(weights, ())
        results += (shape_of((width, 3 * span), BF), shape_of((width, width), BF))
    return run(
        functools.partial(attend_first_kernel, counts),
        "attend_first",
        owners + (unit, norms) + weights,
        results,
        4,
        scalars=len(owners),
    )


def attend_second(normed, mixed, out_w, owners, weights):
    images, rows, width = normed.shape
    span = width // 2
    given = (mixed, out_w) if owners else (mixed,)
    results = tuple(shape_of(g.shape, BF) for g in given) + (
        shape_of((images, rows, 3 * span), BF),
        shape_of((images, span // HEAD_DIM, rows, rows), BF),
    )
    counts = None
    if owners:
        counts = tuple(map(len, weights))
        weights = sum(weights, ())
        results += (shape_of((width, 3 * span), BF),)
    return run(
        functools.partial(attend_second_kernel, counts),
        "attend_second",
        owners + (normed,) + given + weights,
        results,
        4,
        scalars=len(owners),
        aliases=[(len(owners) + 1 + i, i) for i in range(len(given))],
    )


def softmaxes(logits):
    ok = lane_ids(logits.shape) < SEQ
    masked = jnp.where(ok, logits, -1e30)
    up = jnp.exp(masked - jnp.max(masked, axis=1, keepdims=True))
    dispatch = up / jnp.sum(up, axis=1, keepdims=True)
    up = jnp.exp(logits - jnp.max(logits, axis=0, keepdims=True))
    combine = up / jnp.sum(up, axis=0, keepdims=True)
    return dispatch, combine


def by_image(experts, places, low, back=False):
    shape = (experts * BLOCK, places * experts)
    shape = shape[::-1] if back else shape
    blocked, other = (lane_ids(shape), row_ids(shape)) if back else (row_ids(shape), lane_ids(shape))
    place = jnp.bitwise_and(blocked, BLOCK - 1) - low
    inside = jnp.logical_and(place >= 0, place < places)
    return jnp.logical_and(inside, other == place * experts + lax.div(blocked, BLOCK)).astype(BF)


def to_blocks(first, second):
    experts, width = first[0].shape
    half = width // 2
    head = dot(by_image(experts, BLOCK, 0), jnp.concatenate(first + second[:2], axis=0))
    rest = jnp.concatenate(second[2:], axis=0)
    rest = dot(by_image(experts, 4, 0), rest[:, :half]) + dot(by_image(experts, 4, 4), rest[:, half:])
    return head.astype(BF), rest.astype(BF)


def from_blocks(blocks, experts, width):
    head = dot(by_image(experts, BLOCK, 0, True), blocks[:, :width])
    rest = [dot(by_image(experts, 4, low, True), blocks[:, width:]) for low in (0, 4)]
    rest = jnp.concatenate(rest, axis=1)
    head, rest = ([v[at : at + experts].astype(BF) for at in range(0, v.shape[0], experts)] for v in (head, rest))
    return head[:6], head[6:] + rest


def route_kernel(
    x_ref, mixed_ref, out_w_ref, norms_ref, router_ref, g_ref, y_ref, n_ref, logits_ref, send_ref
):
    images, rows, width = x_ref.shape
    experts = router_ref.shape[0]
    for at in range(0, images, 2):
        some = slice(at, min(at + 2, images))
        y = flat(x_ref.at[some]).astype(F32) + dot(flat(mixed_ref.at[some]), out_w_ref[...], LAST)
        y_ref[some] = y.reshape(-1, rows, width)
        unit, _ = layer_stats(y)
        n_ref[some] = (unit * norms_ref[2:3, :] + norms_ref[3:4, :]).astype(BF).reshape(-1, rows, width)
    first, second = [], []
    for i in range(images):
        logits = dot(router_ref[...], n_ref[i], LAST)
        logits_ref[i] = logits
        dispatch, combine = softmaxes(logits)
        first.append(dot(dispatch.astype(BF), n_ref[i]).astype(BF))
        second.append(dot(combine.astype(BF), g_ref[i]).astype(BF))
    send_ref[:, :width], send_ref[:, width:] = to_blocks(first, second)


def route(x_img, mixed, out_w, norms, router, g_img):
    images, rows, width = x_img.shape
    experts = router.shape[0]
    return run(
        route_kernel,
        "route",
        (x_img, mixed, out_w, norms, router, g_img),
        (
            shape_of((images, rows, width), F32),
            shape_of((images, rows, width), BF),
            shape_of((images, experts, rows), F32),
            shape_of((experts * BLOCK, width + width // 2), BF),
        ),
        4,
    )


def turned(blocks, shift):
    return pltpu.roll(blocks, shift, 1)


def split_rows(blocks):
    rows, lanes = blocks.shape
    width = lanes // 3 * 2
    wide = blocks.astype(F32).reshape(rows // BLOCK, BLOCK, lanes)
    head, rest = wide[:, :, :width], wide[:, :, width:]
    place = row_ids(head.shape)
    first = jnp.where(place < 6, head, 0.0)
    second = jnp.concatenate([turned(rest, 2), turned(rest, BLOCK - 2)], axis=2)
    second = jnp.where(place < 2, turned(head, 2), jnp.where(place < 6, second, 0.0))
    return first.reshape(rows, width).astype(BF), second.reshape(rows, width).astype(BF)


def join_rows(first, second):
    rows, width = first.shape
    half = width // 2
    first = first.reshape(rows // BLOCK, BLOCK, width)
    second = second.reshape(rows // BLOCK, BLOCK, width)
    head = jnp.where(row_ids(first.shape) < 6, first, turned(second, 6))
    left, right = turned(second[:, :, :half], BLOCK - 2), turned(second[:, :, half:], 2)
    rest = jnp.where(row_ids(left.shape) < 4, left, right)
    return head.reshape(rows, width).astype(BF), rest.reshape(rows, half).astype(BF)


def gelu_parts(pre):
    cdf = 0.5 * (1.0 + lax.erf(pre * (0.5**0.5)))
    density = jnp.exp(-0.5 * pre * pre) * 0.3989422804014327
    return pre * cdf, cdf + pre * density


def expert_kernel(a_ref, b_ref, c_ref, d_ref, w1_ref, w2_ref, *refs):
    outs, (slots_ref, grads_ref, hidden_ref, pre_ref) = refs[:4], refs[4:]
    width = w1_ref.shape[0]
    count = a_ref.shape[0]
    blocks = jnp.concatenate([a_ref[...], b_ref[...], c_ref[...], d_ref[...]], axis=0)
    step = min(4 * count, 256)
    for at in range(0, 4 * count, step):
        slots_ref[at : at + step], grads_ref[at : at + step] = split_rows(blocks[at : at + step])
    slots, grads = slots_ref[...], grads_ref[...]
    pre = dot(slots, w1_ref[...])
    hidden, slope = gelu_parts(pre)
    hidden = hidden.astype(BF)
    returned = dot(hidden, w2_ref[...])
    grad_pre = (dot(grads, w2_ref[...], LAST) * slope).astype(BF)
    grad_slots = dot(grad_pre, w1_ref[...], LAST)
    parts = [join_rows(returned[at : at + step], grad_slots[at : at + step]) for at in range(0, 4 * count, step)]
    head, rest = (jnp.concatenate(p, axis=0) for p in zip(*parts, strict=True))
    for i, ref in enumerate(outs):
        ref[:, :width] = head[i * count : (i + 1) * count]
        ref[:, width:] = rest[i * count : (i + 1) * count]
    hidden_ref[...] = hidden
    pre_ref[...] = grad_pre


def run_expert(own, near, first_weight, second_weight):
    width, units = first_weight.shape
    rows = 4 * own[0].shape[0]
    return run(
        expert_kernel,
        "expert",
        own + near + (first_weight, second_weight),
        (shape_of(own[0].shape, BF),) * 4
        + (
            shape_of((rows, width), BF),
            shape_of((rows, width), BF),
            shape_of((rows, units), BF),
            shape_of((rows, units), BF),
        ),
        8 if rows <= 512 else 48,
    )


def expert_grad_kernel(slots_ref, grads_ref, hidden_ref, pre_ref, d1_ref, d2_ref):
    d1_ref[...] = dot(slots_ref[...], pre_ref[...], FIRST)
    d2_ref[...] = dot(hidden_ref[...], grads_ref[...], FIRST)


def expert_grads(slots, grads, hidden, grad_pre):
    rows, width = slots.shape
    units = hidden.shape[1]
    return run(
        expert_grad_kernel,
        "expert_grads",
        (slots, grads, hidden, grad_pre),
        (shape_of((width, units), F32), shape_of((units, width), F32)),
        6 if rows <= 512 else 32,
    )


def moe_ready_kernel(y_ref, logits_ref, unit_ref, inv_ref, dispatch_ref, combine_ref):
    unit, inv_std = layer_stats(flat(y_ref))
    unit_ref[...] = unit.reshape(unit_ref.shape)
    inv_ref[...] = inv_std.reshape(inv_ref.shape)
    for i in range(y_ref.shape[0]):
        dispatch_ref[i], combine_ref[i] = softmaxes(logits_ref[i])


def moe_ready(y, logits):
    images, rows, width = y.shape
    return run(
        moe_ready_kernel,
        "moe_ready",
        (y, logits),
        (
            shape_of((images, rows, width), F32),
            shape_of((images, rows, 1), F32),
            shape_of(logits.shape, F32),
            shape_of(logits.shape, F32),
        ),
        4,
    )


def moe_back_kernel(
    unit_ref,
    inv_ref,
    dispatch_ref,
    combine_ref,
    n_ref,
    g_ref,
    back_ref,
    norms_ref,
    router_ref,
    out_w_ref,
    mixed_ref,
    grad_y_ref,
    grad_mixed_ref,
    out_grad_ref,
    small_ref,
    attn_ref,
):
    images, rows, width = unit_ref.shape
    experts = router_ref.shape[0]
    gain = norms_ref[2:3, :]
    all_returned, all_slots = from_blocks(back_ref[...], experts, width)
    router_grad, gain_grad, shift_grad = 0.0, 0.0, 0.0
    lefts, rights = [], []
    for i in range(images):
        returned, grad_slots = all_returned[i], all_slots[i]
        dispatch, combine = dispatch_ref[i], combine_ref[i]
        grad_combine = dot(returned, g_ref[i], LAST)
        grad_dispatch = dot(grad_slots, n_ref[i], LAST)
        grad_logits = dispatch * (
            grad_dispatch - jnp.sum(grad_dispatch * dispatch, axis=1, keepdims=True)
        ) + combine * (grad_combine - jnp.sum(grad_combine * combine, axis=0, keepdims=True))
        grad_logits = grad_logits.astype(BF)
        router_grad = router_grad + dot(grad_logits, n_ref[i])
        lefts.append(jnp.concatenate([dispatch.astype(BF), grad_logits], axis=0))
        rights.append(jnp.concatenate([grad_slots, router_ref[...]], axis=0))
    for at in range(0, images, 3):
        some = slice(at, min(at + 3, images))
        here = range(some.start, some.stop)
        grad_two = jnp.concatenate([dot(lefts[i], rights[i], FIRST) for i in here], axis=0)
        unit, inv_std = flat(unit_ref.at[some]), flat(inv_ref.at[some])
        gain_grad = gain_grad + jnp.sum(grad_two * unit, axis=0, keepdims=True)
        shift_grad = shift_grad + jnp.sum(grad_two, axis=0, keepdims=True)
        scaled = grad_two * gain
        mean_one = jnp.mean(scaled, axis=-1, keepdims=True)
        mean_two = jnp.mean(scaled * unit, axis=-1, keepdims=True)
        grad_y = flat(g_ref.at[some]).astype(F32) + inv_std * (scaled - mean_one - unit * mean_two)
        grad_y_ref[some] = grad_y.reshape(-1, rows, width)
        grad_attn = grad_y.astype(BF)
        attn_ref[some] = grad_attn.reshape(-1, rows, width)
        grad_mixed_ref[some] = dot(grad_attn, out_w_ref[...]).astype(BF).reshape(-1, rows, width)
    small_ref[...] = jnp.zeros_like(small_ref)
    small_ref[0:1, :] = gain_grad
    small_ref[1:2, :] = shift_grad
    small_ref[8 : 8 + experts, :] = router_grad
    grad_attn = flat(attn_ref)
    out_grad_ref[...] = dot(grad_attn, flat(mixed_ref), FIRST).astype(out_grad_ref.dtype)


def moe_back(ready, normed, g_img, back, norms, router, out_w, mixed, dtype):
    images, rows, width = normed.shape
    experts = router.shape[0]
    return run(
        moe_back_kernel,
        "moe_back",
        ready + (normed, g_img, back, norms, router, out_w, mixed),
        (
            shape_of((images, rows, width), F32),
            shape_of((images, rows, width), BF),
            shape_of((width, width), dtype),
            shape_of((8 + experts, width), F32),
        ),
        10,
        scratch=[pltpu.VMEM((images, rows, width), BF)],
    )


def output_kernel(y_ref, logits_ref, back_ref, out_ref, wide):
    images, experts, _ = logits_ref.shape
    all_returned, _ = from_blocks(back_ref[...], experts, y_ref.shape[2])
    for i in range(images):
        returned = all_returned[i]
        _, combine = softmaxes(logits_ref[i])
        total = y_ref[i] + dot(combine.astype(BF), returned, FIRST)
        wide[SEQ * i : SEQ * (i + 1), :] = total[0:SEQ]
    out_ref[...] = wide[...].astype(BF)


def block_output(y, logits, back):
    images, rows, width = y.shape
    count = images * SEQ
    return run(
        output_kernel,
        "block_output",
        (y, logits, back),
        (shape_of((count, width), BF),),
        7,
        scratch=[pltpu.VMEM((count, width), F32)],
    )[0]


def deal_rows(owners, full_ref, first, kinds, refs, columns):
    for side, (owner, ref) in enumerate(zip(owners, refs, strict=True)):
        blocks, count, _ = ref.shape
        for p in range(blocks):
            row = pl.multiple_of(count * owner[p], 16)
            for at, kind in enumerate(kinds):
                lane = first + (2 * at + side) * columns
                ref[p, :, kind * columns : (kind + 1) * columns] = full_ref[pl.ds(row, count), lane : lane + columns]


def attend_back_kernel(stepwise, piece, *refs):
    if stepwise:
        owners, refs = refs[:2], refs[2:]
        n_ref, qkv_ref, probs_ref, mixed_ref, gm_ref, og_ref, grads_ref, own_ref, sib_ref, dw_ref = refs
    else:
        n_ref, qkv_ref, probs_ref, mixed_ref, gm_ref, grads_ref, dw_ref = refs
    images, rows, width = mixed_ref.shape
    span = width // 2
    low = lane_ids((rows, 128)) < HEAD_DIM
    zero = jnp.zeros((rows, 128), BF)
    minus = jnp.full((rows, 128), -1.0, BF)

    def image(i, carry):
        for p in range(span // 128):
            at = slice(p * 128, (p + 1) * 128)
            at_k = slice(span + p * 128, span + (p + 1) * 128)
            at_v = slice(2 * span + p * 128, 2 * span + (p + 1) * 128)
            q, k, v = qkv_ref[i, :, at], qkv_ref[i, :, at_k], qkv_ref[i, :, at_v]
            here = slice(piece * span + p * 128, piece * span + (p + 1) * 128)
            gm = gm_ref[i, :, here]
            inner = pltpu.roll(gm.astype(F32) * mixed_ref[i, :, here].astype(F32), HEAD_DIM, 1).astype(BF)
            grad_q, grad_k, grad_v = 0.0, 0.0, 0.0
            for h in range(2):
                mine = low if h == 0 else jnp.logical_not(low)
                weights = probs_ref[i, 2 * p + h]
                centred = dot(jnp.where(mine, v, minus), jnp.where(mine, gm, inner), LAST)
                grad_scores = (weights.astype(F32) * centred).astype(BF)
                grad_v = grad_v + dot(weights, jnp.where(mine, gm, zero))
                grad_k = grad_k + dot(grad_scores, jnp.where(mine, q, zero))
                grad_q = grad_q + dot(grad_scores, jnp.where(mine, k, zero), FIRST)
            grads_ref[i, :, at] = (grad_q * HEAD_DIM ** (-0.5)).astype(BF)
            grads_ref[i, :, at_k] = grad_k.astype(BF)
            grads_ref[i, :, at_v] = grad_v.astype(BF)
        return carry

    lax.fori_loop(0, images, image, 0, unroll=images)
    dw_ref[...] = dot(flat(n_ref), flat(grads_ref), FIRST).astype(dw_ref.dtype)
    if stepwise:
        deal_rows(owners, dw_ref, 0, range(3), (own_ref, sib_ref), span // 2)
        deal_rows(owners, og_ref, piece * span, [3], (own_ref, sib_ref), span // 2)


def attend_back(normed, qkv, probs, mixed, grad_mixed, out_grad_t, piece, owners, sizes):
    images, rows, width = normed.shape
    span = width // 2
    operands = (normed, qkv, probs, mixed, grad_mixed)
    results = (shape_of((images, rows, 3 * span), BF),)
    scratch = ()
    if owners:
        operands += (out_grad_t,)
        results += (shape_of((sizes[0], width // sizes[0], 2 * span), BF),) * 2
        scratch = (pltpu.VMEM((width, 3 * span), BF),)
    else:
        results += (shape_of((width, 3 * span), F32),)
    return run(
        functools.partial(attend_back_kernel, bool(owners), piece),
        "attend_back",
        owners + operands,
        results,
        7,
        scratch,
        scalars=len(owners),
    )


def input_part_kernel(p_ref, w_ref, out_ref):
    out_ref[...] = dot(flat(p_ref), w_ref[...], LAST).reshape(out_ref.shape)


def input_part(grads, weight):
    images, rows, _ = grads.shape
    return run(
        input_part_kernel, "input_part", (grads, weight), (shape_of((images, rows, weight.shape[0]), F32),), 6
    )[0]


def input_sum_kernel(unit_ref, p1_ref, part_ref, w1_ref, two_ref, grad_ref, small_ref):
    images, rows, width = unit_ref.shape
    gain_grad, shift_grad = 0.0, 0.0
    for i in range(images):
        if i % 2 == 0:
            some = slice(i, min(i + 2, images))
            grad = dot(flat(p1_ref.at[some]), w1_ref[...], LAST) + flat(part_ref.at[some])
            grad_ref[some] = grad.reshape(-1, rows, width)
        gain_grad = gain_grad + jnp.sum(grad_ref[i] * unit_ref[i], axis=0, keepdims=True)
        shift_grad = shift_grad + jnp.sum(grad_ref[i], axis=0, keepdims=True)
    rows = [gain_grad, shift_grad, two_ref[0:2, :], two_ref[8:, :]]
    count = 4 + two_ref.shape[0] - 8
    if small_ref.shape[0] > count:
        rows.append(jnp.zeros((small_ref.shape[0] - count, width), F32))
    small_ref[...] = jnp.concatenate(rows, axis=0).astype(small_ref.dtype)


def input_sum(unit, grads_one, grad_part, weight_one, small_two, low):
    width = unit.shape[2]
    count = small_two.shape[0] - 4
    small = shape_of((-(-count // 16) * 16, width), BF) if low else shape_of((count, width), F32)
    return run(
        input_sum_kernel,
        "input_sum",
        (unit, grads_one, grad_part, weight_one, small_two),
        (shape_of(unit.shape, F32), small),
        7,
    )


def input_back_kernel(unit_ref, inv_ref, gy_ref, grad_ref, norms_ref, out_ref):
    gain = norms_ref[0:1, :]
    for i in range(unit_ref.shape[0]):
        unit, inv_std = unit_ref[i], inv_ref[i]
        scaled = grad_ref[i] * gain
        mean_one = jnp.mean(scaled, axis=-1, keepdims=True)
        mean_two = jnp.mean(scaled * unit, axis=-1, keepdims=True)
        total = gy_ref[i] + inv_std * (scaled - mean_one - unit * mean_two)
        out_ref[SEQ * i : SEQ * (i + 1), :] = total[0:SEQ]


def input_back(unit, inv_std, grad_y, grad_one, norms):
    images, _, width = unit.shape
    return run(
        input_back_kernel,
        "input_back",
        (unit, inv_std, grad_y, grad_one, norms),
        (shape_of((images * SEQ, width), F32),),
        9,
    )[0]


def spot(shape, start):
    return (lane_ids(shape) == row_ids(shape) + start).astype(BF)


def place_kernel(rows, index_ref, pair_ref, small_ref):
    columns, width = pair_ref.shape[1], small_ref.shape[1]
    dp_index, tensor_index = index_ref[0], index_ref[1]
    shape = (columns, width)
    inside = jnp.logical_and(lane_ids(shape) == row_ids(shape) + dp_index * rows, row_ids(shape) < rows)
    norm = dot(jnp.broadcast_to(pair_ref[0:1], (16, columns)), inside.astype(BF))
    router = dot(jnp.broadcast_to(pair_ref[1:2], (16, columns)), spot(shape, tensor_index * columns))
    row = row_ids(small_ref.shape)
    small_ref[...] = jnp.where(
        row == tensor_index, norm[0:1], jnp.where(row == width // columns + dp_index, router[0:1], 0.0)
    ).astype(BF)


def place(index, norm_params, router, experts):
    rows, columns = norm_params.shape[1], router.shape[0]
    width = rows * experts
    pair = jnp.concatenate([jnp.pad(norm_params, ((0, 0), (0, columns - rows))), router.T], axis=0)
    return run(
        functools.partial(place_kernel, rows),
        "place",
        (index, pair),
        (shape_of((-(-(width // columns + experts) // 16) * 16, width), BF),),
        4,
        scalars=1,
    )[0]


def pack_kernel(qkv_ref, out_ref, block_ref):
    kinds, _, columns = qkv_ref.shape
    for kind in range(kinds):
        block_ref[:, kind * columns : (kind + 1) * columns] = qkv_ref[kind]
    block_ref[:, kinds * columns :] = out_ref[...].T


def pack(qkv_weight, out_weight):
    kinds, rows, columns = qkv_weight.shape
    return run(
        pack_kernel,
        "pack",
        (qkv_weight, out_weight),
        (shape_of((rows, (kinds + 1) * columns), BF),),
        4,
    )[0]


def unpack_kernel(index_ref, own_ref, got_ref, near_ref, corner_ref, qkv_ref, out_ref, norm_ref, router_ref):
    kinds, rows, columns = qkv_ref.shape
    total = own_ref[...].astype(F32) + got_ref[...].astype(F32)
    for kind in range(kinds):
        qkv_ref[kind] = total[0:rows, kind * columns : (kind + 1) * columns]
    out_ref[...] = total[0:rows, kinds * columns :].T
    small = total[rows:] + near_ref[...].astype(F32) + corner_ref[...].astype(F32)
    dp_index, tensor_index = index_ref[0], index_ref[1]
    width = small.shape[1]
    row = row_ids(small.shape)
    norm = jnp.sum(jnp.where(row == tensor_index, small, 0.0), axis=0, keepdims=True)
    router = jnp.sum(jnp.where(row == width // columns + dp_index, small, 0.0), axis=0, keepdims=True)
    pair = jnp.concatenate([norm, router, jnp.zeros((6, width), F32)], axis=0)
    high = pair.astype(BF)
    parts = jnp.concatenate([high, (pair - high.astype(F32)).astype(BF)], axis=0)
    spots = [spot((rows, width), dp_index * rows), spot((columns, width), tensor_index * columns)]
    moved = [dot(parts, at, LAST) for at in spots]
    norm_ref[...] = moved[0][0:1] + moved[0][8:9]
    router_ref[...] = moved[1][1:2] + moved[1][9:10]


def unpack(index, own, got, near, corner, sizes):
    width = own.shape[1]
    rows, columns = width // sizes[0], width // sizes[1]
    return run(
        unpack_kernel,
        "unpack",
        (index, own, got, near, corner),
        (
            shape_of((width // columns - 1, rows, columns), F32),
            shape_of((columns, rows), F32),
            shape_of((1, rows), F32),
            shape_of((1, columns), F32),
        ),
        4,
        scalars=1,
    )


def swap(value, dp_size, tensor_size, dp_mask, tensor_mask):
    pairs = [
        (d * tensor_size + t, (d ^ dp_mask) * tensor_size + (t ^ tensor_mask))
        for d in range(dp_size)
        for t in range(tensor_size)
    ]
    return lax.ppermute(value, AXES, pairs)


def steps_of(dp_size):
    bits = dp_size.bit_length() - 1
    down = list(range(bits))[::-1]
    return [down, down[-1:] + down[:-1]]


def step_pairs(dp_size, tensor_size, *steps):
    masks = [functools.reduce(lambda mask, step: mask ^ (1 << order[step]), steps, 0) for order in steps_of(dp_size)]
    return [
        (d * tensor_size + t, (d ^ masks[t % 2]) * tensor_size + t)
        for d in range(dp_size)
        for t in range(tensor_size)
    ]


def owners_of(dp_size, dp_index, core):
    both = []
    for order in steps_of(dp_size):
        place = jnp.arange(dp_size, dtype=jnp.int32)
        away = jnp.zeros_like(place)
        for step, bit in enumerate(order):
            away = away | (((place >> step) & 1) << bit)
        both.append(away ^ dp_index)
    return jnp.where(core == 0, both[0], both[1]), jnp.where(core == 0, both[1], both[0])


def exchange(blocks, dp_size):
    shape = blocks.shape
    blocks = blocks.reshape(dp_size, shape[0] // dp_size, shape[1])
    return lax.all_to_all(blocks, "dp", split_axis=0, concat_axis=0, tiled=True).reshape(shape)


def together(*values):
    return lax.optimization_barrier(values)


def send(value, sizes, *steps):
    return lax.ppermute(value, AXES, step_pairs(*sizes, *steps))


def across_core(value, sizes):
    return swap(value, *sizes, 0, 1)


def across_core_after(value, sizes, step):
    pairs = [(a, b ^ 1) for a, b in step_pairs(*sizes, step)]
    return lax.ppermute(value, AXES, pairs)


def high_pairs(dp_size, tensor_size, *steps):
    return [(a, b ^ 2) for a, b in step_pairs(dp_size, tensor_size, *steps)]


def across_high(value, sizes, *steps):
    return lax.ppermute(value, AXES, high_pairs(*sizes, *steps))


def gather_first(block, small, sizes, along):
    rows = block.shape[0]
    far = lax.ppermute(small, AXES, [(p, q ^ 1) for p, q in high_pairs(*sizes)])
    *smalls, block = together(across_core(small, sizes), across_high(small, sizes), far, block)
    small = sum(smalls, small)
    first = jnp.concatenate([block, small], axis=0)
    got, high = together(send(first, sizes, 0), across_high(block, sizes))
    held = jnp.concatenate([block, got[:rows], small + got[rows:]], axis=0)

    got, near, high_got = together(send(held, sizes, 1), across_core(held, sizes), across_high(got[:rows], sizes))
    high = jnp.concatenate([high, high_got], axis=0)
    small = held[2 * rows :] + got[2 * rows :]
    four = jnp.concatenate([held[: 2 * rows], got[: 2 * rows], small], axis=0)

    last, near_two, high_two, high_near, along = together(
        send(four, sizes, 2), across_core(got, sizes), across_high(got[: 2 * rows], sizes), across_core(high, sizes), prepare(*along)
    )
    small = four[4 * rows :] + last[4 * rows :]
    own = (four, last), (near, near_two, across_core(last, sizes))
    high = jnp.concatenate([high, high_two], axis=0)
    return own, (high, high_near, across_core(high_two, sizes)), small, along


def gather_weights_plain(qkv_weight, out_weight, router, norm_params):
    qkv = lax.all_gather(qkv_weight, "dp", axis=1, tiled=True)
    qkv = lax.all_gather(qkv, "tensor", axis=2, tiled=True)
    out_w, router, norms = (
        lax.all_gather(lax.all_gather(w, "dp", axis=1, tiled=True), "tensor", axis=0, tiled=True)
        for w in (out_weight, router, norm_params)
    )
    width = qkv.shape[1]
    half = width // 2
    one = qkv[:, :, :half].transpose(1, 0, 2).reshape(width, 3 * half)
    two = qkv[:, :, half:].transpose(1, 0, 2).reshape(width, 3 * half)
    return one, two, out_w.T, norms.astype(F32), router.T


def add_low(*values):
    return sum(v.astype(F32) for v in values).astype(BF)


def sum_small(values, sizes):
    dp_size, tensor_size = sizes
    mask = 1
    while mask < tensor_size:
        values = values + swap(values, dp_size, tensor_size, 0, mask)
        mask *= 2
    mask = 1
    while mask < dp_size:
        values = values + swap(values, dp_size, tensor_size, mask, 0)
        mask *= 2
    return values


def on_device(
    sizes, tokens, qkv_weight, out_weight, router, norm_params, expert_in, expert_out, cotangent
):
    dp_size, tensor_size = sizes
    dp_index = lax.axis_index("dp")
    tensor_index = lax.axis_index("tensor")
    core = jnp.bitwise_and(tensor_index, 1)
    width = tokens.shape[1]
    half = width // 2
    rows = qkv_weight.shape[1]
    columns = qkv_weight.shape[2]
    experts = dp_size * router.shape[1]
    stepwise = rows % 16 == 0 and sizes == (8, 4)
    owners = ()
    if stepwise:
        owners = owners_of(dp_size, dp_index, core)
        index = jnp.stack([dp_index, tensor_index]).astype(jnp.int32)
        *owners, index, qkv_weight, out_weight, norm_params, router = together(
            *owners, index, qkv_weight, out_weight, norm_params, router
        )
        owners = tuple(owners)
        small = place(index, norm_params, router, experts)
        block = pack(qkv_weight, out_weight)
        (own, near), high, small, (x_img, g_img, unit, inv_std) = gather_first(block, small, sizes, (tokens, cotangent))
        norms, router_t = small[:tensor_size].astype(F32), small[tensor_size : tensor_size + experts]
        high, near_first, near_second = high
        last_high = send(high, sizes, 2)
        normed, qkv_one, mixed, probs_one, weight_one, out_w = attend_first(unit, norms, owners, (own, near))
        last_high, near_second, normed = together(last_high, near_second, normed)
        parts = (high, last_high), (near_first, near_second, across_core(last_high, sizes))
        mixed, out_w, qkv_two, probs_two, weight_two = attend_second(normed, mixed, out_w, owners, parts)
    else:
        x_img, g_img, unit, inv_std = prepare(tokens, cotangent)
        weight_one, weight_two, out_w, norms, router_t = gather_weights_plain(
            qkv_weight, out_weight, router, norm_params
        )
        normed, qkv_one, mixed, probs_one = attend_first(unit, norms, (), (weight_one,))
        mixed, qkv_two, probs_two = attend_second(normed, mixed, None, (), (weight_two,))
    y, normed_two, logits, outgoing = route(x_img, mixed, out_w, norms, router_t, g_img)

    arrived = exchange(outgoing, dp_size)
    across = across_high(arrived, sizes)
    near = across_core(arrived, sizes)
    across, near, ready = lax.optimization_barrier((across, near, tuple(moe_ready(y, logits))))
    keep, keep_high, away, away_high, *kept = run_expert(
        (arrived, across), (near, across_core(across, sizes)), expert_in[0], expert_out[0]
    )
    got = across_high(add_low(keep_high, across_core(away_high, sizes)), sizes)
    got, near, (first_grad, second_grad) = lax.optimization_barrier(
        (got, across_core(away, sizes), tuple(expert_grads(*kept)))
    )
    back = exchange(add_low(keep, near, got), dp_size)

    grad_y, grad_mixed, out_grad_t, small_two = moe_back(
        ready, normed_two, g_img, back, norms, router_t, out_w, mixed, BF if stepwise else F32
    )
    grads_two, *dealt_two = attend_back(
        normed, qkv_two, probs_two, mixed, grad_mixed, out_grad_t, 1, owners, sizes
    )
    grad_part = input_part(grads_two, weight_two)
    if stepwise:
        mine = dealt_two[0].reshape(width, width)
        got, grad_part = together(across_core(dealt_two[1].reshape(width, width), sizes), grad_part)
        cut = [rows * place for place in range(9)]
        terms = mine[: cut[4]], got[: cut[4]]
        along, grad_mixed = together(add_low(mine[cut[4] :], got[cut[4] :]), grad_mixed)
        along = send(along, sizes, 2)
    grads_one, *dealt_one = attend_back(
        normed, qkv_one, probs_one, mixed, grad_mixed, out_grad_t, 0, owners, sizes
    )
    if stepwise:
        along, mine, sent, grads_one = together(along, *dealt_one, grads_one)
        mine, sent = mine.reshape(width, width), sent.reshape(width, width)
        high = add_low(mine[cut[4] :], across_core(sent[cut[4] :], sizes))
        low = add_low(*terms, along)
        high, low, grads_one, sent = together(high, low, grads_one, sent)
        got, near = send(high, sizes, 2), across_core(sent[: cut[4]], sizes)
        got_high, got_low = across_high(low[cut[2] :], sizes), across_high(low[: cut[2]], sizes)
    grad_one, small = input_sum(unit, grads_one, grad_part, weight_one, small_two, stepwise)
    if stepwise:
        near, small = together(near, small)
        smalls = across_high(small, sizes), send(small, sizes, 2), across_high(small, sizes, 2)
        got, got_high, near, smalls = together(got, got_high, near, smalls)
        small = add_low(small, *smalls)
        held = mine[: cut[4]], near, got
        low = add_low(*(h[: cut[2]] for h in held))
        high = [add_low(*(h[cut[2] : cut[4]] for h in held), got_high), small]
        low, high, grad_one = together(low, jnp.concatenate(high, axis=0), grad_one)
    input_grad = input_back(unit, inv_std, grad_y, grad_one, norms)
    output = block_output(y, logits, back)
    if stepwise:
        got, got_low, input_grad = together(send(high, sizes, 1), got_low, input_grad)
        low = add_low(low, got[: cut[2]], got_low)
        small = add_low(small, got[cut[2] :])
        near, corner = across_core(small, sizes), across_core_after(small, sizes, 0)
        got, output, near, corner = together(
            send(jnp.concatenate([low[rows:], small], axis=0), sizes, 0), output, near, corner
        )
        low = jnp.concatenate([low[:rows], small], axis=0)
        qkv_grad, out_grad, norm_grad, router_grad = unpack(index, low, got, near, corner, sizes)
        router_grad = router_grad.reshape(columns, 1)
    else:
        small = sum_small(small, sizes)
        full = jnp.concatenate(
            [dealt_one[0].reshape(width, 3, half), dealt_two[0].reshape(width, 3, half)], axis=2
        ).transpose(1, 0, 2)
        qkv_grad = lax.psum_scatter(full, "dp", scatter_dimension=1, tiled=True)
        qkv_grad = lax.psum_scatter(qkv_grad, "tensor", scatter_dimension=2, tiled=True)
        out_grad = lax.psum_scatter(out_grad_t.T, "dp", scatter_dimension=1, tiled=True)
        out_grad = lax.psum_scatter(out_grad, "tensor", scatter_dimension=0, tiled=True)
        norm_grad = lax.dynamic_slice(small, (tensor_index, dp_index * rows), (1, rows))
        router_grad = lax.dynamic_slice(
            small, (tensor_size + dp_index, tensor_index * columns), (1, columns)
        ).reshape(columns, 1)
    return (
        output,
        input_grad,
        qkv_grad,
        out_grad,
        router_grad,
        norm_grad,
        first_grad[None],
        second_grad[None],
    )


def solution(mesh):
    sizes = (mesh.shape["dp"], mesh.shape["tensor"])
    return jax.shard_map(
        functools.partial(on_device, sizes),
        mesh=mesh,
        in_specs=(
            P(("dp", "tensor"), None),
            P(None, "dp", "tensor"),
            P("tensor", "dp"),
            P("tensor", "dp"),
            P("tensor", "dp"),
            P("dp", None, "tensor"),
            P("dp", "tensor", None),
            P(("dp", "tensor"), None),
        ),
        out_specs=(
            P(("dp", "tensor"), None),
            P(("dp", "tensor"), None),
            P(None, "dp", "tensor"),
            P("tensor", "dp"),
            P("tensor", "dp"),
            P("tensor", "dp"),
            P("dp", None, "tensor"),
            P("dp", "tensor", None),
        ),
        check_vma=False,
    )
```
